32 devices in a mesh: seg: 4 (over y, core), chan: 8 (over z, x).
Axes of the slice: x: 2, y: 2, z: 4, core: 2. Of those that a mesh axis runs over, the one named last changes fastest.
Arguments:
- spectra: bfloat16 [4, 2048, 2, 2048], P('seg', 'chan'), may hold values from -40 to 40
- source_ids: int32 [64], replicated, may hold values from 0 to 2047, as said below
- pair_source: int32 [8192], P('chan'), may hold values from 0 to 63
- pair_offset: int32 [8192], P('chan'), may hold values from -128 to 383, as said below
- pair_counts: int32 [8], P('chan'), may hold values from 256 to 1024, as said below
Outputs:
- correlations: float32 [1024, 8192], P('seg', 'chan')
The draws below stay inside these ranges and needn't reach their ends.
Inputs may be any that keep to these rules, and one draw needn't show every extreme that they name: `source_ids`: distinct channels. `pair_offset`: blocks at the fibre's ends never reach beyond it: block 0 has offsets of 0 or more, the last block offsets under 256. `pair_counts`: one block holds exactly 1024 live slots in every draw; the others hold 256 to 768.
All inputs are finite; a program needn't handle non-finite values.
Results may differ from the reference program's by a relative error of at most 0.0055.
Values may be sent and summed in bfloat16 or wider, within the bound.
No kernel may reach another device: no remote copies, remote signals or barrier semaphores. Data moves between devices by JAX's collectives and lax.ppermute only.
A program may use at most 192 MiB of HBM per device.

```python
import math
import jax
import jax.numpy as jnp
from jax import lax

FREQ = 2048
SOURCES = 64
LAGS = 1024
WBLOCK = 64
CH_DEV = 256
PAIR_CAP = 1024
SEGS = 4
CHANNELS = 2048
BAND = 128
PAIRS_ALL = 8192
N_CHAN = 8


def draw_spectra(key, part):
    key_base = jax.random.fold_in(key, 11)
    key_chan = jax.random.fold_in(key, 12)
    key_bins = jax.random.fold_in(key, 13)
    key_segs = jax.random.fold_in(key, 14)
    base = jnp.clip(jax.random.normal(key_base, (SEGS, CHANNELS, 2, FREQ), jnp.float32), -4.0, 4.0)
    low, high = (math.log(0.3), math.log(3.0))
    chan_gain = jnp.exp(jax.random.uniform(key_chan, (1, CHANNELS, 1, 1), jnp.float32, low, high))
    bin_gain = jnp.exp(jax.random.uniform(key_bins, (1, 1, 1, FREQ), jnp.float32, low, high))
    seg_gain = jnp.exp(jax.random.uniform(key_segs, (SEGS, 1, 1, 1), jnp.float32, -0.5, 0.5))
    return jnp.clip(base * chan_gain * bin_gain * seg_gain, -40.0, 40.0).astype(jnp.bfloat16)


def draw_source_ids(key, part):
    order = jax.random.permutation(jax.random.fold_in(key, 21), CHANNELS)
    return order[:SOURCES].astype(jnp.int32)


def draw_pair_offset(key, part):
    block_total = PAIRS_ALL // PAIR_CAP
    block_index = jnp.arange(block_total, dtype=jnp.int32)[:, None]
    lower = jnp.where(block_index == 0, 0, -BAND).astype(jnp.int32)
    upper = jnp.where(block_index == block_total - 1, CH_DEV, CH_DEV + BAND).astype(jnp.int32)
    lower = jnp.broadcast_to(lower, (block_total, PAIR_CAP))
    upper = jnp.broadcast_to(upper, (block_total, PAIR_CAP))
    picked = jax.random.randint(jax.random.fold_in(key, 31), (block_total, PAIR_CAP), lower, upper, jnp.int32)
    return picked.reshape(PAIRS_ALL)


def draw_pair_counts(key, part):
    block_total = PAIRS_ALL // PAIR_CAP
    counts = jax.random.randint(jax.random.fold_in(key, 41), (block_total,), PAIR_CAP // 4, 3 * PAIR_CAP // 4 + 1, jnp.int32)
    busiest = jax.random.randint(jax.random.fold_in(key, 42), (), 0, block_total, jnp.int32)
    filled = jnp.arange(block_total, dtype=jnp.int32) == busiest
    return jnp.where(filled, PAIR_CAP, counts).astype(jnp.int32)


def plant(entries, rng, smallest, largest):
    extent = entries.shape
    spot = [jax.random.randint(jax.random.fold_in(rng, axis), (), 0, extent[axis]) for axis in range(len(extent))]
    entries = entries.at[tuple(spot)].set(smallest)
    longest = extent.index(max(extent))
    spot[longest] = (spot[longest] + 1) % extent[longest]
    return entries.at[tuple(spot)].set(largest)


def setup_inputs(seed: int = 0) -> dict:
    keys = jax.random.split(jax.random.key(seed), 6)
    spectra = draw_spectra(jax.random.fold_in(keys[5], 71), 0)
    source_ids = draw_source_ids(jax.random.fold_in(keys[5], 71), 0)
    pair_source = plant(jax.random.randint(keys[2], (PAIRS_ALL,), 0, SOURCES), jax.random.fold_in(keys[2], 1), 0, SOURCES - 1).astype(jnp.int32)
    pair_offset = draw_pair_offset(jax.random.fold_in(keys[5], 71), 0)
    pair_counts = draw_pair_counts(jax.random.fold_in(keys[5], 71), 0)
    return dict(spectra=spectra, source_ids=source_ids, pair_source=pair_source, pair_offset=pair_offset, pair_counts=pair_counts)


def whiten(values):
    power = values[..., 0, :] ** 2 + values[..., 1, :] ** 2
    grouped = power.reshape(power.shape[:-1] + (FREQ // WBLOCK, WBLOCK))
    level = lax.optimization_barrier(jnp.mean(grouped, axis=-1))
    inverse = lax.rsqrt(level + 1e-06)
    spread = jnp.repeat(inverse, WBLOCK, axis=-1)
    return (values * spread[..., None, :]).astype(jnp.bfloat16)

def lag_matrix(start, count, total_segs):
    lag_steps = start + jnp.arange(count, dtype=jnp.int32) - LAGS // 2
    bin_steps = jnp.arange(FREQ, dtype=jnp.int32)
    phase = jnp.mod(lag_steps[:, None] * bin_steps[None, :], 2 * FREQ).astype(jnp.float32)
    theta = phase * (math.pi / FREQ)
    factor = 1.0 / math.sqrt(FREQ * total_segs)
    return jnp.concatenate([jnp.cos(theta) * factor, -jnp.sin(theta) * factor], axis=1).astype(jnp.bfloat16)

def cross_spectrum(source_rows, receiver_rows, live_slots):
    src_f = source_rows.astype(jnp.float32)
    rec_f = receiver_rows.astype(jnp.float32)
    real_part = src_f[:, 0] * rec_f[:, 0] + src_f[:, 1] * rec_f[:, 1]
    imag_part = src_f[:, 1] * rec_f[:, 0] - src_f[:, 0] * rec_f[:, 1]
    joined = jnp.concatenate([real_part, imag_part], axis=1).astype(jnp.bfloat16)
    return jnp.where(live_slots[:, None], joined, jnp.zeros_like(joined))

def reference(spectra, source_ids, pair_source, pair_offset, pair_counts):
    whitened = lax.map(lambda segment: whiten(segment.astype(jnp.float32)), spectra)
    source_spec = whitened[:, source_ids]
    lag_table = lag_matrix(0, LAGS, SEGS).astype(jnp.float32)
    blocks_src = pair_source.reshape(N_CHAN, PAIR_CAP)
    blocks_off = pair_offset.reshape(N_CHAN, PAIR_CAP)

    def one_block(packed):
        block_index, block_src, block_off, block_count = packed
        receivers = block_index * CH_DEV + block_off
        live_slots = jnp.arange(PAIR_CAP, dtype=jnp.int32) < block_count
        stacked = jnp.zeros((PAIR_CAP, 2 * FREQ), jnp.float32)
        for segment in range(SEGS):
            cross_spec = cross_spectrum(source_spec[segment][block_src], whitened[segment][receivers], live_slots)
            stacked = stacked + cross_spec.astype(jnp.float32)
        return jnp.dot(lag_table, stacked.T, precision=lax.Precision.HIGHEST, preferred_element_type=jnp.float32)
    results = lax.map(one_block, (jnp.arange(N_CHAN, dtype=jnp.int32), blocks_src, blocks_off, pair_counts))
    return jnp.transpose(results, (1, 0, 2)).reshape(LAGS, N_CHAN * PAIR_CAP)
```

```python
import functools
import math

import jax
import jax.numpy as jnp
from jax import lax
from jax.experimental import pallas as pl
from jax.experimental.pallas import tpu as pltpu
from jax.sharding import PartitionSpec as P

LAGS = 1024
HALF = LAGS // 2
WBLOCK = 64
PICK = 16
BINS_STEP = 512
TABLE_ROWS = 64
VMEM_LIMIT = 56 * 1024 * 1024


def params():
    return pltpu.CompilerParams(vmem_limit_bytes=VMEM_LIMIT)


def cost(flops, moved):
    return pl.CostEstimate(flops=int(flops), bytes_accessed=int(moved), transcendentals=0)


def whole(shape):
    return pl.BlockSpec(shape, lambda *_: (0,) * len(shape))


def pick_kernel(rows_ref, cells_ref, out_ref, sems):
    copies = [
        pltpu.make_async_copy(cells_ref.at[rows_ref[i]], out_ref.at[i], sems.at[i])
        for i in range(PICK)
    ]
    for copy in copies:
        copy.start()
    for copy in copies:
        copy.wait()


def pick_rows(rows, cells):
    shape = (PICK,) + cells.shape[1:]
    return pl.pallas_call(
        pick_kernel,
        out_shape=jax.ShapeDtypeStruct(shape, cells.dtype),
        in_specs=[
            pl.BlockSpec(memory_space=pltpu.SMEM),
            pl.BlockSpec(memory_space=pl.ANY),
        ],
        out_specs=pl.BlockSpec(memory_space=pltpu.VMEM),
        scratch_shapes=[pltpu.SemaphoreType.DMA((PICK,))],
        cost_estimate=cost(0, 2 * PICK * 8192),
        compiler_params=params(),
        name="pick_rows",
    )(rows, cells)


def block_mean(power):
    width = power.shape[1]
    row_group = lax.broadcasted_iota(jnp.int32, (width, width), 0) // WBLOCK
    col_group = lax.broadcasted_iota(jnp.int32, (width, width), 1) // WBLOCK
    spread = jnp.where(row_group == col_group, 1.0 / WBLOCK, 0.0).astype(jnp.bfloat16)
    high = power.astype(jnp.bfloat16)
    rest = power - high.astype(jnp.float32)
    middle = rest.astype(jnp.bfloat16)
    low = (rest - middle.astype(jnp.float32)).astype(jnp.bfloat16)
    total = jnp.dot(low, spread, preferred_element_type=jnp.float32)
    total = total + jnp.dot(middle, spread, preferred_element_type=jnp.float32)
    return total + jnp.dot(high, spread, preferred_element_type=jnp.float32)


def whitened_pair(real, imag):
    inverse = lax.rsqrt(block_mean(real * real + imag * imag) + 1e-06)
    return (real * inverse).astype(jnp.bfloat16), (imag * inverse).astype(jnp.bfloat16)


def whiten_kernel(cells_ref, out_ref):
    real = cells_ref[0].astype(jnp.float32)
    imag = cells_ref[1].astype(jnp.float32)
    out_ref[0], out_ref[1] = whitened_pair(real, imag)


def whiten_rows(cells):
    _, rows, bins = cells.shape
    step = min(256, bins)
    spec = pl.BlockSpec((2, rows, step), lambda i: (0, 0, i))
    return pl.pallas_call(
        whiten_kernel,
        grid=(bins // step,),
        out_shape=jax.ShapeDtypeStruct(cells.shape, jnp.bfloat16),
        in_specs=[spec],
        out_specs=spec,
        cost_estimate=cost(rows * bins * step * 6, 8 * rows * bins),
        compiler_params=params(),
        name="whiten_rows",
    )(cells)


def source_kernel(count, where_ref, *refs):
    chunk_refs, out_ref = refs[:-1], refs[-1]
    held = PICK * len(chunk_refs)
    columns = lax.broadcasted_iota(jnp.int32, (count, held), 1)
    chosen = jnp.where(where_ref[:, 0:1] == columns, 1.0, 0.0).astype(jnp.bfloat16)
    real = jnp.concatenate([ref[0] for ref in chunk_refs], axis=0)
    imag = jnp.concatenate([ref[1] for ref in chunk_refs], axis=0)
    real = jnp.dot(chosen, real, preferred_element_type=jnp.float32)
    imag = jnp.dot(chosen, imag, preferred_element_type=jnp.float32)
    out_ref[0], out_ref[1] = whitened_pair(real, imag)


def source_rows(where, chunks):
    count = where.shape[0]
    bins = chunks[0].shape[2]
    step = min(256, bins)
    where = jnp.broadcast_to(where[:, None], (count, 128))
    return pl.pallas_call(
        functools.partial(source_kernel, count),
        grid=(bins // step,),
        out_shape=jax.ShapeDtypeStruct((2, count, bins), jnp.bfloat16),
        in_specs=[whole((count, 128))]
        + [pl.BlockSpec((2, PICK, step), lambda i: (0, 0, i)) for _ in chunks],
        out_specs=pl.BlockSpec((2, count, step), lambda i: (0, 0, i)),
        cost_estimate=cost(count * bins * step * 8, 4 * bins * (count + PICK * len(chunks))),
        compiler_params=params(),
        name="source_rows",
    )(where, *chunks)


def table_kernel(scale, coarse_ref, fine_ref, cos_ref, sin_ref):
    step = pl.program_id(0)
    cos_a = coarse_ref[0, pl.ds(step, 1), :] * scale
    sin_a = coarse_ref[1, pl.ds(step, 1), :] * scale
    cos_b = fine_ref[0]
    sin_b = fine_ref[1]
    first = lax.broadcasted_iota(jnp.int32, cos_b.shape, 1) == 0
    cos_ref[...] = jnp.where(first, scale, cos_a * cos_b - sin_a * sin_b).astype(jnp.bfloat16)
    sin_ref[...] = (sin_a * cos_b + cos_a * sin_b).astype(jnp.bfloat16)


def lag_tables(bins, scale):
    steps = jnp.arange(HALF, dtype=jnp.int32)
    steps = jnp.where(steps == 0, HALF, steps)

    def circle(rows):
        theta = jnp.mod(rows[:, None] * steps[None, :], 2 * bins).astype(jnp.float32) * (math.pi / bins)
        return jnp.stack([jnp.cos(theta), jnp.sin(theta)])

    count = bins // TABLE_ROWS
    coarse = circle(jnp.arange(count, dtype=jnp.int32) * TABLE_ROWS)
    fine = circle(jnp.arange(TABLE_ROWS, dtype=jnp.int32))
    spec = pl.BlockSpec((TABLE_ROWS, HALF), lambda i: (i, 0))
    shape = jax.ShapeDtypeStruct((bins, HALF), jnp.bfloat16)
    return pl.pallas_call(
        functools.partial(table_kernel, scale),
        grid=(count,),
        out_shape=(shape, shape),
        in_specs=[whole(coarse.shape), whole(fine.shape)],
        out_specs=(spec, spec),
        cost_estimate=cost(bins * HALF * 8, bins * HALF * 4),
        compiler_params=params(),
        name="lag_tables",
    )(coarse, fine)


def prepare_kernel(chan_rows, band, slots, window, scalars_ref, packed_ref, jobs_ref, place_ref):
    turn = scalars_ref[0]
    packed = packed_ref[...]
    live = packed > 0
    code = packed - 1
    offset = (code & (4 * band - 1)) - band
    source = code >> int(math.log2(4 * band))
    below = live & (offset < 0)
    above = live & (offset >= chan_rows)
    inside = live & (offset >= 0) & (offset < chan_rows)
    row = lax.broadcasted_iota(jnp.int32, packed.shape, 0)
    taken = jnp.where(
        row == 0,
        above.astype(jnp.int32),
        jnp.where(row == 1, below.astype(jnp.int32), inside.astype(jnp.int32)),
    )
    taken = jnp.where(row == 3, below.astype(jnp.int32), taken)
    taken = jnp.where(row == 4, above.astype(jnp.int32), taken)
    earlier = lax.broadcasted_iota(jnp.int32, (slots, slots), 0) < lax.broadcasted_iota(
        jnp.int32, (slots, slots), 1
    )
    marks = taken.astype(jnp.float32).astype(jnp.bfloat16)
    rank = jnp.dot(
        marks, jnp.where(earlier, 1.0, 0.0).astype(jnp.bfloat16), preferred_element_type=jnp.float32
    ).astype(jnp.int32)
    totals = jnp.sum(taken.astype(jnp.float32), axis=1, keepdims=True).astype(jnp.int32)
    left_total = totals[0:1, :]
    right_total = totals[1:2, :]

    def done_before(total, index):
        return jnp.minimum(total, index * window)

    left_before = done_before(left_total, turn)
    right_before = done_before(right_total, turn)
    left_now = done_before(left_total, turn + 1) - left_before
    right_now = done_before(right_total, turn + 1) - right_before
    own_before = turn * slots - left_before - right_before
    own_room = slots - left_now - right_now
    held = taken > 0

    def in_window(index):
        shifted = rank[index : index + 1, :] - turn * window
        inside_window = held[index : index + 1, :] & (shifted >= 0) & (shifted < window)
        return shifted, inside_window

    left_rank, left_ok = in_window(0)
    right_rank, right_ok = in_window(1)
    left_pos = jnp.where(left_ok, left_rank, -1)
    right_pos = jnp.where(right_ok, right_rank + window, -1)
    own_rank = rank[2:3, :] - own_before
    own_ok = held[2:3, :] & (own_rank >= 0) & (own_rank < own_room)
    own_pos = own_rank + left_now
    own_pos = jnp.where(own_pos < window, own_pos, own_pos + right_now)
    own_pos = jnp.where(own_ok, own_pos, -1)
    below_rank, below_ok = in_window(3)
    above_rank, above_ok = in_window(4)
    place = jnp.where(below_ok, below_rank + slots, own_pos)
    place = jnp.where(above_ok, above_rank + slots + window, place)
    place_ref[...] = jnp.broadcast_to(place, place_ref.shape)

    wanted = lax.broadcasted_iota(jnp.int32, (slots, slots), 0)
    receiver = jnp.where(row == 0, offset - chan_rows, jnp.where(row == 1, offset + chan_rows, offset))
    jobs = jnp.zeros(jobs_ref.shape, jnp.float32)
    lane_row = lax.broadcasted_iota(jnp.int32, (8, slots), 0)
    for index, position in enumerate((left_pos, right_pos, own_pos)):
        fields = jnp.where(
            lane_row == 0,
            source[index : index + 1, :] + 1,
            jnp.where(lane_row == 1, receiver[index : index + 1, :] + 1, 0),
        )
        fields = jnp.where(position >= 0, fields, 0).astype(jnp.float32).astype(jnp.bfloat16)
        chosen = jnp.where(wanted == position, 1.0, 0.0).astype(jnp.bfloat16)
        jobs = jobs + lax.dot_general(
            chosen, fields, (((1,), (1,)), ((), ())), preferred_element_type=jnp.float32
        )
    jobs_ref[...] = jobs


def prepare(turn, packed_rows, chan_rows, band, window):
    slots = packed_rows[0].shape[0]
    left, right, own = packed_rows
    blank = jnp.zeros_like(own)
    packed = jnp.stack([left, right, own, own, own, blank, blank, blank])
    return pl.pallas_call(
        functools.partial(prepare_kernel, chan_rows, band, slots, window),
        out_shape=(
            jax.ShapeDtypeStruct((slots, 8), jnp.float32),
            jax.ShapeDtypeStruct((8, slots), jnp.int32),
        ),
        in_specs=[
            pl.BlockSpec(memory_space=pltpu.SMEM),
            pl.BlockSpec(memory_space=pltpu.VMEM),
        ],
        out_specs=(
            pl.BlockSpec(memory_space=pltpu.VMEM),
            pl.BlockSpec(memory_space=pltpu.VMEM),
        ),
        cost_estimate=cost(4 * slots * slots * 256, 64 * slots),
        compiler_params=params(),
        name="prepare",
    )(turn.reshape(1), packed)


def transform_kernel(
    shards, scale, me_ref, jobs_ref, source_ref, cells_ref, cos_ref, sin_ref,
    keep_ref, send_ref, pick_src, pick_rec, acc_cos, acc_sin, acc_edge,
):
    step = pl.program_id(0)
    rows = jobs_ref.shape[0]
    bins = cos_ref.shape[0]

    @pl.when(step == 0)
    def _():
        fields = jobs_ref[...].astype(jnp.int32) - 1
        lanes = lax.broadcasted_iota(jnp.int32, pick_src.shape, 1)
        pick_src[...] = jnp.where(fields[:, 0:1] == lanes, 1.0, 0.0).astype(jnp.bfloat16)
        lanes = lax.broadcasted_iota(jnp.int32, pick_rec.shape, 1)
        pick_rec[...] = jnp.where(fields[:, 1:2] == lanes, 1.0, 0.0).astype(jnp.bfloat16)
        acc_cos[...] = jnp.zeros_like(acc_cos)
        acc_sin[...] = jnp.zeros_like(acc_sin)
        acc_edge[...] = jnp.zeros_like(acc_edge)

    eighth = lax.broadcasted_iota(jnp.int32, (1, 128), 1) % 8
    root = math.sqrt(0.5)
    edge = jnp.where((eighth == 1) | (eighth == 7), root, 0.0)
    edge = jnp.where((eighth == 3) | (eighth == 5), -root, edge)
    edge = jnp.where(eighth == 0, 1.0, jnp.where(eighth == 4, -1.0, edge)) * scale
    edge = edge.astype(jnp.bfloat16).astype(jnp.float32)

    tile = 128
    for start in range(0, rows, tile):
        part = pl.ds(start, tile)
        by_src = pick_src[part, :]
        by_rec = pick_rec[part, :]
        sr = jnp.dot(by_src, source_ref[0], preferred_element_type=jnp.float32)
        si = jnp.dot(by_src, source_ref[1], preferred_element_type=jnp.float32)
        rr = jnp.dot(by_rec, cells_ref[0], preferred_element_type=jnp.float32)
        ri = jnp.dot(by_rec, cells_ref[1], preferred_element_type=jnp.float32)
        real = (sr * rr + si * ri).astype(jnp.bfloat16)
        imag = (si * rr - sr * ri).astype(jnp.bfloat16)
        acc_cos[part, :] += jnp.dot(real, cos_ref[...], preferred_element_type=jnp.float32)
        acc_sin[part, :] += jnp.dot(imag, sin_ref[...], preferred_element_type=jnp.float32)
        wide = real.astype(jnp.float32)
        sums = wide[:, 0:128]
        for lane in range(128, bins, 128):
            sums = sums + wide[:, lane : lane + 128]
        acc_edge[part, :] += sums * edge

    @pl.when(step == pl.num_programs(0) - 1)
    def _():
        me = me_ref[0]
        width = LAGS // shards
        even = acc_cos[...]
        odd = acc_sin[...]
        corner = jnp.sum(acc_edge[...], axis=1, keepdims=True)
        first = lax.broadcasted_iota(jnp.int32, even.shape, 1) == 0
        later = even - jnp.where(first, 0.0, odd)
        sooner = jnp.where(first, corner, even) + odd
        sooner = pltpu.roll(sooner, HALF - 1, 1)
        for shard in range(shards):
            half = shards // 2
            if shard < half:
                lane = (half - 1 - shard) * width
                value = sooner[:, lane : lane + width]
            else:
                lane = (shard - half) * width
                value = later[:, lane : lane + width]
            place = me ^ shard

            @pl.when(place % 2 == 0)
            def _():
                keep_ref[place // 2] = value

            @pl.when(place % 2 == 1)
            def _():
                send_ref[place // 2] = value.astype(jnp.bfloat16)


def transform(me, jobs, sources, cells, tables, shards, scale):
    rows = jobs.shape[0]
    bins = cells.shape[2]
    step = min(BINS_STEP, bins)
    width = LAGS // shards
    shape = (shards // 2, rows, width)
    table_spec = pl.BlockSpec((step, HALF), lambda i: (i, 0))
    return pl.pallas_call(
        functools.partial(transform_kernel, shards, scale),
        grid=(bins // step,),
        out_shape=(
            jax.ShapeDtypeStruct(shape, jnp.float32),
            jax.ShapeDtypeStruct(shape, jnp.bfloat16),
        ),
        in_specs=[
            pl.BlockSpec(memory_space=pltpu.SMEM),
            whole(jobs.shape),
            pl.BlockSpec((2, sources.shape[1], step), lambda i: (0, 0, i)),
            pl.BlockSpec((2, cells.shape[1], step), lambda i: (0, 0, i)),
            table_spec,
            table_spec,
        ],
        out_specs=(whole(shape), whole(shape)),
        scratch_shapes=[
            pltpu.VMEM((rows, sources.shape[1]), jnp.bfloat16),
            pltpu.VMEM((rows, cells.shape[1]), jnp.bfloat16),
            pltpu.VMEM((rows, HALF), jnp.float32),
            pltpu.VMEM((rows, HALF), jnp.float32),
            pltpu.VMEM((rows, 128), jnp.float32),
        ],
        cost_estimate=cost(rows * bins * 4 * (HALF + 512), 8 * bins * HALF),
        compiler_params=params(),
        name="transform",
    )(me.reshape(1), jobs, sources, cells, *tables)


def reduce_over_seg(keep, send):
    size = lax.axis_size("seg")
    bit = 1
    while True:
        got = lax.ppermute(send, "seg", [(i, i ^ bit) for i in range(size)])
        total = keep + got.astype(jnp.float32)
        if total.shape[0] == 1:
            return total[0].astype(jnp.bfloat16)
        keep = total[0::2]
        send = total[1::2].astype(jnp.bfloat16)
        bit *= 2


def place_kernel(flip_ref, place_ref, *refs):
    parts, out_ref = refs[:-1], refs[-1]
    width, slots = out_ref.shape
    flip = flip_ref[0]
    rows = lax.broadcasted_iota(jnp.int32, (width, width), 0)
    columns = lax.broadcasted_iota(jnp.int32, (width, width), 1)
    wanted = jnp.where(flip > 0, width - 1 - rows, rows)
    turned = jnp.where(wanted == columns, 1.0, 0.0).astype(jnp.bfloat16)
    total = jnp.zeros((width, slots), jnp.float32)
    start = 0
    for ref in parts:
        count = ref.shape[0]
        spot = lax.broadcasted_iota(jnp.int32, (count, slots), 0) + start
        chosen = jnp.where(spot == place_ref[0:1, :], 1.0, 0.0).astype(jnp.bfloat16)
        across = lax.dot_general(
            turned, ref[...], (((1,), (1,)), ((), ())), preferred_element_type=jnp.float32
        ).astype(jnp.bfloat16)
        total = total + jnp.dot(across, chosen, preferred_element_type=jnp.float32)
        start += count
    out_ref[...] = total


def place_rows(flip, place, parts):
    width = parts[0].shape[1]
    slots = place.shape[1]
    return pl.pallas_call(
        place_kernel,
        out_shape=jax.ShapeDtypeStruct((width, slots), jnp.float32),
        in_specs=[pl.BlockSpec(memory_space=pltpu.SMEM)]
        + [pl.BlockSpec(memory_space=pltpu.VMEM) for _ in range(1 + len(parts))],
        out_specs=pl.BlockSpec(memory_space=pltpu.VMEM),
        cost_estimate=cost(4 * slots * width * slots, 4 * slots * width),
        compiler_params=params(),
        name="place_rows",
    )(flip.reshape(1), place, *parts)


def per_device(spectra, source_ids, pair_source, pair_offset, pair_counts):
    chan_rows = spectra.shape[1]
    bins = spectra.shape[3]
    band = chan_rows // 2
    seg_size = lax.axis_size("seg")
    chan_size = lax.axis_size("chan")
    slots = pair_source.shape[0]
    window = 3 * slots // 8
    scale = 1.0 / math.sqrt(bins * seg_size)
    me_seg = lax.axis_index("seg")
    me_chan = lax.axis_index("chan")
    cells = spectra[0]

    live = jnp.arange(slots, dtype=jnp.int32) < pair_counts[0]
    packed = jnp.where(live, 1 + pair_source * (4 * band) + pair_offset + band, 0)
    rightward = [(i, i + 1) for i in range(chan_size - 1)]
    leftward = [(i + 1, i) for i in range(chan_size - 1)]
    packed_rows = (
        lax.ppermute(packed, "chan", rightward),
        lax.ppermute(packed, "chan", leftward),
        packed,
    )

    owner = source_ids // chan_rows
    same = owner[:, None] == owner[None, :]
    index = jnp.arange(source_ids.shape[0], dtype=jnp.int32)
    rank = jnp.sum((same & (index[None, :] < index[:, None])).astype(jnp.int32), axis=1)
    ring = list(range(0, chan_size, 2)) + list(range(1, chan_size, 2))[::-1]

    def ring_place(block):
        return jnp.where(block % 2 == 0, block // 2, chan_size - 1 - block // 2)

    forward_steps = chan_size // 2
    distance = (ring_place(me_chan) - ring_place(owner)) % chan_size
    hop = jnp.where(distance <= forward_steps, distance, forward_steps + chan_size - distance)
    source_turns = (jnp.max(rank) + PICK) // PICK
    ahead = [(ring[i], ring[(i + 1) % chan_size]) for i in range(chan_size)]
    back = [(b, a) for a, b in ahead]

    def gather_sources(turn):
        wanted = turn * PICK + jnp.arange(PICK, dtype=jnp.int32)
        mine = (owner[None, :] == me_chan) & (rank[None, :] == wanted[:, None])
        rows = jnp.sum(jnp.where(mine, source_ids[None, :] - me_chan * chan_rows, 0), axis=1)
        own = jnp.transpose(pick_rows(rows, cells), (1, 0, 2))
        forward, backward = [own], [own]
        for step in range(1, forward_steps + 1):
            forward.append(lax.ppermute(forward[-1], "chan", ahead))
            if step < chan_size - forward_steps:
                backward.append(lax.ppermute(backward[-1], "chan", back))
        spot = jnp.where(rank // PICK == turn, hop * PICK + rank % PICK, -1)
        return source_rows(spot, forward + backward[1:])

    flat = jnp.transpose(cells, (1, 0, 2))
    whitened = whiten_rows(flat)
    tables = lag_tables(bins, scale)

    def one_turn(source_turn, pair_turn):
        sources = gather_sources(source_turn)
        jobs, place = prepare(pair_turn, packed_rows, chan_rows, band, window)
        reduced = []
        returned = []
        bounds = (0, window, 2 * window, slots)
        for part in range(3):
            piece = jobs[bounds[part] : bounds[part + 1]]
            total = reduce_over_seg(
                *transform(me_seg, piece, sources, whitened, tables, seg_size, scale)
            )
            reduced.append(total)
            if part == 0:
                returned.append(lax.ppermute(total, "chan", leftward))
            if part == 1:
                returned.append(lax.ppermute(total, "chan", rightward))
        flip = (me_seg < seg_size // 2).astype(jnp.int32)
        return place_rows(flip, place, reduced + returned[::-1])

    offsets = [((row - 1) & (4 * band - 1)) - band for row in packed_rows]
    lives = [row > 0 for row in packed_rows]
    left_total = jnp.sum((lives[0] & (offsets[0] >= chan_rows)).astype(jnp.int32))
    right_total = jnp.sum((lives[1] & (offsets[1] < 0)).astype(jnp.int32))
    own_total = jnp.sum((lives[2] & (offsets[2] >= 0) & (offsets[2] < chan_rows)).astype(jnp.int32))
    needed = jnp.maximum(
        (jnp.maximum(left_total, right_total) + window - 1) // window,
        (left_total + right_total + own_total + slots - 1) // slots,
    )
    pair_turns = jnp.maximum(lax.pmax(needed, "chan"), 1)
    turns = source_turns * pair_turns

    zero = jnp.int32(0)
    first = one_turn(zero, zero)

    def further(state):
        turn, total = state
        return turn + 1, total + one_turn(turn // pair_turns, turn % pair_turns)

    return lax.while_loop(lambda state: state[0] < turns, further, (jnp.int32(1), first))[1]


def solution(mesh):
    in_specs = (P("seg", "chan", None, None), P(), P("chan"), P("chan"), P("chan"))
    out_specs = P("seg", "chan")
    return jax.shard_map(
        per_device, mesh=mesh, in_specs=in_specs, out_specs=out_specs, check_vma=False
    )
```

```python
import functools
import math

import jax
import jax.numpy as jnp
from jax import lax
from jax.experimental import pallas as pl
from jax.experimental.pallas import tpu as pltpu
from jax.sharding import PartitionSpec as P

LAGS = 1024
HALF = LAGS // 2
WBLOCK = 64
PICK = 16
BINS_STEP = 512
TABLE_ROWS = 64
VMEM_LIMIT = 56 * 1024 * 1024


def params():
    return pltpu.CompilerParams(vmem_limit_bytes=VMEM_LIMIT)


def cost(flops, moved):
    return pl.CostEstimate(flops=int(flops), bytes_accessed=int(moved), transcendentals=0)


def whole(shape):
    return pl.BlockSpec(shape, lambda *_: (0,) * len(shape))


def pick_kernel(chan_rows, scalars_ref, ids_ref, cells_ref, out_ref, rows_ref, held_ref, sems):
    first = scalars_ref[0] * chan_rows
    turn = scalars_ref[1]
    for i in range(PICK):
        rows_ref[i] = 0

    def look(i, rank):
        row = ids_ref[i] - first
        mine = (row >= 0) & (row < chan_rows)
        spot = rank - turn * PICK
        rows_ref[jnp.where(mine & (spot >= 0) & (spot < PICK), spot, PICK)] = row
        return rank + mine.astype(jnp.int32)

    lax.fori_loop(0, ids_ref.shape[0], look, jnp.int32(0))
    copies = [
        pltpu.make_async_copy(cells_ref.at[0, rows_ref[i]], held_ref.at[i], sems.at[i])
        for i in range(PICK)
    ]
    for copy in copies:
        copy.start()
    for copy in copies:
        copy.wait()
    out_ref[0] = held_ref[:, 0, :]
    out_ref[1] = held_ref[:, 1, :]


def pick_rows(scalars, source_ids, spectra):
    _, chan_rows, parts, bins = spectra.shape
    return pl.pallas_call(
        functools.partial(pick_kernel, chan_rows),
        out_shape=jax.ShapeDtypeStruct((parts, PICK, bins), spectra.dtype),
        in_specs=[
            pl.BlockSpec(memory_space=pltpu.SMEM),
            pl.BlockSpec(memory_space=pltpu.SMEM),
            pl.BlockSpec(memory_space=pl.ANY),
        ],
        out_specs=pl.BlockSpec(memory_space=pltpu.VMEM),
        scratch_shapes=[
            pltpu.SMEM((PICK + 1,), jnp.int32),
            pltpu.VMEM((PICK, parts, bins), spectra.dtype),
            pltpu.SemaphoreType.DMA((PICK,)),
        ],
        cost_estimate=cost(0, 2 * PICK * 8192),
        compiler_params=params(),
        name="pick_rows",
    )(scalars, source_ids, spectra)


def block_mean(power):
    width = power.shape[1]
    row_group = lax.broadcasted_iota(jnp.int32, (width, width), 0) // WBLOCK
    col_group = lax.broadcasted_iota(jnp.int32, (width, width), 1) // WBLOCK
    spread = jnp.where(row_group == col_group, 1.0 / WBLOCK, 0.0).astype(jnp.bfloat16)
    high = power.astype(jnp.bfloat16)
    low = (power - high.astype(jnp.float32)).astype(jnp.bfloat16)
    total = jnp.dot(low, spread, preferred_element_type=jnp.float32)
    return total + jnp.dot(high, spread, preferred_element_type=jnp.float32)


def whitened_pair(real, imag):
    inverse = lax.rsqrt(block_mean(real * real + imag * imag) + 1e-06)
    return (real * inverse).astype(jnp.bfloat16), (imag * inverse).astype(jnp.bfloat16)


def whiten_kernel(cells_ref, after_ref, out_ref):
    for start in range(0, cells_ref.shape[2], 256):
        lanes = pl.ds(start, 256)
        real = cells_ref[0, :, lanes].astype(jnp.float32)
        imag = cells_ref[1, :, lanes].astype(jnp.float32)
        out_ref[0, :, lanes], out_ref[1, :, lanes] = whitened_pair(real, imag)


def whiten_rows(cells, after):
    _, rows, bins = cells.shape
    spec = pl.BlockSpec((2, rows, BINS_STEP), lambda i: (0, 0, i))
    return pl.pallas_call(
        whiten_kernel,
        grid=(bins // BINS_STEP,),
        out_shape=jax.ShapeDtypeStruct(cells.shape, jnp.bfloat16),
        in_specs=[spec, pl.BlockSpec(memory_space=pl.ANY)],
        out_specs=spec,
        cost_estimate=cost(rows * bins * 256 * 4, 8 * rows * bins),
        compiler_params=params(),
        name="whiten_rows",
    )(cells, after)


def source_kernel(chan_rows, chan_size, scalars_ref, ids_ref, *refs):
    chunk_refs, out_ref, turns_ref = refs[:-2], refs[-2], refs[-1]
    me = scalars_ref[0]
    turn = scalars_ref[1]
    count = ids_ref.shape[1]
    shift = chan_rows.bit_length() - 1
    ids_row = jnp.broadcast_to(ids_ref[...], (count, count))
    rows = lax.broadcasted_iota(jnp.int32, (count, count), 0)
    columns = lax.broadcasted_iota(jnp.int32, (count, count), 1)
    ids = jnp.sum(jnp.where(rows == columns, ids_row, 0).astype(jnp.float32), axis=1, keepdims=True)
    owner = jnp.broadcast_to(ids.astype(jnp.int32) >> shift, (count, count))
    earlier = (owner == (ids_row >> shift)) & (columns < rows)
    rank = jnp.sum(jnp.where(earlier, 1.0, 0.0), axis=1, keepdims=True)
    turns_ref[0] = (jnp.max(rank).astype(jnp.int32) + PICK) // PICK
    rank = rank.astype(jnp.int32) - turn * PICK
    owner = owner[:, 0:1]

    def ring_place(block):
        return jnp.where(block % 2 == 0, block >> 1, chan_size - 1 - (block >> 1))

    steps = chan_size // 2
    distance = ring_place(me) - ring_place(owner)
    distance = jnp.where(distance < 0, distance + chan_size, distance)
    hop = jnp.where(distance <= steps, distance, steps + chan_size - distance)
    spot = jnp.where((rank >= 0) & (rank < PICK), hop * PICK + rank, -1)
    held = PICK * len(chunk_refs)
    lanes = lax.broadcasted_iota(jnp.int32, (count, held), 1)
    chosen = jnp.where(spot == lanes, 1.0, 0.0).astype(jnp.bfloat16)
    for start in range(0, out_ref.shape[2], 256):
        lanes = pl.ds(start, 256)
        real = jnp.concatenate([ref[0, :, lanes] for ref in chunk_refs], axis=0)
        imag = jnp.concatenate([ref[1, :, lanes] for ref in chunk_refs], axis=0)
        real = jnp.dot(chosen, real, preferred_element_type=jnp.float32)
        imag = jnp.dot(chosen, imag, preferred_element_type=jnp.float32)
        out_ref[0, :, lanes], out_ref[1, :, lanes] = whitened_pair(real, imag)


def source_rows(scalars, source_ids, chunks, chan_rows, chan_size):
    count = source_ids.shape[0]
    bins = chunks[0].shape[2]
    vmem = pl.BlockSpec(memory_space=pltpu.VMEM)
    smem = pl.BlockSpec(memory_space=pltpu.SMEM)
    return pl.pallas_call(
        functools.partial(source_kernel, chan_rows, chan_size),
        out_shape=(
            jax.ShapeDtypeStruct((2, count, bins), jnp.bfloat16),
            jax.ShapeDtypeStruct((1,), jnp.int32),
        ),
        in_specs=[smem, vmem] + [vmem for _ in chunks],
        out_specs=(vmem, smem),
        cost_estimate=cost(count * bins * 256 * 8, 4 * bins * (count + PICK * len(chunks))),
        compiler_params=params(),
        name="source_rows",
    )(scalars, source_ids.reshape(1, count), *chunks)


def table_kernel(scale, all_bins, after_ref, cos_ref, sin_ref, coarse_ref, fine_ref):
    step = pl.program_id(0)
    groups = cos_ref.shape[0] // TABLE_ROWS

    @pl.when(step == 0)
    def _():
        def circle(ref, stride, factor):
            shape = ref.shape[1:]
            bins = lax.broadcasted_iota(jnp.int32, shape, 0) * stride
            lags = lax.broadcasted_iota(jnp.int32, shape, 1)
            lags = jnp.where(lags == 0, HALF, lags)
            theta = ((bins * lags) & (2 * all_bins - 1)).astype(jnp.float32) * (math.pi / all_bins)
            ref[0] = jnp.cos(theta) * factor
            ref[1] = jnp.sin(theta) * factor

        circle(coarse_ref, TABLE_ROWS, scale)
        circle(fine_ref, 1, 1.0)

    cos_b = fine_ref[0]
    sin_b = fine_ref[1]
    first = lax.broadcasted_iota(jnp.int32, cos_b.shape, 1) == 0
    for group in range(groups):
        cos_a = coarse_ref[0, pl.ds(step * groups + group, 1), :]
        sin_a = coarse_ref[1, pl.ds(step * groups + group, 1), :]
        rows = pl.ds(group * TABLE_ROWS, TABLE_ROWS)
        cos = jnp.where(first, scale, cos_a * cos_b - sin_a * sin_b)
        cos_ref[rows, :] = cos.astype(jnp.bfloat16)
        sin_ref[rows, :] = (sin_a * cos_b + cos_a * sin_b).astype(jnp.bfloat16)


def lag_tables(bins, scale, after):
    spec = pl.BlockSpec((BINS_STEP, HALF), lambda i: (i, 0))
    shape = jax.ShapeDtypeStruct((bins, HALF), jnp.bfloat16)
    return pl.pallas_call(
        functools.partial(table_kernel, scale, bins),
        grid=(bins // BINS_STEP,),
        out_shape=(shape, shape),
        in_specs=[pl.BlockSpec(memory_space=pl.ANY)],
        out_specs=(spec, spec),
        scratch_shapes=[
            pltpu.VMEM((2, bins // TABLE_ROWS, HALF), jnp.float32),
            pltpu.VMEM((2, TABLE_ROWS, HALF), jnp.float32),
        ],
        cost_estimate=cost(bins * HALF * 8, bins * HALF * 4),
        compiler_params=params(),
        name="lag_tables",
    )(after)


def prepare_kernel(
    chan_rows, band, window, scalars_ref, packed_ref, after_ref, src_ref, rec_ref, place_ref, turns_ref
):
    me = scalars_ref[0]
    turn = scalars_ref[1]
    blocks, slots = packed_ref.shape

    def sort_out(packed):
        live = packed > 0
        code = packed - 1
        offset = (code & (4 * band - 1)) - band
        source = code >> ((4 * band).bit_length() - 1)
        below = jnp.where(live & (offset < 0), 1.0, 0.0)
        above = jnp.where(live & (offset >= chan_rows), 1.0, 0.0)
        inside = jnp.where(live & (offset >= 0) & (offset < chan_rows), 1.0, 0.0)
        return offset, source, below, above, inside

    _, _, below, above, inside = sort_out(packed_ref[...])

    def totals(marks):
        return jnp.broadcast_to(jnp.sum(marks, axis=1, keepdims=True), (blocks, 128))

    block = lax.broadcasted_iota(jnp.int32, (blocks, 128), 0)
    from_left = jnp.where(block == 0, 0.0, pltpu.roll(totals(above), 1, 0))
    from_right = jnp.where(block == blocks - 1, 0.0, pltpu.roll(totals(below), blocks - 1, 0))
    aside = jnp.max(jnp.maximum(from_left, from_right)).astype(jnp.int32)
    whole_sum = jnp.max(from_left + from_right + totals(inside)).astype(jnp.int32)
    needed = jnp.maximum((aside + window - 1) // window, (whole_sum + slots - 1) // slots)
    turns_ref[0] = jnp.maximum(needed, 1)

    left = jnp.where(me > 0, packed_ref[pl.ds(jnp.maximum(me - 1, 0), 1), :], 0)
    right = jnp.where(me < blocks - 1, packed_ref[pl.ds(jnp.minimum(me + 1, blocks - 1), 1), :], 0)
    own = packed_ref[pl.ds(me, 1), :]
    row = lax.broadcasted_iota(jnp.int32, (8, slots), 0)
    packed = jnp.where(row == 0, left, jnp.where(row == 1, right, jnp.where(row < 5, own, 0)))
    offset, source, below, above, inside = sort_out(packed)
    taken = jnp.where((row == 0) | (row == 4), above, jnp.where((row == 1) | (row == 3), below, inside))
    earlier = lax.broadcasted_iota(jnp.int32, (slots, slots), 0) < lax.broadcasted_iota(
        jnp.int32, (slots, slots), 1
    )
    rank = jnp.dot(
        taken.astype(jnp.bfloat16),
        jnp.where(earlier, 1.0, 0.0).astype(jnp.bfloat16),
        preferred_element_type=jnp.float32,
    ).astype(jnp.int32)
    total = jnp.sum(taken, axis=1, keepdims=True).astype(jnp.int32)
    left_total = total[0:1, :]
    right_total = total[1:2, :]

    def done_before(amount, index):
        return jnp.minimum(amount, index * window)

    left_before = done_before(left_total, turn)
    right_before = done_before(right_total, turn)
    left_now = done_before(left_total, turn + 1) - left_before
    right_now = done_before(right_total, turn + 1) - right_before
    own_before = turn * slots - left_before - right_before
    own_room = slots - left_now - right_now
    held = taken > 0

    def in_window(index):
        shifted = rank[index : index + 1, :] - turn * window
        return shifted, held[index : index + 1, :] & (shifted >= 0) & (shifted < window)

    left_rank, left_ok = in_window(0)
    right_rank, right_ok = in_window(1)
    left_pos = jnp.where(left_ok, left_rank, -1)
    right_pos = jnp.where(right_ok, right_rank + window, -1)
    own_rank = rank[2:3, :] - own_before
    own_ok = held[2:3, :] & (own_rank >= 0) & (own_rank < own_room)
    own_pos = own_rank + left_now
    own_pos = jnp.where(own_pos < window, own_pos, own_pos + right_now)
    own_pos = jnp.where(own_ok, own_pos, -1)
    below_rank, below_ok = in_window(3)
    above_rank, above_ok = in_window(4)
    place = jnp.where(below_ok, below_rank + slots, own_pos)
    place = jnp.where(above_ok, above_rank + slots + window, place)
    place_ref[...] = jnp.broadcast_to(place, place_ref.shape)

    wanted = lax.broadcasted_iota(jnp.int32, (slots, slots), 0)
    receiver = jnp.where(row == 0, offset - chan_rows, jnp.where(row == 1, offset + chan_rows, offset))
    jobs = jnp.zeros((slots, 8), jnp.float32)
    for index, position in enumerate((left_pos, right_pos, own_pos)):
        fields = jnp.where(
            row == 0,
            source[index : index + 1, :] + 1,
            jnp.where(row == 1, receiver[index : index + 1, :] + 1, 0),
        )
        fields = jnp.where(position >= 0, fields, 0).astype(jnp.float32).astype(jnp.bfloat16)
        chosen = jnp.where(wanted == position, 1.0, 0.0).astype(jnp.bfloat16)
        jobs = jobs + lax.dot_general(
            chosen, fields, (((1,), (1,)), ((), ())), preferred_element_type=jnp.float32
        )
    jobs = jobs.astype(jnp.int32) - 1
    lanes = lax.broadcasted_iota(jnp.int32, src_ref.shape, 1)
    src_ref[...] = jnp.where(jobs[:, 0:1] == lanes, 1.0, 0.0).astype(jnp.bfloat16)
    lanes = lax.broadcasted_iota(jnp.int32, rec_ref.shape, 1)
    rec_ref[...] = jnp.where(jobs[:, 1:2] == lanes, 1.0, 0.0).astype(jnp.bfloat16)


def prepare(scalars, packed, source_count, chan_rows, band, window, after):
    slots = packed.shape[1]
    vmem = pl.BlockSpec(memory_space=pltpu.VMEM)
    smem = pl.BlockSpec(memory_space=pltpu.SMEM)
    return pl.pallas_call(
        functools.partial(prepare_kernel, chan_rows, band, window),
        out_shape=(
            jax.ShapeDtypeStruct((slots, source_count), jnp.bfloat16),
            jax.ShapeDtypeStruct((slots, chan_rows), jnp.bfloat16),
            jax.ShapeDtypeStruct((8, slots), jnp.int32),
            jax.ShapeDtypeStruct((1,), jnp.int32),
        ),
        in_specs=[smem, vmem, pl.BlockSpec(memory_space=pl.ANY)],
        out_specs=(vmem, vmem, vmem, smem),
        cost_estimate=cost(4 * slots * slots * 256, 64 * slots),
        compiler_params=params(),
        name="prepare",
    )(scalars, packed, after)


def transform_kernel(
    shards, scale, start, me_ref, src_ref, rec_ref, source_ref, cells_ref, cos_ref, sin_ref, after_ref,
    keep_ref, send_ref, acc_cos, acc_sin, acc_edge,
):
    step = pl.program_id(0)
    rows = acc_cos.shape[0]
    bins = cos_ref.shape[0]

    @pl.when(step == 0)
    def _():
        acc_cos[...] = jnp.zeros_like(acc_cos)
        acc_sin[...] = jnp.zeros_like(acc_sin)
        acc_edge[...] = jnp.zeros_like(acc_edge)

    eighth = lax.broadcasted_iota(jnp.int32, (1, 128), 1) % 8
    root = math.sqrt(0.5)
    edge = jnp.where((eighth == 1) | (eighth == 7), root, 0.0)
    edge = jnp.where((eighth == 3) | (eighth == 5), -root, edge)
    edge = jnp.where(eighth == 0, 1.0, jnp.where(eighth == 4, -1.0, edge)) * scale
    edge = edge.astype(jnp.bfloat16).astype(jnp.float32)

    by_src = src_ref[pl.ds(start, rows), :]
    by_rec = rec_ref[pl.ds(start, rows), :]
    sr = jnp.dot(by_src, source_ref[0], preferred_element_type=jnp.float32)
    si = jnp.dot(by_src, source_ref[1], preferred_element_type=jnp.float32)
    rr = jnp.dot(by_rec, cells_ref[0], preferred_element_type=jnp.float32)
    ri = jnp.dot(by_rec, cells_ref[1], preferred_element_type=jnp.float32)
    real = (sr * rr + si * ri).astype(jnp.bfloat16)
    imag = (si * rr - sr * ri).astype(jnp.bfloat16)
    acc_cos[...] += jnp.dot(real, cos_ref[...], preferred_element_type=jnp.float32)
    acc_sin[...] += jnp.dot(imag, sin_ref[...], preferred_element_type=jnp.float32)
    wide = real.astype(jnp.float32)
    sums = wide[:, 0:128]
    for lane in range(128, bins, 128):
        sums = sums + wide[:, lane : lane + 128]
    acc_edge[...] += sums * edge

    @pl.when(step == pl.num_programs(0) - 1)
    def _():
        me = me_ref[0]
        width = LAGS // shards
        even = acc_cos[...]
        odd = acc_sin[...]
        corner = jnp.sum(acc_edge[...], axis=1, keepdims=True)
        first = lax.broadcasted_iota(jnp.int32, even.shape, 1) == 0
        later = even - jnp.where(first, 0.0, odd)
        sooner = jnp.where(first, corner, even) + odd
        sooner = pltpu.roll(sooner, HALF - 1, 1)
        for shard in range(shards):
            half = shards // 2
            if shard < half:
                lane = (half - 1 - shard) * width
                value = sooner[:, lane : lane + width]
            else:
                lane = (shard - half) * width
                value = later[:, lane : lane + width]
            place = me ^ shard

            @pl.when(place % 2 == 0)
            def _():
                keep_ref[place // 2] = value

            @pl.when(place % 2 == 1)
            def _():
                send_ref[place // 2] = value.astype(jnp.bfloat16)


def transform(me, picks, sources, cells, tables, shards, scale, start, rows, after):
    bins = cells.shape[2]
    step = BINS_STEP
    width = LAGS // shards
    shape = (shards // 2, rows, width)
    table_spec = pl.BlockSpec((step, HALF), lambda i: (i, 0))
    return pl.pallas_call(
        functools.partial(transform_kernel, shards, scale, start),
        grid=(bins // step,),
        out_shape=(
            jax.ShapeDtypeStruct(shape, jnp.float32),
            jax.ShapeDtypeStruct(shape, jnp.bfloat16),
        ),
        in_specs=[
            pl.BlockSpec(memory_space=pltpu.SMEM),
            whole(picks[0].shape),
            whole(picks[1].shape),
            pl.BlockSpec((2, sources.shape[1], step), lambda i: (0, 0, i)),
            pl.BlockSpec((2, cells.shape[1], step), lambda i: (0, 0, i)),
            table_spec,
            table_spec,
            pl.BlockSpec(memory_space=pl.ANY),
        ],
        out_specs=(whole(shape), whole(shape)),
        scratch_shapes=[
            pltpu.VMEM((rows, HALF), jnp.float32),
            pltpu.VMEM((rows, HALF), jnp.float32),
            pltpu.VMEM((rows, 128), jnp.float32),
        ],
        cost_estimate=cost(rows * bins * 4 * (HALF + 512), 8 * bins * HALF),
        compiler_params=params(),
        name="transform",
    )(me.reshape(1), *picks, sources, cells, *tables, after)


def reduce_over_seg(keep, send):
    size = lax.axis_size("seg")
    bit = 1
    while True:
        got = lax.ppermute(send, "seg", [(i, i ^ bit) for i in range(size)])
        total = keep + got.astype(jnp.float32)
        if total.shape[0] == 1:
            return total[0].astype(jnp.bfloat16)
        keep = total[0::2]
        send = total[1::2].astype(jnp.bfloat16)
        bit *= 2


def place_kernel(flip_ref, place_ref, *refs):
    parts, out_ref = refs[:-1], refs[-1]
    width, slots = out_ref.shape
    flip = flip_ref[0]
    rows = lax.broadcasted_iota(jnp.int32, (width, width), 0)
    columns = lax.broadcasted_iota(jnp.int32, (width, width), 1)
    wanted = jnp.where(flip > 0, width - 1 - rows, rows)
    turned = jnp.where(wanted == columns, 1.0, 0.0).astype(jnp.bfloat16)
    total = jnp.zeros((width, slots), jnp.float32)
    start = 0
    for ref in parts:
        count = ref.shape[0]
        spot = lax.broadcasted_iota(jnp.int32, (count, slots), 0) + start
        chosen = jnp.where(spot == place_ref[0:1, :], 1.0, 0.0).astype(jnp.bfloat16)
        across = lax.dot_general(
            turned, ref[...], (((1,), (1,)), ((), ())), preferred_element_type=jnp.float32
        ).astype(jnp.bfloat16)
        total = total + jnp.dot(across, chosen, preferred_element_type=jnp.float32)
        start += count
    out_ref[...] = total


def place_rows(flip, place, parts):
    width = parts[0].shape[1]
    slots = place.shape[1]
    return pl.pallas_call(
        place_kernel,
        out_shape=jax.ShapeDtypeStruct((width, slots), jnp.float32),
        in_specs=[pl.BlockSpec(memory_space=pltpu.SMEM)]
        + [pl.BlockSpec(memory_space=pltpu.VMEM) for _ in range(1 + len(parts))],
        out_specs=pl.BlockSpec(memory_space=pltpu.VMEM),
        cost_estimate=cost(4 * slots * width * slots, 4 * slots * width),
        compiler_params=params(),
        name="place_rows",
    )(flip.reshape(1), place, *parts)


def per_device(spectra, source_ids, pair_source, pair_offset, pair_counts):
    chan_rows = spectra.shape[1]
    bins = spectra.shape[3]
    band = chan_rows // 2
    seg_size = lax.axis_size("seg")
    chan_size = lax.axis_size("chan")
    slots = pair_source.shape[0]
    window = 3 * slots // 8
    scale = 1.0 / math.sqrt(bins * seg_size)
    me_seg = lax.axis_index("seg")
    me_chan = lax.axis_index("chan")

    live = jnp.arange(slots, dtype=jnp.int32) < pair_counts[0]
    packed = jnp.where(live, 1 + pair_source * (4 * band) + pair_offset + band, 0)
    packed = lax.all_gather(packed, "chan")

    ring = list(range(0, chan_size, 2)) + list(range(1, chan_size, 2))[::-1]
    ahead = [(ring[i], ring[(i + 1) % chan_size]) for i in range(chan_size)]
    back = [(b, a) for a, b in ahead]
    leftward = [(i + 1, i) for i in range(chan_size - 1)]
    rightward = [(i, i + 1) for i in range(chan_size - 1)]

    def spread(turn):
        scalars = jnp.stack([me_chan, turn])
        own = pick_rows(scalars, source_ids, spectra)
        forward, backward = [own], [own]
        steps = chan_size // 2
        for step in range(1, steps + 1):
            forward.append(lax.ppermute(forward[-1], "chan", ahead))
            if step < chan_size - steps:
                backward.append(lax.ppermute(backward[-1], "chan", back))
        return forward, backward[1:]

    def gathered(turn, forward, backward):
        scalars = jnp.stack([me_chan, turn])
        return source_rows(scalars, source_ids, forward + backward, chan_rows, chan_size)

    def prepared(turn, after):
        scalars = jnp.stack([me_chan, turn])
        return prepare(scalars, packed, source_ids.shape[0], chan_rows, band, window, after)

    def correlate(sources, whitened, tables, picks, place):
        reduced, returned = [], []
        bounds = (0, window, 2 * window, slots)
        after = sources
        for part in range(3):
            start, stop = bounds[part], bounds[part + 1]
            keep, send = transform(
                me_seg, picks, sources, whitened, tables, seg_size, scale, start, stop - start, after
            )
            after = send
            total = reduce_over_seg(keep, send)
            reduced.append(total)
            if part == 0:
                returned.append(lax.ppermute(total, "chan", leftward))
            if part == 1:
                returned.append(lax.ppermute(total, "chan", rightward))
        flip = (me_seg < seg_size // 2).astype(jnp.int32)
        return place_rows(flip, place, reduced + returned[::-1])

    zero = jnp.int32(0)
    forward, backward = spread(zero)
    tables = lag_tables(bins, scale, forward[0])
    whitened = whiten_rows(jnp.transpose(spectra[0], (1, 0, 2)), forward[1])
    pick_src, pick_rec, place, pair_turns = prepared(zero, forward[2])
    sources, source_turns = gathered(zero, forward, backward)
    first = correlate(sources, whitened, tables, (pick_src, pick_rec), place)
    pair_turns = pair_turns[0]
    turns = source_turns[0] * pair_turns

    def further(state):
        turn, total = state
        source_turn, pair_turn = turn // pair_turns, turn % pair_turns
        ahead_chunks, back_chunks = spread(source_turn)
        sources, _ = gathered(source_turn, ahead_chunks, back_chunks)
        pick_src, pick_rec, place, _ = prepared(pair_turn, sources)
        return turn + 1, total + correlate(sources, whitened, tables, (pick_src, pick_rec), place)

    return lax.while_loop(lambda state: state[0] < turns, further, (jnp.int32(1), first))[1]


def solution(mesh):
    in_specs = (P("seg", "chan", None, None), P(), P("chan"), P("chan"), P("chan"))
    out_specs = P("seg", "chan")
    return jax.shard_map(
        per_device, mesh=mesh, in_specs=in_specs, out_specs=out_specs, check_vma=False
    )
```

```python
import functools
import math

import jax
import jax.numpy as jnp
from jax import lax
from jax.experimental import pallas as pl
from jax.experimental.pallas import tpu as pltpu
from jax.sharding import PartitionSpec as P

LAGS = 1024
HALF = LAGS // 2
WBLOCK = 64
PICK = 16
BINS_STEP = 512
TABLE_ROWS = 64
EXTRA = 128


def params(mebibytes):
    return pltpu.CompilerParams(vmem_limit_bytes=mebibytes * 1024 * 1024)


def light():
    return pl.CostEstimate(flops=1024, bytes_accessed=1024, transcendentals=0)


def whole(shape):
    return pl.BlockSpec(shape, lambda *_: (0,) * len(shape))


def pick_kernel(
    chan_rows, band, turn_ref, counts_ref, ids_ref, source_ref, offset_ref, cells_ref, out_ref,
    rows_ref, held_ref, sems,
):
    first = lax.axis_index("chan") * chan_rows
    turn = turn_ref[0]
    bins = cells_ref.shape[3]
    for i in range(PICK):
        rows_ref[i] = 0
    rank = jnp.int32(0)
    for i in range(ids_ref.shape[0]):
        row = ids_ref[i] - first
        mine = (row >= 0) & (row < chan_rows)
        spot = rank - turn * PICK
        rows_ref[jnp.where(mine & (spot >= 0) & (spot < PICK), spot, PICK)] = row
        rank = rank + mine.astype(jnp.int32)
    copies = [
        pltpu.make_async_copy(cells_ref.at[0, rows_ref[i]], held_ref.at[i], sems.at[i])
        for i in range(PICK)
    ]
    for copy in copies:
        copy.start()

    offset = offset_ref[...]
    slot = lax.broadcasted_iota(jnp.int32, offset.shape, 0) * offset.shape[1]
    slot = slot + lax.broadcasted_iota(jnp.int32, offset.shape, 1)
    live = slot < counts_ref[0]
    kinds = (
        live & (offset >= chan_rows),
        live & (offset < 0),
        live & (offset >= 0) & (offset < chan_rows),
    )
    lane = lax.broadcasted_iota(jnp.int32, (PICK, EXTRA), 1)
    notes = jnp.zeros((PICK, EXTRA), jnp.int32)
    for index, kind in enumerate(kinds):
        total = jnp.sum(jnp.where(kind, 1.0, 0.0)).astype(jnp.int32)
        notes = jnp.where(lane == 2 * index, total >> 5, notes)
        notes = jnp.where(lane == 2 * index + 1, total & 31, notes)
    notes = notes.astype(jnp.float32).astype(jnp.bfloat16)
    out_ref[0, :, pl.ds(bins, EXTRA)] = notes
    out_ref[1, :, pl.ds(bins, EXTRA)] = notes

    for copy in copies:
        copy.wait()
    real = held_ref[:, 0, :].astype(jnp.float32)
    imag = held_ref[:, 1, :].astype(jnp.float32)
    width = min(256, bins)

    def stacked(values):
        return jnp.concatenate([values[:, i : i + width] for i in range(0, bins, width)], axis=0)

    real, imag = whitened_pair(stacked(real), stacked(imag))
    for index in range(bins // width):
        lanes = pl.ds(index * width, width)
        out_ref[0, :, lanes] = real[index * PICK : (index + 1) * PICK]
        out_ref[1, :, lanes] = imag[index * PICK : (index + 1) * PICK]


def pick_rows(turn, counts, source_ids, pair_source, pair_offset, spectra, band):
    _, chan_rows, parts, bins = spectra.shape
    smem = pl.BlockSpec(memory_space=pltpu.SMEM)
    vmem = pl.BlockSpec(memory_space=pltpu.VMEM)
    return pl.pallas_call(
        functools.partial(pick_kernel, chan_rows, band),
        out_shape=jax.ShapeDtypeStruct((parts, PICK, bins + EXTRA), spectra.dtype),
        in_specs=[smem, smem, smem, vmem, vmem, pl.BlockSpec(memory_space=pl.ANY)],
        out_specs=vmem,
        scratch_shapes=[
            pltpu.SMEM((PICK + 1,), jnp.int32),
            pltpu.VMEM((PICK, parts, bins), spectra.dtype),
            pltpu.SemaphoreType.DMA((PICK,)),
        ],
        cost_estimate=light(),
        compiler_params=params(8),
        name="pick_rows",
    )(
        turn.reshape(1), counts, source_ids, pair_source.reshape(-1, 128),
        pair_offset.reshape(-1, 128), spectra,
    )


def block_mean(power):
    width = power.shape[1]
    row_group = lax.broadcasted_iota(jnp.int32, (width, width), 0) // WBLOCK
    col_group = lax.broadcasted_iota(jnp.int32, (width, width), 1) // WBLOCK
    spread = jnp.where(row_group == col_group, 1.0 / WBLOCK, 0.0).astype(jnp.bfloat16)
    high = power.astype(jnp.bfloat16)
    low = (power - high.astype(jnp.float32)).astype(jnp.bfloat16)
    total = jnp.dot(low, spread, preferred_element_type=jnp.float32)
    return total + jnp.dot(high, spread, preferred_element_type=jnp.float32)


def whitened_pair(real, imag):
    inverse = lax.rsqrt(block_mean(real * real + imag * imag) + 1e-06)
    return (real * inverse).astype(jnp.bfloat16), (imag * inverse).astype(jnp.bfloat16)


def whiten_kernel(cells_ref, after_ref, out_ref):
    for start in range(0, cells_ref.shape[2], 256):
        lanes = pl.ds(start, 256)
        real = cells_ref[0, :, lanes].astype(jnp.float32)
        imag = cells_ref[1, :, lanes].astype(jnp.float32)
        out_ref[0, :, lanes], out_ref[1, :, lanes] = whitened_pair(real, imag)


def whiten_rows(cells, after):
    _, rows, bins = cells.shape
    spec = pl.BlockSpec((2, rows, BINS_STEP), lambda i: (0, 0, i))
    return pl.pallas_call(
        whiten_kernel,
        grid=(bins // BINS_STEP,),
        out_shape=jax.ShapeDtypeStruct(cells.shape, jnp.bfloat16),
        in_specs=[spec, pl.BlockSpec(memory_space=pl.ANY)],
        out_specs=spec,
        cost_estimate=light(),
        compiler_params=params(12),
        name="whiten_rows",
    )(cells, after)


def table_kernel(scale, all_bins, after_ref, cos_ref, sin_ref, coarse_ref, fine_ref):
    step = pl.program_id(0)
    groups = cos_ref.shape[0] // TABLE_ROWS

    @pl.when(step == 0)
    def _():
        def circle(ref, stride, factor):
            shape = ref.shape[1:]
            bins = lax.broadcasted_iota(jnp.int32, shape, 0) * stride
            lags = lax.broadcasted_iota(jnp.int32, shape, 1)
            lags = jnp.where(lags == 0, HALF, lags)
            theta = ((bins * lags) & (2 * all_bins - 1)).astype(jnp.float32) * (math.pi / all_bins)
            ref[0] = jnp.cos(theta) * factor
            ref[1] = jnp.sin(theta) * factor

        circle(coarse_ref, TABLE_ROWS, scale)
        circle(fine_ref, 1, 1.0)

    cos_b = fine_ref[0]
    sin_b = fine_ref[1]
    first = lax.broadcasted_iota(jnp.int32, cos_b.shape, 1) == 0
    for group in range(groups):
        cos_a = coarse_ref[0, pl.ds(step * groups + group, 1), :]
        sin_a = coarse_ref[1, pl.ds(step * groups + group, 1), :]
        rows = pl.ds(group * TABLE_ROWS, TABLE_ROWS)
        cos = jnp.where(first, scale, cos_a * cos_b - sin_a * sin_b)
        cos_ref[rows, :] = cos.astype(jnp.bfloat16)
        sin_ref[rows, :] = (sin_a * cos_b + cos_a * sin_b).astype(jnp.bfloat16)


def lag_tables(bins, scale, after):
    spec = pl.BlockSpec((BINS_STEP, HALF), lambda i: (i, 0))
    shape = jax.ShapeDtypeStruct((bins, HALF), jnp.bfloat16)
    return pl.pallas_call(
        functools.partial(table_kernel, scale, bins),
        grid=(bins // BINS_STEP,),
        out_shape=(shape, shape),
        in_specs=[pl.BlockSpec(memory_space=pl.ANY)],
        out_specs=(spec, spec),
        scratch_shapes=[
            pltpu.VMEM((2, bins // TABLE_ROWS, HALF), jnp.float32),
            pltpu.VMEM((2, TABLE_ROWS, HALF), jnp.float32),
        ],
        cost_estimate=light(),
        compiler_params=params(12),
        name="lag_tables",
    )(after)


def source_spots(chan_rows, chan_size, me, turn, ids_row):
    count = ids_row.shape[1]
    shift = chan_rows.bit_length() - 1
    ids_row = jnp.broadcast_to(ids_row, (count, count))
    rows = lax.broadcasted_iota(jnp.int32, (count, count), 0)
    columns = lax.broadcasted_iota(jnp.int32, (count, count), 1)
    ids = jnp.sum(jnp.where(rows == columns, ids_row, 0).astype(jnp.float32), axis=1, keepdims=True)
    owner = jnp.broadcast_to(ids.astype(jnp.int32) >> shift, (count, count))
    earlier = (owner == (ids_row >> shift)) & (columns < rows)
    rank = jnp.sum(jnp.where(earlier, 1.0, 0.0), axis=1, keepdims=True)
    turns = (jnp.max(rank).astype(jnp.int32) + PICK) // PICK
    rank = rank.astype(jnp.int32) - turn * PICK
    owner = owner[:, 0:1]

    def ring_place(block):
        return jnp.where((block & 1) == 0, block >> 1, chan_size - 1 - (block >> 1))

    steps = chan_size // 2
    distance = ring_place(me) - ring_place(owner)
    distance = jnp.where(distance < 0, distance + chan_size, distance)
    hop = jnp.where(distance <= steps, distance, steps + chan_size - distance)
    return jnp.where((rank >= 0) & (rank < PICK), hop * PICK + rank, -1), turns


def prepare_kernel(
    chan_rows, chan_size, band, window, turns_ref, ids_ref, left_ref, right_ref, own_ref, after_ref,
    src_ref, rec_ref, place_ref, needed_ref,
):
    me = lax.axis_index("chan")
    source_turn = turns_ref[0]
    turn = turns_ref[1]
    slots = own_ref.shape[1]
    spots, needed = source_spots(chan_rows, chan_size, me, source_turn, ids_ref[...])
    needed_ref[0] = needed

    row = lax.broadcasted_iota(jnp.int32, (8, slots), 0)
    packed = jnp.where(row < 5, own_ref[...], 0)
    packed = jnp.where(row == 0, left_ref[...], jnp.where(row == 1, right_ref[...], packed))
    live = packed > 0
    code = packed - 1
    offset = (code & (4 * band - 1)) - band
    source = code >> ((4 * band).bit_length() - 1)
    below = jnp.where(live & (offset < 0), 1.0, 0.0)
    above = jnp.where(live & (offset >= chan_rows), 1.0, 0.0)
    inside = jnp.where(live & (offset >= 0) & (offset < chan_rows), 1.0, 0.0)
    taken = jnp.where((row == 0) | (row == 4), above, jnp.where((row == 1) | (row == 3), below, inside))
    earlier = lax.broadcasted_iota(jnp.int32, (slots, slots), 0) < lax.broadcasted_iota(
        jnp.int32, (slots, slots), 1
    )
    rank = jnp.dot(
        taken.astype(jnp.bfloat16),
        jnp.where(earlier, 1.0, 0.0).astype(jnp.bfloat16),
        preferred_element_type=jnp.float32,
    ).astype(jnp.int32)
    total = jnp.sum(taken, axis=1, keepdims=True).astype(jnp.int32)
    left_total = total[0:1, :]
    right_total = total[1:2, :]

    def done_before(amount, index):
        return jnp.minimum(amount, index * window)

    left_before = done_before(left_total, turn)
    right_before = done_before(right_total, turn)
    left_now = done_before(left_total, turn + 1) - left_before
    right_now = done_before(right_total, turn + 1) - right_before
    own_before = turn * slots - left_before - right_before
    own_room = slots - left_now - right_now
    held = taken > 0

    def in_window(index):
        shifted = rank[index : index + 1, :] - turn * window
        return shifted, held[index : index + 1, :] & (shifted >= 0) & (shifted < window)

    left_rank, left_ok = in_window(0)
    right_rank, right_ok = in_window(1)
    left_pos = jnp.where(left_ok, left_rank, -1)
    right_pos = jnp.where(right_ok, right_rank + window, -1)
    own_rank = rank[2:3, :] - own_before
    own_ok = held[2:3, :] & (own_rank >= 0) & (own_rank < own_room)
    own_pos = own_rank + left_now
    own_pos = jnp.where(own_pos < window, own_pos, own_pos + right_now)
    own_pos = jnp.where(own_ok, own_pos, -1)
    below_rank, below_ok = in_window(3)
    above_rank, above_ok = in_window(4)
    place = jnp.where(below_ok, below_rank + slots, own_pos)
    place = jnp.where(above_ok, above_rank + slots + window, place)
    place_ref[...] = jnp.broadcast_to(place, place_ref.shape)

    wanted = lax.broadcasted_iota(jnp.int32, (slots, slots), 0)
    names = lax.broadcasted_iota(jnp.int32, (spots.shape[0], slots), 0)
    receiver = jnp.where(row == 0, offset - chan_rows, jnp.where(row == 1, offset + chan_rows, offset))
    jobs = jnp.zeros((slots, 8), jnp.float32)
    for index, position in enumerate((left_pos, right_pos, own_pos)):
        spot = jnp.where(names == source[index : index + 1, :], spots + 1, 0).astype(jnp.float32)
        spot = jnp.sum(spot, axis=0, keepdims=True).astype(jnp.int32) - 1
        fields = jnp.where(row == 0, spot >> 4, jnp.where(row == 1, spot & (PICK - 1), 0))
        fields = jnp.where(row == 2, receiver[index : index + 1, :], jnp.where(row == 3, 1, fields))
        fields = jnp.where((position >= 0) & (spot >= 0), fields, 0)
        chosen = jnp.where(wanted == position, 1.0, 0.0).astype(jnp.bfloat16)
        jobs = jobs + lax.dot_general(
            chosen,
            fields.astype(jnp.float32).astype(jnp.bfloat16),
            (((1,), (1,)), ((), ())),
            preferred_element_type=jnp.float32,
        )
    jobs = jobs.astype(jnp.int32)
    busy = jobs[:, 3:4] > 0
    column = jnp.where(busy, jobs[:, 0:1] * PICK + jobs[:, 1:2], -1)
    lanes = lax.broadcasted_iota(jnp.int32, src_ref.shape, 1)
    src_ref[...] = jnp.where(column == lanes, 1.0, 0.0).astype(jnp.bfloat16)
    column = jnp.where(busy, jobs[:, 2:3], -1)
    lanes = lax.broadcasted_iota(jnp.int32, rec_ref.shape, 1)
    rec_ref[...] = jnp.where(column == lanes, 1.0, 0.0).astype(jnp.bfloat16)


def prepare(turns, source_ids, pairs, chan_rows, chan_size, band, window, after):
    slots = pairs[0].shape[0]
    vmem = pl.BlockSpec(memory_space=pltpu.VMEM)
    smem = pl.BlockSpec(memory_space=pltpu.SMEM)
    return pl.pallas_call(
        functools.partial(prepare_kernel, chan_rows, chan_size, band, window),
        out_shape=(
            jax.ShapeDtypeStruct((slots, chan_size * PICK), jnp.bfloat16),
            jax.ShapeDtypeStruct((slots, chan_rows), jnp.bfloat16),
            jax.ShapeDtypeStruct((8, slots), jnp.int32),
            jax.ShapeDtypeStruct((1,), jnp.int32),
        ),
        in_specs=[smem, vmem, vmem, vmem, vmem, pl.BlockSpec(memory_space=pl.ANY)],
        out_specs=(vmem, vmem, vmem, smem),
        cost_estimate=light(),
        compiler_params=params(24),
        name="prepare",
    )(turns, source_ids.reshape(1, -1), *[row.reshape(1, slots) for row in pairs], after)


def turns_kernel(chan_size, slots, window, *refs):
    chunk_refs, out_ref = refs[:-1], refs[-1]
    me = lax.axis_index("chan")
    steps = chan_size // 2
    place = jnp.where((me & 1) == 0, me >> 1, chan_size - 1 - (me >> 1))
    block = lax.broadcasted_iota(jnp.int32, (chan_size, EXTRA), 0)
    notes = jnp.zeros((chan_size, EXTRA), jnp.float32)
    for hop, ref in enumerate(chunk_refs):
        spot = place - hop if hop <= steps else place + hop - steps
        spot = jnp.where(spot < 0, spot + chan_size, spot)
        spot = jnp.where(spot >= chan_size, spot - chan_size, spot)
        owner = jnp.where(spot < steps, 2 * spot, 2 * (chan_size - spot) - 1)
        notes = jnp.where(block == owner, ref[0][0:1, :].astype(jnp.float32), notes)
    lane = lax.broadcasted_iota(jnp.int32, notes.shape, 1)

    def total(index):
        value = jnp.where(lane == 2 * index, 32.0 * notes, 0.0)
        value = value + jnp.where(lane == 2 * index + 1, notes, 0.0)
        return jnp.broadcast_to(jnp.sum(value, axis=1, keepdims=True), notes.shape)

    left = jnp.where(block == 0, 0.0, pltpu.roll(total(0), 1, 0))
    right = jnp.where(block == chan_size - 1, 0.0, pltpu.roll(total(1), chan_size - 1, 0))
    aside = jnp.max(jnp.maximum(left, right)).astype(jnp.int32)
    whole_sum = jnp.max(left + right + total(2)).astype(jnp.int32)
    needed = jnp.maximum((aside + window - 1) // window, (whole_sum + slots - 1) // slots)
    out_ref[0] = jnp.maximum(needed, 1)


def pair_turns(chunks, slots, window):
    _, _, width = chunks[0].shape
    last = width // EXTRA - 1
    return pl.pallas_call(
        functools.partial(turns_kernel, len(chunks), slots, window),
        grid=(1,),
        out_shape=jax.ShapeDtypeStruct((1,), jnp.int32),
        in_specs=[pl.BlockSpec((1, PICK, EXTRA), lambda i: (0, 0, last)) for _ in chunks],
        out_specs=pl.BlockSpec(memory_space=pltpu.SMEM),
        cost_estimate=light(),
        compiler_params=params(8),
        name="pair_turns",
    )(*chunks)


def transform_kernel(shards, scale, start, chunks, me_ref, src_ref, rec_ref, *refs):
    chunk_refs = refs[:chunks]
    cells_ref, cos_ref, sin_ref, after_ref, keep_ref, send_ref = refs[chunks:]
    rows = keep_ref.shape[1]
    bins = cos_ref.shape[0]
    step = min(BINS_STEP, bins)
    eighth = lax.broadcasted_iota(jnp.int32, (1, 128), 1) & 7
    root = math.sqrt(0.5)
    edge = jnp.where((eighth == 1) | (eighth == 7), root, 0.0)
    edge = jnp.where((eighth == 3) | (eighth == 5), -root, edge)
    edge = jnp.where(eighth == 0, 1.0, jnp.where(eighth == 4, -1.0, edge)) * scale
    edge = edge.astype(jnp.bfloat16).astype(jnp.float32)

    by_src = src_ref[pl.ds(start, rows), :]
    by_rec = rec_ref[pl.ds(start, rows), :]
    even = odd = corner = None
    for first in range(0, bins, step):
        lanes = pl.ds(first, step)
        source_real = jnp.concatenate([ref[0, :, lanes] for ref in chunk_refs], axis=0)
        source_imag = jnp.concatenate([ref[1, :, lanes] for ref in chunk_refs], axis=0)
        sr = jnp.dot(by_src, source_real, preferred_element_type=jnp.float32)
        si = jnp.dot(by_src, source_imag, preferred_element_type=jnp.float32)
        rr = jnp.dot(by_rec, cells_ref[0, :, lanes], preferred_element_type=jnp.float32)
        ri = jnp.dot(by_rec, cells_ref[1, :, lanes], preferred_element_type=jnp.float32)
        real = (sr * rr + si * ri).astype(jnp.bfloat16)
        imag = (si * rr - sr * ri).astype(jnp.bfloat16)
        more_even = jnp.dot(real, cos_ref[lanes, :], preferred_element_type=jnp.float32)
        more_odd = jnp.dot(imag, sin_ref[lanes, :], preferred_element_type=jnp.float32)
        wide = real.astype(jnp.float32)
        sums = wide[:, 0:128]
        for lane in range(128, step, 128):
            sums = sums + wide[:, lane : lane + 128]
        even = more_even if even is None else even + more_even
        odd = more_odd if odd is None else odd + more_odd
        corner = sums if corner is None else corner + sums

    me = me_ref[0]
    width = LAGS // shards
    corner = jnp.sum(corner * edge, axis=1, keepdims=True)
    first = lax.broadcasted_iota(jnp.int32, even.shape, 1) == 0
    later = even - jnp.where(first, 0.0, odd)
    sooner = jnp.where(first, corner, even) + odd
    sooner = pltpu.roll(sooner, HALF - 1, 1)
    for shard in range(shards):
        half = shards // 2
        if shard < half:
            lane = (half - 1 - shard) * width
            value = sooner[:, lane : lane + width]
        else:
            lane = (shard - half) * width
            value = later[:, lane : lane + width]
        place = me ^ shard

        @pl.when((place & 1) == 0)
        def _():
            keep_ref[place >> 1] = value

        @pl.when((place & 1) == 1)
        def _():
            send_ref[place >> 1] = value.astype(jnp.bfloat16)


def transform(me, picks, chunks, cells, tables, shards, scale, start, rows, after):
    width = LAGS // shards
    shape = (shards // 2, rows, width)
    vmem = pl.BlockSpec(memory_space=pltpu.VMEM)
    return pl.pallas_call(
        functools.partial(transform_kernel, shards, scale, start, len(chunks)),
        out_shape=(
            jax.ShapeDtypeStruct(shape, jnp.float32),
            jax.ShapeDtypeStruct(shape, jnp.bfloat16),
        ),
        in_specs=[pl.BlockSpec(memory_space=pltpu.SMEM)]
        + [vmem] * (5 + len(chunks))
        + [pl.BlockSpec(memory_space=pl.ANY)],
        out_specs=(vmem, vmem),
        cost_estimate=light(),
        compiler_params=params(28),
        name="transform",
    )(me.reshape(1), *picks, *chunks, cells, *tables, after)


def reduce_over_seg(keep, send):
    size = lax.axis_size("seg")
    bit = 1
    while True:
        got = lax.ppermute(send, "seg", [(i, i ^ bit) for i in range(size)])
        total = keep + got.astype(jnp.float32)
        if total.shape[0] == 1:
            return total[0].astype(jnp.bfloat16)
        keep = total[0::2]
        send = total[1::2].astype(jnp.bfloat16)
        bit *= 2


def place_kernel(start, further, flip_ref, place_ref, *refs):
    out_ref = refs[-1]
    parts = refs[1:-1] if further else refs[:-1]
    width, slots = out_ref.shape
    flip = flip_ref[0]
    rows = lax.broadcasted_iota(jnp.int32, (width, width), 0)
    columns = lax.broadcasted_iota(jnp.int32, (width, width), 1)
    wanted = jnp.where(flip > 0, width - 1 - rows, rows)
    turned = jnp.where(wanted == columns, 1.0, 0.0).astype(jnp.bfloat16)
    total = refs[0][...] if further else jnp.zeros((width, slots), jnp.float32)
    for ref in parts:
        count = ref.shape[0]
        spot = lax.broadcasted_iota(jnp.int32, (count, slots), 0) + start
        chosen = jnp.where(spot == place_ref[0:1, :], 1.0, 0.0).astype(jnp.bfloat16)
        across = lax.dot_general(
            turned, ref[...], (((1,), (1,)), ((), ())), preferred_element_type=jnp.float32
        ).astype(jnp.bfloat16)
        total = total + jnp.dot(across, chosen, preferred_element_type=jnp.float32)
        start += count
    out_ref[...] = total


def place_rows(flip, place, parts, start, total=None):
    width = parts[0].shape[1]
    slots = place.shape[1]
    given = list(parts) if total is None else [total, *parts]
    vmem = pl.BlockSpec(memory_space=pltpu.VMEM)
    return pl.pallas_call(
        functools.partial(place_kernel, start, total is not None),
        out_shape=jax.ShapeDtypeStruct((width, slots), jnp.float32),
        in_specs=[pl.BlockSpec(memory_space=pltpu.SMEM)] + [vmem] * (1 + len(given)),
        out_specs=vmem,
        cost_estimate=light(),
        compiler_params=params(16),
        name="place_rows",
    )(flip.reshape(1), place, *given)


def per_device(spectra, source_ids, pair_source, pair_offset, pair_counts):
    chan_rows = spectra.shape[1]
    bins = spectra.shape[3]
    band = chan_rows // 2
    seg_size = lax.axis_size("seg")
    chan_size = lax.axis_size("chan")
    slots = pair_source.shape[0]
    window = 3 * slots // 8
    scale = 1.0 / math.sqrt(bins * seg_size)
    me_seg = lax.axis_index("seg")

    ring = list(range(0, chan_size, 2)) + list(range(1, chan_size, 2))[::-1]
    ahead = [(ring[i], ring[(i + 1) % chan_size]) for i in range(chan_size)]
    back = [(b, a) for a, b in ahead]
    leftward = [(i + 1, i) for i in range(chan_size - 1)]
    rightward = [(i, i + 1) for i in range(chan_size - 1)]

    live = jnp.arange(slots, dtype=jnp.int32) < pair_counts[0]
    packed = jnp.where(live, 1 + pair_source * (4 * band) + pair_offset + band, 0)
    pairs = (lax.ppermute(packed, "chan", rightward), lax.ppermute(packed, "chan", leftward), packed)

    def spread(turn):
        own = pick_rows(turn, pair_counts, source_ids, pair_source, pair_offset, spectra, band)
        forward, backward = [own], [own]
        steps = chan_size // 2
        for step in range(1, steps + 1):
            forward.append(lax.ppermute(forward[-1], "chan", ahead))
            if step < chan_size - steps:
                backward.append(lax.ppermute(backward[-1], "chan", back))
        return forward + backward[1:]

    def prepared(source_turn, turn, after):
        turns = jnp.stack([source_turn, turn])
        return prepare(turns, source_ids, pairs, chan_rows, chan_size, band, window, after)

    def correlate(chunks, whitened, tables, picks, place):
        reduced, returned = [], []
        bounds = (0, window, 2 * window, slots)
        after = chunks[0]
        for part in range(3):
            start, stop = bounds[part], bounds[part + 1]
            keep, send = transform(
                me_seg, picks, chunks, whitened, tables, seg_size, scale, start, stop - start, after
            )
            after = send
            total = reduce_over_seg(keep, send)
            reduced.append(total)
            if part == 0:
                returned.append(lax.ppermute(total, "chan", leftward))
            if part == 1:
                returned.append(lax.ppermute(total, "chan", rightward))
        flip = (me_seg < seg_size // 2).astype(jnp.int32)
        own = place_rows(flip, place, reduced, 0)
        return place_rows(flip, place, returned[::-1], slots, own)

    zero = jnp.int32(0)
    chunks = spread(zero)
    tables = lag_tables(bins, scale, chunks[0])
    whitened = whiten_rows(jnp.transpose(spectra[0], (1, 0, 2)), chunks[1])
    *picks, place, source_turns = prepared(zero, zero, chunks[2])
    first = correlate(chunks, whitened, tables, picks, place)
    pair_count = pair_turns(chunks, slots, window)[0]
    turns = source_turns[0] * pair_count

    def further(state):
        turn, total = state
        chunks = spread(turn // pair_count)
        *picks, place, _ = prepared(turn // pair_count, turn % pair_count, chunks[0])
        return turn + 1, total + correlate(chunks, whitened, tables, picks, place)

    return lax.while_loop(lambda state: state[0] < turns, further, (jnp.int32(1), first))[1]


def solution(mesh):
    in_specs = (P("seg", "chan", None, None), P(), P("chan"), P("chan"), P("chan"))
    out_specs = P("seg", "chan")
    return jax.shard_map(
        per_device, mesh=mesh, in_specs=in_specs, out_specs=out_specs, check_vma=False
    )
```

```python
import functools
import math

import jax
import jax.numpy as jnp
from jax import lax
from jax.experimental import pallas as pl
from jax.experimental.pallas import tpu as pltpu
from jax.sharding import PartitionSpec as P

LAGS = 1024
HALF = LAGS // 2
WBLOCK = 64
PICK = 16
BINS_STEP = 512
TABLE_ROWS = 64
EXTRA = 128


def params(mebibytes):
    return pltpu.CompilerParams(vmem_limit_bytes=mebibytes * 1024 * 1024)


def light():
    return pl.CostEstimate(flops=1024, bytes_accessed=1024, transcendentals=0)


def whole(shape):
    return pl.BlockSpec(shape, lambda *_: (0,) * len(shape))


def pick_kernel(
    chan_rows, band, turn_ref, counts_ref, ids_ref, source_ref, offset_ref, cells_ref, out_ref,
    rows_ref, held_ref, sems,
):
    first = lax.axis_index("chan") * chan_rows
    turn = turn_ref[0]
    bins = cells_ref.shape[3]
    for i in range(PICK):
        rows_ref[i] = 0
    rank = jnp.int32(0)
    for i in range(ids_ref.shape[0]):
        row = ids_ref[i] - first
        mine = (row >= 0) & (row < chan_rows)
        spot = rank - turn * PICK
        rows_ref[jnp.where(mine & (spot >= 0) & (spot < PICK), spot, PICK)] = row
        rank = rank + mine.astype(jnp.int32)
    copies = [
        pltpu.make_async_copy(cells_ref.at[0, rows_ref[i]], held_ref.at[i], sems.at[i])
        for i in range(PICK)
    ]
    for copy in copies:
        copy.start()

    offset = offset_ref[...]
    slot = lax.broadcasted_iota(jnp.int32, offset.shape, 0) * offset.shape[1]
    slot = slot + lax.broadcasted_iota(jnp.int32, offset.shape, 1)
    live = slot < counts_ref[0]
    kinds = (
        live & (offset >= chan_rows),
        live & (offset < 0),
        live & (offset >= 0) & (offset < chan_rows),
    )
    lane = lax.broadcasted_iota(jnp.int32, (PICK, EXTRA), 1)
    notes = jnp.zeros((PICK, EXTRA), jnp.int32)
    for index, kind in enumerate(kinds):
        total = jnp.sum(jnp.where(kind, 1.0, 0.0)).astype(jnp.int32)
        notes = jnp.where(lane == 2 * index, total >> 5, notes)
        notes = jnp.where(lane == 2 * index + 1, total & 31, notes)
    notes = notes.astype(jnp.float32).astype(jnp.bfloat16)
    out_ref[0, :, pl.ds(bins, EXTRA)] = notes
    out_ref[1, :, pl.ds(bins, EXTRA)] = notes

    for copy in copies:
        copy.wait()
    real = held_ref[:, 0, :].astype(jnp.float32)
    imag = held_ref[:, 1, :].astype(jnp.float32)
    width = min(256, bins)

    def stacked(values):
        return jnp.concatenate([values[:, i : i + width] for i in range(0, bins, width)], axis=0)

    real, imag = whitened_pair(stacked(real), stacked(imag))
    for index in range(bins // width):
        lanes = pl.ds(index * width, width)
        out_ref[0, :, lanes] = real[index * PICK : (index + 1) * PICK]
        out_ref[1, :, lanes] = imag[index * PICK : (index + 1) * PICK]


def pick_rows(turn, counts, source_ids, pair_source, pair_offset, spectra, band):
    _, chan_rows, parts, bins = spectra.shape
    smem = pl.BlockSpec(memory_space=pltpu.SMEM)
    vmem = pl.BlockSpec(memory_space=pltpu.VMEM)
    return pl.pallas_call(
        functools.partial(pick_kernel, chan_rows, band),
        out_shape=jax.ShapeDtypeStruct((parts, PICK, bins + EXTRA), spectra.dtype),
        in_specs=[smem, smem, smem, vmem, vmem, pl.BlockSpec(memory_space=pl.ANY)],
        out_specs=vmem,
        scratch_shapes=[
            pltpu.SMEM((PICK + 1,), jnp.int32),
            pltpu.VMEM((PICK, parts, bins), spectra.dtype),
            pltpu.SemaphoreType.DMA((PICK,)),
        ],
        cost_estimate=light(),
        compiler_params=params(8),
        name="pick_rows",
    )(
        turn.reshape(1), counts, source_ids, pair_source.reshape(-1, 128),
        pair_offset.reshape(-1, 128), spectra,
    )


def block_mean(power):
    width = power.shape[1]
    row_group = lax.broadcasted_iota(jnp.int32, (width, width), 0) // WBLOCK
    col_group = lax.broadcasted_iota(jnp.int32, (width, width), 1) // WBLOCK
    spread = jnp.where(row_group == col_group, 1.0 / WBLOCK, 0.0).astype(jnp.bfloat16)
    high = power.astype(jnp.bfloat16)
    low = (power - high.astype(jnp.float32)).astype(jnp.bfloat16)
    total = jnp.dot(low, spread, preferred_element_type=jnp.float32)
    return total + jnp.dot(high, spread, preferred_element_type=jnp.float32)


def whitened_pair(real, imag):
    inverse = lax.rsqrt(block_mean(real * real + imag * imag) + 1e-06)
    return (real * inverse).astype(jnp.bfloat16), (imag * inverse).astype(jnp.bfloat16)


def whiten_kernel(cells_ref, after_ref, out_ref):
    for start in range(0, cells_ref.shape[2], 256):
        lanes = pl.ds(start, 256)
        real = cells_ref[0, :, lanes].astype(jnp.float32)
        imag = cells_ref[1, :, lanes].astype(jnp.float32)
        out_ref[0, :, lanes], out_ref[1, :, lanes] = whitened_pair(real, imag)


def whiten_rows(cells, after):
    _, rows, bins = cells.shape
    spec = pl.BlockSpec((2, rows, BINS_STEP), lambda i: (0, 0, i))
    return pl.pallas_call(
        whiten_kernel,
        grid=(bins // BINS_STEP,),
        out_shape=jax.ShapeDtypeStruct(cells.shape, jnp.bfloat16),
        in_specs=[spec, pl.BlockSpec(memory_space=pl.ANY)],
        out_specs=spec,
        cost_estimate=light(),
        compiler_params=params(12),
        name="whiten_rows",
    )(cells, after)


def table_kernel(scale, all_bins, after_ref, cos_ref, sin_ref, coarse_ref, fine_ref):
    step = pl.program_id(0)
    groups = cos_ref.shape[0] // TABLE_ROWS

    @pl.when(step == 0)
    def _():
        def circle(ref, stride, factor):
            shape = ref.shape[1:]
            bins = lax.broadcasted_iota(jnp.int32, shape, 0) * stride
            lags = lax.broadcasted_iota(jnp.int32, shape, 1)
            lags = jnp.where(lags == 0, HALF, lags)
            theta = ((bins * lags) & (2 * all_bins - 1)).astype(jnp.float32) * (math.pi / all_bins)
            ref[0] = jnp.cos(theta) * factor
            ref[1] = jnp.sin(theta) * factor

        circle(coarse_ref, TABLE_ROWS, scale)
        circle(fine_ref, 1, 1.0)

    cos_b = fine_ref[0]
    sin_b = fine_ref[1]
    first = lax.broadcasted_iota(jnp.int32, cos_b.shape, 1) == 0
    for group in range(groups):
        cos_a = coarse_ref[0, pl.ds(step * groups + group, 1), :]
        sin_a = coarse_ref[1, pl.ds(step * groups + group, 1), :]
        rows = pl.ds(group * TABLE_ROWS, TABLE_ROWS)
        cos = jnp.where(first, scale, cos_a * cos_b - sin_a * sin_b)
        cos_ref[rows, :] = cos.astype(jnp.bfloat16)
        sin_ref[rows, :] = (sin_a * cos_b + cos_a * sin_b).astype(jnp.bfloat16)


def lag_tables(bins, scale, after):
    spec = pl.BlockSpec((BINS_STEP, HALF), lambda i: (i, 0))
    shape = jax.ShapeDtypeStruct((bins, HALF), jnp.bfloat16)
    return pl.pallas_call(
        functools.partial(table_kernel, scale, bins),
        grid=(bins // BINS_STEP,),
        out_shape=(shape, shape),
        in_specs=[pl.BlockSpec(memory_space=pl.ANY)],
        out_specs=(spec, spec),
        scratch_shapes=[
            pltpu.VMEM((2, bins // TABLE_ROWS, HALF), jnp.float32),
            pltpu.VMEM((2, TABLE_ROWS, HALF), jnp.float32),
        ],
        cost_estimate=light(),
        compiler_params=params(12),
        name="lag_tables",
    )(after)


def source_spots(chan_rows, chan_size, me, turn, ids_row):
    count = ids_row.shape[1]
    shift = chan_rows.bit_length() - 1
    ids_row = jnp.broadcast_to(ids_row, (count, count))
    rows = lax.broadcasted_iota(jnp.int32, (count, count), 0)
    columns = lax.broadcasted_iota(jnp.int32, (count, count), 1)
    ids = jnp.sum(jnp.where(rows == columns, ids_row, 0).astype(jnp.float32), axis=1, keepdims=True)
    owner = jnp.broadcast_to(ids.astype(jnp.int32) >> shift, (count, count))
    earlier = (owner == (ids_row >> shift)) & (columns < rows)
    rank = jnp.sum(jnp.where(earlier, 1.0, 0.0), axis=1, keepdims=True)
    turns = (jnp.max(rank).astype(jnp.int32) + PICK) // PICK
    rank = rank.astype(jnp.int32) - turn * PICK
    owner = owner[:, 0:1]

    def ring_place(block):
        return jnp.where((block & 1) == 0, block >> 1, chan_size - 1 - (block >> 1))

    steps = chan_size // 2
    distance = ring_place(me) - ring_place(owner)
    distance = jnp.where(distance < 0, distance + chan_size, distance)
    hop = jnp.where(distance <= steps, distance, steps + chan_size - distance)
    return jnp.where((rank >= 0) & (rank < PICK), hop * PICK + rank, -1), turns


def prepare_kernel(
    chan_rows, chan_size, band, window, turns_ref, ids_ref, left_ref, right_ref, own_ref, after_ref,
    src_ref, rec_ref, place_ref, needed_ref,
):
    me = lax.axis_index("chan")
    source_turn = turns_ref[0]
    turn = turns_ref[1]
    slots = own_ref.shape[1]
    spots, needed = source_spots(chan_rows, chan_size, me, source_turn, ids_ref[...])
    needed_ref[0] = needed

    row = lax.broadcasted_iota(jnp.int32, (8, slots), 0)
    packed = jnp.where(row < 5, own_ref[...], 0)
    packed = jnp.where(row == 0, left_ref[...], jnp.where(row == 1, right_ref[...], packed))
    live = packed > 0
    code = packed - 1
    offset = (code & (4 * band - 1)) - band
    source = code >> ((4 * band).bit_length() - 1)
    below = jnp.where(live & (offset < 0), 1.0, 0.0)
    above = jnp.where(live & (offset >= chan_rows), 1.0, 0.0)
    inside = jnp.where(live & (offset >= 0) & (offset < chan_rows), 1.0, 0.0)
    taken = jnp.where((row == 0) | (row == 4), above, jnp.where((row == 1) | (row == 3), below, inside))
    earlier = lax.broadcasted_iota(jnp.int32, (slots, slots), 0) < lax.broadcasted_iota(
        jnp.int32, (slots, slots), 1
    )
    rank = jnp.dot(
        taken.astype(jnp.bfloat16),
        jnp.where(earlier, 1.0, 0.0).astype(jnp.bfloat16),
        preferred_element_type=jnp.float32,
    ).astype(jnp.int32)
    total = jnp.sum(taken, axis=1, keepdims=True).astype(jnp.int32)
    left_total = total[0:1, :]
    right_total = total[1:2, :]

    def done_before(amount, index):
        return jnp.minimum(amount, index * window)

    left_before = done_before(left_total, turn)
    right_before = done_before(right_total, turn)
    left_now = done_before(left_total, turn + 1) - left_before
    right_now = done_before(right_total, turn + 1) - right_before
    own_before = turn * slots - left_before - right_before
    own_room = slots - left_now - right_now
    held = taken > 0

    def in_window(index):
        shifted = rank[index : index + 1, :] - turn * window
        return shifted, held[index : index + 1, :] & (shifted >= 0) & (shifted < window)

    left_rank, left_ok = in_window(0)
    right_rank, right_ok = in_window(1)
    left_pos = jnp.where(left_ok, left_rank, -1)
    right_pos = jnp.where(right_ok, right_rank + window, -1)
    own_rank = rank[2:3, :] - own_before
    own_ok = held[2:3, :] & (own_rank >= 0) & (own_rank < own_room)
    own_pos = own_rank + left_now
    own_pos = jnp.where(own_pos < window, own_pos, own_pos + right_now)
    own_pos = jnp.where(own_ok, own_pos, -1)
    below_rank, below_ok = in_window(3)
    above_rank, above_ok = in_window(4)
    place = jnp.where(below_ok, below_rank + slots, own_pos)
    place = jnp.where(above_ok, above_rank + slots + window, place)
    place_ref[...] = jnp.broadcast_to(place, place_ref.shape)

    wanted = lax.broadcasted_iota(jnp.int32, (slots, slots), 0)
    names = lax.broadcasted_iota(jnp.int32, (spots.shape[0], slots), 0)
    receiver = jnp.where(row == 0, offset - chan_rows, jnp.where(row == 1, offset + chan_rows, offset))
    jobs = jnp.zeros((slots, 8), jnp.float32)
    for index, position in enumerate((left_pos, right_pos, own_pos)):
        spot = jnp.where(names == source[index : index + 1, :], spots + 1, 0).astype(jnp.float32)
        spot = jnp.sum(spot, axis=0, keepdims=True).astype(jnp.int32) - 1
        fields = jnp.where(row == 0, spot >> 4, jnp.where(row == 1, spot & (PICK - 1), 0))
        fields = jnp.where(row == 2, receiver[index : index + 1, :], jnp.where(row == 3, 1, fields))
        fields = jnp.where((position >= 0) & (spot >= 0), fields, 0)
        chosen = jnp.where(wanted == position, 1.0, 0.0).astype(jnp.bfloat16)
        jobs = jobs + lax.dot_general(
            chosen,
            fields.astype(jnp.float32).astype(jnp.bfloat16),
            (((1,), (1,)), ((), ())),
            preferred_element_type=jnp.float32,
        )
    jobs = jobs.astype(jnp.int32)
    busy = jobs[:, 3:4] > 0
    column = jnp.where(busy, jobs[:, 0:1] * PICK + jobs[:, 1:2], -1)
    lanes = lax.broadcasted_iota(jnp.int32, src_ref.shape, 1)
    src_ref[...] = jnp.where(column == lanes, 1.0, 0.0).astype(jnp.bfloat16)
    column = jnp.where(busy, jobs[:, 2:3], -1)
    lanes = lax.broadcasted_iota(jnp.int32, rec_ref.shape, 1)
    rec_ref[...] = jnp.where(column == lanes, 1.0, 0.0).astype(jnp.bfloat16)


def prepare(turns, source_ids, pairs, chan_rows, chan_size, band, window, after):
    slots = pairs[0].shape[0]
    vmem = pl.BlockSpec(memory_space=pltpu.VMEM)
    smem = pl.BlockSpec(memory_space=pltpu.SMEM)
    return pl.pallas_call(
        functools.partial(prepare_kernel, chan_rows, chan_size, band, window),
        out_shape=(
            jax.ShapeDtypeStruct((slots, chan_size * PICK), jnp.bfloat16),
            jax.ShapeDtypeStruct((slots, chan_rows), jnp.bfloat16),
            jax.ShapeDtypeStruct((8, slots), jnp.int32),
            jax.ShapeDtypeStruct((1,), jnp.int32),
        ),
        in_specs=[smem, vmem, vmem, vmem, vmem, pl.BlockSpec(memory_space=pl.ANY)],
        out_specs=(vmem, vmem, vmem, smem),
        cost_estimate=light(),
        compiler_params=params(24),
        name="prepare",
    )(turns, source_ids.reshape(1, -1), *[row.reshape(1, slots) for row in pairs], after)


def turns_kernel(chan_size, slots, window, *refs):
    chunk_refs, out_ref = refs[:-1], refs[-1]
    me = lax.axis_index("chan")
    steps = chan_size // 2
    place = jnp.where((me & 1) == 0, me >> 1, chan_size - 1 - (me >> 1))
    block = lax.broadcasted_iota(jnp.int32, (chan_size, EXTRA), 0)
    notes = jnp.zeros((chan_size, EXTRA), jnp.float32)
    for hop, ref in enumerate(chunk_refs):
        spot = place - hop if hop <= steps else place + hop - steps
        spot = jnp.where(spot < 0, spot + chan_size, spot)
        spot = jnp.where(spot >= chan_size, spot - chan_size, spot)
        owner = jnp.where(spot < steps, 2 * spot, 2 * (chan_size - spot) - 1)
        notes = jnp.where(block == owner, ref[0][0:1, :].astype(jnp.float32), notes)
    lane = lax.broadcasted_iota(jnp.int32, notes.shape, 1)

    def total(index):
        value = jnp.where(lane == 2 * index, 32.0 * notes, 0.0)
        value = value + jnp.where(lane == 2 * index + 1, notes, 0.0)
        return jnp.broadcast_to(jnp.sum(value, axis=1, keepdims=True), notes.shape)

    left = jnp.where(block == 0, 0.0, pltpu.roll(total(0), 1, 0))
    right = jnp.where(block == chan_size - 1, 0.0, pltpu.roll(total(1), chan_size - 1, 0))
    aside = jnp.max(jnp.maximum(left, right)).astype(jnp.int32)
    whole_sum = jnp.max(left + right + total(2)).astype(jnp.int32)
    needed = jnp.maximum((aside + window - 1) // window, (whole_sum + slots - 1) // slots)
    out_ref[0] = jnp.maximum(needed, 1)


def pair_turns(chunks, slots, window):
    _, _, width = chunks[0].shape
    last = width // EXTRA - 1
    return pl.pallas_call(
        functools.partial(turns_kernel, len(chunks), slots, window),
        grid=(1,),
        out_shape=jax.ShapeDtypeStruct((1,), jnp.int32),
        in_specs=[pl.BlockSpec((1, PICK, EXTRA), lambda i: (0, 0, last)) for _ in chunks],
        out_specs=pl.BlockSpec(memory_space=pltpu.SMEM),
        cost_estimate=light(),
        compiler_params=params(8),
        name="pair_turns",
    )(*chunks)


def transform_kernel(shards, scale, start, chunks, me_ref, src_ref, rec_ref, *refs):
    chunk_refs = refs[:chunks]
    cells_ref, cos_ref, sin_ref, after_ref, keep_ref, send_ref = refs[chunks:]
    rows = keep_ref.shape[1]
    bins = cos_ref.shape[0]
    step = min(BINS_STEP, bins)
    eighth = lax.broadcasted_iota(jnp.int32, (1, 128), 1) & 7
    root = math.sqrt(0.5)
    edge = jnp.where((eighth == 1) | (eighth == 7), root, 0.0)
    edge = jnp.where((eighth == 3) | (eighth == 5), -root, edge)
    edge = jnp.where(eighth == 0, 1.0, jnp.where(eighth == 4, -1.0, edge)) * scale
    edge = edge.astype(jnp.bfloat16).astype(jnp.float32)

    by_src = src_ref[pl.ds(start, rows), :]
    by_rec = rec_ref[pl.ds(start, rows), :]
    even = odd = corner = None
    for first in range(0, bins, step):
        lanes = pl.ds(first, step)
        source_real = jnp.concatenate([ref[0, :, lanes] for ref in chunk_refs], axis=0)
        source_imag = jnp.concatenate([ref[1, :, lanes] for ref in chunk_refs], axis=0)
        sr = jnp.dot(by_src, source_real, preferred_element_type=jnp.float32)
        si = jnp.dot(by_src, source_imag, preferred_element_type=jnp.float32)
        rr = jnp.dot(by_rec, cells_ref[0, :, lanes], preferred_element_type=jnp.float32)
        ri = jnp.dot(by_rec, cells_ref[1, :, lanes], preferred_element_type=jnp.float32)
        real = (sr * rr + si * ri).astype(jnp.bfloat16)
        imag = (si * rr - sr * ri).astype(jnp.bfloat16)
        more_even = jnp.dot(real, cos_ref[lanes, :], preferred_element_type=jnp.float32)
        more_odd = jnp.dot(imag, sin_ref[lanes, :], preferred_element_type=jnp.float32)
        wide = real.astype(jnp.float32)
        sums = wide[:, 0:128]
        for lane in range(128, step, 128):
            sums = sums + wide[:, lane : lane + 128]
        even = more_even if even is None else even + more_even
        odd = more_odd if odd is None else odd + more_odd
        corner = sums if corner is None else corner + sums

    me = me_ref[0]
    width = LAGS // shards
    corner = jnp.sum(corner * edge, axis=1, keepdims=True)
    first = lax.broadcasted_iota(jnp.int32, even.shape, 1) == 0
    later = even - jnp.where(first, 0.0, odd)
    sooner = jnp.where(first, corner, even) + odd
    sooner = pltpu.roll(sooner, HALF - 1, 1)
    for shard in range(shards):
        half = shards // 2
        if shard < half:
            lane = (half - 1 - shard) * width
            value = sooner[:, lane : lane + width]
        else:
            lane = (shard - half) * width
            value = later[:, lane : lane + width]
        place = me ^ shard

        @pl.when((place & 1) == 0)
        def _():
            keep_ref[place >> 1] = value

        @pl.when((place & 1) == 1)
        def _():
            send_ref[place >> 1] = value.astype(jnp.bfloat16)


def transform(me, picks, chunks, cells, tables, shards, scale, start, rows, after):
    width = LAGS // shards
    shape = (shards // 2, rows, width)
    vmem = pl.BlockSpec(memory_space=pltpu.VMEM)
    return pl.pallas_call(
        functools.partial(transform_kernel, shards, scale, start, len(chunks)),
        out_shape=(
            jax.ShapeDtypeStruct(shape, jnp.float32),
            jax.ShapeDtypeStruct(shape, jnp.bfloat16),
        ),
        in_specs=[pl.BlockSpec(memory_space=pltpu.SMEM)]
        + [vmem] * (5 + len(chunks))
        + [pl.BlockSpec(memory_space=pl.ANY)],
        out_specs=(vmem, vmem),
        cost_estimate=light(),
        compiler_params=params(28),
        name="transform",
    )(me.reshape(1), *picks, *chunks, cells, *tables, after)


def swap(send, bit):
    size = lax.axis_size("seg")
    return lax.ppermute(send, "seg", [(i, i ^ bit) for i in range(size)])


def halve(keep, got):
    total = keep + got.astype(jnp.float32)
    return total[0::2], total[1::2].astype(jnp.bfloat16)


def reduce_further(keep, got, bit):
    while keep.shape[0] > 1:
        keep, send = halve(keep, got)
        bit *= 2
        got = swap(send, bit)
    return (keep[0] + got[0].astype(jnp.float32)).astype(jnp.bfloat16)


def place_kernel(start, further, flip_ref, place_ref, *refs):
    out_ref = refs[-1]
    parts = refs[1:-1] if further else refs[:-1]
    width, slots = out_ref.shape
    flip = flip_ref[0]
    rows = lax.broadcasted_iota(jnp.int32, (width, width), 0)
    columns = lax.broadcasted_iota(jnp.int32, (width, width), 1)
    wanted = jnp.where(flip > 0, width - 1 - rows, rows)
    turned = jnp.where(wanted == columns, 1.0, 0.0).astype(jnp.bfloat16)
    total = refs[0][...] if further else jnp.zeros((width, slots), jnp.float32)
    for ref in parts:
        count = ref.shape[0]
        spot = lax.broadcasted_iota(jnp.int32, (count, slots), 0) + start
        chosen = jnp.where(spot == place_ref[0:1, :], 1.0, 0.0).astype(jnp.bfloat16)
        across = lax.dot_general(
            turned, ref[...], (((1,), (1,)), ((), ())), preferred_element_type=jnp.float32
        ).astype(jnp.bfloat16)
        total = total + jnp.dot(across, chosen, preferred_element_type=jnp.float32)
        start += count
    out_ref[...] = total


def place_rows(flip, place, parts, start, total=None):
    width = parts[0].shape[1]
    slots = place.shape[1]
    given = list(parts) if total is None else [total, *parts]
    vmem = pl.BlockSpec(memory_space=pltpu.VMEM)
    return pl.pallas_call(
        functools.partial(place_kernel, start, total is not None),
        out_shape=jax.ShapeDtypeStruct((width, slots), jnp.float32),
        in_specs=[pl.BlockSpec(memory_space=pltpu.SMEM)] + [vmem] * (1 + len(given)),
        out_specs=vmem,
        cost_estimate=light(),
        compiler_params=params(16),
        name="place_rows",
    )(flip.reshape(1), place, *given)


def per_device(spectra, source_ids, pair_source, pair_offset, pair_counts):
    chan_rows = spectra.shape[1]
    bins = spectra.shape[3]
    band = chan_rows // 2
    seg_size = lax.axis_size("seg")
    chan_size = lax.axis_size("chan")
    slots = pair_source.shape[0]
    window = 3 * slots // 8
    scale = 1.0 / math.sqrt(bins * seg_size)
    me_seg = lax.axis_index("seg")

    ring = list(range(0, chan_size, 2)) + list(range(1, chan_size, 2))[::-1]
    ahead = [(ring[i], ring[(i + 1) % chan_size]) for i in range(chan_size)]
    back = [(b, a) for a, b in ahead]
    leftward = [(i + 1, i) for i in range(chan_size - 1)]
    rightward = [(i, i + 1) for i in range(chan_size - 1)]

    live = jnp.arange(slots, dtype=jnp.int32) < pair_counts[0]
    packed = jnp.where(live, 1 + pair_source * (4 * band) + pair_offset + band, 0)
    from_left = lax.ppermute(packed, "chan", rightward)
    from_right = lax.ppermute(packed, "chan", leftward)

    def spread(turn, beside=(), last=None):
        own = pick_rows(turn, pair_counts, source_ids, pair_source, pair_offset, spectra, band)
        forward, backward = [own], [own]
        steps = chan_size // 2
        results = []
        for step in range(1, steps + 1):
            forward.append(lax.ppermute(forward[-1], "chan", ahead))
            if step < chan_size - steps:
                backward.append(lax.ppermute(backward[-1], "chan", back))
            if step <= len(beside) or (step == len(beside) + 1 and last is not None):
                if step <= len(beside):
                    result = beside[step - 1](forward[step - 1])
                else:
                    result = last(results[0][1], forward[step - 1])
                result, forward[-1], backward[-1] = lax.optimization_barrier(
                    (result, forward[-1], backward[-1])
                )
                results.append(result)
        return forward + backward[1:], results

    def prepared(source_turn, turn, pairs, after):
        turns = jnp.stack([source_turn, turn])
        return prepare(turns, source_ids, pairs, chan_rows, chan_size, band, window, after)

    def correlate(chunks, whitened, tables, picks, place):
        bounds = (0, window, 2 * window, slots)

        def piece(part, after):
            start, stop = bounds[part], bounds[part + 1]
            return transform(
                me_seg, picks, chunks, whitened, tables, seg_size, scale, start, stop - start, after
            )

        join = lax.optimization_barrier
        keep_left, send = piece(0, chunks[0])
        got_left = swap(send, 1)
        (keep_right, send), got_left = join((piece(1, send), got_left))
        keep_left, send_left = halve(keep_left, got_left)
        got_right = swap(send, 1)
        got_left = swap(send_left, 2)
        (keep_own, send), got_left, got_right = join((piece(2, send_left), got_left, got_right))
        left = reduce_further(keep_left, got_left, 2)
        right = reduce_further(keep_right, got_right, 1)
        own = reduce_further(keep_own, swap(send, 1), 1)
        from_right = lax.ppermute(left, "chan", leftward)
        from_left = lax.ppermute(right, "chan", rightward)
        flip = (me_seg < seg_size // 2).astype(jnp.int32)
        total = place_rows(flip, place, (left, right, own), 0)
        return place_rows(flip, place, (from_left, from_right), slots, total)

    zero = jnp.int32(0)
    chunks, results = spread(
        zero,
        (
            lambda after: (lag_tables(bins, scale, after), (from_left, from_right, packed)),
            lambda after: whiten_rows(jnp.transpose(spectra[0], (1, 0, 2)), after),
        ),
        lambda pairs, after: prepared(zero, zero, pairs, after),
    )
    (tables, pairs), whitened, (*picks, place, source_turns) = results
    first = correlate(chunks, whitened, tables, picks, place)
    pair_count = pair_turns(chunks, slots, window)[0]
    turns = source_turns[0] * pair_count

    def further(state):
        turn, total = state
        chunks, _ = spread(turn // pair_count)
        *picks, place, _ = prepared(turn // pair_count, turn % pair_count, pairs, chunks[0])
        return turn + 1, total + correlate(chunks, whitened, tables, picks, place)

    return lax.while_loop(lambda state: state[0] < turns, further, (jnp.int32(1), first))[1]


def solution(mesh):
    in_specs = (P("seg", "chan", None, None), P(), P("chan"), P("chan"), P("chan"))
    out_specs = P("seg", "chan")
    return jax.shard_map(
        per_device, mesh=mesh, in_specs=in_specs, out_specs=out_specs, check_vma=False
    )
```

```python
import functools
import math

import jax
import jax.numpy as jnp
from jax import lax
from jax.experimental import pallas as pl
from jax.experimental.pallas import tpu as pltpu
from jax.sharding import PartitionSpec as P

LAGS = 1024
HALF = LAGS // 2
WBLOCK = 64
PICK = 16
BINS_STEP = 512
TABLE_ROWS = 64
EXTRA = 128


def params(mebibytes):
    return pltpu.CompilerParams(vmem_limit_bytes=mebibytes * 1024 * 1024)


def light():
    return pl.CostEstimate(flops=1024, bytes_accessed=1024, transcendentals=0)


def whole(shape):
    return pl.BlockSpec(shape, lambda *_: (0,) * len(shape))


def pick_kernel(
    chan_rows, turn_ref, counts_ref, ids_ref, offset_ref, cells_ref, out_ref,
    rows_ref, held_ref, sems,
):
    first = lax.axis_index("chan") * chan_rows
    turn = turn_ref[0]
    bins = cells_ref.shape[3]
    for i in range(PICK):
        rows_ref[i] = 0
    rank = jnp.int32(0)
    for i in range(ids_ref.shape[0]):
        row = ids_ref[i] - first
        mine = (row >= 0) & (row < chan_rows)
        spot = rank - turn * PICK
        rows_ref[jnp.where(mine & (spot >= 0) & (spot < PICK), spot, PICK)] = row
        rank = rank + mine.astype(jnp.int32)
    copies = [
        pltpu.make_async_copy(cells_ref.at[0, rows_ref[i]], held_ref.at[i], sems.at[i])
        for i in range(PICK)
    ]
    for copy in copies:
        copy.start()

    offset = offset_ref[...]
    slot = lax.broadcasted_iota(jnp.int32, offset.shape, 0) * offset.shape[1]
    slot = slot + lax.broadcasted_iota(jnp.int32, offset.shape, 1)
    live = slot < counts_ref[0]
    kinds = (
        live & (offset >= chan_rows),
        live & (offset < 0),
        live & (offset >= 0) & (offset < chan_rows),
    )
    lane = lax.broadcasted_iota(jnp.int32, (PICK, EXTRA), 1)
    notes = jnp.zeros((PICK, EXTRA), jnp.int32)
    for index, kind in enumerate(kinds):
        total = jnp.sum(jnp.where(kind, 1.0, 0.0)).astype(jnp.int32)
        notes = jnp.where(lane == 2 * index, total >> 5, notes)
        notes = jnp.where(lane == 2 * index + 1, total & 31, notes)
    notes = notes.astype(jnp.float32).astype(jnp.bfloat16)
    out_ref[0, :, pl.ds(bins, EXTRA)] = notes
    out_ref[1, :, pl.ds(bins, EXTRA)] = notes

    for copy in copies:
        copy.wait()
    real = held_ref[:, 0, :].astype(jnp.float32)
    imag = held_ref[:, 1, :].astype(jnp.float32)
    width = min(256, bins)

    def stacked(values):
        return jnp.concatenate([values[:, i : i + width] for i in range(0, bins, width)], axis=0)

    real, imag = whitened_pair(stacked(real), stacked(imag))
    for index in range(bins // width):
        lanes = pl.ds(index * width, width)
        out_ref[0, :, lanes] = real[index * PICK : (index + 1) * PICK]
        out_ref[1, :, lanes] = imag[index * PICK : (index + 1) * PICK]


def pick_rows(turn, counts, source_ids, pair_offset, spectra):
    _, chan_rows, parts, bins = spectra.shape
    smem = pl.BlockSpec(memory_space=pltpu.SMEM)
    vmem = pl.BlockSpec(memory_space=pltpu.VMEM)
    return pl.pallas_call(
        functools.partial(pick_kernel, chan_rows),
        out_shape=jax.ShapeDtypeStruct((parts, PICK, bins + EXTRA), spectra.dtype),
        in_specs=[smem, smem, smem, vmem, pl.BlockSpec(memory_space=pl.ANY)],
        out_specs=vmem,
        scratch_shapes=[
            pltpu.SMEM((PICK + 1,), jnp.int32),
            pltpu.VMEM((PICK, parts, bins), spectra.dtype),
            pltpu.SemaphoreType.DMA((PICK,)),
        ],
        cost_estimate=light(),
        compiler_params=params(8),
        name="pick_rows",
    )(turn.reshape(1), counts, source_ids, pair_offset.reshape(-1, 128), spectra)


def block_mean(power):
    width = power.shape[1]
    row_group = lax.broadcasted_iota(jnp.int32, (width, width), 0) // WBLOCK
    col_group = lax.broadcasted_iota(jnp.int32, (width, width), 1) // WBLOCK
    spread = jnp.where(row_group == col_group, 1.0 / WBLOCK, 0.0).astype(jnp.bfloat16)
    high = power.astype(jnp.bfloat16)
    low = (power - high.astype(jnp.float32)).astype(jnp.bfloat16)
    total = jnp.dot(low, spread, preferred_element_type=jnp.float32)
    return total + jnp.dot(high, spread, preferred_element_type=jnp.float32)


def whitened_pair(real, imag):
    inverse = lax.rsqrt(block_mean(real * real + imag * imag) + 1e-06)
    return (real * inverse).astype(jnp.bfloat16), (imag * inverse).astype(jnp.bfloat16)


def whiten_kernel(cells_ref, after_ref, out_ref):
    for start in range(0, cells_ref.shape[2], 256):
        lanes = pl.ds(start, 256)
        real = cells_ref[0, :, lanes].astype(jnp.float32)
        imag = cells_ref[1, :, lanes].astype(jnp.float32)
        out_ref[0, :, lanes], out_ref[1, :, lanes] = whitened_pair(real, imag)


def whiten_rows(cells, after):
    _, rows, bins = cells.shape
    spec = pl.BlockSpec((2, rows, BINS_STEP), lambda i: (0, 0, i))
    return pl.pallas_call(
        whiten_kernel,
        grid=(bins // BINS_STEP,),
        out_shape=jax.ShapeDtypeStruct(cells.shape, jnp.bfloat16),
        in_specs=[spec, pl.BlockSpec(memory_space=pl.ANY)],
        out_specs=spec,
        cost_estimate=light(),
        compiler_params=params(12),
        name="whiten_rows",
    )(cells, after)


def table_kernel(scale, all_bins, after_ref, cos_ref, sin_ref, coarse_ref, fine_ref):
    step = pl.program_id(0)
    groups = cos_ref.shape[0] // TABLE_ROWS

    @pl.when(step == 0)
    def _():
        def circle(ref, stride, factor):
            shape = ref.shape[1:]
            bins = lax.broadcasted_iota(jnp.int32, shape, 0) * stride
            lags = lax.broadcasted_iota(jnp.int32, shape, 1)
            lags = jnp.where(lags == 0, HALF, lags)
            theta = ((bins * lags) & (2 * all_bins - 1)).astype(jnp.float32) * (math.pi / all_bins)
            ref[0] = jnp.cos(theta) * factor
            ref[1] = jnp.sin(theta) * factor

        circle(coarse_ref, TABLE_ROWS, scale)
        circle(fine_ref, 1, 1.0)

    cos_b = fine_ref[0]
    sin_b = fine_ref[1]
    first = lax.broadcasted_iota(jnp.int32, cos_b.shape, 1) == 0
    for group in range(groups):
        cos_a = coarse_ref[0, pl.ds(step * groups + group, 1), :]
        sin_a = coarse_ref[1, pl.ds(step * groups + group, 1), :]
        rows = pl.ds(group * TABLE_ROWS, TABLE_ROWS)
        cos = jnp.where(first, scale, cos_a * cos_b - sin_a * sin_b)
        cos_ref[rows, :] = cos.astype(jnp.bfloat16)
        sin_ref[rows, :] = (sin_a * cos_b + cos_a * sin_b).astype(jnp.bfloat16)


def lag_tables(bins, scale, after):
    spec = pl.BlockSpec((BINS_STEP, HALF), lambda i: (i, 0))
    shape = jax.ShapeDtypeStruct((bins, HALF), jnp.bfloat16)
    return pl.pallas_call(
        functools.partial(table_kernel, scale, bins),
        grid=(bins // BINS_STEP,),
        out_shape=(shape, shape),
        in_specs=[pl.BlockSpec(memory_space=pl.ANY)],
        out_specs=(spec, spec),
        scratch_shapes=[
            pltpu.VMEM((2, bins // TABLE_ROWS, HALF), jnp.float32),
            pltpu.VMEM((2, TABLE_ROWS, HALF), jnp.float32),
        ],
        cost_estimate=light(),
        compiler_params=params(12),
        name="lag_tables",
    )(after)


def source_spots(chan_rows, chan_size, me, turn, ids_row):
    count = ids_row.shape[1]
    shift = chan_rows.bit_length() - 1
    ids_row = jnp.broadcast_to(ids_row, (count, count))
    rows = lax.broadcasted_iota(jnp.int32, (count, count), 0)
    columns = lax.broadcasted_iota(jnp.int32, (count, count), 1)
    ids = jnp.sum(jnp.where(rows == columns, ids_row, 0).astype(jnp.float32), axis=1, keepdims=True)
    owner = jnp.broadcast_to(ids.astype(jnp.int32) >> shift, (count, count))
    earlier = (owner == (ids_row >> shift)) & (columns < rows)
    rank = jnp.sum(jnp.where(earlier, 1.0, 0.0), axis=1, keepdims=True)
    turns = (jnp.max(rank).astype(jnp.int32) + PICK) // PICK
    rank = rank.astype(jnp.int32) - turn * PICK
    owner = owner[:, 0:1]

    def ring_place(block):
        return jnp.where((block & 1) == 0, block >> 1, chan_size - 1 - (block >> 1))

    steps = chan_size // 2
    distance = ring_place(me) - ring_place(owner)
    distance = jnp.where(distance < 0, distance + chan_size, distance)
    hop = jnp.where(distance <= steps, distance, steps + chan_size - distance)
    return jnp.where((rank >= 0) & (rank < PICK), hop * PICK + rank, -1), turns


def prepare_kernel(
    chan_rows, chan_size, band, window, turns_ref, ids_ref, left_ref, right_ref, own_ref, after_ref,
    src_ref, rec_ref, place_ref, needed_ref,
):
    me = lax.axis_index("chan")
    source_turn = turns_ref[0]
    turn = turns_ref[1]
    slots = own_ref.shape[1]
    spots, needed = source_spots(chan_rows, chan_size, me, source_turn, ids_ref[...])
    needed_ref[0] = needed

    row = lax.broadcasted_iota(jnp.int32, (8, slots), 0)
    packed = jnp.where(row < 5, own_ref[...], 0)
    packed = jnp.where(row == 0, left_ref[...], jnp.where(row == 1, right_ref[...], packed))
    live = packed > 0
    code = packed - 1
    offset = (code & (4 * band - 1)) - band
    source = code >> ((4 * band).bit_length() - 1)
    below = jnp.where(live & (offset < 0), 1.0, 0.0)
    above = jnp.where(live & (offset >= chan_rows), 1.0, 0.0)
    inside = jnp.where(live & (offset >= 0) & (offset < chan_rows), 1.0, 0.0)
    taken = jnp.where((row == 0) | (row == 4), above, jnp.where((row == 1) | (row == 3), below, inside))
    earlier = lax.broadcasted_iota(jnp.int32, (slots, slots), 0) < lax.broadcasted_iota(
        jnp.int32, (slots, slots), 1
    )
    rank = jnp.dot(
        taken.astype(jnp.bfloat16),
        jnp.where(earlier, 1.0, 0.0).astype(jnp.bfloat16),
        preferred_element_type=jnp.float32,
    ).astype(jnp.int32)
    total = jnp.sum(taken, axis=1, keepdims=True).astype(jnp.int32)
    left_total = total[0:1, :]
    right_total = total[1:2, :]

    def done_before(amount, index):
        return jnp.minimum(amount, index * window)

    left_before = done_before(left_total, turn)
    right_before = done_before(right_total, turn)
    left_now = done_before(left_total, turn + 1) - left_before
    right_now = done_before(right_total, turn + 1) - right_before
    own_before = turn * slots - left_before - right_before
    own_room = slots - left_now - right_now
    held = taken > 0

    def in_window(index):
        shifted = rank[index : index + 1, :] - turn * window
        return shifted, held[index : index + 1, :] & (shifted >= 0) & (shifted < window)

    left_rank, left_ok = in_window(0)
    right_rank, right_ok = in_window(1)
    left_pos = jnp.where(left_ok, left_rank, -1)
    right_pos = jnp.where(right_ok, right_rank + window, -1)
    own_rank = rank[2:3, :] - own_before
    own_ok = held[2:3, :] & (own_rank >= 0) & (own_rank < own_room)
    own_pos = own_rank + left_now
    own_pos = jnp.where(own_pos < window, own_pos, own_pos + right_now)
    own_pos = jnp.where(own_ok, own_pos, -1)
    below_rank, below_ok = in_window(3)
    above_rank, above_ok = in_window(4)
    place = jnp.where(below_ok, below_rank + slots, own_pos)
    place = jnp.where(above_ok, above_rank + slots + window, place)
    place_ref[...] = jnp.broadcast_to(place, place_ref.shape)

    wanted = lax.broadcasted_iota(jnp.int32, (slots, slots), 0)
    names = lax.broadcasted_iota(jnp.int32, (spots.shape[0], slots), 0)
    receiver = jnp.where(row == 0, offset - chan_rows, jnp.where(row == 1, offset + chan_rows, offset))
    jobs = jnp.zeros((slots, 8), jnp.float32)
    for index, position in enumerate((left_pos, right_pos, own_pos)):
        spot = jnp.where(names == source[index : index + 1, :], spots + 1, 0).astype(jnp.float32)
        spot = jnp.sum(spot, axis=0, keepdims=True).astype(jnp.int32) - 1
        fields = jnp.where(row == 0, spot >> 4, jnp.where(row == 1, spot & (PICK - 1), 0))
        fields = jnp.where(row == 2, receiver[index : index + 1, :], jnp.where(row == 3, 1, fields))
        fields = jnp.where((position >= 0) & (spot >= 0), fields, 0)
        chosen = jnp.where(wanted == position, 1.0, 0.0).astype(jnp.bfloat16)
        jobs = jobs + lax.dot_general(
            chosen,
            fields.astype(jnp.float32).astype(jnp.bfloat16),
            (((1,), (1,)), ((), ())),
            preferred_element_type=jnp.float32,
        )
    jobs = jobs.astype(jnp.int32)
    busy = jobs[:, 3:4] > 0
    column = jnp.where(busy, jobs[:, 0:1] * PICK + jobs[:, 1:2], -1)
    lanes = lax.broadcasted_iota(jnp.int32, src_ref.shape, 1)
    src_ref[...] = jnp.where(column == lanes, 1.0, 0.0).astype(jnp.bfloat16)
    column = jnp.where(busy, jobs[:, 2:3], -1)
    lanes = lax.broadcasted_iota(jnp.int32, rec_ref.shape, 1)
    rec_ref[...] = jnp.where(column == lanes, 1.0, 0.0).astype(jnp.bfloat16)


def prepare(turns, source_ids, pairs, chan_rows, chan_size, band, window, after):
    slots = pairs[0].shape[0]
    vmem = pl.BlockSpec(memory_space=pltpu.VMEM)
    smem = pl.BlockSpec(memory_space=pltpu.SMEM)
    return pl.pallas_call(
        functools.partial(prepare_kernel, chan_rows, chan_size, band, window),
        out_shape=(
            jax.ShapeDtypeStruct((slots, chan_size * PICK), jnp.bfloat16),
            jax.ShapeDtypeStruct((slots, chan_rows), jnp.bfloat16),
            jax.ShapeDtypeStruct((8, slots), jnp.int32),
            jax.ShapeDtypeStruct((1,), jnp.int32),
        ),
        in_specs=[smem, vmem, vmem, vmem, vmem, pl.BlockSpec(memory_space=pl.ANY)],
        out_specs=(vmem, vmem, vmem, smem),
        cost_estimate=light(),
        compiler_params=params(16),
        name="prepare",
    )(turns, source_ids.reshape(1, -1), *[row.reshape(1, slots) for row in pairs], after)


def turns_kernel(chan_size, slots, window, *refs):
    chunk_refs, out_ref = refs[:-2], refs[-1]
    me = lax.axis_index("chan")
    steps = chan_size // 2
    place = jnp.where((me & 1) == 0, me >> 1, chan_size - 1 - (me >> 1))
    block = lax.broadcasted_iota(jnp.int32, (chan_size, EXTRA), 0)
    notes = jnp.zeros((chan_size, EXTRA), jnp.float32)
    for hop, ref in enumerate(chunk_refs):
        spot = place - hop if hop <= steps else place + hop - steps
        spot = jnp.where(spot < 0, spot + chan_size, spot)
        spot = jnp.where(spot >= chan_size, spot - chan_size, spot)
        owner = jnp.where(spot < steps, 2 * spot, 2 * (chan_size - spot) - 1)
        notes = jnp.where(block == owner, ref[0][0:1, :].astype(jnp.float32), notes)
    lane = lax.broadcasted_iota(jnp.int32, notes.shape, 1)

    def total(index):
        value = jnp.where(lane == 2 * index, 32.0 * notes, 0.0)
        value = value + jnp.where(lane == 2 * index + 1, notes, 0.0)
        return jnp.broadcast_to(jnp.sum(value, axis=1, keepdims=True), notes.shape)

    left = jnp.where(block == 0, 0.0, pltpu.roll(total(0), 1, 0))
    right = jnp.where(block == chan_size - 1, 0.0, pltpu.roll(total(1), chan_size - 1, 0))
    aside = jnp.max(jnp.maximum(left, right)).astype(jnp.int32)
    whole_sum = jnp.max(left + right + total(2)).astype(jnp.int32)
    needed = jnp.maximum((aside + window - 1) // window, (whole_sum + slots - 1) // slots)
    out_ref[0] = jnp.maximum(needed, 1)


def pair_turns(chunks, slots, window, after):
    _, _, width = chunks[0].shape
    last = width // EXTRA - 1
    return pl.pallas_call(
        functools.partial(turns_kernel, len(chunks), slots, window),
        grid=(1,),
        out_shape=jax.ShapeDtypeStruct((1,), jnp.int32),
        in_specs=[pl.BlockSpec((1, PICK, EXTRA), lambda i: (0, 0, last)) for _ in chunks]
        + [pl.BlockSpec(memory_space=pl.ANY)],
        out_specs=pl.BlockSpec(memory_space=pltpu.SMEM),
        cost_estimate=light(),
        compiler_params=params(8),
        name="pair_turns",
    )(*chunks, after)


def transform_kernel(shards, scale, start, chunks, me_ref, src_ref, rec_ref, *refs):
    chunk_refs = refs[:chunks]
    cells_ref, cos_ref, sin_ref, after_ref, keep_ref, send_ref = refs[chunks:]
    rows = keep_ref.shape[1]
    bins = cos_ref.shape[0]
    step = min(BINS_STEP, bins)
    eighth = lax.broadcasted_iota(jnp.int32, (1, 128), 1) & 7
    root = math.sqrt(0.5)
    edge = jnp.where((eighth == 1) | (eighth == 7), root, 0.0)
    edge = jnp.where((eighth == 3) | (eighth == 5), -root, edge)
    edge = jnp.where(eighth == 0, 1.0, jnp.where(eighth == 4, -1.0, edge)) * scale
    edge = edge.astype(jnp.bfloat16).astype(jnp.float32)

    by_src = src_ref[pl.ds(start, rows), :]
    by_rec = rec_ref[pl.ds(start, rows), :]
    even = odd = corner = None
    for first in range(0, bins, step):
        lanes = pl.ds(first, step)
        source_real = jnp.concatenate([ref[0, :, lanes] for ref in chunk_refs], axis=0)
        source_imag = jnp.concatenate([ref[1, :, lanes] for ref in chunk_refs], axis=0)
        sr = jnp.dot(by_src, source_real, preferred_element_type=jnp.float32)
        si = jnp.dot(by_src, source_imag, preferred_element_type=jnp.float32)
        rr = jnp.dot(by_rec, cells_ref[0, :, lanes], preferred_element_type=jnp.float32)
        ri = jnp.dot(by_rec, cells_ref[1, :, lanes], preferred_element_type=jnp.float32)
        real = (sr * rr + si * ri).astype(jnp.bfloat16)
        imag = (si * rr - sr * ri).astype(jnp.bfloat16)
        more_even = jnp.dot(real, cos_ref[lanes, :], preferred_element_type=jnp.float32)
        more_odd = jnp.dot(imag, sin_ref[lanes, :], preferred_element_type=jnp.float32)
        wide = real.astype(jnp.float32)
        sums = wide[:, 0:128]
        for lane in range(128, step, 128):
            sums = sums + wide[:, lane : lane + 128]
        even = more_even if even is None else even + more_even
        odd = more_odd if odd is None else odd + more_odd
        corner = sums if corner is None else corner + sums

    me = me_ref[0]
    width = LAGS // shards
    corner = jnp.sum(corner * edge, axis=1, keepdims=True)
    first = lax.broadcasted_iota(jnp.int32, even.shape, 1) == 0
    later = even - jnp.where(first, 0.0, odd)
    sooner = jnp.where(first, corner, even) + odd
    sooner = pltpu.roll(sooner, HALF - 1, 1)
    for shard in range(shards):
        half = shards // 2
        if shard < half:
            lane = (half - 1 - shard) * width
            value = sooner[:, lane : lane + width]
        else:
            lane = (shard - half) * width
            value = later[:, lane : lane + width]
        place = me ^ shard

        @pl.when((place & 1) == 0)
        def _():
            keep_ref[place >> 1] = value

        @pl.when((place & 1) == 1)
        def _():
            send_ref[place >> 1] = value.astype(jnp.bfloat16)


def transform(me, picks, chunks, cells, tables, shards, scale, start, rows, after):
    width = LAGS // shards
    shape = (shards // 2, rows, width)
    vmem = pl.BlockSpec(memory_space=pltpu.VMEM)
    return pl.pallas_call(
        functools.partial(transform_kernel, shards, scale, start, len(chunks)),
        out_shape=(
            jax.ShapeDtypeStruct(shape, jnp.float32),
            jax.ShapeDtypeStruct(shape, jnp.bfloat16),
        ),
        in_specs=[pl.BlockSpec(memory_space=pltpu.SMEM)]
        + [vmem] * (5 + len(chunks))
        + [pl.BlockSpec(memory_space=pl.ANY)],
        out_specs=(vmem, vmem),
        cost_estimate=light(),
        compiler_params=params(20),
        name="transform",
    )(me.reshape(1), *picks, *chunks, cells, *tables, after)


def swap(send, bit):
    size = lax.axis_size("seg")
    return lax.ppermute(send, "seg", [(i, i ^ bit) for i in range(size)])


def halve(keep, got):
    total = keep + got.astype(jnp.float32)
    return total[0::2], total[1::2].astype(jnp.bfloat16)


def reduce_further(keep, got, bit):
    while keep.shape[0] > 1:
        keep, send = halve(keep, got)
        bit *= 2
        got = swap(send, bit)
    return (keep[0] + got[0].astype(jnp.float32)).astype(jnp.bfloat16)


def place_kernel(start, further, flip_ref, place_ref, *refs):
    out_ref = refs[-1]
    parts = refs[1:-1] if further else refs[:-1]
    width, slots = out_ref.shape
    flip = flip_ref[0]
    rows = lax.broadcasted_iota(jnp.int32, (width, width), 0)
    columns = lax.broadcasted_iota(jnp.int32, (width, width), 1)
    wanted = jnp.where(flip > 0, width - 1 - rows, rows)
    turned = jnp.where(wanted == columns, 1.0, 0.0).astype(jnp.bfloat16)
    total = refs[0][...] if further else jnp.zeros((width, slots), jnp.float32)
    for ref in parts:
        count = ref.shape[0]
        spot = lax.broadcasted_iota(jnp.int32, (count, slots), 0) + start
        chosen = jnp.where(spot == place_ref[0:1, :], 1.0, 0.0).astype(jnp.bfloat16)
        across = lax.dot_general(
            turned, ref[...], (((1,), (1,)), ((), ())), preferred_element_type=jnp.float32
        ).astype(jnp.bfloat16)
        total = total + jnp.dot(across, chosen, preferred_element_type=jnp.float32)
        start += count
    out_ref[...] = total


def place_rows(flip, place, parts, start, total=None):
    width = parts[0].shape[1]
    slots = place.shape[1]
    given = list(parts) if total is None else [total, *parts]
    vmem = pl.BlockSpec(memory_space=pltpu.VMEM)
    return pl.pallas_call(
        functools.partial(place_kernel, start, total is not None),
        out_shape=jax.ShapeDtypeStruct((width, slots), jnp.float32),
        in_specs=[pl.BlockSpec(memory_space=pltpu.SMEM)] + [vmem] * (1 + len(given)),
        out_specs=vmem,
        cost_estimate=light(),
        compiler_params=params(16),
        name="place_rows",
    )(flip.reshape(1), place, *given)


def per_device(spectra, source_ids, pair_source, pair_offset, pair_counts):
    chan_rows = spectra.shape[1]
    bins = spectra.shape[3]
    band = chan_rows // 2
    seg_size = lax.axis_size("seg")
    chan_size = lax.axis_size("chan")
    slots = pair_source.shape[0]
    window = 3 * slots // 8
    scale = 1.0 / math.sqrt(bins * seg_size)
    me_seg = lax.axis_index("seg")

    ring = list(range(0, chan_size, 2)) + list(range(1, chan_size, 2))[::-1]
    ahead = [(ring[i], ring[(i + 1) % chan_size]) for i in range(chan_size)]
    back = [(b, a) for a, b in ahead]
    leftward = [(i + 1, i) for i in range(chan_size - 1)]
    rightward = [(i, i + 1) for i in range(chan_size - 1)]

    join = lax.optimization_barrier

    def pair_lists():
        live = jnp.arange(slots, dtype=jnp.int32) < pair_counts[0]
        packed = jnp.where(live, 1 + pair_source * (4 * band) + pair_offset + band, 0)
        return lax.ppermute(packed, "chan", rightward), lax.ppermute(packed, "chan", leftward), packed

    def gathered(source_turn, turn):
        own = pick_rows(source_turn, pair_counts, source_ids, pair_offset, spectra)
        own, pairs = join((own, pair_lists()))
        turns = jnp.stack([source_turn, turn])
        beside = (
            lambda after: lag_tables(bins, scale, after),
            lambda after: whiten_rows(jnp.transpose(spectra[0], (1, 0, 2)), after),
            lambda after: prepare(
                turns, source_ids, pairs, chan_rows, chan_size, band, window, after
            ),
        )
        forward, backward = [own], [own]
        steps = chan_size // 2
        results = []
        for step in range(1, steps + 1):
            forward.append(lax.ppermute(forward[-1], "chan", ahead))
            if step < chan_size - steps:
                backward.append(lax.ppermute(backward[-1], "chan", back))
            if step <= len(beside):
                result = beside[step - 1](forward[step - 1])
                result, forward[-1], backward[-1] = join((result, forward[-1], backward[-1]))
                results.append(result)
        return forward + backward[1:], *results

    def correlate(chunks, whitened, tables, picks, place):
        bounds = (0, window, 2 * window, slots)

        def piece(part, after):
            start, stop = bounds[part], bounds[part + 1]
            return transform(
                me_seg, picks, chunks, whitened, tables, seg_size, scale, start, stop - start, after
            )

        keep_left, send = piece(0, chunks[0])
        got_left = swap(send, 1)
        (keep_right, send), got_left = join((piece(1, send), got_left))
        keep_left, send_left = halve(keep_left, got_left)
        got_right = swap(send, 1)
        got_left = swap(send_left, 2)
        (keep_own, send), got_left, got_right = join((piece(2, send_left), got_left, got_right))
        left = reduce_further(keep_left, got_left, 2)
        right = reduce_further(keep_right, got_right, 1)
        own = reduce_further(keep_own, swap(send, 1), 1)
        from_right = lax.ppermute(left, "chan", leftward)
        from_left = lax.ppermute(right, "chan", rightward)
        flip = (me_seg < seg_size // 2).astype(jnp.int32)
        total = place_rows(flip, place, (left, right, own), 0)
        return place_rows(flip, place, (from_left, from_right), slots, total), own

    def one_turn(source_turn, turn):
        chunks, tables, whitened, (*picks, place, source_turns) = gathered(source_turn, turn)
        result, own = correlate(chunks, whitened, tables, picks, place)
        return result, own, chunks, source_turns

    zero = jnp.int32(0)
    first, own, chunks, source_turns = one_turn(zero, zero)
    pair_count = pair_turns(chunks, slots, window, own)[0]
    turns = source_turns[0] * pair_count

    def further(state):
        turn, total = state
        return turn + 1, total + one_turn(turn // pair_count, turn % pair_count)[0]

    return lax.while_loop(lambda state: state[0] < turns, further, (jnp.int32(1), first))[1]


def solution(mesh):
    in_specs = (P("seg", "chan", None, None), P(), P("chan"), P("chan"), P("chan"))
    out_specs = P("seg", "chan")
    return jax.shard_map(
        per_device, mesh=mesh, in_specs=in_specs, out_specs=out_specs, check_vma=False
    )
```

```python
import functools
import math

import jax
import jax.numpy as jnp
from jax import lax
from jax.experimental import pallas as pl
from jax.experimental.pallas import tpu as pltpu
from jax.sharding import PartitionSpec as P

LAGS = 1024
HALF = LAGS // 2
WBLOCK = 64
PICK = 16
BINS_STEP = 512
TABLE_ROWS = 64
EXTRA = 128


def params(mebibytes):
    return pltpu.CompilerParams(vmem_limit_bytes=mebibytes * 1024 * 1024)


def light():
    return pl.CostEstimate(flops=1024, bytes_accessed=1024, transcendentals=0)


TOKEN = jax.ShapeDtypeStruct((8, 128), jnp.float32)


def whole(shape):
    return pl.BlockSpec(shape, lambda *_: (0,) * len(shape))


def pick_kernel(
    chan_rows, turn_ref, counts_ref, ids_ref, offset_ref, cells_ref, out_ref,
    rows_ref, held_ref, sems,
):
    first = lax.axis_index("chan") * chan_rows
    turn = turn_ref[0]
    bins = cells_ref.shape[3]
    for i in range(PICK):
        rows_ref[i] = 0
    rank = jnp.int32(0)
    for i in range(ids_ref.shape[0]):
        row = ids_ref[i] - first
        mine = (row >= 0) & (row < chan_rows)
        spot = rank - turn * PICK
        rows_ref[jnp.where(mine & (spot >= 0) & (spot < PICK), spot, PICK)] = row
        rank = rank + mine.astype(jnp.int32)
    copies = [
        pltpu.make_async_copy(cells_ref.at[0, rows_ref[i]], held_ref.at[i], sems.at[i])
        for i in range(PICK)
    ]
    for copy in copies:
        copy.start()

    offset = offset_ref[...]
    slot = lax.broadcasted_iota(jnp.int32, offset.shape, 0) * offset.shape[1]
    slot = slot + lax.broadcasted_iota(jnp.int32, offset.shape, 1)
    live = slot < counts_ref[0]
    kinds = (
        live & (offset >= chan_rows),
        live & (offset < 0),
        live & (offset >= 0) & (offset < chan_rows),
    )
    lane = lax.broadcasted_iota(jnp.int32, (PICK, EXTRA), 1)
    notes = jnp.zeros((PICK, EXTRA), jnp.int32)
    for index, kind in enumerate(kinds):
        total = jnp.sum(jnp.where(kind, 1.0, 0.0)).astype(jnp.int32)
        notes = jnp.where(lane == 2 * index, total >> 5, notes)
        notes = jnp.where(lane == 2 * index + 1, total & 31, notes)
    notes = notes.astype(jnp.float32).astype(jnp.bfloat16)
    out_ref[0, :, pl.ds(bins, EXTRA)] = notes
    out_ref[1, :, pl.ds(bins, EXTRA)] = notes

    for copy in copies:
        copy.wait()
    real = held_ref[:, 0, :].astype(jnp.float32)
    imag = held_ref[:, 1, :].astype(jnp.float32)
    width = min(256, bins)

    def stacked(values):
        return jnp.concatenate([values[:, i : i + width] for i in range(0, bins, width)], axis=0)

    real, imag = whitened_pair(stacked(real), stacked(imag))
    for index in range(bins // width):
        lanes = pl.ds(index * width, width)
        out_ref[0, :, lanes] = real[index * PICK : (index + 1) * PICK]
        out_ref[1, :, lanes] = imag[index * PICK : (index + 1) * PICK]


def pick_rows(turn, counts, source_ids, pair_offset, spectra):
    _, chan_rows, parts, bins = spectra.shape
    smem = pl.BlockSpec(memory_space=pltpu.SMEM)
    vmem = pl.BlockSpec(memory_space=pltpu.VMEM)
    return pl.pallas_call(
        functools.partial(pick_kernel, chan_rows),
        out_shape=jax.ShapeDtypeStruct((parts, PICK, bins + EXTRA), spectra.dtype),
        in_specs=[smem, smem, smem, vmem, pl.BlockSpec(memory_space=pl.ANY)],
        out_specs=vmem,
        scratch_shapes=[
            pltpu.SMEM((PICK + 1,), jnp.int32),
            pltpu.VMEM((PICK, parts, bins), spectra.dtype),
            pltpu.SemaphoreType.DMA((PICK,)),
        ],
        cost_estimate=light(),
        compiler_params=params(8),
        name="pick_rows",
    )(turn.reshape(1), counts, source_ids, pair_offset.reshape(-1, 128), spectra)


def block_mean(power):
    width = power.shape[1]
    row_group = lax.broadcasted_iota(jnp.int32, (width, width), 0) // WBLOCK
    col_group = lax.broadcasted_iota(jnp.int32, (width, width), 1) // WBLOCK
    spread = jnp.where(row_group == col_group, 1.0 / WBLOCK, 0.0).astype(jnp.bfloat16)
    high = power.astype(jnp.bfloat16)
    low = (power - high.astype(jnp.float32)).astype(jnp.bfloat16)
    total = jnp.dot(low, spread, preferred_element_type=jnp.float32)
    return total + jnp.dot(high, spread, preferred_element_type=jnp.float32)


def whitened_pair(real, imag):
    inverse = lax.rsqrt(block_mean(real * real + imag * imag) + 1e-06)
    return (real * inverse).astype(jnp.bfloat16), (imag * inverse).astype(jnp.bfloat16)


def whiten_kernel(cells_ref, after_ref, out_ref, token_ref):
    token_ref[...] = jnp.zeros_like(token_ref)
    for start in range(0, cells_ref.shape[2], 256):
        lanes = pl.ds(start, 256)
        real = cells_ref[0, :, lanes].astype(jnp.float32)
        imag = cells_ref[1, :, lanes].astype(jnp.float32)
        out_ref[0, :, lanes], out_ref[1, :, lanes] = whitened_pair(real, imag)


def whiten_rows(cells, after):
    _, rows, bins = cells.shape
    spec = pl.BlockSpec((2, rows, BINS_STEP), lambda i: (0, 0, i))
    return pl.pallas_call(
        whiten_kernel,
        grid=(bins // BINS_STEP,),
        out_shape=(jax.ShapeDtypeStruct(cells.shape, jnp.bfloat16), TOKEN),
        in_specs=[spec, pl.BlockSpec(memory_space=pl.ANY)],
        out_specs=(spec, whole(TOKEN.shape)),
        cost_estimate=light(),
        compiler_params=params(12),
        name="whiten_rows",
    )(cells, after)


def table_kernel(scale, all_bins, after_ref, cos_ref, sin_ref, token_ref, coarse_ref, fine_ref):
    token_ref[...] = jnp.zeros_like(token_ref)
    step = pl.program_id(0)
    groups = cos_ref.shape[0] // TABLE_ROWS

    @pl.when(step == 0)
    def _():
        def circle(ref, stride, factor):
            shape = ref.shape[1:]
            bins = lax.broadcasted_iota(jnp.int32, shape, 0) * stride
            lags = lax.broadcasted_iota(jnp.int32, shape, 1)
            lags = jnp.where(lags == 0, HALF, lags)
            theta = ((bins * lags) & (2 * all_bins - 1)).astype(jnp.float32) * (math.pi / all_bins)
            ref[0] = jnp.cos(theta) * factor
            ref[1] = jnp.sin(theta) * factor

        circle(coarse_ref, TABLE_ROWS, scale)
        circle(fine_ref, 1, 1.0)

    cos_b = fine_ref[0]
    sin_b = fine_ref[1]
    first = lax.broadcasted_iota(jnp.int32, cos_b.shape, 1) == 0
    for group in range(groups):
        cos_a = coarse_ref[0, pl.ds(step * groups + group, 1), :]
        sin_a = coarse_ref[1, pl.ds(step * groups + group, 1), :]
        rows = pl.ds(group * TABLE_ROWS, TABLE_ROWS)
        cos = jnp.where(first, scale, cos_a * cos_b - sin_a * sin_b)
        cos_ref[rows, :] = cos.astype(jnp.bfloat16)
        sin_ref[rows, :] = (sin_a * cos_b + cos_a * sin_b).astype(jnp.bfloat16)


def lag_tables(bins, scale, after):
    spec = pl.BlockSpec((BINS_STEP, HALF), lambda i: (i, 0))
    shape = jax.ShapeDtypeStruct((bins, HALF), jnp.bfloat16)
    return pl.pallas_call(
        functools.partial(table_kernel, scale, bins),
        grid=(bins // BINS_STEP,),
        out_shape=(shape, shape, TOKEN),
        in_specs=[pl.BlockSpec(memory_space=pl.ANY)],
        out_specs=(spec, spec, whole(TOKEN.shape)),
        scratch_shapes=[
            pltpu.VMEM((2, bins // TABLE_ROWS, HALF), jnp.float32),
            pltpu.VMEM((2, TABLE_ROWS, HALF), jnp.float32),
        ],
        cost_estimate=light(),
        compiler_params=params(12),
        name="lag_tables",
    )(after)


def source_spots(chan_rows, chan_size, me, turn, ids_row):
    count = ids_row.shape[1]
    shift = chan_rows.bit_length() - 1
    ids_row = jnp.broadcast_to(ids_row, (count, count))
    rows = lax.broadcasted_iota(jnp.int32, (count, count), 0)
    columns = lax.broadcasted_iota(jnp.int32, (count, count), 1)
    ids = jnp.sum(jnp.where(rows == columns, ids_row, 0).astype(jnp.float32), axis=1, keepdims=True)
    owner = jnp.broadcast_to(ids.astype(jnp.int32) >> shift, (count, count))
    earlier = (owner == (ids_row >> shift)) & (columns < rows)
    rank = jnp.sum(jnp.where(earlier, 1.0, 0.0), axis=1, keepdims=True)
    turns = (jnp.max(rank).astype(jnp.int32) + PICK) // PICK
    rank = rank.astype(jnp.int32) - turn * PICK
    owner = owner[:, 0:1]

    def ring_place(block):
        return jnp.where((block & 1) == 0, block >> 1, chan_size - 1 - (block >> 1))

    steps = chan_size // 2
    distance = ring_place(me) - ring_place(owner)
    distance = jnp.where(distance < 0, distance + chan_size, distance)
    hop = jnp.where(distance <= steps, distance, steps + chan_size - distance)
    return jnp.where((rank >= 0) & (rank < PICK), hop * PICK + rank, -1), turns


def prepare_kernel(
    chan_rows, chan_size, band, window, turns_ref, ids_ref, left_ref, right_ref, own_ref, after_ref,
    src_ref, rec_ref, place_ref, needed_ref, token_ref,
):
    token_ref[...] = jnp.zeros_like(token_ref)
    me = lax.axis_index("chan")
    source_turn = turns_ref[0]
    turn = turns_ref[1]
    slots = own_ref.shape[1]
    spots, needed = source_spots(chan_rows, chan_size, me, source_turn, ids_ref[...])
    needed_ref[0] = needed

    row = lax.broadcasted_iota(jnp.int32, (8, slots), 0)
    packed = jnp.where(row < 5, own_ref[...], 0)
    packed = jnp.where(row == 0, left_ref[...], jnp.where(row == 1, right_ref[...], packed))
    live = packed > 0
    code = packed - 1
    offset = (code & (4 * band - 1)) - band
    source = code >> ((4 * band).bit_length() - 1)
    below = jnp.where(live & (offset < 0), 1.0, 0.0)
    above = jnp.where(live & (offset >= chan_rows), 1.0, 0.0)
    inside = jnp.where(live & (offset >= 0) & (offset < chan_rows), 1.0, 0.0)
    taken = jnp.where((row == 0) | (row == 4), above, jnp.where((row == 1) | (row == 3), below, inside))
    earlier = lax.broadcasted_iota(jnp.int32, (slots, slots), 0) < lax.broadcasted_iota(
        jnp.int32, (slots, slots), 1
    )
    rank = jnp.dot(
        taken.astype(jnp.bfloat16),
        jnp.where(earlier, 1.0, 0.0).astype(jnp.bfloat16),
        preferred_element_type=jnp.float32,
    ).astype(jnp.int32)
    total = jnp.sum(taken, axis=1, keepdims=True).astype(jnp.int32)
    left_total = total[0:1, :]
    right_total = total[1:2, :]

    def done_before(amount, index):
        return jnp.minimum(amount, index * window)

    left_before = done_before(left_total, turn)
    right_before = done_before(right_total, turn)
    left_now = done_before(left_total, turn + 1) - left_before
    right_now = done_before(right_total, turn + 1) - right_before
    own_before = turn * slots - left_before - right_before
    own_room = slots - left_now - right_now
    held = taken > 0

    def in_window(index):
        shifted = rank[index : index + 1, :] - turn * window
        return shifted, held[index : index + 1, :] & (shifted >= 0) & (shifted < window)

    left_rank, left_ok = in_window(0)
    right_rank, right_ok = in_window(1)
    left_pos = jnp.where(left_ok, left_rank, -1)
    right_pos = jnp.where(right_ok, right_rank + window, -1)
    own_rank = rank[2:3, :] - own_before
    own_ok = held[2:3, :] & (own_rank >= 0) & (own_rank < own_room)
    own_pos = own_rank + left_now
    own_pos = jnp.where(own_pos < window, own_pos, own_pos + right_now)
    own_pos = jnp.where(own_ok, own_pos, -1)
    below_rank, below_ok = in_window(3)
    above_rank, above_ok = in_window(4)
    place = jnp.where(below_ok, below_rank + slots, own_pos)
    place = jnp.where(above_ok, above_rank + slots + window, place)
    place_ref[...] = jnp.broadcast_to(place, place_ref.shape)

    wanted = lax.broadcasted_iota(jnp.int32, (slots, slots), 0)
    names = lax.broadcasted_iota(jnp.int32, (spots.shape[0], slots), 0)
    receiver = jnp.where(row == 0, offset - chan_rows, jnp.where(row == 1, offset + chan_rows, offset))
    jobs = jnp.zeros((slots, 8), jnp.float32)
    for index, position in enumerate((left_pos, right_pos, own_pos)):
        spot = jnp.where(names == source[index : index + 1, :], spots + 1, 0).astype(jnp.float32)
        spot = jnp.sum(spot, axis=0, keepdims=True).astype(jnp.int32) - 1
        fields = jnp.where(row == 0, spot >> 4, jnp.where(row == 1, spot & (PICK - 1), 0))
        fields = jnp.where(row == 2, receiver[index : index + 1, :], jnp.where(row == 3, 1, fields))
        fields = jnp.where((position >= 0) & (spot >= 0), fields, 0)
        chosen = jnp.where(wanted == position, 1.0, 0.0).astype(jnp.bfloat16)
        jobs = jobs + lax.dot_general(
            chosen,
            fields.astype(jnp.float32).astype(jnp.bfloat16),
            (((1,), (1,)), ((), ())),
            preferred_element_type=jnp.float32,
        )
    jobs = jobs.astype(jnp.int32)
    busy = jobs[:, 3:4] > 0
    column = jnp.where(busy, jobs[:, 0:1] * PICK + jobs[:, 1:2], -1)
    lanes = lax.broadcasted_iota(jnp.int32, src_ref.shape, 1)
    src_ref[...] = jnp.where(column == lanes, 1.0, 0.0).astype(jnp.bfloat16)
    column = jnp.where(busy, jobs[:, 2:3], -1)
    lanes = lax.broadcasted_iota(jnp.int32, rec_ref.shape, 1)
    rec_ref[...] = jnp.where(column == lanes, 1.0, 0.0).astype(jnp.bfloat16)


def prepare(turns, source_ids, pairs, chan_rows, chan_size, band, window, after):
    slots = pairs[0].shape[0]
    vmem = pl.BlockSpec(memory_space=pltpu.VMEM)
    smem = pl.BlockSpec(memory_space=pltpu.SMEM)
    return pl.pallas_call(
        functools.partial(prepare_kernel, chan_rows, chan_size, band, window),
        out_shape=(
            jax.ShapeDtypeStruct((slots, chan_size * PICK), jnp.bfloat16),
            jax.ShapeDtypeStruct((slots, chan_rows), jnp.bfloat16),
            jax.ShapeDtypeStruct((8, slots), jnp.int32),
            jax.ShapeDtypeStruct((1,), jnp.int32),
            TOKEN,
        ),
        in_specs=[smem, vmem, vmem, vmem, vmem, pl.BlockSpec(memory_space=pl.ANY)],
        out_specs=(vmem, vmem, vmem, smem, vmem),
        cost_estimate=light(),
        compiler_params=params(16),
        name="prepare",
    )(turns, source_ids.reshape(1, -1), *[row.reshape(1, slots) for row in pairs], after)


def turns_kernel(chan_size, slots, window, *refs):
    chunk_refs, out_ref = refs[:chan_size], refs[-1]
    me = lax.axis_index("chan")
    steps = chan_size // 2
    place = jnp.where((me & 1) == 0, me >> 1, chan_size - 1 - (me >> 1))
    block = lax.broadcasted_iota(jnp.int32, (chan_size, EXTRA), 0)
    notes = jnp.zeros((chan_size, EXTRA), jnp.float32)
    for hop, ref in enumerate(chunk_refs):
        spot = place - hop if hop <= steps else place + hop - steps
        spot = jnp.where(spot < 0, spot + chan_size, spot)
        spot = jnp.where(spot >= chan_size, spot - chan_size, spot)
        owner = jnp.where(spot < steps, 2 * spot, 2 * (chan_size - spot) - 1)
        notes = jnp.where(block == owner, ref[0][0:1, :].astype(jnp.float32), notes)
    lane = lax.broadcasted_iota(jnp.int32, notes.shape, 1)

    def total(index):
        value = jnp.where(lane == 2 * index, 32.0 * notes, 0.0)
        value = value + jnp.where(lane == 2 * index + 1, notes, 0.0)
        return jnp.broadcast_to(jnp.sum(value, axis=1, keepdims=True), notes.shape)

    left = jnp.where(block == 0, 0.0, pltpu.roll(total(0), 1, 0))
    right = jnp.where(block == chan_size - 1, 0.0, pltpu.roll(total(1), chan_size - 1, 0))
    aside = jnp.max(jnp.maximum(left, right)).astype(jnp.int32)
    whole_sum = jnp.max(left + right + total(2)).astype(jnp.int32)
    needed = jnp.maximum((aside + window - 1) // window, (whole_sum + slots - 1) // slots)
    out_ref[0] = jnp.maximum(needed, 1)


def pair_turns(chunks, slots, window, after):
    _, _, width = chunks[0].shape
    last = width // EXTRA - 1
    return pl.pallas_call(
        functools.partial(turns_kernel, len(chunks), slots, window),
        grid=(1,),
        out_shape=jax.ShapeDtypeStruct((1,), jnp.int32),
        in_specs=[pl.BlockSpec((1, PICK, EXTRA), lambda i: (0, 0, last)) for _ in chunks]
        + [pl.BlockSpec(memory_space=pl.ANY)] * len(after),
        out_specs=pl.BlockSpec(memory_space=pltpu.SMEM),
        cost_estimate=light(),
        compiler_params=params(8),
        name="pair_turns",
    )(*chunks, *after)


def transform_kernel(shards, scale, start, chunks, me_ref, src_ref, rec_ref, *refs):
    chunk_refs = refs[:chunks]
    cells_ref, cos_ref, sin_ref = refs[chunks : chunks + 3]
    keep_ref, send_ref, token_ref = refs[-3:]
    token_ref[...] = jnp.zeros_like(token_ref)
    rows = keep_ref.shape[1]
    bins = cos_ref.shape[0]
    step = min(BINS_STEP, bins)
    eighth = lax.broadcasted_iota(jnp.int32, (1, 128), 1) & 7
    root = math.sqrt(0.5)
    edge = jnp.where((eighth == 1) | (eighth == 7), root, 0.0)
    edge = jnp.where((eighth == 3) | (eighth == 5), -root, edge)
    edge = jnp.where(eighth == 0, 1.0, jnp.where(eighth == 4, -1.0, edge)) * scale
    edge = edge.astype(jnp.bfloat16).astype(jnp.float32)

    by_src = src_ref[pl.ds(start, rows), :]
    by_rec = rec_ref[pl.ds(start, rows), :]
    even = odd = corner = None
    for first in range(0, bins, step):
        lanes = pl.ds(first, step)
        source_real = jnp.concatenate([ref[0, :, lanes] for ref in chunk_refs], axis=0)
        source_imag = jnp.concatenate([ref[1, :, lanes] for ref in chunk_refs], axis=0)
        sr = jnp.dot(by_src, source_real, preferred_element_type=jnp.float32)
        si = jnp.dot(by_src, source_imag, preferred_element_type=jnp.float32)
        rr = jnp.dot(by_rec, cells_ref[0, :, lanes], preferred_element_type=jnp.float32)
        ri = jnp.dot(by_rec, cells_ref[1, :, lanes], preferred_element_type=jnp.float32)
        real = (sr * rr + si * ri).astype(jnp.bfloat16)
        imag = (si * rr - sr * ri).astype(jnp.bfloat16)
        more_even = jnp.dot(real, cos_ref[lanes, :], preferred_element_type=jnp.float32)
        more_odd = jnp.dot(imag, sin_ref[lanes, :], preferred_element_type=jnp.float32)
        wide = real.astype(jnp.float32)
        sums = wide[:, 0:128]
        for lane in range(128, step, 128):
            sums = sums + wide[:, lane : lane + 128]
        even = more_even if even is None else even + more_even
        odd = more_odd if odd is None else odd + more_odd
        corner = sums if corner is None else corner + sums

    me = me_ref[0]
    width = LAGS // shards
    corner = jnp.sum(corner * edge, axis=1, keepdims=True)
    first = lax.broadcasted_iota(jnp.int32, even.shape, 1) == 0
    later = even - jnp.where(first, 0.0, odd)
    sooner = jnp.where(first, corner, even) + odd
    sooner = pltpu.roll(sooner, HALF - 1, 1)
    for shard in range(shards):
        half = shards // 2
        if shard < half:
            lane = (half - 1 - shard) * width
            value = sooner[:, lane : lane + width]
        else:
            lane = (shard - half) * width
            value = later[:, lane : lane + width]
        place = me ^ shard

        @pl.when((place & 1) == 0)
        def _():
            keep_ref[place >> 1] = value

        @pl.when((place & 1) == 1)
        def _():
            send_ref[place >> 1] = value.astype(jnp.bfloat16)


def transform(me, picks, chunks, cells, tables, shards, scale, start, rows, *after):
    width = LAGS // shards
    shape = (shards // 2, rows, width)
    vmem = pl.BlockSpec(memory_space=pltpu.VMEM)
    return pl.pallas_call(
        functools.partial(transform_kernel, shards, scale, start, len(chunks)),
        out_shape=(
            jax.ShapeDtypeStruct(shape, jnp.float32),
            jax.ShapeDtypeStruct(shape, jnp.bfloat16),
            TOKEN,
        ),
        in_specs=[pl.BlockSpec(memory_space=pltpu.SMEM)]
        + [vmem] * (5 + len(chunks))
        + [pl.BlockSpec(memory_space=pl.ANY)] * len(after),
        out_specs=(vmem, vmem, vmem),
        cost_estimate=light(),
        compiler_params=params(20),
        name="transform",
    )(me.reshape(1), *picks, *chunks, cells, *tables, *after)


def swap(send, bit):
    size = lax.axis_size("seg")
    return lax.ppermute(send, "seg", [(i, i ^ bit) for i in range(size)])


def halve(keep, got):
    total = keep + got.astype(jnp.float32)
    return total[0::2], total[1::2].astype(jnp.bfloat16)


def reduce_further(keep, got, bit):
    while keep.shape[0] > 1:
        keep, send = halve(keep, got)
        bit *= 2
        got = swap(send, bit)
    return (keep[0] + got[0].astype(jnp.float32)).astype(jnp.bfloat16)


def place_kernel(start, further, flip_ref, place_ref, *refs):
    out_ref = refs[-1]
    parts = refs[1:-1] if further else refs[:-1]
    width, slots = out_ref.shape
    flip = flip_ref[0]
    rows = lax.broadcasted_iota(jnp.int32, (width, width), 0)
    columns = lax.broadcasted_iota(jnp.int32, (width, width), 1)
    wanted = jnp.where(flip > 0, width - 1 - rows, rows)
    turned = jnp.where(wanted == columns, 1.0, 0.0).astype(jnp.bfloat16)
    total = refs[0][...] if further else jnp.zeros((width, slots), jnp.float32)
    for ref in parts:
        count = ref.shape[0]
        spot = lax.broadcasted_iota(jnp.int32, (count, slots), 0) + start
        chosen = jnp.where(spot == place_ref[0:1, :], 1.0, 0.0).astype(jnp.bfloat16)
        across = lax.dot_general(
            turned, ref[...], (((1,), (1,)), ((), ())), preferred_element_type=jnp.float32
        ).astype(jnp.bfloat16)
        total = total + jnp.dot(across, chosen, preferred_element_type=jnp.float32)
        start += count
    out_ref[...] = total


def place_rows(flip, place, parts, start, total=None):
    width = parts[0].shape[1]
    slots = place.shape[1]
    given = list(parts) if total is None else [total, *parts]
    vmem = pl.BlockSpec(memory_space=pltpu.VMEM)
    return pl.pallas_call(
        functools.partial(place_kernel, start, total is not None),
        out_shape=jax.ShapeDtypeStruct((width, slots), jnp.float32),
        in_specs=[pl.BlockSpec(memory_space=pltpu.SMEM)] + [vmem] * (1 + len(given)),
        out_specs=vmem,
        cost_estimate=light(),
        compiler_params=params(16),
        name="place_rows",
    )(flip.reshape(1), place, *given)


def per_device(spectra, source_ids, pair_source, pair_offset, pair_counts):
    chan_rows = spectra.shape[1]
    bins = spectra.shape[3]
    band = chan_rows // 2
    seg_size = lax.axis_size("seg")
    chan_size = lax.axis_size("chan")
    slots = pair_source.shape[0]
    window = 3 * slots // 8
    scale = 1.0 / math.sqrt(bins * seg_size)
    me_seg = lax.axis_index("seg")

    ring = list(range(0, chan_size, 2)) + list(range(1, chan_size, 2))[::-1]
    ahead = [(ring[i], ring[(i + 1) % chan_size]) for i in range(chan_size)]
    back = [(b, a) for a, b in ahead]
    leftward = [(i + 1, i) for i in range(chan_size - 1)]
    rightward = [(i, i + 1) for i in range(chan_size - 1)]

    join = lax.optimization_barrier

    def pair_lists():
        live = jnp.arange(slots, dtype=jnp.int32) < pair_counts[0]
        packed = jnp.where(live, 1 + pair_source * (4 * band) + pair_offset + band, 0)
        return lax.ppermute(packed, "chan", rightward), lax.ppermute(packed, "chan", leftward), packed

    def gathered(source_turn, turn):
        turns = jnp.stack([source_turn, turn])
        own = pick_rows(source_turn, pair_counts, source_ids, pair_offset, spectra)
        forward, backward = [own], [own]
        steps = chan_size // 2

        def step_beside(work=None):
            forward.append(lax.ppermute(forward[-1], "chan", ahead))
            if len(backward) < chan_size - steps:
                backward.append(lax.ppermute(backward[-1], "chan", back))
            if work is not None:
                *results, token = work()
                token, forward[-1], backward[-1] = join((token, forward[-1], backward[-1]))
                return results, token

        *pairs, mine = pair_lists()
        _, pairs = step_beside(lambda: (pairs,))
        pairs = (*pairs, mine)
        tables, token = step_beside(lambda: lag_tables(bins, scale, pairs[0]))
        flat = jnp.transpose(spectra[0], (1, 0, 2))
        (whitened,), token = step_beside(lambda: whiten_rows(flat, token))
        for _ in range(4, steps):
            step_beside()
        picks, token = step_beside(
            lambda: prepare(turns, source_ids, pairs, chan_rows, chan_size, band, window, token)
        )
        return forward + backward[1:], tables, whitened, picks, token

    def correlate(chunks, whitened, tables, picks, place, token):
        bounds = (0, window, 2 * window, slots)

        def piece(part, *after):
            start, stop = bounds[part], bounds[part + 1]
            return transform(
                me_seg, picks, chunks, whitened, tables, seg_size, scale, start, stop - start, *after
            )

        keep_left, send, _ = piece(0, token)
        got_left = swap(send, 1)
        keep_right, send, token = piece(1, send)
        token, got_left = join((token, got_left))
        keep_left, send_left = halve(keep_left, got_left)
        got_right = swap(send, 1)
        got_left = swap(send_left, 2)
        keep_own, send, token = piece(2, send_left, token)
        token, got_left, got_right = join((token, got_left, got_right))
        left = reduce_further(keep_left, got_left, 2)
        right = reduce_further(keep_right, got_right, 1)
        own = reduce_further(keep_own, swap(send, 1), 1)
        from_right = lax.ppermute(left, "chan", leftward)
        from_left = lax.ppermute(right, "chan", rightward)
        flip = (me_seg < seg_size // 2).astype(jnp.int32)
        total = place_rows(flip, place, (left, right, own), 0)
        return place_rows(flip, place, (from_left, from_right), slots, total), (own, token)

    def one_turn(source_turn, turn):
        chunks, tables, whitened, (*picks, place, source_turns), token = gathered(source_turn, turn)
        result, after = correlate(chunks, whitened, tables, picks, place, token)
        return result, after, chunks, source_turns

    zero = jnp.int32(0)
    first, after, chunks, source_turns = one_turn(zero, zero)
    pair_count = pair_turns(chunks, slots, window, after)[0]
    turns = source_turns[0] * pair_count

    def further(state):
        turn, total = state
        return turn + 1, total + one_turn(turn // pair_count, turn % pair_count)[0]

    return lax.while_loop(lambda state: state[0] < turns, further, (jnp.int32(1), first))[1]


def solution(mesh):
    in_specs = (P("seg", "chan", None, None), P(), P("chan"), P("chan"), P("chan"))
    out_specs = P("seg", "chan")
    return jax.shard_map(
        per_device, mesh=mesh, in_specs=in_specs, out_specs=out_specs, check_vma=False
    )
```

```python
import functools
import math

import jax
import jax.numpy as jnp
from jax import lax
from jax.experimental import pallas as pl
from jax.experimental.pallas import tpu as pltpu
from jax.sharding import PartitionSpec as P

LAGS = 1024
HALF = LAGS // 2
WBLOCK = 64
PICK = 16
BINS_STEP = 512
TABLE_ROWS = 64
EXTRA = 128


def params(mebibytes):
    return pltpu.CompilerParams(vmem_limit_bytes=mebibytes * 1024 * 1024)


def light():
    return pl.CostEstimate(flops=1024, bytes_accessed=1024, transcendentals=0)


TOKEN = jax.ShapeDtypeStruct((8, 128), jnp.float32)


def whole(shape):
    return pl.BlockSpec(shape, lambda *_: (0,) * len(shape))


def pick_kernel(
    chan_rows, band, turns_ref, counts_ref, ids_ref, source_ref, offset_ref, cells_ref, out_ref,
    rows_ref, held_ref, sems,
):
    first = lax.axis_index("chan") * chan_rows
    turn = turns_ref[0]
    bins = cells_ref.shape[3]
    for i in range(PICK):
        rows_ref[i] = 0
    rank = jnp.int32(0)
    for i in range(ids_ref.shape[0]):
        row = ids_ref[i] - first
        mine = (row >= 0) & (row < chan_rows)
        spot = rank - turn * PICK
        rows_ref[jnp.where(mine & (spot >= 0) & (spot < PICK), spot, PICK)] = row
        rank = rank + mine.astype(jnp.int32)
    copies = [
        pltpu.make_async_copy(cells_ref.at[0, rows_ref[i]], held_ref.at[i], sems.at[i])
        for i in range(PICK)
    ]
    for copy in copies:
        copy.start()

    offset = offset_ref[...]
    slot = lax.broadcasted_iota(jnp.int32, offset.shape, 0) * offset.shape[1]
    slot = slot + lax.broadcasted_iota(jnp.int32, offset.shape, 1)
    live = slot < counts_ref[0]
    kinds = (
        live & (offset >= chan_rows),
        live & (offset < 0),
        live & (offset >= 0) & (offset < chan_rows),
    )
    lane = lax.broadcasted_iota(jnp.int32, offset.shape, 1)
    notes = jnp.zeros(offset.shape, jnp.int32)
    for index, kind in enumerate(kinds):
        total = jnp.sum(jnp.where(kind, 1.0, 0.0)).astype(jnp.int32)
        notes = jnp.where(lane == 2 * index, total >> 5, notes)
        notes = jnp.where(lane == 2 * index + 1, total & 31, notes)
    shifted = offset + band
    source = jnp.where(live, source_ref[...] + 1, 0)

    def coded(upper, lower):
        both = jnp.concatenate([upper.astype(jnp.float32), lower.astype(jnp.float32)], axis=0)
        return both.astype(jnp.bfloat16)

    out_ref[0, :, pl.ds(bins, EXTRA)] = coded(source, shifted >> 4)
    out_ref[1, :, pl.ds(bins, EXTRA)] = coded(shifted & 15, notes)

    for copy in copies:
        copy.wait()
    real = held_ref[:, 0, :].astype(jnp.float32)
    imag = held_ref[:, 1, :].astype(jnp.float32)
    width = min(256, bins)

    def stacked(values):
        return jnp.concatenate([values[:, i : i + width] for i in range(0, bins, width)], axis=0)

    real, imag = whitened_pair(stacked(real), stacked(imag))
    for index in range(bins // width):
        lanes = pl.ds(index * width, width)
        out_ref[0, :, lanes] = real[index * PICK : (index + 1) * PICK]
        out_ref[1, :, lanes] = imag[index * PICK : (index + 1) * PICK]


def pick_rows(turns, counts, source_ids, pair_source, pair_offset, spectra):
    _, chan_rows, parts, bins = spectra.shape
    smem = pl.BlockSpec(memory_space=pltpu.SMEM)
    vmem = pl.BlockSpec(memory_space=pltpu.VMEM)
    return pl.pallas_call(
        functools.partial(pick_kernel, chan_rows, chan_rows // 2),
        out_shape=jax.ShapeDtypeStruct((parts, PICK, bins + EXTRA), spectra.dtype),
        in_specs=[smem, smem, smem, vmem, vmem, pl.BlockSpec(memory_space=pl.ANY)],
        out_specs=vmem,
        scratch_shapes=[
            pltpu.SMEM((PICK + 1,), jnp.int32),
            pltpu.VMEM((PICK, parts, bins), spectra.dtype),
            pltpu.SemaphoreType.DMA((PICK,)),
        ],
        cost_estimate=light(),
        compiler_params=params(8),
        name="pick_rows",
    )(
        turns, counts, source_ids, pair_source.reshape(-1, EXTRA), pair_offset.reshape(-1, EXTRA), spectra
    )


def block_mean(power):
    width = power.shape[1]
    row_group = lax.broadcasted_iota(jnp.int32, (width, width), 0) // WBLOCK
    col_group = lax.broadcasted_iota(jnp.int32, (width, width), 1) // WBLOCK
    spread = jnp.where(row_group == col_group, 1.0 / WBLOCK, 0.0).astype(jnp.bfloat16)
    high = power.astype(jnp.bfloat16)
    low = (power - high.astype(jnp.float32)).astype(jnp.bfloat16)
    total = jnp.dot(low, spread, preferred_element_type=jnp.float32)
    return total + jnp.dot(high, spread, preferred_element_type=jnp.float32)


def whitened_pair(real, imag):
    inverse = lax.rsqrt(block_mean(real * real + imag * imag) + 1e-06)
    return (real * inverse).astype(jnp.bfloat16), (imag * inverse).astype(jnp.bfloat16)


def whiten_kernel(cells_ref, after_ref, out_ref, token_ref):
    token_ref[...] = jnp.zeros_like(token_ref)
    for start in range(0, cells_ref.shape[2], 256):
        lanes = pl.ds(start, 256)
        real = cells_ref[0, :, lanes].astype(jnp.float32)
        imag = cells_ref[1, :, lanes].astype(jnp.float32)
        out_ref[0, :, lanes], out_ref[1, :, lanes] = whitened_pair(real, imag)


def whiten_rows(cells, after):
    _, rows, bins = cells.shape
    spec = pl.BlockSpec((2, rows, BINS_STEP), lambda i: (0, 0, i))
    return pl.pallas_call(
        whiten_kernel,
        grid=(bins // BINS_STEP,),
        out_shape=(jax.ShapeDtypeStruct(cells.shape, jnp.bfloat16), TOKEN),
        in_specs=[spec, pl.BlockSpec(memory_space=pl.ANY)],
        out_specs=(spec, whole(TOKEN.shape)),
        cost_estimate=light(),
        compiler_params=params(12),
        name="whiten_rows",
    )(cells, after)


def table_kernel(scale, all_bins, after_ref, cos_ref, sin_ref, token_ref, coarse_ref, fine_ref):
    token_ref[...] = jnp.zeros_like(token_ref)
    step = pl.program_id(0)
    groups = cos_ref.shape[0] // TABLE_ROWS

    @pl.when(step == 0)
    def _():
        def circle(ref, stride, factor):
            shape = ref.shape[1:]
            bins = lax.broadcasted_iota(jnp.int32, shape, 0) * stride
            lags = lax.broadcasted_iota(jnp.int32, shape, 1)
            lags = jnp.where(lags == 0, HALF, lags)
            theta = ((bins * lags) & (2 * all_bins - 1)).astype(jnp.float32) * (math.pi / all_bins)
            ref[0] = jnp.cos(theta) * factor
            ref[1] = jnp.sin(theta) * factor

        circle(coarse_ref, TABLE_ROWS, scale)
        circle(fine_ref, 1, 1.0)

    cos_b = fine_ref[0]
    sin_b = fine_ref[1]
    first = lax.broadcasted_iota(jnp.int32, cos_b.shape, 1) == 0
    for group in range(groups):
        cos_a = coarse_ref[0, pl.ds(step * groups + group, 1), :]
        sin_a = coarse_ref[1, pl.ds(step * groups + group, 1), :]
        rows = pl.ds(group * TABLE_ROWS, TABLE_ROWS)
        cos = jnp.where(first, scale, cos_a * cos_b - sin_a * sin_b)
        cos_ref[rows, :] = cos.astype(jnp.bfloat16)
        sin_ref[rows, :] = (sin_a * cos_b + cos_a * sin_b).astype(jnp.bfloat16)


def lag_tables(bins, scale, after):
    spec = pl.BlockSpec((BINS_STEP, HALF), lambda i: (i, 0))
    shape = jax.ShapeDtypeStruct((bins, HALF), jnp.bfloat16)
    return pl.pallas_call(
        functools.partial(table_kernel, scale, bins),
        grid=(bins // BINS_STEP,),
        out_shape=(shape, shape, TOKEN),
        in_specs=[pl.BlockSpec(memory_space=pl.ANY)],
        out_specs=(spec, spec, whole(TOKEN.shape)),
        scratch_shapes=[
            pltpu.VMEM((2, bins // TABLE_ROWS, HALF), jnp.float32),
            pltpu.VMEM((2, TABLE_ROWS, HALF), jnp.float32),
        ],
        cost_estimate=light(),
        compiler_params=params(12),
        name="lag_tables",
    )(after)


def source_spots(chan_rows, chan_size, me, turn, ids_row):
    count = ids_row.shape[1]
    shift = chan_rows.bit_length() - 1
    ids_row = jnp.broadcast_to(ids_row, (count, count))
    rows = lax.broadcasted_iota(jnp.int32, (count, count), 0)
    columns = lax.broadcasted_iota(jnp.int32, (count, count), 1)
    ids = jnp.sum(jnp.where(rows == columns, ids_row, 0).astype(jnp.float32), axis=1, keepdims=True)
    owner = jnp.broadcast_to(ids.astype(jnp.int32) >> shift, (count, count))
    earlier = (owner == (ids_row >> shift)) & (columns < rows)
    rank = jnp.sum(jnp.where(earlier, 1.0, 0.0), axis=1, keepdims=True)
    turns = (jnp.max(rank).astype(jnp.int32) + PICK) // PICK
    rank = rank.astype(jnp.int32) - turn * PICK
    owner = owner[:, 0:1]

    def ring_place(block):
        return jnp.where((block & 1) == 0, block >> 1, chan_size - 1 - (block >> 1))

    steps = chan_size // 2
    distance = ring_place(me) - ring_place(owner)
    distance = jnp.where(distance < 0, distance + chan_size, distance)
    hop = jnp.where(distance <= steps, distance, steps + chan_size - distance)
    return jnp.where((rank >= 0) & (rank < PICK), hop * PICK + rank, -1), turns


def prepare_kernel(
    chan_rows, chan_size, band, window, turns_ref, ids_ref, after_ref, *refs
):
    chunk_refs = refs[:chan_size]
    src_ref, rec_ref, place_ref, needed_ref, token_ref = refs[chan_size:]
    token_ref[...] = jnp.zeros_like(token_ref)
    me = lax.axis_index("chan")
    source_turn = turns_ref[0]
    turn = turns_ref[1]
    slots = place_ref.shape[1]
    bins = chunk_refs[0].shape[2] - EXTRA
    spots, needed = source_spots(chan_rows, chan_size, me, source_turn, ids_ref[...])
    needed_ref[0] = needed

    def ring_place(block):
        return jnp.where((block & 1) == 0, block >> 1, chan_size - 1 - (block >> 1))

    def hop_of(block):
        steps = chan_size // 2
        distance = ring_place(me) - ring_place(block)
        distance = jnp.where(distance < 0, distance + chan_size, distance)
        return jnp.where(distance <= steps, distance, steps + chan_size - distance)

    lanes = pl.ds(bins, EXTRA)
    left_hop = jnp.where(me > 0, hop_of(me - 1), -1)
    right_hop = jnp.where(me < chan_size - 1, hop_of(me + 1), -1)
    listed = []
    for wanted in (left_hop, right_hop, None):
        halves = []
        for half in range(2):
            if wanted is None:
                value = chunk_refs[0][half, :, lanes].astype(jnp.float32)
            else:
                value = jnp.zeros((PICK, EXTRA), jnp.float32)
                for hop, ref in enumerate(chunk_refs):
                    value = jnp.where(wanted == hop, ref[half, :, lanes].astype(jnp.float32), value)
            halves.append(value.astype(jnp.int32))
        source = halves[0][0:8] - 1
        offset = halves[0][8:16] * 16 + halves[1][0:8] - band
        listed.append((source, offset))
    (left_src, left_off), (right_src, right_off), (own_src, own_off) = listed
    own_live = own_src >= 0
    taken = (
        (left_src >= 0) & (left_off >= chan_rows),
        (right_src >= 0) & (right_off < 0),
        own_live & (own_off >= 0) & (own_off < chan_rows),
        own_live & (own_off < 0),
        own_live & (own_off >= chan_rows),
    )

    marks = jnp.concatenate([jnp.where(mask, 1.0, 0.0) for mask in taken], axis=0)
    rows = marks.shape[0]
    earlier = lax.broadcasted_iota(jnp.int32, (EXTRA, EXTRA), 0) < lax.broadcasted_iota(
        jnp.int32, (EXTRA, EXTRA), 1
    )
    rank = jnp.dot(
        marks.astype(jnp.bfloat16),
        jnp.where(earlier, 1.0, 0.0).astype(jnp.bfloat16),
        preferred_element_type=jnp.float32,
    )
    sums = jnp.broadcast_to(jnp.sum(marks, axis=1, keepdims=True), marks.shape)
    row = lax.broadcasted_iota(jnp.int32, (rows, rows), 0)
    column = lax.broadcasted_iota(jnp.int32, (rows, rows), 1)
    above_it = ((row >> 3) == (column >> 3)) & (column < row)
    rank = rank + jnp.dot(
        jnp.where(above_it, 1.0, 0.0).astype(jnp.bfloat16),
        sums.astype(jnp.bfloat16),
        preferred_element_type=jnp.float32,
    )
    rank = rank.astype(jnp.int32)
    ranks = [rank[8 * i : 8 * i + 8] for i in range(5)]
    left_total = jnp.sum(marks[0:8]).astype(jnp.int32)
    right_total = jnp.sum(marks[8:16]).astype(jnp.int32)

    def done_before(amount, index):
        return jnp.minimum(amount, index * window)

    left_before = done_before(left_total, turn)
    right_before = done_before(right_total, turn)
    left_now = done_before(left_total, turn + 1) - left_before
    right_now = done_before(right_total, turn + 1) - right_before
    own_before = turn * slots - left_before - right_before
    own_room = slots - left_now - right_now

    def in_window(index):
        shifted = ranks[index] - turn * window
        return shifted, taken[index] & (shifted >= 0) & (shifted < window)

    def flat(value):
        return jnp.concatenate([value[i : i + 1, :] for i in range(8)], axis=1)

    left_rank, left_ok = in_window(0)
    right_rank, right_ok = in_window(1)
    own_rank = ranks[2] - own_before
    own_ok = taken[2] & (own_rank >= 0) & (own_rank < own_room)
    own_pos = own_rank + left_now
    own_pos = jnp.where(own_pos < window, own_pos, own_pos + right_now)
    own_pos = jnp.where(own_ok, own_pos, -1)
    below_rank, below_ok = in_window(3)
    above_rank, above_ok = in_window(4)
    place = jnp.where(below_ok, below_rank + slots, own_pos)
    place = jnp.where(above_ok, above_rank + slots + window, place)
    place_ref[...] = jnp.broadcast_to(flat(place), place_ref.shape)

    names = lax.broadcasted_iota(jnp.int32, (spots.shape[0], slots), 0)
    field_row = lax.broadcasted_iota(jnp.int32, (8, slots), 0)

    def jobs_of(source, receiver, position, count):
        source, receiver, position = flat(source), flat(receiver), flat(position)
        spot = jnp.where(names == source, spots + 1, 0).astype(jnp.float32)
        spot = jnp.sum(spot, axis=0, keepdims=True).astype(jnp.int32) - 1
        fields = jnp.where(field_row == 0, spot >> 4, jnp.where(field_row == 1, spot & (PICK - 1), 0))
        fields = jnp.where(field_row == 2, receiver, jnp.where(field_row == 3, 1, fields))
        fields = jnp.where((position >= 0) & (spot >= 0), fields, 0)
        wanted = lax.broadcasted_iota(jnp.int32, (count, slots), 0)
        chosen = jnp.where(wanted == position, 1.0, 0.0).astype(jnp.bfloat16)
        return lax.dot_general(
            chosen,
            fields.astype(jnp.float32).astype(jnp.bfloat16),
            (((1,), (1,)), ((), ())),
            preferred_element_type=jnp.float32,
        )

    left_jobs = jobs_of(left_src, left_off - chan_rows, jnp.where(left_ok, left_rank, -1), window)
    right_jobs = jobs_of(right_src, right_off + chan_rows, jnp.where(right_ok, right_rank, -1), window)
    own_jobs = jobs_of(own_src, own_off, own_pos, slots)
    pieces = (
        (0, window, left_jobs + own_jobs[0:window]),
        (window, window, right_jobs + own_jobs[window : 2 * window]),
        (2 * window, slots - 2 * window, own_jobs[2 * window :]),
    )
    for start, count, jobs in pieces:
        jobs = jobs.astype(jnp.int32)
        busy = jobs[:, 3:4] > 0
        part = pl.ds(start, count)
        column = jnp.where(busy, jobs[:, 0:1] * PICK + jobs[:, 1:2], -1)
        lane = lax.broadcasted_iota(jnp.int32, (count, src_ref.shape[1]), 1)
        src_ref[part, :] = jnp.where(column == lane, 1.0, 0.0).astype(jnp.bfloat16)
        column = jnp.where(busy, jobs[:, 2:3], -1)
        lane = lax.broadcasted_iota(jnp.int32, (count, rec_ref.shape[1]), 1)
        rec_ref[part, :] = jnp.where(column == lane, 1.0, 0.0).astype(jnp.bfloat16)


def prepare(turns, source_ids, chunks, slots, chan_rows, window, after):
    chan_size = len(chunks)
    vmem = pl.BlockSpec(memory_space=pltpu.VMEM)
    smem = pl.BlockSpec(memory_space=pltpu.SMEM)
    return pl.pallas_call(
        functools.partial(prepare_kernel, chan_rows, chan_size, chan_rows // 2, window),
        out_shape=(
            jax.ShapeDtypeStruct((slots, chan_size * PICK), jnp.bfloat16),
            jax.ShapeDtypeStruct((slots, chan_rows), jnp.bfloat16),
            jax.ShapeDtypeStruct((8, slots), jnp.int32),
            jax.ShapeDtypeStruct((1,), jnp.int32),
            TOKEN,
        ),
        in_specs=[smem, vmem, pl.BlockSpec(memory_space=pl.ANY)] + [vmem] * chan_size,
        out_specs=(vmem, vmem, vmem, smem, vmem),
        cost_estimate=light(),
        compiler_params=params(16),
        name="prepare",
    )(turns, source_ids.reshape(1, -1), after, *chunks)


def turns_kernel(chan_size, slots, window, source_turns_ref, *refs):
    chunk_refs, out_ref = refs[:chan_size], refs[-1]
    me = lax.axis_index("chan")
    steps = chan_size // 2
    place = jnp.where((me & 1) == 0, me >> 1, chan_size - 1 - (me >> 1))
    out_ref[0] = 1
    block = lax.broadcasted_iota(jnp.int32, (chan_size, EXTRA), 0)
    notes = jnp.zeros((chan_size, EXTRA), jnp.float32)
    for hop, ref in enumerate(chunk_refs):
        spot = place - hop if hop <= steps else place + hop - steps
        spot = jnp.where(spot < 0, spot + chan_size, spot)
        spot = jnp.where(spot >= chan_size, spot - chan_size, spot)
        owner = jnp.where(spot < steps, 2 * spot, 2 * (chan_size - spot) - 1)
        notes = jnp.where(block == owner, ref[0][8:9, :].astype(jnp.float32), notes)
    lane = lax.broadcasted_iota(jnp.int32, notes.shape, 1)

    def total(index):
        value = jnp.where(lane == 2 * index, 32.0 * notes, 0.0)
        value = value + jnp.where(lane == 2 * index + 1, notes, 0.0)
        return jnp.broadcast_to(jnp.sum(value, axis=1, keepdims=True), notes.shape)

    left = jnp.where(block == 0, 0.0, pltpu.roll(total(0), 1, 0))
    right = jnp.where(block == chan_size - 1, 0.0, pltpu.roll(total(1), chan_size - 1, 0))
    aside = jnp.max(jnp.maximum(left, right)).astype(jnp.int32)
    whole_sum = jnp.max(left + right + total(2)).astype(jnp.int32)
    needed = jnp.maximum((aside + window - 1) // window, (whole_sum + slots - 1) // slots)
    needed = jnp.maximum(needed, 1)
    out_ref[1] = needed
    out_ref[2] = needed * source_turns_ref[0]


def count_turns(source_turns, chunks, slots, window, after):
    _, _, width = chunks[0].shape
    last = width // EXTRA - 1
    return pl.pallas_call(
        functools.partial(turns_kernel, len(chunks), slots, window),
        grid=(1,),
        out_shape=jax.ShapeDtypeStruct((3,), jnp.int32),
        in_specs=[pl.BlockSpec(memory_space=pltpu.SMEM)]
        + [pl.BlockSpec((1, PICK, EXTRA), lambda i: (1, 0, last)) for _ in chunks]
        + [pl.BlockSpec(memory_space=pl.ANY)] * len(after),
        out_specs=pl.BlockSpec(memory_space=pltpu.SMEM),
        cost_estimate=light(),
        compiler_params=params(8),
        name="count_turns",
    )(source_turns, *chunks, *after)


def transform_kernel(shards, scale, start, chunks, src_ref, rec_ref, *refs):
    chunk_refs = refs[:chunks]
    cells_ref, cos_ref, sin_ref = refs[chunks : chunks + 3]
    keep_ref, send_ref, token_ref = refs[-3:]
    token_ref[...] = jnp.zeros_like(token_ref)
    rows = keep_ref.shape[1]
    bins = cos_ref.shape[0]
    step = min(BINS_STEP, bins)
    eighth = lax.broadcasted_iota(jnp.int32, (1, 128), 1) & 7
    root = math.sqrt(0.5)
    edge = jnp.where((eighth == 1) | (eighth == 7), root, 0.0)
    edge = jnp.where((eighth == 3) | (eighth == 5), -root, edge)
    edge = jnp.where(eighth == 0, 1.0, jnp.where(eighth == 4, -1.0, edge)) * scale
    edge = edge.astype(jnp.bfloat16).astype(jnp.float32)

    by_src = src_ref[pl.ds(start, rows), :]
    by_rec = rec_ref[pl.ds(start, rows), :]
    even = odd = corner = None
    for first in range(0, bins, step):
        lanes = pl.ds(first, step)
        source_real = jnp.concatenate([ref[0, :, lanes] for ref in chunk_refs], axis=0)
        source_imag = jnp.concatenate([ref[1, :, lanes] for ref in chunk_refs], axis=0)
        sr = jnp.dot(by_src, source_real, preferred_element_type=jnp.float32)
        si = jnp.dot(by_src, source_imag, preferred_element_type=jnp.float32)
        rr = jnp.dot(by_rec, cells_ref[0, :, lanes], preferred_element_type=jnp.float32)
        ri = jnp.dot(by_rec, cells_ref[1, :, lanes], preferred_element_type=jnp.float32)
        real = (sr * rr + si * ri).astype(jnp.bfloat16)
        imag = (si * rr - sr * ri).astype(jnp.bfloat16)
        more_even = jnp.dot(real, cos_ref[lanes, :], preferred_element_type=jnp.float32)
        more_odd = jnp.dot(imag, sin_ref[lanes, :], preferred_element_type=jnp.float32)
        wide = real.astype(jnp.float32)
        sums = wide[:, 0:128]
        for lane in range(128, step, 128):
            sums = sums + wide[:, lane : lane + 128]
        even = more_even if even is None else even + more_even
        odd = more_odd if odd is None else odd + more_odd
        corner = sums if corner is None else corner + sums

    me = lax.axis_index("seg")
    width = LAGS // shards
    corner = jnp.sum(corner * edge, axis=1, keepdims=True)
    first = lax.broadcasted_iota(jnp.int32, even.shape, 1) == 0
    later = even - jnp.where(first, 0.0, odd)
    sooner = jnp.where(first, corner, even) + odd
    sooner = pltpu.roll(sooner, HALF - 1, 1)
    for shard in range(shards):
        half = shards // 2
        if shard < half:
            lane = (half - 1 - shard) * width
            value = sooner[:, lane : lane + width]
        else:
            lane = (shard - half) * width
            value = later[:, lane : lane + width]
        place = me ^ shard

        @pl.when((place & 1) == 0)
        def _():
            keep_ref[place >> 1] = value

        @pl.when((place & 1) == 1)
        def _():
            send_ref[place >> 1] = value.astype(jnp.bfloat16)


def transform(picks, chunks, cells, tables, shards, scale, start, rows, *after):
    width = LAGS // shards
    shape = (shards // 2, rows, width)
    vmem = pl.BlockSpec(memory_space=pltpu.VMEM)
    return pl.pallas_call(
        functools.partial(transform_kernel, shards, scale, start, len(chunks)),
        out_shape=(
            jax.ShapeDtypeStruct(shape, jnp.float32),
            jax.ShapeDtypeStruct(shape, jnp.bfloat16),
            TOKEN,
        ),
        in_specs=[vmem] * (5 + len(chunks))
        + [pl.BlockSpec(memory_space=pl.ANY)] * len(after),
        out_specs=(vmem, vmem, vmem),
        cost_estimate=light(),
        compiler_params=params(16),
        name="transform",
    )(*picks, *chunks, cells, *tables, *after)


def swap(send, bit):
    size = lax.axis_size("seg")
    return lax.ppermute(send, "seg", [(i, i ^ bit) for i in range(size)])


def halve(keep, got):
    total = keep + got.astype(jnp.float32)
    return total[0::2], total[1::2].astype(jnp.bfloat16)


def reduce_further(keep, got, bit):
    while keep.shape[0] > 1:
        keep, send = halve(keep, got)
        bit *= 2
        got = swap(send, bit)
    return (keep[0] + got[0].astype(jnp.float32)).astype(jnp.bfloat16)


def place_kernel(start, further, place_ref, *refs):
    out_ref = refs[-1]
    parts = refs[1:-1] if further else refs[:-1]
    width, slots = out_ref.shape
    flip = lax.axis_index("seg") < lax.axis_size("seg") // 2
    rows = lax.broadcasted_iota(jnp.int32, (width, width), 0)
    columns = lax.broadcasted_iota(jnp.int32, (width, width), 1)
    wanted = jnp.where(flip, width - 1 - rows, rows)
    turned = jnp.where(wanted == columns, 1.0, 0.0).astype(jnp.bfloat16)
    total = refs[0][...] if further else jnp.zeros((width, slots), jnp.float32)
    for ref in parts:
        count = ref.shape[0]
        spot = lax.broadcasted_iota(jnp.int32, (count, slots), 0) + start
        chosen = jnp.where(spot == place_ref[0:1, :], 1.0, 0.0).astype(jnp.bfloat16)
        across = lax.dot_general(
            turned, ref[...], (((1,), (1,)), ((), ())), preferred_element_type=jnp.float32
        ).astype(jnp.bfloat16)
        total = total + jnp.dot(across, chosen, preferred_element_type=jnp.float32)
        start += count
    out_ref[...] = total


def place_rows(place, parts, start, total=None):
    width = parts[0].shape[1]
    slots = place.shape[1]
    given = list(parts) if total is None else [total, *parts]
    vmem = pl.BlockSpec(memory_space=pltpu.VMEM)
    return pl.pallas_call(
        functools.partial(place_kernel, start, total is not None),
        out_shape=jax.ShapeDtypeStruct((width, slots), jnp.float32),
        in_specs=[vmem] * (1 + len(given)),
        out_specs=vmem,
        cost_estimate=light(),
        compiler_params=params(16),
        name="place_rows",
    )(place, *given)


def per_device(spectra, source_ids, pair_source, pair_offset, pair_counts):
    chan_rows = spectra.shape[1]
    bins = spectra.shape[3]
    seg_size = lax.axis_size("seg")
    chan_size = lax.axis_size("chan")
    slots = pair_source.shape[0]
    window = 3 * slots // 8
    scale = 1.0 / math.sqrt(bins * seg_size)
    join = lax.optimization_barrier

    ring = list(range(0, chan_size, 2)) + list(range(1, chan_size, 2))[::-1]
    ahead = [(ring[i], ring[(i + 1) % chan_size]) for i in range(chan_size)]
    back = [(b, a) for a, b in ahead]
    leftward = [(i + 1, i) for i in range(chan_size - 1)]
    rightward = [(i, i + 1) for i in range(chan_size - 1)]

    def gathered(turns):
        own = pick_rows(turns, pair_counts, source_ids, pair_source, pair_offset, spectra)
        forward, backward = [own], [own]
        steps = chan_size // 2

        def step_beside(work=None):
            forward.append(lax.ppermute(forward[-1], "chan", ahead))
            if len(backward) < chan_size - steps:
                backward.append(lax.ppermute(backward[-1], "chan", back))
            if work is not None:
                *results, token = work()
                token, forward[-1], backward[-1] = join((token, forward[-1], backward[-1]))
                return results, token

        tables, token = step_beside(lambda: lag_tables(bins, scale, own))
        flat = jnp.transpose(spectra[0], (1, 0, 2))
        (whitened,), token = step_beside(lambda: whiten_rows(flat, token))
        for _ in range(2, steps):
            step_beside()
        chunks = forward + backward[1:]
        *picks, token = prepare(turns, source_ids, chunks, slots, chan_rows, window, token)
        return chunks, tables, whitened, picks, token

    def correlate(chunks, whitened, tables, picks, place, token):
        bounds = (0, window, 2 * window, slots)

        def piece(part, *after):
            start, stop = bounds[part], bounds[part + 1]
            return transform(
                picks, chunks, whitened, tables, seg_size, scale, start, stop - start, *after
            )

        keep_left, send, _ = piece(0, token)
        got_left = swap(send, 1)
        keep_right, send, token = piece(1, send)
        token, got_left = join((token, got_left))
        keep_left, send_left = halve(keep_left, got_left)
        got_right = swap(send, 1)
        got_left = swap(send_left, 2)
        keep_own, send, token = piece(2, send_left, token)
        token, got_left, got_right = join((token, got_left, got_right))
        left = reduce_further(keep_left, got_left, 2)
        right = reduce_further(keep_right, got_right, 1)
        own = reduce_further(keep_own, swap(send, 1), 1)
        from_right = lax.ppermute(left, "chan", leftward)
        from_left = lax.ppermute(right, "chan", rightward)
        total = place_rows(place, (left, right, own), 0)
        return place_rows(place, (from_left, from_right), slots, total), (own, token)

    def one_turn(turns):
        chunks, tables, whitened, (*picks, place, source_turns), token = gathered(turns)
        result, after = correlate(chunks, whitened, tables, picks, place, token)
        return result, after, chunks, source_turns

    first, after, chunks, source_turns = one_turn(jnp.zeros((2,), jnp.int32))
    counts = count_turns(source_turns, chunks, slots, window, after)

    def unfinished(state):
        counts, _ = state
        return counts[0] < counts[2]

    def further(state):
        counts, total = state
        turns = jnp.stack([lax.div(counts[0], counts[1]), lax.rem(counts[0], counts[1])])
        counts = counts + jnp.array([1, 0, 0], jnp.int32)
        return counts, total + one_turn(turns)[0]

    return lax.while_loop(unfinished, further, (counts, first))[1]


def solution(mesh):
    in_specs = (P("seg", "chan", None, None), P(), P("chan"), P("chan"), P("chan"))
    out_specs = P("seg", "chan")
    return jax.shard_map(
        per_device, mesh=mesh, in_specs=in_specs, out_specs=out_specs, check_vma=False
    )
```

```python
import functools
import math

import jax
import jax.numpy as jnp
from jax import lax
from jax.experimental import pallas as pl
from jax.experimental.pallas import tpu as pltpu
from jax.sharding import PartitionSpec as P

LAGS = 1024
HALF = LAGS // 2
WBLOCK = 64
PICK = 16
BINS_STEP = 512
TABLE_ROWS = 64
EXTRA = 128


def params(mebibytes):
    return pltpu.CompilerParams(vmem_limit_bytes=mebibytes * 1024 * 1024)


def light():
    return pl.CostEstimate(flops=1024, bytes_accessed=1024, transcendentals=0)


class Halves:
    def __init__(self, real, imag):
        self.refs = (real, imag)
        self.shape = real.shape

    def __getitem__(self, index):
        return self.refs[index[0]][(0, *index[1:])]


def as_chunks(refs):
    middle = (len(refs) - 1) // 2
    return [*refs[:middle], Halves(*refs[middle : middle + 2]), *refs[middle + 2 :]]


TOKEN = jax.ShapeDtypeStruct((8, 128), jnp.float32)


def whole(shape):
    return pl.BlockSpec(shape, lambda *_: (0,) * len(shape))


def pick_kernel(
    chan_rows, band, turns_ref, counts_ref, ids_ref, source_ref, offset_ref, cells_ref, out_ref,
    rows_ref, held_ref, sems,
):
    first = lax.axis_index("chan") * chan_rows
    turn = turns_ref[0]
    bins = cells_ref.shape[3]
    for i in range(PICK):
        rows_ref[i] = 0
    rank = jnp.int32(0)
    for i in range(ids_ref.shape[0]):
        row = ids_ref[i] - first
        mine = (row >= 0) & (row < chan_rows)
        spot = rank - turn * PICK
        rows_ref[jnp.where(mine & (spot >= 0) & (spot < PICK), spot, PICK)] = row
        rank = rank + mine.astype(jnp.int32)
    copies = [
        pltpu.make_async_copy(cells_ref.at[0, rows_ref[i]], held_ref.at[i], sems.at[i])
        for i in range(PICK)
    ]
    for copy in copies:
        copy.start()

    offset = offset_ref[...]
    slot = lax.broadcasted_iota(jnp.int32, offset.shape, 0) * offset.shape[1]
    slot = slot + lax.broadcasted_iota(jnp.int32, offset.shape, 1)
    live = slot < counts_ref[0]
    kinds = (
        live & (offset >= chan_rows),
        live & (offset < 0),
        live & (offset >= 0) & (offset < chan_rows),
    )
    lane = lax.broadcasted_iota(jnp.int32, offset.shape, 1)
    notes = jnp.zeros(offset.shape, jnp.int32)
    for index, kind in enumerate(kinds):
        total = jnp.sum(jnp.where(kind, 1.0, 0.0)).astype(jnp.int32)
        notes = jnp.where(lane == 2 * index, total >> 5, notes)
        notes = jnp.where(lane == 2 * index + 1, total & 31, notes)
    shifted = offset + band
    source = jnp.where(live, source_ref[...] + 1, 0)

    def coded(upper, lower):
        both = jnp.concatenate([upper.astype(jnp.float32), lower.astype(jnp.float32)], axis=0)
        return both.astype(jnp.bfloat16)

    out_ref[0, :, pl.ds(bins, EXTRA)] = coded(source, shifted >> 4)
    out_ref[1, :, pl.ds(bins, EXTRA)] = coded(shifted & 15, notes)

    for copy in copies:
        copy.wait()
    real = held_ref[:, 0, :].astype(jnp.float32)
    imag = held_ref[:, 1, :].astype(jnp.float32)
    width = min(256, bins)

    def stacked(values):
        return jnp.concatenate([values[:, i : i + width] for i in range(0, bins, width)], axis=0)

    real, imag = whitened_pair(stacked(real), stacked(imag))
    for index in range(bins // width):
        lanes = pl.ds(index * width, width)
        out_ref[0, :, lanes] = real[index * PICK : (index + 1) * PICK]
        out_ref[1, :, lanes] = imag[index * PICK : (index + 1) * PICK]


def pick_rows(turns, counts, source_ids, pair_source, pair_offset, spectra):
    _, chan_rows, parts, bins = spectra.shape
    smem = pl.BlockSpec(memory_space=pltpu.SMEM)
    vmem = pl.BlockSpec(memory_space=pltpu.VMEM)
    return pl.pallas_call(
        functools.partial(pick_kernel, chan_rows, chan_rows // 2),
        out_shape=jax.ShapeDtypeStruct((parts, PICK, bins + EXTRA), spectra.dtype),
        in_specs=[smem, smem, smem, vmem, vmem, pl.BlockSpec(memory_space=pltpu.HBM)],
        out_specs=vmem,
        scratch_shapes=[
            pltpu.SMEM((PICK + 1,), jnp.int32),
            pltpu.VMEM((PICK, parts, bins), spectra.dtype),
            pltpu.SemaphoreType.DMA((PICK,)),
        ],
        cost_estimate=light(),
        compiler_params=params(8),
        name="pick_rows",
    )(
        turns, counts, source_ids, pair_source.reshape(-1, EXTRA), pair_offset.reshape(-1, EXTRA), spectra
    )


def block_mean(power):
    width = power.shape[1]
    row_group = lax.broadcasted_iota(jnp.int32, (width, width), 0) // WBLOCK
    col_group = lax.broadcasted_iota(jnp.int32, (width, width), 1) // WBLOCK
    spread = jnp.where(row_group == col_group, 1.0 / WBLOCK, 0.0).astype(jnp.bfloat16)
    high = power.astype(jnp.bfloat16)
    low = (power - high.astype(jnp.float32)).astype(jnp.bfloat16)
    total = jnp.dot(low, spread, preferred_element_type=jnp.float32)
    return total + jnp.dot(high, spread, preferred_element_type=jnp.float32)


def whitened_pair(real, imag):
    inverse = lax.rsqrt(block_mean(real * real + imag * imag) + 1e-06)
    return (real * inverse).astype(jnp.bfloat16), (imag * inverse).astype(jnp.bfloat16)


def whiten_kernel(cells_ref, after_ref, out_ref, token_ref):
    token_ref[...] = jnp.zeros_like(token_ref)
    for start in range(0, cells_ref.shape[2], 256):
        lanes = pl.ds(start, 256)
        real = cells_ref[0, :, lanes].astype(jnp.float32)
        imag = cells_ref[1, :, lanes].astype(jnp.float32)
        out_ref[0, :, lanes], out_ref[1, :, lanes] = whitened_pair(real, imag)


def whiten_rows(cells, after):
    _, rows, bins = cells.shape
    spec = pl.BlockSpec((2, rows, BINS_STEP), lambda i: (0, 0, i))
    return pl.pallas_call(
        whiten_kernel,
        grid=(bins // BINS_STEP,),
        out_shape=(jax.ShapeDtypeStruct(cells.shape, jnp.bfloat16), TOKEN),
        in_specs=[spec, pl.BlockSpec(memory_space=pl.ANY)],
        out_specs=(spec, whole(TOKEN.shape)),
        cost_estimate=light(),
        compiler_params=params(12),
        name="whiten_rows",
    )(cells, after)


def table_kernel(scale, all_bins, after_ref, cos_ref, sin_ref, token_ref, coarse_ref, fine_ref):
    token_ref[...] = jnp.zeros_like(token_ref)
    step = pl.program_id(0)
    groups = cos_ref.shape[0] // TABLE_ROWS

    @pl.when(step == 0)
    def _():
        def circle(ref, stride, factor):
            shape = ref.shape[1:]
            bins = lax.broadcasted_iota(jnp.int32, shape, 0) * stride
            lags = lax.broadcasted_iota(jnp.int32, shape, 1)
            lags = jnp.where(lags == 0, HALF, lags)
            theta = ((bins * lags) & (2 * all_bins - 1)).astype(jnp.float32) * (math.pi / all_bins)
            ref[0] = jnp.cos(theta) * factor
            ref[1] = jnp.sin(theta) * factor

        circle(coarse_ref, TABLE_ROWS, scale)
        circle(fine_ref, 1, 1.0)

    cos_b = fine_ref[0]
    sin_b = fine_ref[1]
    first = lax.broadcasted_iota(jnp.int32, cos_b.shape, 1) == 0
    for group in range(groups):
        cos_a = coarse_ref[0, pl.ds(step * groups + group, 1), :]
        sin_a = coarse_ref[1, pl.ds(step * groups + group, 1), :]
        rows = pl.ds(group * TABLE_ROWS, TABLE_ROWS)
        cos = jnp.where(first, scale, cos_a * cos_b - sin_a * sin_b)
        cos_ref[rows, :] = cos.astype(jnp.bfloat16)
        sin_ref[rows, :] = (sin_a * cos_b + cos_a * sin_b).astype(jnp.bfloat16)


def lag_tables(bins, scale, after):
    spec = pl.BlockSpec((BINS_STEP, HALF), lambda i: (i, 0))
    shape = jax.ShapeDtypeStruct((bins, HALF), jnp.bfloat16)
    return pl.pallas_call(
        functools.partial(table_kernel, scale, bins),
        grid=(bins // BINS_STEP,),
        out_shape=(shape, shape, TOKEN),
        in_specs=[pl.BlockSpec(memory_space=pl.ANY)],
        out_specs=(spec, spec, whole(TOKEN.shape)),
        scratch_shapes=[
            pltpu.VMEM((2, bins // TABLE_ROWS, HALF), jnp.float32),
            pltpu.VMEM((2, TABLE_ROWS, HALF), jnp.float32),
        ],
        cost_estimate=light(),
        compiler_params=params(12),
        name="lag_tables",
    )(after)


def source_spots(chan_rows, chan_size, me, turn, ids_row):
    count = ids_row.shape[1]
    shift = chan_rows.bit_length() - 1
    ids_row = jnp.broadcast_to(ids_row, (count, count))
    rows = lax.broadcasted_iota(jnp.int32, (count, count), 0)
    columns = lax.broadcasted_iota(jnp.int32, (count, count), 1)
    ids = jnp.sum(jnp.where(rows == columns, ids_row, 0).astype(jnp.float32), axis=1, keepdims=True)
    owner = jnp.broadcast_to(ids.astype(jnp.int32) >> shift, (count, count))
    earlier = (owner == (ids_row >> shift)) & (columns < rows)
    rank = jnp.sum(jnp.where(earlier, 1.0, 0.0), axis=1, keepdims=True)
    turns = (jnp.max(rank).astype(jnp.int32) + PICK) // PICK
    rank = rank.astype(jnp.int32) - turn * PICK
    owner = owner[:, 0:1]

    def ring_place(block):
        return jnp.where((block & 1) == 0, block >> 1, chan_size - 1 - (block >> 1))

    steps = chan_size // 2
    distance = ring_place(me) - ring_place(owner)
    distance = jnp.where(distance < 0, distance + chan_size, distance)
    hop = jnp.where(distance <= steps, distance, steps + chan_size - distance)
    return jnp.where((rank >= 0) & (rank < PICK), hop * PICK + rank, -1), turns


def prepare_kernel(
    chan_rows, chan_size, band, window, turns_ref, ids_ref, after_ref, *refs
):
    chunk_refs = as_chunks(refs[: chan_size + 1])
    src_ref, rec_ref, place_ref, needed_ref, token_ref = refs[chan_size + 1 :]
    token_ref[...] = jnp.zeros_like(token_ref)
    me = lax.axis_index("chan")
    source_turn = turns_ref[0]
    turn = turns_ref[1]
    slots = place_ref.shape[1]
    bins = chunk_refs[0].shape[2] - EXTRA
    spots, needed = source_spots(chan_rows, chan_size, me, source_turn, ids_ref[...])
    needed_ref[0] = needed

    def ring_place(block):
        return jnp.where((block & 1) == 0, block >> 1, chan_size - 1 - (block >> 1))

    def hop_of(block):
        steps = chan_size // 2
        distance = ring_place(me) - ring_place(block)
        distance = jnp.where(distance < 0, distance + chan_size, distance)
        return jnp.where(distance <= steps, distance, steps + chan_size - distance)

    lanes = pl.ds(bins, EXTRA)
    left_hop = jnp.where(me > 0, hop_of(me - 1), -1)
    right_hop = jnp.where(me < chan_size - 1, hop_of(me + 1), -1)
    listed = []
    for wanted in (left_hop, right_hop, None):
        halves = []
        for half in range(2):
            if wanted is None:
                value = chunk_refs[0][half, :, lanes].astype(jnp.float32)
            else:
                value = jnp.zeros((PICK, EXTRA), jnp.float32)
                for hop, ref in enumerate(chunk_refs):
                    value = jnp.where(wanted == hop, ref[half, :, lanes].astype(jnp.float32), value)
            halves.append(value.astype(jnp.int32))
        source = halves[0][0:8] - 1
        offset = halves[0][8:16] * 16 + halves[1][0:8] - band
        listed.append((source, offset))
    (left_src, left_off), (right_src, right_off), (own_src, own_off) = listed
    own_live = own_src >= 0
    taken = (
        (left_src >= 0) & (left_off >= chan_rows),
        (right_src >= 0) & (right_off < 0),
        own_live & (own_off >= 0) & (own_off < chan_rows),
        own_live & (own_off < 0),
        own_live & (own_off >= chan_rows),
    )

    marks = jnp.concatenate([jnp.where(mask, 1.0, 0.0) for mask in taken], axis=0)
    rows = marks.shape[0]
    earlier = lax.broadcasted_iota(jnp.int32, (EXTRA, EXTRA), 0) < lax.broadcasted_iota(
        jnp.int32, (EXTRA, EXTRA), 1
    )
    rank = jnp.dot(
        marks.astype(jnp.bfloat16),
        jnp.where(earlier, 1.0, 0.0).astype(jnp.bfloat16),
        preferred_element_type=jnp.float32,
    )
    sums = jnp.broadcast_to(jnp.sum(marks, axis=1, keepdims=True), marks.shape)
    row = lax.broadcasted_iota(jnp.int32, (rows, rows), 0)
    column = lax.broadcasted_iota(jnp.int32, (rows, rows), 1)
    above_it = ((row >> 3) == (column >> 3)) & (column < row)
    rank = rank + jnp.dot(
        jnp.where(above_it, 1.0, 0.0).astype(jnp.bfloat16),
        sums.astype(jnp.bfloat16),
        preferred_element_type=jnp.float32,
    )
    rank = rank.astype(jnp.int32)
    ranks = [rank[8 * i : 8 * i + 8] for i in range(5)]
    left_total = jnp.sum(marks[0:8]).astype(jnp.int32)
    right_total = jnp.sum(marks[8:16]).astype(jnp.int32)

    def done_before(amount, index):
        return jnp.minimum(amount, index * window)

    left_before = done_before(left_total, turn)
    right_before = done_before(right_total, turn)
    left_now = done_before(left_total, turn + 1) - left_before
    right_now = done_before(right_total, turn + 1) - right_before
    own_before = turn * slots - left_before - right_before
    own_room = slots - left_now - right_now

    def in_window(index):
        shifted = ranks[index] - turn * window
        return shifted, taken[index] & (shifted >= 0) & (shifted < window)

    def flat(value):
        return jnp.concatenate([value[i : i + 1, :] for i in range(8)], axis=1)

    left_rank, left_ok = in_window(0)
    right_rank, right_ok = in_window(1)
    own_rank = ranks[2] - own_before
    own_ok = taken[2] & (own_rank >= 0) & (own_rank < own_room)
    own_pos = own_rank + left_now
    own_pos = jnp.where(own_pos < window, own_pos, own_pos + right_now)
    own_pos = jnp.where(own_ok, own_pos, -1)
    below_rank, below_ok = in_window(3)
    above_rank, above_ok = in_window(4)
    place = jnp.where(below_ok, below_rank + slots, own_pos)
    place = jnp.where(above_ok, above_rank + slots + window, place)
    place_ref[...] = jnp.broadcast_to(flat(place), place_ref.shape)

    names = lax.broadcasted_iota(jnp.int32, (spots.shape[0], slots), 0)
    field_row = lax.broadcasted_iota(jnp.int32, (8, slots), 0)

    def jobs_of(source, receiver, position, count):
        source, receiver, position = flat(source), flat(receiver), flat(position)
        spot = jnp.where(names == source, spots + 1, 0).astype(jnp.float32)
        spot = jnp.sum(spot, axis=0, keepdims=True).astype(jnp.int32) - 1
        fields = jnp.where(field_row == 0, spot >> 4, jnp.where(field_row == 1, spot & (PICK - 1), 0))
        fields = jnp.where(field_row == 2, receiver, jnp.where(field_row == 3, 1, fields))
        fields = jnp.where((position >= 0) & (spot >= 0), fields, 0)
        wanted = lax.broadcasted_iota(jnp.int32, (count, slots), 0)
        chosen = jnp.where(wanted == position, 1.0, 0.0).astype(jnp.bfloat16)
        return lax.dot_general(
            chosen,
            fields.astype(jnp.float32).astype(jnp.bfloat16),
            (((1,), (1,)), ((), ())),
            preferred_element_type=jnp.float32,
        )

    left_jobs = jobs_of(left_src, left_off - chan_rows, jnp.where(left_ok, left_rank, -1), window)
    right_jobs = jobs_of(right_src, right_off + chan_rows, jnp.where(right_ok, right_rank, -1), window)
    own_jobs = jobs_of(own_src, own_off, own_pos, slots)
    pieces = (
        (0, window, left_jobs + own_jobs[0:window]),
        (window, window, right_jobs + own_jobs[window : 2 * window]),
        (2 * window, slots - 2 * window, own_jobs[2 * window :]),
    )
    for start, count, jobs in pieces:
        jobs = jobs.astype(jnp.int32)
        busy = jobs[:, 3:4] > 0
        part = pl.ds(start, count)
        column = jnp.where(busy, jobs[:, 0:1] * PICK + jobs[:, 1:2], -1)
        lane = lax.broadcasted_iota(jnp.int32, (count, src_ref.shape[1]), 1)
        src_ref[part, :] = jnp.where(column == lane, 1.0, 0.0).astype(jnp.bfloat16)
        column = jnp.where(busy, jobs[:, 2:3], -1)
        lane = lax.broadcasted_iota(jnp.int32, (count, rec_ref.shape[1]), 1)
        rec_ref[part, :] = jnp.where(column == lane, 1.0, 0.0).astype(jnp.bfloat16)


def prepare(turns, source_ids, chunks, slots, chan_rows, window, after):
    chan_size = len(chunks) - 1
    vmem = pl.BlockSpec(memory_space=pltpu.VMEM)
    smem = pl.BlockSpec(memory_space=pltpu.SMEM)
    return pl.pallas_call(
        functools.partial(prepare_kernel, chan_rows, chan_size, chan_rows // 2, window),
        out_shape=(
            jax.ShapeDtypeStruct((slots, chan_size * PICK), jnp.bfloat16),
            jax.ShapeDtypeStruct((slots, chan_rows), jnp.bfloat16),
            jax.ShapeDtypeStruct((8, slots), jnp.int32),
            jax.ShapeDtypeStruct((1,), jnp.int32),
            TOKEN,
        ),
        in_specs=[smem, vmem, pl.BlockSpec(memory_space=pl.ANY)] + [vmem] * len(chunks),
        out_specs=(vmem, vmem, vmem, smem, vmem),
        cost_estimate=light(),
        compiler_params=params(16),
        name="prepare",
    )(turns, source_ids.reshape(1, -1), after, *chunks)


def turns_kernel(chan_size, slots, window, source_turns_ref, *refs):
    chunk_refs = refs[:chan_size]
    one_ref, pairs_ref, all_ref = refs[-3:]
    me = lax.axis_index("chan")
    steps = chan_size // 2
    place = jnp.where((me & 1) == 0, me >> 1, chan_size - 1 - (me >> 1))
    one_ref[0] = 1
    block = lax.broadcasted_iota(jnp.int32, (chan_size, EXTRA), 0)
    notes = jnp.zeros((chan_size, EXTRA), jnp.float32)
    for hop, ref in enumerate(chunk_refs):
        spot = place - hop if hop <= steps else place + hop - steps
        spot = jnp.where(spot < 0, spot + chan_size, spot)
        spot = jnp.where(spot >= chan_size, spot - chan_size, spot)
        owner = jnp.where(spot < steps, 2 * spot, 2 * (chan_size - spot) - 1)
        notes = jnp.where(block == owner, ref[0][8:9, :].astype(jnp.float32), notes)
    lane = lax.broadcasted_iota(jnp.int32, notes.shape, 1)

    def total(index):
        value = jnp.where(lane == 2 * index, 32.0 * notes, 0.0)
        value = value + jnp.where(lane == 2 * index + 1, notes, 0.0)
        return jnp.broadcast_to(jnp.sum(value, axis=1, keepdims=True), notes.shape)

    left = jnp.where(block == 0, 0.0, pltpu.roll(total(0), 1, 0))
    right = jnp.where(block == chan_size - 1, 0.0, pltpu.roll(total(1), chan_size - 1, 0))
    aside = jnp.max(jnp.maximum(left, right)).astype(jnp.int32)
    whole_sum = jnp.max(left + right + total(2)).astype(jnp.int32)
    needed = jnp.maximum((aside + window - 1) // window, (whole_sum + slots - 1) // slots)
    needed = jnp.maximum(needed, 1)
    pairs_ref[0] = needed
    all_ref[0] = needed * source_turns_ref[0]


def count_turns(source_turns, chunks, slots, window, after):
    _, _, width = chunks[0].shape
    last = width // EXTRA - 1
    steps = (len(chunks) - 1) // 2
    chunks = [*chunks[:steps], *chunks[steps + 1 :]]
    specs = [
        pl.BlockSpec((1, PICK, EXTRA), functools.partial(lambda half, i: (half, 0, last), len(x) - 1))
        for x in chunks
    ]
    return pl.pallas_call(
        functools.partial(turns_kernel, len(chunks), slots, window),
        grid=(1,),
        out_shape=[jax.ShapeDtypeStruct((1,), jnp.int32)] * 3,
        in_specs=[pl.BlockSpec(memory_space=pltpu.SMEM), *specs]
        + [pl.BlockSpec(memory_space=pl.ANY)] * len(after),
        out_specs=[pl.BlockSpec(memory_space=pltpu.SMEM)] * 3,
        cost_estimate=light(),
        compiler_params=params(8),
        name="count_turns",
    )(source_turns, *chunks, *after)


def transform_kernel(shards, scale, start, chunks, src_ref, rec_ref, *refs):
    chunk_refs = as_chunks(refs[:chunks])
    cells_ref, cos_ref, sin_ref = refs[chunks : chunks + 3]
    keep_ref, send_ref, token_ref = refs[-3:]
    token_ref[...] = jnp.zeros_like(token_ref)
    rows = keep_ref.shape[1]
    bins = cos_ref.shape[0]
    step = min(BINS_STEP, bins)
    eighth = lax.broadcasted_iota(jnp.int32, (1, 128), 1) & 7
    root = math.sqrt(0.5)
    edge = jnp.where((eighth == 1) | (eighth == 7), root, 0.0)
    edge = jnp.where((eighth == 3) | (eighth == 5), -root, edge)
    edge = jnp.where(eighth == 0, 1.0, jnp.where(eighth == 4, -1.0, edge)) * scale
    edge = edge.astype(jnp.bfloat16).astype(jnp.float32)

    by_src = src_ref[pl.ds(start, rows), :]
    by_rec = rec_ref[pl.ds(start, rows), :]
    even = odd = corner = None
    for first in range(0, bins, step):
        lanes = pl.ds(first, step)
        source_real = jnp.concatenate([ref[0, :, lanes] for ref in chunk_refs], axis=0)
        source_imag = jnp.concatenate([ref[1, :, lanes] for ref in chunk_refs], axis=0)
        sr = jnp.dot(by_src, source_real, preferred_element_type=jnp.float32)
        si = jnp.dot(by_src, source_imag, preferred_element_type=jnp.float32)
        rr = jnp.dot(by_rec, cells_ref[0, :, lanes], preferred_element_type=jnp.float32)
        ri = jnp.dot(by_rec, cells_ref[1, :, lanes], preferred_element_type=jnp.float32)
        real = (sr * rr + si * ri).astype(jnp.bfloat16)
        imag = (si * rr - sr * ri).astype(jnp.bfloat16)
        more_even = jnp.dot(real, cos_ref[lanes, :], preferred_element_type=jnp.float32)
        more_odd = jnp.dot(imag, sin_ref[lanes, :], preferred_element_type=jnp.float32)
        wide = real.astype(jnp.float32)
        sums = wide[:, 0:128]
        for lane in range(128, step, 128):
            sums = sums + wide[:, lane : lane + 128]
        even = more_even if even is None else even + more_even
        odd = more_odd if odd is None else odd + more_odd
        corner = sums if corner is None else corner + sums

    me = lax.axis_index("seg")
    width = LAGS // shards
    corner = jnp.sum(corner * edge, axis=1, keepdims=True)
    first = lax.broadcasted_iota(jnp.int32, even.shape, 1) == 0
    later = even - jnp.where(first, 0.0, odd)
    sooner = jnp.where(first, corner, even) + odd
    sooner = pltpu.roll(sooner, HALF - 1, 1)
    for shard in range(shards):
        half = shards // 2
        if shard < half:
            lane = (half - 1 - shard) * width
            value = sooner[:, lane : lane + width]
        else:
            lane = (shard - half) * width
            value = later[:, lane : lane + width]
        place = me ^ shard

        @pl.when((place & 1) == 0)
        def _():
            keep_ref[place >> 1] = value

        @pl.when((place & 1) == 1)
        def _():
            send_ref[place >> 1] = value.astype(jnp.bfloat16)


def transform(picks, chunks, cells, tables, shards, scale, start, rows, *after):
    width = LAGS // shards
    shape = (shards // 2, rows, width)
    vmem = pl.BlockSpec(memory_space=pltpu.VMEM)
    return pl.pallas_call(
        functools.partial(transform_kernel, shards, scale, start, len(chunks)),
        out_shape=(
            jax.ShapeDtypeStruct(shape, jnp.float32),
            jax.ShapeDtypeStruct(shape, jnp.bfloat16),
            TOKEN,
        ),
        in_specs=[vmem] * (5 + len(chunks))
        + [pl.BlockSpec(memory_space=pl.ANY)] * len(after),
        out_specs=(vmem, vmem, vmem),
        cost_estimate=light(),
        compiler_params=params(16),
        name="transform",
    )(*picks, *chunks, cells, *tables, *after)


def swap(send, bit):
    size = lax.axis_size("seg")
    return lax.ppermute(send, "seg", [(i, i ^ bit) for i in range(size)])


def halve(keep, got):
    total = keep + got.astype(jnp.float32)
    return total[0::2], total[1::2].astype(jnp.bfloat16)


def reduce_further(keep, got, bit):
    while keep.shape[0] > 1:
        keep, send = halve(keep, got)
        bit *= 2
        got = swap(send, bit)
    return (keep[0] + got[0].astype(jnp.float32)).astype(jnp.bfloat16)


def place_kernel(start, further, place_ref, *refs):
    parts, (out_ref, made_ref, sems) = refs[:-3], refs[-3:]
    width, slots = made_ref.shape
    flip = lax.axis_index("seg") < lax.axis_size("seg") // 2
    rows = lax.broadcasted_iota(jnp.int32, (width, width), 0)
    columns = lax.broadcasted_iota(jnp.int32, (width, width), 1)
    wanted = jnp.where(flip, width - 1 - rows, rows)
    turned = jnp.where(wanted == columns, 1.0, 0.0).astype(jnp.bfloat16)
    across = [
        lax.dot_general(
            turned, ref[...], (((1,), (1,)), ((), ())), preferred_element_type=jnp.float32
        ).astype(jnp.bfloat16)
        for ref in parts[further:]
    ]
    step = min(256, slots)
    copies = []
    for index in range(slots // step):
        lanes = pl.ds(index * step, step)
        first = start
        total = parts[0][:, lanes] if further else None
        for part in across:
            count = part.shape[1]
            spot = lax.broadcasted_iota(jnp.int32, (count, step), 0) + first
            chosen = jnp.where(spot == place_ref[0:1, lanes], 1.0, 0.0).astype(jnp.bfloat16)
            more = jnp.dot(part, chosen, preferred_element_type=jnp.float32)
            total = more if total is None else total + more
            first += count
        if further:
            made_ref[:, lanes] = total
            copy = pltpu.make_async_copy(made_ref.at[:, lanes], out_ref.at[:, lanes], sems.at[index])
            copy.start()
            copies.append(copy)
        else:
            out_ref[:, lanes] = total
    for copy in copies:
        copy.wait()


def place_rows(place, parts, start, total=None):
    width = parts[0].shape[1]
    slots = place.shape[1]
    further = total is not None
    given = [total, *parts] if further else list(parts)
    vmem = pl.BlockSpec(memory_space=pltpu.VMEM)
    return pl.pallas_call(
        functools.partial(place_kernel, start, further),
        out_shape=jax.ShapeDtypeStruct((width, slots), jnp.float32),
        in_specs=[vmem] * (1 + len(given)),
        out_specs=pl.BlockSpec(memory_space=pltpu.HBM) if further else vmem,
        scratch_shapes=[
            pltpu.VMEM((width, slots), jnp.float32),
            pltpu.SemaphoreType.DMA((slots // min(256, slots),)),
        ],
        cost_estimate=light(),
        compiler_params=params(16),
        name="place_rows",
    )(place, *given)


def per_device(spectra, source_ids, pair_source, pair_offset, pair_counts):
    chan_rows = spectra.shape[1]
    bins = spectra.shape[3]
    seg_size = lax.axis_size("seg")
    chan_size = lax.axis_size("chan")
    slots = pair_source.shape[0]
    window = 3 * slots // 8
    scale = 1.0 / math.sqrt(bins * seg_size)
    join = lax.optimization_barrier

    ring = list(range(0, chan_size, 2)) + list(range(1, chan_size, 2))[::-1]
    ahead = [(ring[i], ring[(i + 1) % chan_size]) for i in range(chan_size)]
    back = [(b, a) for a, b in ahead]
    leftward = [(i + 1, i) for i in range(chan_size - 1)]
    rightward = [(i, i + 1) for i in range(chan_size - 1)]

    def gathered(turns):
        own = pick_rows(turns, pair_counts, source_ids, pair_source, pair_offset, spectra)
        forward, backward = [own], [own]
        steps = chan_size // 2

        def step_beside(work=None):
            forward.append(lax.ppermute(forward[-1], "chan", ahead))
            if len(backward) < chan_size - steps:
                backward.append(lax.ppermute(backward[-1], "chan", back))
            if work is not None:
                *results, token = work()
                token, forward[-1], backward[-1] = join((token, forward[-1], backward[-1]))
                return results, token

        tables, token = step_beside(lambda: lag_tables(bins, scale, own))
        flat = jnp.transpose(spectra[0], (1, 0, 2))
        (whitened,), token = step_beside(lambda: whiten_rows(flat, token))
        for _ in range(3, steps):
            step_beside()
        real = lax.ppermute(forward[-1][0:1], "chan", ahead)
        imag = lax.ppermute(backward[-1][1:2], "chan", back)
        chunks = [*forward, real, imag, *backward[1:]]
        *picks, token = prepare(turns, source_ids, chunks, slots, chan_rows, window, token)
        return chunks, tables, whitened, picks, token

    def correlate(chunks, whitened, tables, picks, place, token):
        bounds = (0, window, 2 * window, slots)

        def piece(part, *after):
            start, stop = bounds[part], bounds[part + 1]
            return transform(
                picks, chunks, whitened, tables, seg_size, scale, start, stop - start, *after
            )

        keep_left, send, _ = piece(0, token)
        got_left = swap(send, 1)
        keep_right, send, token = piece(1, send)
        token, got_left = join((token, got_left))
        keep_left, send_left = halve(keep_left, got_left)
        got_right = swap(send, 1)
        got_left = swap(send_left, 2)
        keep_own, send, token = piece(2, send_left, token)
        token, got_left, got_right = join((token, got_left, got_right))
        left = reduce_further(keep_left, got_left, 2)
        right = reduce_further(keep_right, got_right, 1)
        own = reduce_further(keep_own, swap(send, 1), 1)
        from_right = lax.ppermute(left, "chan", leftward)
        from_left = lax.ppermute(right, "chan", rightward)
        total = place_rows(place, (left, right, own), 0)
        return place_rows(place, (from_left, from_right), slots, total), (own, token)

    def one_turn(turns):
        chunks, tables, whitened, (*picks, place, source_turns), token = gathered(turns)
        result, after = correlate(chunks, whitened, tables, picks, place, token)
        return result, after, chunks, source_turns

    first, after, chunks, source_turns = one_turn(jnp.zeros((2,), jnp.int32))
    turn, pair_turns, all_turns = [
        count[0] for count in count_turns(source_turns, chunks, slots, window, after)
    ]

    def further(state):
        turn, total = state
        turns = jnp.stack([lax.div(turn, pair_turns), lax.rem(turn, pair_turns)])
        return turn + 1, total + one_turn(turns)[0]

    return lax.while_loop(lambda state: state[0] < all_turns, further, (turn, first))[1]


def solution(mesh):
    in_specs = (P("seg", "chan", None, None), P(), P("chan"), P("chan"), P("chan"))
    out_specs = P("seg", "chan")
    return jax.shard_map(
        per_device, mesh=mesh, in_specs=in_specs, out_specs=out_specs, check_vma=False
    )
```

```python
import functools
import math

import jax
import jax.numpy as jnp
from jax import lax
from jax.experimental import pallas as pl
from jax.experimental.pallas import tpu as pltpu
from jax.sharding import PartitionSpec as P

LAGS = 1024
HALF = LAGS // 2
WBLOCK = 64
PICK = 16
BINS_STEP = 512
TABLE_ROWS = 64
EXTRA = 128


def params(mebibytes):
    return pltpu.CompilerParams(vmem_limit_bytes=mebibytes * 1024 * 1024)


def light():
    return pl.CostEstimate(flops=1024, bytes_accessed=1024, transcendentals=0)


TOKEN = jax.ShapeDtypeStruct((8, 128), jnp.float32)


def whole(shape):
    return pl.BlockSpec(shape, lambda *_: (0,) * len(shape))


def ring_place(block, chan_size):
    return jnp.where((block & 1) == 0, block >> 1, chan_size - 1 - (block >> 1))


def ring_block(place, chan_size):
    return jnp.where(place < chan_size // 2, 2 * place, 2 * (chan_size - place) - 1)


def far_block(me, chan_size):
    place = ring_place(me, chan_size) - chan_size // 2
    return ring_block(jnp.where(place < 0, place + chan_size, place), chan_size)


def ring_hop(me, block, chan_size):
    steps = chan_size // 2
    distance = ring_place(me, chan_size) - ring_place(block, chan_size)
    distance = jnp.where(distance < 0, distance + chan_size, distance)
    return jnp.where(distance <= steps, distance, steps + chan_size - distance)


def pick_kernel(
    chan_rows, band, first_rows, turns_ref, counts_ref, ids_ref, source_ref, offset_ref, cells_ref, out_ref,
    rows_ref, held_ref, sems,
):
    first = lax.axis_index("chan") * chan_rows
    turn = turns_ref[0]
    bins = cells_ref.shape[3]
    for i in range(PICK):
        rows_ref[i] = 0
    rank = jnp.int32(0)
    for i in range(ids_ref.shape[0]):
        row = ids_ref[i] - first
        mine = (row >= 0) & (row < chan_rows)
        spot = rank - turn * PICK
        rows_ref[jnp.where(mine & (spot >= 0) & (spot < PICK), spot, PICK)] = row
        rank = rank + mine.astype(jnp.int32)
    far = far_block(lax.axis_index("chan"), lax.axis_size("chan")) * chan_rows
    late = [jnp.int32(0), jnp.int32(0)]
    for i in range(ids_ref.shape[0]):
        row = ids_ref[i] - far
        late[i // 32] = late[i // 32] | (((row >= 0) & (row < chan_rows)).astype(jnp.int32) << (i % 32))
    copies = [
        pltpu.make_async_copy(cells_ref.at[0, rows_ref[i]], held_ref.at[i], sems.at[i])
        for i in range(PICK)
    ]
    for copy in copies:
        copy.start()

    offset = offset_ref[...]
    slot = lax.broadcasted_iota(jnp.int32, offset.shape, 0) * offset.shape[1]
    slot = slot + lax.broadcasted_iota(jnp.int32, offset.shape, 1)
    live = slot < counts_ref[0]
    source = source_ref[...]
    bits = jnp.where(source < 32, late[0], late[1])
    is_late = lax.shift_right_logical(bits, source & 31) & 1
    inside = live & (offset >= 0) & (offset < chan_rows)
    kinds = (live & (offset >= chan_rows), live & (offset < 0), inside, inside & (is_late == 0))
    lane = lax.broadcasted_iota(jnp.int32, offset.shape, 1)
    notes = jnp.zeros(offset.shape, jnp.int32)
    totals = [jnp.sum(jnp.where(kind, 1.0, 0.0)).astype(jnp.int32) for kind in kinds]
    totals = (totals[0], totals[1], totals[2] - jnp.minimum(totals[3], first_rows))
    for index, total in enumerate(totals):
        notes = jnp.where(lane == 2 * index, total >> 5, notes)
        notes = jnp.where(lane == 2 * index + 1, total & 31, notes)
    shifted = offset + band
    source = jnp.where(live, source + 1, 0)

    def coded(upper, lower):
        both = jnp.concatenate([upper.astype(jnp.float32), lower.astype(jnp.float32)], axis=0)
        return both.astype(jnp.bfloat16)

    out_ref[0, :, pl.ds(bins, EXTRA)] = coded(source, shifted >> 4)
    out_ref[1, :, pl.ds(bins, EXTRA)] = coded((shifted & 15) + 16 * is_late, notes)

    for copy in copies:
        copy.wait()
    real = held_ref[:, 0, :].astype(jnp.float32)
    imag = held_ref[:, 1, :].astype(jnp.float32)
    width = min(256, bins)

    def stacked(values):
        return jnp.concatenate([values[:, i : i + width] for i in range(0, bins, width)], axis=0)

    real, imag = whitened_pair(stacked(real), stacked(imag))
    for index in range(bins // width):
        lanes = pl.ds(index * width, width)
        out_ref[0, :, lanes] = real[index * PICK : (index + 1) * PICK]
        out_ref[1, :, lanes] = imag[index * PICK : (index + 1) * PICK]


def pick_rows(turns, counts, source_ids, pair_source, pair_offset, spectra, first_rows):
    _, chan_rows, parts, bins = spectra.shape
    smem = pl.BlockSpec(memory_space=pltpu.SMEM)
    vmem = pl.BlockSpec(memory_space=pltpu.VMEM)
    return pl.pallas_call(
        functools.partial(pick_kernel, chan_rows, chan_rows // 2, first_rows),
        out_shape=jax.ShapeDtypeStruct((parts, PICK, bins + EXTRA), spectra.dtype),
        in_specs=[smem, smem, smem, vmem, vmem, pl.BlockSpec(memory_space=pltpu.HBM)],
        out_specs=vmem,
        scratch_shapes=[
            pltpu.SMEM((PICK + 1,), jnp.int32),
            pltpu.VMEM((PICK, parts, bins), spectra.dtype),
            pltpu.SemaphoreType.DMA((PICK,)),
        ],
        cost_estimate=light(),
        compiler_params=params(59),
        name="pick_rows",
    )(
        turns, counts, source_ids, pair_source.reshape(-1, EXTRA), pair_offset.reshape(-1, EXTRA), spectra
    )


def block_mean(power):
    width = power.shape[1]
    row_group = lax.broadcasted_iota(jnp.int32, (width, width), 0) // WBLOCK
    col_group = lax.broadcasted_iota(jnp.int32, (width, width), 1) // WBLOCK
    spread = jnp.where(row_group == col_group, 1.0 / WBLOCK, 0.0).astype(jnp.bfloat16)
    high = power.astype(jnp.bfloat16)
    low = (power - high.astype(jnp.float32)).astype(jnp.bfloat16)
    total = jnp.dot(low, spread, preferred_element_type=jnp.float32)
    return total + jnp.dot(high, spread, preferred_element_type=jnp.float32)


def whitened_pair(real, imag):
    inverse = lax.rsqrt(block_mean(real * real + imag * imag) + 1e-06)
    return (real * inverse).astype(jnp.bfloat16), (imag * inverse).astype(jnp.bfloat16)


def whiten_kernel(cells_ref, after_ref, out_ref, token_ref):
    token_ref[...] = jnp.zeros_like(token_ref)
    for start in range(0, cells_ref.shape[2], 256):
        lanes = pl.ds(start, 256)
        real = cells_ref[0, :, lanes].astype(jnp.float32)
        imag = cells_ref[1, :, lanes].astype(jnp.float32)
        out_ref[0, :, lanes], out_ref[1, :, lanes] = whitened_pair(real, imag)


def whiten_rows(cells, after):
    _, rows, bins = cells.shape
    spec = pl.BlockSpec((2, rows, BINS_STEP), lambda i: (0, 0, i))
    return pl.pallas_call(
        whiten_kernel,
        grid=(bins // BINS_STEP,),
        out_shape=(jax.ShapeDtypeStruct(cells.shape, jnp.bfloat16), TOKEN),
        in_specs=[spec, pl.BlockSpec(memory_space=pl.ANY)],
        out_specs=(spec, whole(TOKEN.shape)),
        cost_estimate=light(),
        compiler_params=params(12),
        name="whiten_rows",
    )(cells, after)


def table_kernel(scale, all_bins, after_ref, cos_ref, sin_ref, token_ref, coarse_ref, fine_ref):
    token_ref[...] = jnp.zeros_like(token_ref)
    step = pl.program_id(0)
    groups = cos_ref.shape[0] // TABLE_ROWS

    @pl.when(step == 0)
    def _():
        def circle(ref, stride, factor):
            shape = ref.shape[1:]
            bins = lax.broadcasted_iota(jnp.int32, shape, 0) * stride
            lags = lax.broadcasted_iota(jnp.int32, shape, 1)
            lags = jnp.where(lags == 0, HALF, lags)
            theta = ((bins * lags) & (2 * all_bins - 1)).astype(jnp.float32) * (math.pi / all_bins)
            ref[0] = jnp.cos(theta) * factor
            ref[1] = jnp.sin(theta) * factor

        circle(coarse_ref, TABLE_ROWS, scale)
        circle(fine_ref, 1, 1.0)

    cos_b = fine_ref[0]
    sin_b = fine_ref[1]
    first = lax.broadcasted_iota(jnp.int32, cos_b.shape, 1) == 0
    for group in range(groups):
        cos_a = coarse_ref[0, pl.ds(step * groups + group, 1), :]
        sin_a = coarse_ref[1, pl.ds(step * groups + group, 1), :]
        rows = pl.ds(group * TABLE_ROWS, TABLE_ROWS)
        cos = jnp.where(first, scale, cos_a * cos_b - sin_a * sin_b)
        cos_ref[rows, :] = cos.astype(jnp.bfloat16)
        sin_ref[rows, :] = (sin_a * cos_b + cos_a * sin_b).astype(jnp.bfloat16)


def lag_tables(bins, scale, after):
    spec = pl.BlockSpec((BINS_STEP, HALF), lambda i: (i, 0))
    shape = jax.ShapeDtypeStruct((bins, HALF), jnp.bfloat16)
    return pl.pallas_call(
        functools.partial(table_kernel, scale, bins),
        grid=(bins // BINS_STEP,),
        out_shape=(shape, shape, TOKEN),
        in_specs=[pl.BlockSpec(memory_space=pl.ANY)],
        out_specs=(spec, spec, whole(TOKEN.shape)),
        scratch_shapes=[
            pltpu.VMEM((2, bins // TABLE_ROWS, HALF), jnp.float32),
            pltpu.VMEM((2, TABLE_ROWS, HALF), jnp.float32),
        ],
        cost_estimate=light(),
        compiler_params=params(12),
        name="lag_tables",
    )(after)


def source_spots(chan_rows, chan_size, me, turn, ids_row):
    count = ids_row.shape[1]
    shift = chan_rows.bit_length() - 1
    ids_row = jnp.broadcast_to(ids_row, (count, count))
    rows = lax.broadcasted_iota(jnp.int32, (count, count), 0)
    columns = lax.broadcasted_iota(jnp.int32, (count, count), 1)
    ids = jnp.sum(jnp.where(rows == columns, ids_row, 0).astype(jnp.float32), axis=1, keepdims=True)
    owner = jnp.broadcast_to(ids.astype(jnp.int32) >> shift, (count, count))
    earlier = (owner == (ids_row >> shift)) & (columns < rows)
    rank = jnp.sum(jnp.where(earlier, 1.0, 0.0), axis=1, keepdims=True)
    turns = (jnp.max(rank).astype(jnp.int32) + PICK) // PICK
    rank = rank.astype(jnp.int32) - turn * PICK
    owner = owner[:, 0:1]

    hop = ring_hop(me, owner, chan_size)
    return jnp.where((rank >= 0) & (rank < PICK), hop * PICK + rank, -1), turns


def flat(value):
    return jnp.concatenate([value[i : i + 1, :] for i in range(8)], axis=1)


def unlisted(halves, band):
    upper, lower = [half.astype(jnp.int32) for half in halves]
    return upper[0:8] - 1, upper[8:16] * 16 + (lower[0:8] & 15) - band, lower[0:8] >> 4


def ranked(taken):
    marks = jnp.concatenate([jnp.where(mask, 1.0, 0.0) for mask in taken], axis=0)
    rows = marks.shape[0]
    earlier = lax.broadcasted_iota(jnp.int32, (EXTRA, EXTRA), 0) < lax.broadcasted_iota(
        jnp.int32, (EXTRA, EXTRA), 1
    )
    rank = jnp.dot(
        marks.astype(jnp.bfloat16),
        jnp.where(earlier, 1.0, 0.0).astype(jnp.bfloat16),
        preferred_element_type=jnp.float32,
    )
    sums = jnp.broadcast_to(jnp.sum(marks, axis=1, keepdims=True), marks.shape)
    row = lax.broadcasted_iota(jnp.int32, (rows, rows), 0)
    column = lax.broadcasted_iota(jnp.int32, (rows, rows), 1)
    above_it = ((row >> 3) == (column >> 3)) & (column < row)
    rank = rank + jnp.dot(
        jnp.where(above_it, 1.0, 0.0).astype(jnp.bfloat16),
        sums.astype(jnp.bfloat16),
        preferred_element_type=jnp.float32,
    )
    rank = rank.astype(jnp.int32)
    return [rank[8 * i : 8 * i + 8] for i in range(len(taken))]


def jobs_of(spots, source, receiver, position, count):
    source, receiver, position = flat(source), flat(receiver), flat(position)
    slots = source.shape[1]
    names = lax.broadcasted_iota(jnp.int32, (spots.shape[0], slots), 0)
    field_row = lax.broadcasted_iota(jnp.int32, (8, slots), 0)
    spot = jnp.where(names == source, spots + 1, 0).astype(jnp.float32)
    spot = jnp.sum(spot, axis=0, keepdims=True).astype(jnp.int32) - 1
    fields = jnp.where(field_row == 0, spot >> 4, jnp.where(field_row == 1, spot & (PICK - 1), 0))
    fields = jnp.where(field_row == 2, receiver, jnp.where(field_row == 3, 1, fields))
    fields = jnp.where((position >= 0) & (spot >= 0), fields, 0)
    wanted = lax.broadcasted_iota(jnp.int32, (count, slots), 0)
    chosen = jnp.where(wanted == position, 1.0, 0.0).astype(jnp.bfloat16)
    return lax.dot_general(
        chosen,
        fields.astype(jnp.float32).astype(jnp.bfloat16),
        (((1,), (1,)), ((), ())),
        preferred_element_type=jnp.float32,
    )


def write_picks(jobs, start, src_ref, rec_ref):
    count = jobs.shape[0]
    jobs = jobs.astype(jnp.int32)
    busy = jobs[:, 3:4] > 0
    part = pl.ds(start, count)
    column = jnp.where(busy, jobs[:, 0:1] * PICK + jobs[:, 1:2], -1)
    lane = lax.broadcasted_iota(jnp.int32, (count, src_ref.shape[1]), 1)
    src_ref[part, :] = jnp.where(column == lane, 1.0, 0.0).astype(jnp.bfloat16)
    column = jnp.where(busy, jobs[:, 2:3], -1)
    lane = lax.broadcasted_iota(jnp.int32, (count, rec_ref.shape[1]), 1)
    rec_ref[part, :] = jnp.where(column == lane, 1.0, 0.0).astype(jnp.bfloat16)


def early_kernel(chan_rows, chan_size, turns_ref, ids_ref, after_ref, own_ref, src_ref, rec_ref, token_ref):
    token_ref[...] = jnp.zeros_like(token_ref)
    me = lax.axis_index("chan")
    count = src_ref.shape[0]
    lanes = pl.ds(own_ref.shape[2] - EXTRA, EXTRA)
    spots, _ = source_spots(chan_rows, chan_size, me, turns_ref[0], ids_ref[...])
    halves = [own_ref[half, :, lanes].astype(jnp.float32) for half in range(2)]
    source, offset, late = unlisted(halves, chan_rows // 2)
    early = (source >= 0) & (offset >= 0) & (offset < chan_rows) & (late == 0)
    (rank,) = ranked((early,))
    rank = jnp.where(early & (rank < count) & (turns_ref[1] == 0), rank, -1)
    write_picks(jobs_of(spots, source, offset, rank, count), 0, src_ref, rec_ref)


def prepare_early(turns, source_ids, own, chan_rows, chan_size, count, after):
    vmem = pl.BlockSpec(memory_space=pltpu.VMEM)
    return pl.pallas_call(
        functools.partial(early_kernel, chan_rows, chan_size),
        out_shape=(
            jax.ShapeDtypeStruct((count, chan_size * PICK), jnp.bfloat16),
            jax.ShapeDtypeStruct((count, chan_rows), jnp.bfloat16),
            TOKEN,
        ),
        in_specs=[
            pl.BlockSpec(memory_space=pltpu.SMEM), vmem, pl.BlockSpec(memory_space=pl.ANY), vmem,
        ],
        out_specs=(vmem, vmem, vmem),
        cost_estimate=light(),
        compiler_params=params(12),
        name="prepare_early",
    )(turns, source_ids.reshape(1, -1), after, own)


def prepare_kernel(chan_rows, chan_size, window, turns_ref, ids_ref, after_ref, passed_ref, *refs):
    chunk_refs = refs[:chan_size]
    src_ref, rec_ref, place_ref, needed_ref, _, token_ref = refs[chan_size:]
    token_ref[...] = jnp.zeros_like(token_ref)
    me = lax.axis_index("chan")
    turn = turns_ref[1]
    slots = place_ref.shape[1]
    room = 2 * window
    spots, needed = source_spots(chan_rows, chan_size, me, turns_ref[0], ids_ref[...])
    needed_ref[0] = needed

    lanes = pl.ds(chunk_refs[0].shape[2] - EXTRA, EXTRA)
    left_hop = jnp.where(me > 0, ring_hop(me, me - 1, chan_size), -1)
    right_hop = jnp.where(me < chan_size - 1, ring_hop(me, me + 1, chan_size), -1)
    listed = []
    for wanted in (left_hop, right_hop, 0):
        halves = []
        for half in range(2):
            value = jnp.zeros((PICK, EXTRA), jnp.float32)
            for hop, ref in enumerate(chunk_refs):
                value = jnp.where(wanted == hop, ref[half, :, lanes].astype(jnp.float32), value)
            halves.append(value)
        listed.append(unlisted(halves, chan_rows // 2))
    (left_src, left_off, _), (right_src, right_off, _), (own_src, own_off, own_late) = listed
    inside = (own_src >= 0) & (own_off >= 0) & (own_off < chan_rows)
    early = inside & (own_late == 0)
    taken = (
        (left_src >= 0) & (left_off >= chan_rows),
        (right_src >= 0) & (right_off < 0),
        (own_src >= 0) & (own_off < 0),
        (own_src >= 0) & (own_off >= chan_rows),
        inside,
        early,
    )
    ranks = ranked(taken)
    left_total = jnp.sum(jnp.where(taken[0], 1.0, 0.0)).astype(jnp.int32)
    right_total = jnp.sum(jnp.where(taken[1], 1.0, 0.0)).astype(jnp.int32)

    def done_before(amount, index):
        return jnp.minimum(amount, index * window)

    left_before = done_before(left_total, turn)
    right_before = done_before(right_total, turn)
    left_now = done_before(left_total, turn + 1) - left_before
    right_now = done_before(right_total, turn + 1) - right_before

    def in_window(index):
        shifted = ranks[index] - turn * window
        return shifted, taken[index] & (shifted >= 0) & (shifted < window)

    left_rank, left_ok = in_window(0)
    right_rank, right_ok = in_window(1)
    below_rank, below_ok = in_window(2)
    above_rank, above_ok = in_window(3)

    first = early & (ranks[5] < slots - room)
    own_rank = ranks[4] - jnp.minimum(ranks[5], slots - room)
    own_rank = own_rank - (turn * room - left_before - right_before)
    own_ok = inside & ~first & (own_rank >= 0) & (own_rank < room - left_now - right_now)
    own_pos = own_rank + left_now
    own_pos = jnp.where(own_pos < window, own_pos, own_pos + right_now)
    own_pos = jnp.where(own_ok, own_pos, -1)
    place = jnp.where(first & (turn == 0), ranks[5] + room, own_pos)
    place = jnp.where(below_ok, below_rank + slots, place)
    place = jnp.where(above_ok, above_rank + slots + window, place)
    place_ref[...] = jnp.broadcast_to(flat(place), place_ref.shape)

    left_jobs = jobs_of(spots, left_src, left_off - chan_rows, jnp.where(left_ok, left_rank, -1), window)
    right_jobs = jobs_of(
        spots, right_src, right_off + chan_rows, jnp.where(right_ok, right_rank, -1), window
    )
    own_jobs = jobs_of(spots, own_src, own_off, own_pos, room)
    write_picks(left_jobs + own_jobs[0:window], 0, src_ref, rec_ref)
    write_picks(right_jobs + own_jobs[window:room], window, src_ref, rec_ref)


def prepare(turns, source_ids, chunks, slots, chan_rows, window, after, passed):
    chan_size = len(chunks)
    vmem = pl.BlockSpec(memory_space=pltpu.VMEM)
    smem = pl.BlockSpec(memory_space=pltpu.SMEM)
    return pl.pallas_call(
        functools.partial(prepare_kernel, chan_rows, chan_size, window),
        out_shape=(
            jax.ShapeDtypeStruct((2 * window, chan_size * PICK), jnp.bfloat16),
            jax.ShapeDtypeStruct((2 * window, chan_rows), jnp.bfloat16),
            jax.ShapeDtypeStruct((8, slots), jnp.int32),
            jax.ShapeDtypeStruct((1,), jnp.int32),
            jax.ShapeDtypeStruct(passed.shape, passed.dtype),
            TOKEN,
        ),
        in_specs=[smem, vmem] + [pl.BlockSpec(memory_space=pl.ANY)] * 2 + [vmem] * len(chunks),
        out_specs=(vmem, vmem, vmem, smem, pl.BlockSpec(memory_space=pl.ANY), vmem),
        input_output_aliases={3: 4},
        cost_estimate=light(),
        compiler_params=params(16),
        name="prepare",
    )(turns, source_ids.reshape(1, -1), after, passed, *chunks)


def turns_kernel(chan_size, window, source_turns_ref, *refs):
    chunk_refs = refs[:chan_size]
    left_ref, pairs_ref = refs[-2:]
    me = lax.axis_index("chan")
    steps = chan_size // 2
    place = ring_place(me, chan_size)
    block = lax.broadcasted_iota(jnp.int32, (chan_size, EXTRA), 0)
    notes = jnp.zeros((chan_size, EXTRA), jnp.float32)
    for hop, ref in enumerate(chunk_refs):
        spot = place - hop if hop <= steps else place + hop - steps
        spot = jnp.where(spot < 0, spot + chan_size, spot)
        spot = jnp.where(spot >= chan_size, spot - chan_size, spot)
        owner = ring_block(spot, chan_size)
        notes = jnp.where(block == owner, ref[0][8:9, :].astype(jnp.float32), notes)
    lane = lax.broadcasted_iota(jnp.int32, notes.shape, 1)

    def total(index):
        value = jnp.where(lane == 2 * index, 32.0 * notes, 0.0)
        value = value + jnp.where(lane == 2 * index + 1, notes, 0.0)
        return jnp.broadcast_to(jnp.sum(value, axis=1, keepdims=True), notes.shape)

    left = jnp.where(block == 0, 0.0, pltpu.roll(total(0), 1, 0))
    right = jnp.where(block == chan_size - 1, 0.0, pltpu.roll(total(1), chan_size - 1, 0))
    aside = jnp.max(jnp.maximum(left, right)).astype(jnp.int32)
    whole_sum = jnp.max(left + right + total(2)).astype(jnp.int32)
    room = 2 * window
    needed = jnp.maximum((aside + window - 1) // window, (whole_sum + room - 1) // room)
    needed = jnp.maximum(needed, 1)
    pairs_ref[0] = needed
    left_ref[0] = needed * source_turns_ref[0] - 1


def count_turns(source_turns, chunks, window, after):
    _, _, width = chunks[0].shape
    last = width // EXTRA - 1
    specs = [pl.BlockSpec((1, PICK, EXTRA), lambda i: (1, 0, last)) for _ in chunks]
    return pl.pallas_call(
        functools.partial(turns_kernel, len(chunks), window),
        grid=(1,),
        out_shape=[jax.ShapeDtypeStruct((1,), jnp.int32)] * 2,
        in_specs=[pl.BlockSpec(memory_space=pltpu.SMEM), *specs]
        + [pl.BlockSpec(memory_space=pl.ANY)] * len(after),
        out_specs=[pl.BlockSpec(memory_space=pltpu.SMEM)] * 2,
        cost_estimate=light(),
        compiler_params=params(8),
        name="count_turns",
    )(source_turns, *chunks, *after)


def transform_kernel(shards, scale, start, chunks, src_ref, rec_ref, *refs):
    chunk_refs = refs[:chunks]
    cells_ref, cos_ref, sin_ref = refs[chunks : chunks + 3]
    keep_ref, send_ref, token_ref = refs[-3:]
    token_ref[...] = jnp.zeros_like(token_ref)
    rows = keep_ref.shape[1]
    bins = cos_ref.shape[0]
    step = min(BINS_STEP, bins)
    eighth = lax.broadcasted_iota(jnp.int32, (1, 128), 1) & 7
    root = math.sqrt(0.5)
    edge = jnp.where((eighth == 1) | (eighth == 7), root, 0.0)
    edge = jnp.where((eighth == 3) | (eighth == 5), -root, edge)
    edge = jnp.where(eighth == 0, 1.0, jnp.where(eighth == 4, -1.0, edge)) * scale
    edge = edge.astype(jnp.bfloat16).astype(jnp.float32)

    by_src = src_ref[pl.ds(start, rows), :]
    by_rec = rec_ref[pl.ds(start, rows), :]
    even = odd = corner = None
    for first in range(0, bins, step):
        lanes = pl.ds(first, step)
        source_real = jnp.concatenate([ref[0, :, lanes] for ref in chunk_refs], axis=0)
        source_imag = jnp.concatenate([ref[1, :, lanes] for ref in chunk_refs], axis=0)
        sr = jnp.dot(by_src, source_real, preferred_element_type=jnp.float32)
        si = jnp.dot(by_src, source_imag, preferred_element_type=jnp.float32)
        rr = jnp.dot(by_rec, cells_ref[0, :, lanes], preferred_element_type=jnp.float32)
        ri = jnp.dot(by_rec, cells_ref[1, :, lanes], preferred_element_type=jnp.float32)
        real = (sr * rr + si * ri).astype(jnp.bfloat16)
        imag = (si * rr - sr * ri).astype(jnp.bfloat16)
        more_even = jnp.dot(real, cos_ref[lanes, :], preferred_element_type=jnp.float32)
        more_odd = jnp.dot(imag, sin_ref[lanes, :], preferred_element_type=jnp.float32)
        wide = real.astype(jnp.float32)
        sums = wide[:, 0:128]
        for lane in range(128, step, 128):
            sums = sums + wide[:, lane : lane + 128]
        even = more_even if even is None else even + more_even
        odd = more_odd if odd is None else odd + more_odd
        corner = sums if corner is None else corner + sums

    me = lax.axis_index("seg")
    width = LAGS // shards
    corner = jnp.sum(corner * edge, axis=1, keepdims=True)
    first = lax.broadcasted_iota(jnp.int32, even.shape, 1) == 0
    later = even - jnp.where(first, 0.0, odd)
    sooner = jnp.where(first, corner, even) + odd
    sooner = pltpu.roll(sooner, HALF - 1, 1)
    for shard in range(shards):
        half = shards // 2
        if shard < half:
            lane = (half - 1 - shard) * width
            value = sooner[:, lane : lane + width]
        else:
            lane = (shard - half) * width
            value = later[:, lane : lane + width]
        place = me ^ shard

        @pl.when((place & 1) == 0)
        def _():
            keep_ref[place >> 1] = value

        @pl.when((place & 1) == 1)
        def _():
            send_ref[place >> 1] = value.astype(jnp.bfloat16)


def transform(picks, chunks, cells, tables, shards, scale, start, rows, weight, *after):
    width = LAGS // shards
    shape = (shards // 2, rows, width)
    vmem = pl.BlockSpec(memory_space=pltpu.VMEM)
    return pl.pallas_call(
        functools.partial(transform_kernel, shards, scale, start, len(chunks)),
        out_shape=(
            jax.ShapeDtypeStruct(shape, jnp.float32),
            jax.ShapeDtypeStruct(shape, jnp.bfloat16),
            TOKEN,
        ),
        in_specs=[vmem] * (5 + len(chunks))
        + [pl.BlockSpec(memory_space=pl.ANY)] * len(after),
        out_specs=(vmem, vmem, vmem),
        cost_estimate=weight,
        compiler_params=params(16),
        name="transform",
    )(*picks, *chunks, cells, *tables, *after)


def swap(send, bit):
    size = lax.axis_size("seg")
    return lax.ppermute(send, "seg", [(i, i ^ bit) for i in range(size)])


def halve(keep, got):
    total = keep + got.astype(jnp.float32)
    return total[0::2], total[1::2].astype(jnp.bfloat16)


def reduce_further(keep, got, bit):
    while keep.shape[0] > 1:
        keep, send = halve(keep, got)
        bit *= 2
        got = swap(send, bit)
    return (keep[0] + got[0].astype(jnp.float32)).astype(jnp.bfloat16)


def place_kernel(start, further, place_ref, *refs):
    parts, (out_ref, made_ref, sems) = refs[:-3], refs[-3:]
    width, slots = made_ref.shape
    flip = lax.axis_index("seg") < lax.axis_size("seg") // 2
    rows = lax.broadcasted_iota(jnp.int32, (width, width), 0)
    columns = lax.broadcasted_iota(jnp.int32, (width, width), 1)
    wanted = jnp.where(flip, width - 1 - rows, rows)
    turned = jnp.where(wanted == columns, 1.0, 0.0).astype(jnp.bfloat16)
    across = [
        lax.dot_general(
            turned, ref[...], (((1,), (1,)), ((), ())), preferred_element_type=jnp.float32
        ).astype(jnp.bfloat16)
        for ref in parts[further:]
    ]
    step = min(256, slots)
    copies = []
    for index in range(slots // step):
        lanes = pl.ds(index * step, step)
        first = start
        total = parts[0][:, lanes] if further else None
        for part in across:
            count = part.shape[1]
            spot = lax.broadcasted_iota(jnp.int32, (count, step), 0) + first
            chosen = jnp.where(spot == place_ref[0:1, lanes], 1.0, 0.0).astype(jnp.bfloat16)
            more = jnp.dot(part, chosen, preferred_element_type=jnp.float32)
            total = more if total is None else total + more
            first += count
        if further:
            made_ref[:, lanes] = total
            copy = pltpu.make_async_copy(made_ref.at[:, lanes], out_ref.at[:, lanes], sems.at[index])
            copy.start()
            copies.append(copy)
        else:
            out_ref[:, lanes] = total
    for copy in copies:
        copy.wait()


def place_rows(place, parts, start, total=None):
    width = parts[0].shape[1]
    slots = place.shape[1]
    further = total is not None
    given = [total, *parts] if further else list(parts)
    vmem = pl.BlockSpec(memory_space=pltpu.VMEM)
    return pl.pallas_call(
        functools.partial(place_kernel, start, further),
        out_shape=jax.ShapeDtypeStruct((width, slots), jnp.float32),
        in_specs=[vmem] * (1 + len(given)),
        out_specs=pl.BlockSpec(memory_space=pltpu.HBM) if further else vmem,
        scratch_shapes=[
            pltpu.VMEM((width, slots), jnp.float32),
            pltpu.SemaphoreType.DMA((slots // min(256, slots),)),
        ],
        cost_estimate=light(),
        compiler_params=params(16),
        name="place_rows",
    )(place, *given)


def per_device(spectra, source_ids, pair_source, pair_offset, pair_counts):
    chan_rows = spectra.shape[1]
    bins = spectra.shape[3]
    seg_size = lax.axis_size("seg")
    chan_size = lax.axis_size("chan")
    slots = pair_source.shape[0]
    window = 3 * slots // 8
    scale = 1.0 / math.sqrt(bins * seg_size)
    join = lax.optimization_barrier

    ring = list(range(0, chan_size, 2)) + list(range(1, chan_size, 2))[::-1]
    ahead = [(ring[i], ring[(i + 1) % chan_size]) for i in range(chan_size)]
    back = [(b, a) for a, b in ahead]
    leftward = [(i + 1, i) for i in range(chan_size - 1)]
    rightward = [(i, i + 1) for i in range(chan_size - 1)]

    def one_turn(turns):
        first_rows = slots - 2 * window
        own = pick_rows(turns, pair_counts, source_ids, pair_source, pair_offset, spectra, first_rows)
        forward, backward = [own], [own]
        steps = chan_size // 2

        def step_beside(work=None):
            ahead_of = forward[-1], backward[-1]
            forward.append(lax.ppermute(ahead_of[0], "chan", ahead))
            if len(backward) < chan_size - steps:
                backward.append(lax.ppermute(ahead_of[1], "chan", back))
            if work is not None:
                *results, token = work()
                if len(backward) == len(forward):
                    token, forward[-1], backward[-1] = join((token, forward[-1], backward[-1]))
                else:
                    token, forward[-1] = join((token, forward[-1]))
                return results, token

        tables, token = step_beside(lambda: lag_tables(bins, scale, own))
        cells = jnp.transpose(spectra[0], (1, 0, 2))
        (whitened,), token = step_beside(lambda: whiten_rows(cells, token))
        for _ in range(3, steps - 1):
            step_beside()
        picks, token = step_beside(
            lambda: prepare_early(turns, source_ids, own, chan_rows, chan_size, first_rows, token)
        )

        def piece(picks, chunks, start, rows, *after, weight=light()):
            return transform(
                picks, chunks, whitened, tables, seg_size, scale, start, rows, weight, *after
            )

        chunks = [*forward, own, *backward[1:]]
        full = pl.CostEstimate(
            flops=first_rows * bins * 4096, bytes_accessed=16 * bins * HALF, transcendentals=0
        )
        (keep_own, send), token = step_beside(
            lambda: piece(picks, chunks, 0, first_rows, token, weight=full)
        )
        chunks = forward + backward[1:]
        *picks, place, source_turns, send, token = prepare(
            turns, source_ids, chunks, slots, chan_rows, window, token, send
        )
        got_own = swap(send, 1)
        keep_left, send, token = piece(picks, chunks, 0, window, token)
        token, got_own = join((token, got_own))
        keep_own, send_own = halve(keep_own, got_own)
        got_left = swap(send, 1)
        got_own = swap(send_own, 2)
        keep_right, send, token = piece(picks, chunks, window, window, token, send_own)
        token, got_left, got_own = join((token, got_left, got_own))
        got_right = swap(send, 1)
        left = reduce_further(keep_left, got_left, 1)
        right = reduce_further(keep_right, got_right, 1)
        own = reduce_further(keep_own, got_own, 2)
        from_right = lax.ppermute(left, "chan", leftward)
        from_left = lax.ppermute(right, "chan", rightward)
        total = place_rows(place, (left, right, own), 0)
        result = place_rows(place, (from_left, from_right), slots, total)
        return result, (right, token), chunks, source_turns

    first, after, chunks, source_turns = one_turn(jnp.zeros((2,), jnp.int32))
    turns_left, pair_turns = [count[0] for count in count_turns(source_turns, chunks, window, after)]

    def further(state):
        turn, total = state
        turns = jnp.stack([lax.div(turn, pair_turns), lax.rem(turn, pair_turns)])
        return turn - 1, total + one_turn(turns)[0]

    return lax.while_loop(lambda state: state[0] > 0, further, (turns_left, first))[1]


def solution(mesh):
    in_specs = (P("seg", "chan", None, None), P(), P("chan"), P("chan"), P("chan"))
    out_specs = P("seg", "chan")
    return jax.shard_map(
        per_device, mesh=mesh, in_specs=in_specs, out_specs=out_specs, check_vma=False
    )
```

```python
import functools
import math

import jax
import jax.numpy as jnp
from jax import lax
from jax.experimental import pallas as pl
from jax.experimental.pallas import tpu as pltpu
from jax.sharding import PartitionSpec as P

LAGS = 1024
HALF = LAGS // 2
WBLOCK = 64
PICK = 16
BINS_STEP = 512
TABLE_ROWS = 64
EXTRA = 128


def params(mebibytes):
    return pltpu.CompilerParams(vmem_limit_bytes=mebibytes * 1024 * 1024)


def light():
    return pl.CostEstimate(flops=1024, bytes_accessed=1024, transcendentals=0)


TOKEN = jax.ShapeDtypeStruct((8, 128), jnp.float32)


def whole(shape):
    return pl.BlockSpec(shape, lambda *_: (0,) * len(shape))


def ring_place(block, chan_size):
    return jnp.where((block & 1) == 0, block >> 1, chan_size - 1 - (block >> 1))


def ring_block(place, chan_size):
    return jnp.where(place < chan_size // 2, 2 * place, 2 * (chan_size - place) - 1)


def far_block(me, chan_size):
    place = ring_place(me, chan_size) - chan_size // 2
    return ring_block(jnp.where(place < 0, place + chan_size, place), chan_size)


def ring_hop(me, block, chan_size):
    steps = chan_size // 2
    distance = ring_place(me, chan_size) - ring_place(block, chan_size)
    distance = jnp.where(distance < 0, distance + chan_size, distance)
    return jnp.where(distance <= steps, distance, steps + chan_size - distance)


def pick_kernel(
    chan_rows, band, first_rows, turns_ref, counts_ref, ids_ref, source_ref, offset_ref, cells_ref, out_ref,
    rows_ref, held_ref, sems,
):
    first = lax.axis_index("chan") * chan_rows
    turn = turns_ref[0]
    bins = cells_ref.shape[3]
    for i in range(PICK):
        rows_ref[i] = 0
    rank = jnp.int32(0)
    for i in range(ids_ref.shape[0]):
        row = ids_ref[i] - first
        mine = (row >= 0) & (row < chan_rows)
        spot = rank - turn * PICK
        rows_ref[jnp.where(mine & (spot >= 0) & (spot < PICK), spot, PICK)] = row
        rank = rank + mine.astype(jnp.int32)
    far = far_block(lax.axis_index("chan"), lax.axis_size("chan")) * chan_rows
    late = [jnp.int32(0), jnp.int32(0)]
    for i in range(ids_ref.shape[0]):
        row = ids_ref[i] - far
        late[i // 32] = late[i // 32] | (((row >= 0) & (row < chan_rows)).astype(jnp.int32) << (i % 32))
    copies = [
        pltpu.make_async_copy(cells_ref.at[0, rows_ref[i]], held_ref.at[i], sems.at[i])
        for i in range(PICK)
    ]
    for copy in copies:
        copy.start()

    offset = offset_ref[...]
    slot = lax.broadcasted_iota(jnp.int32, offset.shape, 0) * offset.shape[1]
    slot = slot + lax.broadcasted_iota(jnp.int32, offset.shape, 1)
    live = slot < counts_ref[0]
    source = source_ref[...]
    bits = jnp.where(source < 32, late[0], late[1])
    is_late = lax.shift_right_logical(bits, source & 31) & 1
    inside = live & (offset >= 0) & (offset < chan_rows)
    kinds = (live & (offset >= chan_rows), live & (offset < 0), inside, inside & (is_late == 0))
    lane = lax.broadcasted_iota(jnp.int32, offset.shape, 1)
    notes = jnp.zeros(offset.shape, jnp.int32)
    totals = [jnp.sum(jnp.where(kind, 1.0, 0.0)).astype(jnp.int32) for kind in kinds]
    totals = (totals[0], totals[1], totals[2] - jnp.minimum(totals[3], first_rows))
    for index, total in enumerate(totals):
        notes = jnp.where(lane == 2 * index, total >> 5, notes)
        notes = jnp.where(lane == 2 * index + 1, total & 31, notes)
    shifted = offset + band
    source = jnp.where(live, source + 1, 0)

    def coded(upper, lower):
        both = jnp.concatenate([upper.astype(jnp.float32), lower.astype(jnp.float32)], axis=0)
        return both.astype(jnp.bfloat16)

    out_ref[0, :, pl.ds(bins, EXTRA)] = coded(source, shifted >> 4)
    out_ref[1, :, pl.ds(bins, EXTRA)] = coded((shifted & 15) + 16 * is_late, notes)

    for copy in copies:
        copy.wait()
    real = held_ref[:, 0, :].astype(jnp.float32)
    imag = held_ref[:, 1, :].astype(jnp.float32)
    width = min(256, bins)

    def stacked(values):
        return jnp.concatenate([values[:, i : i + width] for i in range(0, bins, width)], axis=0)

    real, imag = whitened_pair(stacked(real), stacked(imag))
    for index in range(bins // width):
        lanes = pl.ds(index * width, width)
        out_ref[0, :, lanes] = real[index * PICK : (index + 1) * PICK]
        out_ref[1, :, lanes] = imag[index * PICK : (index + 1) * PICK]


def pick_rows(turns, counts, source_ids, pair_source, pair_offset, spectra, first_rows):
    _, chan_rows, parts, bins = spectra.shape
    smem = pl.BlockSpec(memory_space=pltpu.SMEM)
    vmem = pl.BlockSpec(memory_space=pltpu.VMEM)
    return pl.pallas_call(
        functools.partial(pick_kernel, chan_rows, chan_rows // 2, first_rows),
        out_shape=jax.ShapeDtypeStruct((parts, PICK, bins + EXTRA), spectra.dtype),
        in_specs=[smem, smem, smem, vmem, vmem, pl.BlockSpec(memory_space=pltpu.HBM)],
        out_specs=vmem,
        scratch_shapes=[
            pltpu.SMEM((PICK + 1,), jnp.int32),
            pltpu.VMEM((PICK, parts, bins), spectra.dtype),
            pltpu.SemaphoreType.DMA((PICK,)),
        ],
        cost_estimate=light(),
        compiler_params=params(8),
        name="pick_rows",
    )(
        turns, counts, source_ids, pair_source.reshape(-1, EXTRA), pair_offset.reshape(-1, EXTRA), spectra
    )


def block_mean(power):
    width = power.shape[1]
    row_group = lax.broadcasted_iota(jnp.int32, (width, width), 0) // WBLOCK
    col_group = lax.broadcasted_iota(jnp.int32, (width, width), 1) // WBLOCK
    spread = jnp.where(row_group == col_group, 1.0 / WBLOCK, 0.0).astype(jnp.bfloat16)
    high = power.astype(jnp.bfloat16)
    low = (power - high.astype(jnp.float32)).astype(jnp.bfloat16)
    total = jnp.dot(low, spread, preferred_element_type=jnp.float32)
    return total + jnp.dot(high, spread, preferred_element_type=jnp.float32)


def whitened_pair(real, imag):
    inverse = lax.rsqrt(block_mean(real * real + imag * imag) + 1e-06)
    return (real * inverse).astype(jnp.bfloat16), (imag * inverse).astype(jnp.bfloat16)


def whiten_kernel(cells_ref, after_ref, out_ref, token_ref):
    token_ref[...] = jnp.zeros_like(token_ref)
    for start in range(0, cells_ref.shape[2], 256):
        lanes = pl.ds(start, 256)
        real = cells_ref[0, :, lanes].astype(jnp.float32)
        imag = cells_ref[1, :, lanes].astype(jnp.float32)
        out_ref[0, :, lanes], out_ref[1, :, lanes] = whitened_pair(real, imag)


def whiten_rows(cells, after):
    _, rows, bins = cells.shape
    spec = pl.BlockSpec((2, rows, BINS_STEP), lambda i: (0, 0, i))
    return pl.pallas_call(
        whiten_kernel,
        grid=(bins // BINS_STEP,),
        out_shape=(jax.ShapeDtypeStruct(cells.shape, jnp.bfloat16), TOKEN),
        in_specs=[spec, pl.BlockSpec(memory_space=pl.ANY)],
        out_specs=(spec, whole(TOKEN.shape)),
        cost_estimate=light(),
        compiler_params=params(12),
        name="whiten_rows",
    )(cells, after)


def table_kernel(scale, all_bins, after_ref, cos_ref, sin_ref, token_ref, coarse_ref, fine_ref):
    token_ref[...] = jnp.zeros_like(token_ref)
    step = pl.program_id(0)
    groups = cos_ref.shape[0] // TABLE_ROWS

    @pl.when(step == 0)
    def _():
        def circle(ref, stride, factor):
            shape = ref.shape[1:]
            bins = lax.broadcasted_iota(jnp.int32, shape, 0) * stride
            lags = lax.broadcasted_iota(jnp.int32, shape, 1)
            lags = jnp.where(lags == 0, HALF, lags)
            theta = ((bins * lags) & (2 * all_bins - 1)).astype(jnp.float32) * (math.pi / all_bins)
            ref[0] = jnp.cos(theta) * factor
            ref[1] = jnp.sin(theta) * factor

        circle(coarse_ref, TABLE_ROWS, scale)
        circle(fine_ref, 1, 1.0)

    cos_b = fine_ref[0]
    sin_b = fine_ref[1]
    first = lax.broadcasted_iota(jnp.int32, cos_b.shape, 1) == 0
    for group in range(groups):
        cos_a = coarse_ref[0, pl.ds(step * groups + group, 1), :]
        sin_a = coarse_ref[1, pl.ds(step * groups + group, 1), :]
        rows = pl.ds(group * TABLE_ROWS, TABLE_ROWS)
        cos = jnp.where(first, scale, cos_a * cos_b - sin_a * sin_b)
        cos_ref[rows, :] = cos.astype(jnp.bfloat16)
        sin_ref[rows, :] = (sin_a * cos_b + cos_a * sin_b).astype(jnp.bfloat16)


def lag_tables(bins, scale, after):
    spec = pl.BlockSpec((BINS_STEP, HALF), lambda i: (i, 0))
    shape = jax.ShapeDtypeStruct((bins, HALF), jnp.bfloat16)
    return pl.pallas_call(
        functools.partial(table_kernel, scale, bins),
        grid=(bins // BINS_STEP,),
        out_shape=(shape, shape, TOKEN),
        in_specs=[pl.BlockSpec(memory_space=pl.ANY)],
        out_specs=(spec, spec, whole(TOKEN.shape)),
        scratch_shapes=[
            pltpu.VMEM((2, bins // TABLE_ROWS, HALF), jnp.float32),
            pltpu.VMEM((2, TABLE_ROWS, HALF), jnp.float32),
        ],
        cost_estimate=light(),
        compiler_params=params(12),
        name="lag_tables",
    )(after)


def source_spots(chan_rows, chan_size, me, turn, ids_row):
    count = ids_row.shape[1]
    shift = chan_rows.bit_length() - 1
    ids_row = jnp.broadcast_to(ids_row, (count, count))
    rows = lax.broadcasted_iota(jnp.int32, (count, count), 0)
    columns = lax.broadcasted_iota(jnp.int32, (count, count), 1)
    ids = jnp.sum(jnp.where(rows == columns, ids_row, 0).astype(jnp.float32), axis=1, keepdims=True)
    owner = jnp.broadcast_to(ids.astype(jnp.int32) >> shift, (count, count))
    earlier = (owner == (ids_row >> shift)) & (columns < rows)
    rank = jnp.sum(jnp.where(earlier, 1.0, 0.0), axis=1, keepdims=True)
    turns = (jnp.max(rank).astype(jnp.int32) + PICK) // PICK
    rank = rank.astype(jnp.int32) - turn * PICK
    owner = owner[:, 0:1]

    hop = ring_hop(me, owner, chan_size)
    return jnp.where((rank >= 0) & (rank < PICK), hop * PICK + rank, -1), turns


def flat(value):
    return jnp.concatenate([value[i : i + 1, :] for i in range(8)], axis=1)


def unlisted(halves, band):
    upper, lower = [half.astype(jnp.int32) for half in halves]
    return upper[0:8] - 1, upper[8:16] * 16 + (lower[0:8] & 15) - band, lower[0:8] >> 4


def ranked(taken):
    marks = jnp.concatenate([jnp.where(mask, 1.0, 0.0) for mask in taken], axis=0)
    rows = marks.shape[0]
    earlier = lax.broadcasted_iota(jnp.int32, (EXTRA, EXTRA), 0) < lax.broadcasted_iota(
        jnp.int32, (EXTRA, EXTRA), 1
    )
    rank = jnp.dot(
        marks.astype(jnp.bfloat16),
        jnp.where(earlier, 1.0, 0.0).astype(jnp.bfloat16),
        preferred_element_type=jnp.float32,
    )
    sums = jnp.broadcast_to(jnp.sum(marks, axis=1, keepdims=True), marks.shape)
    row = lax.broadcasted_iota(jnp.int32, (rows, rows), 0)
    column = lax.broadcasted_iota(jnp.int32, (rows, rows), 1)
    above_it = ((row >> 3) == (column >> 3)) & (column < row)
    rank = rank + jnp.dot(
        jnp.where(above_it, 1.0, 0.0).astype(jnp.bfloat16),
        sums.astype(jnp.bfloat16),
        preferred_element_type=jnp.float32,
    )
    rank = rank.astype(jnp.int32)
    return [rank[8 * i : 8 * i + 8] for i in range(len(taken))]


def jobs_of(spots, source, receiver, position, count):
    source, receiver, position = flat(source), flat(receiver), flat(position)
    slots = source.shape[1]
    names = lax.broadcasted_iota(jnp.int32, (spots.shape[0], slots), 0)
    field_row = lax.broadcasted_iota(jnp.int32, (8, slots), 0)
    spot = jnp.where(names == source, spots + 1, 0).astype(jnp.float32)
    spot = jnp.sum(spot, axis=0, keepdims=True).astype(jnp.int32) - 1
    fields = jnp.where(field_row == 0, spot >> 4, jnp.where(field_row == 1, spot & (PICK - 1), 0))
    fields = jnp.where(field_row == 2, receiver, jnp.where(field_row == 3, 1, fields))
    fields = jnp.where((position >= 0) & (spot >= 0), fields, 0)
    wanted = lax.broadcasted_iota(jnp.int32, (count, slots), 0)
    chosen = jnp.where(wanted == position, 1.0, 0.0).astype(jnp.bfloat16)
    return lax.dot_general(
        chosen,
        fields.astype(jnp.float32).astype(jnp.bfloat16),
        (((1,), (1,)), ((), ())),
        preferred_element_type=jnp.float32,
    )


def write_picks(jobs, start, src_ref, rec_ref):
    count = jobs.shape[0]
    jobs = jobs.astype(jnp.int32)
    busy = jobs[:, 3:4] > 0
    part = pl.ds(start, count)
    column = jnp.where(busy, jobs[:, 0:1] * PICK + jobs[:, 1:2], -1)
    lane = lax.broadcasted_iota(jnp.int32, (count, src_ref.shape[1]), 1)
    src_ref[part, :] = jnp.where(column == lane, 1.0, 0.0).astype(jnp.bfloat16)
    column = jnp.where(busy, jobs[:, 2:3], -1)
    lane = lax.broadcasted_iota(jnp.int32, (count, rec_ref.shape[1]), 1)
    rec_ref[part, :] = jnp.where(column == lane, 1.0, 0.0).astype(jnp.bfloat16)


def early_kernel(chan_rows, chan_size, turns_ref, ids_ref, after_ref, own_ref, src_ref, rec_ref, token_ref):
    token_ref[...] = jnp.zeros_like(token_ref)
    me = lax.axis_index("chan")
    count = src_ref.shape[0]
    lanes = pl.ds(own_ref.shape[2] - EXTRA, EXTRA)
    spots, _ = source_spots(chan_rows, chan_size, me, turns_ref[0], ids_ref[...])
    halves = [own_ref[half, :, lanes].astype(jnp.float32) for half in range(2)]
    source, offset, late = unlisted(halves, chan_rows // 2)
    early = (source >= 0) & (offset >= 0) & (offset < chan_rows) & (late == 0)
    (rank,) = ranked((early,))
    rank = jnp.where(early & (rank < count) & (turns_ref[1] == 0), rank, -1)
    write_picks(jobs_of(spots, source, offset, rank, count), 0, src_ref, rec_ref)


def prepare_early(turns, source_ids, own, chan_rows, chan_size, count, after):
    vmem = pl.BlockSpec(memory_space=pltpu.VMEM)
    return pl.pallas_call(
        functools.partial(early_kernel, chan_rows, chan_size),
        out_shape=(
            jax.ShapeDtypeStruct((count, chan_size * PICK), jnp.bfloat16),
            jax.ShapeDtypeStruct((count, chan_rows), jnp.bfloat16),
            TOKEN,
        ),
        in_specs=[
            pl.BlockSpec(memory_space=pltpu.SMEM), vmem, pl.BlockSpec(memory_space=pl.ANY), vmem,
        ],
        out_specs=(vmem, vmem, vmem),
        cost_estimate=light(),
        compiler_params=params(12),
        name="prepare_early",
    )(turns, source_ids.reshape(1, -1), after, own)


def prepare_kernel(chan_rows, chan_size, window, turns_ref, ids_ref, after_ref, passed_ref, *refs):
    chunk_refs = refs[:chan_size]
    src_ref, rec_ref, place_ref, needed_ref, _, token_ref = refs[chan_size:]
    token_ref[...] = jnp.zeros_like(token_ref)
    me = lax.axis_index("chan")
    turn = turns_ref[1]
    slots = place_ref.shape[1]
    room = 2 * window
    spots, needed = source_spots(chan_rows, chan_size, me, turns_ref[0], ids_ref[...])
    needed_ref[0] = needed

    lanes = pl.ds(chunk_refs[0].shape[2] - EXTRA, EXTRA)
    left_hop = jnp.where(me > 0, ring_hop(me, me - 1, chan_size), -1)
    right_hop = jnp.where(me < chan_size - 1, ring_hop(me, me + 1, chan_size), -1)
    listed = []
    for wanted in (left_hop, right_hop, 0):
        halves = []
        for half in range(2):
            value = jnp.zeros((PICK, EXTRA), jnp.float32)
            for hop, ref in enumerate(chunk_refs):
                value = jnp.where(wanted == hop, ref[half, :, lanes].astype(jnp.float32), value)
            halves.append(value)
        listed.append(unlisted(halves, chan_rows // 2))
    (left_src, left_off, _), (right_src, right_off, _), (own_src, own_off, own_late) = listed
    inside = (own_src >= 0) & (own_off >= 0) & (own_off < chan_rows)
    early = inside & (own_late == 0)
    taken = (
        (left_src >= 0) & (left_off >= chan_rows),
        (right_src >= 0) & (right_off < 0),
        (own_src >= 0) & (own_off < 0),
        (own_src >= 0) & (own_off >= chan_rows),
        inside,
        early,
    )
    ranks = ranked(taken)
    left_total = jnp.sum(jnp.where(taken[0], 1.0, 0.0)).astype(jnp.int32)
    right_total = jnp.sum(jnp.where(taken[1], 1.0, 0.0)).astype(jnp.int32)

    def done_before(amount, index):
        return jnp.minimum(amount, index * window)

    left_before = done_before(left_total, turn)
    right_before = done_before(right_total, turn)
    left_now = done_before(left_total, turn + 1) - left_before
    right_now = done_before(right_total, turn + 1) - right_before

    def in_window(index):
        shifted = ranks[index] - turn * window
        return shifted, taken[index] & (shifted >= 0) & (shifted < window)

    left_rank, left_ok = in_window(0)
    right_rank, right_ok = in_window(1)
    below_rank, below_ok = in_window(2)
    above_rank, above_ok = in_window(3)

    first = early & (ranks[5] < slots - room)
    own_rank = ranks[4] - jnp.minimum(ranks[5], slots - room)
    own_rank = own_rank - (turn * room - left_before - right_before)
    own_ok = inside & ~first & (own_rank >= 0) & (own_rank < room - left_now - right_now)
    own_pos = own_rank + left_now
    own_pos = jnp.where(own_pos < window, own_pos, own_pos + right_now)
    own_pos = jnp.where(own_ok, own_pos, -1)
    place = jnp.where(first & (turn == 0), ranks[5] + room, own_pos)
    place = jnp.where(below_ok, below_rank + slots, place)
    place = jnp.where(above_ok, above_rank + slots + window, place)
    place_ref[...] = jnp.broadcast_to(flat(place), place_ref.shape)

    left_jobs = jobs_of(spots, left_src, left_off - chan_rows, jnp.where(left_ok, left_rank, -1), window)
    right_jobs = jobs_of(
        spots, right_src, right_off + chan_rows, jnp.where(right_ok, right_rank, -1), window
    )
    own_jobs = jobs_of(spots, own_src, own_off, own_pos, room)
    write_picks(left_jobs + own_jobs[0:window], 0, src_ref, rec_ref)
    write_picks(right_jobs + own_jobs[window:room], window, src_ref, rec_ref)


def prepare(turns, source_ids, chunks, slots, chan_rows, window, after, passed):
    chan_size = len(chunks)
    vmem = pl.BlockSpec(memory_space=pltpu.VMEM)
    smem = pl.BlockSpec(memory_space=pltpu.SMEM)
    return pl.pallas_call(
        functools.partial(prepare_kernel, chan_rows, chan_size, window),
        out_shape=(
            jax.ShapeDtypeStruct((2 * window, chan_size * PICK), jnp.bfloat16),
            jax.ShapeDtypeStruct((2 * window, chan_rows), jnp.bfloat16),
            jax.ShapeDtypeStruct((8, slots), jnp.int32),
            jax.ShapeDtypeStruct((1,), jnp.int32),
            jax.ShapeDtypeStruct(passed.shape, passed.dtype),
            TOKEN,
        ),
        in_specs=[smem, vmem] + [pl.BlockSpec(memory_space=pl.ANY)] * 2 + [vmem] * len(chunks),
        out_specs=(vmem, vmem, vmem, smem, pl.BlockSpec(memory_space=pl.ANY), vmem),
        input_output_aliases={3: 4},
        cost_estimate=light(),
        compiler_params=params(16),
        name="prepare",
    )(turns, source_ids.reshape(1, -1), after, passed, *chunks)


def turns_kernel(chan_size, window, source_turns_ref, *refs):
    chunk_refs = refs[:chan_size]
    left_ref, pairs_ref = refs[-2:]
    me = lax.axis_index("chan")
    steps = chan_size // 2
    place = ring_place(me, chan_size)
    block = lax.broadcasted_iota(jnp.int32, (chan_size, EXTRA), 0)
    notes = jnp.zeros((chan_size, EXTRA), jnp.float32)
    for hop, ref in enumerate(chunk_refs):
        spot = place - hop if hop <= steps else place + hop - steps
        spot = jnp.where(spot < 0, spot + chan_size, spot)
        spot = jnp.where(spot >= chan_size, spot - chan_size, spot)
        owner = ring_block(spot, chan_size)
        notes = jnp.where(block == owner, ref[0][8:9, :].astype(jnp.float32), notes)
    lane = lax.broadcasted_iota(jnp.int32, notes.shape, 1)

    def total(index):
        value = jnp.where(lane == 2 * index, 32.0 * notes, 0.0)
        value = value + jnp.where(lane == 2 * index + 1, notes, 0.0)
        return jnp.broadcast_to(jnp.sum(value, axis=1, keepdims=True), notes.shape)

    left = jnp.where(block == 0, 0.0, pltpu.roll(total(0), 1, 0))
    right = jnp.where(block == chan_size - 1, 0.0, pltpu.roll(total(1), chan_size - 1, 0))
    aside = jnp.max(jnp.maximum(left, right)).astype(jnp.int32)
    whole_sum = jnp.max(left + right + total(2)).astype(jnp.int32)
    room = 2 * window
    needed = jnp.maximum((aside + window - 1) // window, (whole_sum + room - 1) // room)
    needed = jnp.maximum(needed, 1)
    pairs_ref[0] = needed
    left_ref[0] = needed * source_turns_ref[0] - 1


def count_turns(source_turns, chunks, window, after):
    _, _, width = chunks[0].shape
    last = width // EXTRA - 1
    specs = [pl.BlockSpec((1, PICK, EXTRA), lambda i: (1, 0, last)) for _ in chunks]
    return pl.pallas_call(
        functools.partial(turns_kernel, len(chunks), window),
        grid=(1,),
        out_shape=[jax.ShapeDtypeStruct((1,), jnp.int32)] * 2,
        in_specs=[pl.BlockSpec(memory_space=pltpu.SMEM), *specs]
        + [pl.BlockSpec(memory_space=pl.ANY)] * len(after),
        out_specs=[pl.BlockSpec(memory_space=pltpu.SMEM)] * 2,
        cost_estimate=light(),
        compiler_params=params(8),
        name="count_turns",
    )(source_turns, *chunks, *after)


def transform_kernel(shards, scale, start, chunks, src_ref, rec_ref, *refs):
    chunk_refs = refs[:chunks]
    cells_ref, cos_ref, sin_ref = refs[chunks : chunks + 3]
    keep_ref, send_ref, token_ref = refs[-3:]
    token_ref[...] = jnp.zeros_like(token_ref)
    rows = keep_ref.shape[1]
    bins = cos_ref.shape[0]
    step = min(BINS_STEP, bins)
    eighth = lax.broadcasted_iota(jnp.int32, (1, 128), 1) & 7
    root = math.sqrt(0.5)
    edge = jnp.where((eighth == 1) | (eighth == 7), root, 0.0)
    edge = jnp.where((eighth == 3) | (eighth == 5), -root, edge)
    edge = jnp.where(eighth == 0, 1.0, jnp.where(eighth == 4, -1.0, edge)) * scale
    edge = edge.astype(jnp.bfloat16).astype(jnp.float32)

    by_src = src_ref[pl.ds(start, rows), :]
    by_rec = rec_ref[pl.ds(start, rows), :]
    even = odd = corner = None
    for first in range(0, bins, step):
        lanes = pl.ds(first, step)
        source_real = jnp.concatenate([ref[0, :, lanes] for ref in chunk_refs], axis=0)
        source_imag = jnp.concatenate([ref[1, :, lanes] for ref in chunk_refs], axis=0)
        sr = jnp.dot(by_src, source_real, preferred_element_type=jnp.float32)
        si = jnp.dot(by_src, source_imag, preferred_element_type=jnp.float32)
        rr = jnp.dot(by_rec, cells_ref[0, :, lanes], preferred_element_type=jnp.float32)
        ri = jnp.dot(by_rec, cells_ref[1, :, lanes], preferred_element_type=jnp.float32)
        real = (sr * rr + si * ri).astype(jnp.bfloat16)
        imag = (si * rr - sr * ri).astype(jnp.bfloat16)
        more_even = jnp.dot(real, cos_ref[lanes, :], preferred_element_type=jnp.float32)
        more_odd = jnp.dot(imag, sin_ref[lanes, :], preferred_element_type=jnp.float32)
        wide = real.astype(jnp.float32)
        sums = wide[:, 0:128]
        for lane in range(128, step, 128):
            sums = sums + wide[:, lane : lane + 128]
        even = more_even if even is None else even + more_even
        odd = more_odd if odd is None else odd + more_odd
        corner = sums if corner is None else corner + sums

    me = lax.axis_index("seg")
    width = LAGS // shards
    corner = jnp.sum(corner * edge, axis=1, keepdims=True)
    first = lax.broadcasted_iota(jnp.int32, even.shape, 1) == 0
    later = even - jnp.where(first, 0.0, odd)
    sooner = jnp.where(first, corner, even) + odd
    sooner = pltpu.roll(sooner, HALF - 1, 1)
    for shard in range(shards):
        half = shards // 2
        if shard < half:
            lane = (half - 1 - shard) * width
            value = sooner[:, lane : lane + width]
        else:
            lane = (shard - half) * width
            value = later[:, lane : lane + width]
        place = me ^ shard

        @pl.when((place & 1) == 0)
        def _():
            keep_ref[place >> 1] = value

        @pl.when((place & 1) == 1)
        def _():
            send_ref[place >> 1] = value.astype(jnp.bfloat16)


def transform(picks, chunks, cells, tables, shards, scale, start, rows, weight, *after):
    width = LAGS // shards
    shape = (shards // 2, rows, width)
    vmem = pl.BlockSpec(memory_space=pltpu.VMEM)
    return pl.pallas_call(
        functools.partial(transform_kernel, shards, scale, start, len(chunks)),
        out_shape=(
            jax.ShapeDtypeStruct(shape, jnp.float32),
            jax.ShapeDtypeStruct(shape, jnp.bfloat16),
            TOKEN,
        ),
        in_specs=[vmem] * (5 + len(chunks))
        + [pl.BlockSpec(memory_space=pl.ANY)] * len(after),
        out_specs=(vmem, vmem, vmem),
        cost_estimate=weight,
        compiler_params=params(16),
        name="transform",
    )(*picks, *chunks, cells, *tables, *after)


def swap(send, bit):
    size = lax.axis_size("seg")
    return lax.ppermute(send, "seg", [(i, i ^ bit) for i in range(size)])


def halve(keep, got):
    total = keep + got.astype(jnp.float32)
    return total[0::2], total[1::2].astype(jnp.bfloat16)


def reduce_further(keep, got, bit):
    while keep.shape[0] > 1:
        keep, send = halve(keep, got)
        bit *= 2
        got = swap(send, bit)
    return (keep[0] + got[0].astype(jnp.float32)).astype(jnp.bfloat16)


def place_kernel(start, further, place_ref, *refs):
    parts, (out_ref, made_ref, sems) = refs[:-3], refs[-3:]
    width, slots = made_ref.shape
    flip = lax.axis_index("seg") < lax.axis_size("seg") // 2
    rows = lax.broadcasted_iota(jnp.int32, (width, width), 0)
    columns = lax.broadcasted_iota(jnp.int32, (width, width), 1)
    wanted = jnp.where(flip, width - 1 - rows, rows)
    turned = jnp.where(wanted == columns, 1.0, 0.0).astype(jnp.bfloat16)
    across = [
        lax.dot_general(
            turned, ref[...], (((1,), (1,)), ((), ())), preferred_element_type=jnp.float32
        ).astype(jnp.bfloat16)
        for ref in parts[further:]
    ]
    step = min(256, slots)
    copies = []
    for index in range(slots // step):
        lanes = pl.ds(index * step, step)
        first = start
        total = parts[0][:, lanes] if further else None
        for part in across:
            count = part.shape[1]
            spot = lax.broadcasted_iota(jnp.int32, (count, step), 0) + first
            chosen = jnp.where(spot == place_ref[0:1, lanes], 1.0, 0.0).astype(jnp.bfloat16)
            more = jnp.dot(part, chosen, preferred_element_type=jnp.float32)
            total = more if total is None else total + more
            first += count
        if further:
            made_ref[:, lanes] = total
            copy = pltpu.make_async_copy(made_ref.at[:, lanes], out_ref.at[:, lanes], sems.at[index])
            copy.start()
            copies.append(copy)
        else:
            out_ref[:, lanes] = total
    for copy in copies:
        copy.wait()


def place_rows(place, parts, start, total=None):
    width = parts[0].shape[1]
    slots = place.shape[1]
    further = total is not None
    given = [total, *parts] if further else list(parts)
    vmem = pl.BlockSpec(memory_space=pltpu.VMEM)
    return pl.pallas_call(
        functools.partial(place_kernel, start, further),
        out_shape=jax.ShapeDtypeStruct((width, slots), jnp.float32),
        in_specs=[vmem] * (1 + len(given)),
        out_specs=pl.BlockSpec(memory_space=pltpu.HBM) if further else vmem,
        scratch_shapes=[
            pltpu.VMEM((width, slots), jnp.float32),
            pltpu.SemaphoreType.DMA((slots // min(256, slots),)),
        ],
        cost_estimate=light(),
        compiler_params=params(16),
        name="place_rows",
    )(place, *given)


def per_device(spectra, source_ids, pair_source, pair_offset, pair_counts):
    chan_rows = spectra.shape[1]
    bins = spectra.shape[3]
    seg_size = lax.axis_size("seg")
    chan_size = lax.axis_size("chan")
    slots = pair_source.shape[0]
    window = 3 * slots // 8
    scale = 1.0 / math.sqrt(bins * seg_size)
    join = lax.optimization_barrier

    ring = list(range(0, chan_size, 2)) + list(range(1, chan_size, 2))[::-1]
    ahead = [(ring[i], ring[(i + 1) % chan_size]) for i in range(chan_size)]
    back = [(b, a) for a, b in ahead]
    leftward = [(i + 1, i) for i in range(chan_size - 1)]
    rightward = [(i, i + 1) for i in range(chan_size - 1)]

    def one_turn(turns):
        first_rows = slots - 2 * window
        own = pick_rows(turns, pair_counts, source_ids, pair_source, pair_offset, spectra, first_rows)
        forward, backward = [own], [own]
        steps = chan_size // 2

        def step_beside(work=None):
            ahead_of = forward[-1], backward[-1]
            forward.append(lax.ppermute(ahead_of[0], "chan", ahead))
            if len(backward) < chan_size - steps:
                backward.append(lax.ppermute(ahead_of[1], "chan", back))
            if work is not None:
                *results, token = work()
                if len(backward) == len(forward):
                    token, forward[-1], backward[-1] = join((token, forward[-1], backward[-1]))
                else:
                    token, forward[-1] = join((token, forward[-1]))
                return results, token

        tables, token = step_beside(lambda: lag_tables(bins, scale, own))
        cells = jnp.transpose(spectra[0], (1, 0, 2))
        (whitened,), token = step_beside(lambda: whiten_rows(cells, token))
        for _ in range(3, steps - 1):
            step_beside()
        picks, token = step_beside(
            lambda: prepare_early(turns, source_ids, own, chan_rows, chan_size, first_rows, token)
        )

        def piece(picks, chunks, start, rows, *after, weight=light()):
            return transform(
                picks, chunks, whitened, tables, seg_size, scale, start, rows, weight, *after
            )

        chunks = [*forward, own, *backward[1:]]
        full = pl.CostEstimate(
            flops=first_rows * bins * 4096, bytes_accessed=16 * bins * HALF, transcendentals=0
        )
        (keep_own, send), token = step_beside(
            lambda: piece(picks, chunks, 0, first_rows, token, weight=full)
        )
        chunks = forward + backward[1:]
        *picks, place, source_turns, send, token = prepare(
            turns, source_ids, chunks, slots, chan_rows, window, token, send
        )
        got_own = swap(send, 1)
        keep_left, send, token = piece(picks, chunks, 0, window, token)
        token, got_own = join((token, got_own))
        keep_own, send_own = halve(keep_own, got_own)
        got_left = swap(send, 1)
        got_own = swap(send_own, 2)
        keep_right, send, token = piece(picks, chunks, window, window, token, send_own)
        token, got_left, got_own = join((token, got_left, got_own))
        got_right = swap(send, 1)
        left = reduce_further(keep_left, got_left, 1)
        right = reduce_further(keep_right, got_right, 1)
        own = reduce_further(keep_own, got_own, 2)
        from_right = lax.ppermute(left, "chan", leftward)
        from_left = lax.ppermute(right, "chan", rightward)
        total = place_rows(place, (left, right, own), 0)
        result = place_rows(place, (from_left, from_right), slots, total)
        return result, (right, token), chunks, source_turns

    first, after, chunks, source_turns = one_turn(jnp.zeros((2,), jnp.int32))
    turns_left, pair_turns = [count[0] for count in count_turns(source_turns, chunks, window, after)]

    def further(state):
        turn, total = state
        turns = jnp.stack([lax.div(turn, pair_turns), lax.rem(turn, pair_turns)])
        return turn - 1, total + one_turn(turns)[0]

    return lax.while_loop(lambda state: state[0] > 0, further, (turns_left, first))[1]


def solution(mesh):
    in_specs = (P("seg", "chan", None, None), P(), P("chan"), P("chan"), P("chan"))
    out_specs = P("seg", "chan")
    return jax.shard_map(
        per_device, mesh=mesh, in_specs=in_specs, out_specs=out_specs, check_vma=False
    )
```

```python
import functools
import math

import jax
import jax.numpy as jnp
from jax import lax
from jax.experimental import pallas as pl
from jax.experimental.pallas import tpu as pltpu
from jax.sharding import PartitionSpec as P

LAGS = 1024
HALF = LAGS // 2
WBLOCK = 64
PICK = 16
BINS_STEP = 512
TABLE_ROWS = 64
EXTRA = 128


def params(mebibytes):
    return pltpu.CompilerParams(vmem_limit_bytes=mebibytes * 1024 * 1024)


def light():
    return pl.CostEstimate(flops=1024, bytes_accessed=1024, transcendentals=0)


TOKEN = jax.ShapeDtypeStruct((8, 128), jnp.float32)


def whole(shape):
    return pl.BlockSpec(shape, lambda *_: (0,) * len(shape))


def ring_place(block, chan_size):
    return jnp.where((block & 1) == 0, block >> 1, chan_size - 1 - (block >> 1))


def ring_block(place, chan_size):
    return jnp.where(place < chan_size // 2, 2 * place, 2 * (chan_size - place) - 1)


def far_block(me, chan_size):
    place = ring_place(me, chan_size) - chan_size // 2
    return ring_block(jnp.where(place < 0, place + chan_size, place), chan_size)


def ring_hop(me, block, chan_size):
    steps = chan_size // 2
    distance = ring_place(me, chan_size) - ring_place(block, chan_size)
    distance = jnp.where(distance < 0, distance + chan_size, distance)
    return jnp.where(distance <= steps, distance, steps + chan_size - distance)


def pick_kernel(chan_rows, band, first_rows, *refs):
    counts_ref, ids_ref, source_ref, offset_ref, cells_ref, out_ref, rows_ref, held_ref, sems = refs[-9:]
    first = lax.axis_index("chan") * chan_rows
    turn = refs[0][0] if len(refs) > 9 else 0
    bins = cells_ref.shape[3]
    for i in range(PICK):
        rows_ref[i] = 0
    rank = jnp.int32(0)
    for i in range(ids_ref.shape[0]):
        row = ids_ref[i] - first
        mine = (row >= 0) & (row < chan_rows)
        spot = rank - turn * PICK
        rows_ref[jnp.where(mine & (spot >= 0) & (spot < PICK), spot, PICK)] = row
        rank = rank + mine.astype(jnp.int32)
    far = far_block(lax.axis_index("chan"), lax.axis_size("chan")) * chan_rows
    late = [jnp.int32(0), jnp.int32(0)]
    for i in range(ids_ref.shape[0]):
        row = ids_ref[i] - far
        late[i // 32] = late[i // 32] | (((row >= 0) & (row < chan_rows)).astype(jnp.int32) << (i % 32))
    copies = [
        pltpu.make_async_copy(cells_ref.at[0, rows_ref[i]], held_ref.at[i], sems.at[i])
        for i in range(PICK)
    ]
    for copy in copies:
        copy.start()

    offset = offset_ref[...]
    slot = lax.broadcasted_iota(jnp.int32, offset.shape, 0) * offset.shape[1]
    slot = slot + lax.broadcasted_iota(jnp.int32, offset.shape, 1)
    live = slot < counts_ref[...]
    source = source_ref[...]
    bits = jnp.where(source < 32, late[0], late[1])
    is_late = lax.shift_right_logical(bits, source & 31) & 1
    inside = live & (offset >= 0) & (offset < chan_rows)
    kinds = (live & (offset >= chan_rows), live & (offset < 0), inside, inside & (is_late == 0))
    lane = lax.broadcasted_iota(jnp.int32, offset.shape, 1)
    notes = jnp.zeros(offset.shape, jnp.int32)
    totals = [jnp.sum(jnp.where(kind, 1.0, 0.0)).astype(jnp.int32) for kind in kinds]
    totals = (totals[0], totals[1], totals[2] - jnp.minimum(totals[3], first_rows))
    for index, total in enumerate(totals):
        notes = jnp.where(lane == 2 * index, total >> 5, notes)
        notes = jnp.where(lane == 2 * index + 1, total & 31, notes)
    shifted = offset + band
    source = jnp.where(live, source + 1, 0)

    def coded(upper, lower):
        both = jnp.concatenate([upper.astype(jnp.float32), lower.astype(jnp.float32)], axis=0)
        return both.astype(jnp.bfloat16)

    out_ref[0, :, pl.ds(bins, EXTRA)] = coded(source, shifted >> 4)
    out_ref[1, :, pl.ds(bins, EXTRA)] = coded((shifted & 15) + 16 * is_late, notes)

    for copy in copies:
        copy.wait()
    real = held_ref[:, 0, :].astype(jnp.float32)
    imag = held_ref[:, 1, :].astype(jnp.float32)
    width = min(256, bins)

    def stacked(values):
        return jnp.concatenate([values[:, i : i + width] for i in range(0, bins, width)], axis=0)

    real, imag = whitened_pair(stacked(real), stacked(imag))
    for index in range(bins // width):
        lanes = pl.ds(index * width, width)
        out_ref[0, :, lanes] = real[index * PICK : (index + 1) * PICK]
        out_ref[1, :, lanes] = imag[index * PICK : (index + 1) * PICK]


def pick_rows(turns, counts, source_ids, pair_source, pair_offset, spectra, first_rows):
    _, chan_rows, parts, bins = spectra.shape
    smem = pl.BlockSpec(memory_space=pltpu.SMEM)
    vmem = pl.BlockSpec(memory_space=pltpu.VMEM)
    given = [] if turns is None else [turns]
    return pl.pallas_call(
        functools.partial(pick_kernel, chan_rows, chan_rows // 2, first_rows),
        out_shape=jax.ShapeDtypeStruct((parts, PICK, bins + EXTRA), spectra.dtype),
        in_specs=[smem] * len(given) + [vmem, smem, vmem, vmem, pl.BlockSpec(memory_space=pl.ANY)],
        out_specs=vmem,
        scratch_shapes=[
            pltpu.SMEM((PICK + 1,), jnp.int32),
            pltpu.VMEM((PICK, parts, bins), spectra.dtype),
            pltpu.SemaphoreType.DMA((PICK,)),
        ],
        cost_estimate=light(),
        compiler_params=params(8),
        name="pick_rows",
    )(
        *given,
        counts.reshape(1, 1),
        source_ids,
        pair_source.reshape(-1, EXTRA),
        pair_offset.reshape(-1, EXTRA),
        spectra,
    )


def block_mean(power):
    width = power.shape[1]
    row_group = lax.broadcasted_iota(jnp.int32, (width, width), 0) // WBLOCK
    col_group = lax.broadcasted_iota(jnp.int32, (width, width), 1) // WBLOCK
    spread = jnp.where(row_group == col_group, 1.0 / WBLOCK, 0.0).astype(jnp.bfloat16)
    high = power.astype(jnp.bfloat16)
    low = (power - high.astype(jnp.float32)).astype(jnp.bfloat16)
    total = jnp.dot(low, spread, preferred_element_type=jnp.float32)
    return total + jnp.dot(high, spread, preferred_element_type=jnp.float32)


def whitened_pair(real, imag):
    inverse = lax.rsqrt(block_mean(real * real + imag * imag) + 1e-06)
    return (real * inverse).astype(jnp.bfloat16), (imag * inverse).astype(jnp.bfloat16)


def whiten_kernel(cells_ref, after_ref, out_ref, token_ref):
    token_ref[...] = jnp.zeros_like(token_ref)
    for start in range(0, cells_ref.shape[2], 256):
        lanes = pl.ds(start, 256)
        real = cells_ref[0, :, lanes].astype(jnp.float32)
        imag = cells_ref[1, :, lanes].astype(jnp.float32)
        out_ref[0, :, lanes], out_ref[1, :, lanes] = whitened_pair(real, imag)


def whiten_rows(cells, after):
    _, rows, bins = cells.shape
    spec = pl.BlockSpec((2, rows, BINS_STEP), lambda i: (0, 0, i))
    return pl.pallas_call(
        whiten_kernel,
        grid=(bins // BINS_STEP,),
        out_shape=(jax.ShapeDtypeStruct(cells.shape, jnp.bfloat16), TOKEN),
        in_specs=[spec, pl.BlockSpec(memory_space=pl.ANY)],
        out_specs=(spec, whole(TOKEN.shape)),
        cost_estimate=light(),
        compiler_params=params(12),
        name="whiten_rows",
    )(cells, after)


def table_kernel(scale, all_bins, after_ref, cos_ref, sin_ref, token_ref, coarse_ref, fine_ref):
    token_ref[...] = jnp.zeros_like(token_ref)
    step = pl.program_id(0)
    groups = cos_ref.shape[0] // TABLE_ROWS

    @pl.when(step == 0)
    def _():
        def circle(ref, stride, factor):
            shape = ref.shape[1:]
            bins = lax.broadcasted_iota(jnp.int32, shape, 0) * stride
            lags = lax.broadcasted_iota(jnp.int32, shape, 1)
            lags = jnp.where(lags == 0, HALF, lags)
            theta = ((bins * lags) & (2 * all_bins - 1)).astype(jnp.float32) * (math.pi / all_bins)
            ref[0] = jnp.cos(theta) * factor
            ref[1] = jnp.sin(theta) * factor

        circle(coarse_ref, TABLE_ROWS, scale)
        circle(fine_ref, 1, 1.0)

    cos_b = fine_ref[0]
    sin_b = fine_ref[1]
    first = lax.broadcasted_iota(jnp.int32, cos_b.shape, 1) == 0
    for group in range(groups):
        cos_a = coarse_ref[0, pl.ds(step * groups + group, 1), :]
        sin_a = coarse_ref[1, pl.ds(step * groups + group, 1), :]
        rows = pl.ds(group * TABLE_ROWS, TABLE_ROWS)
        cos = jnp.where(first, scale, cos_a * cos_b - sin_a * sin_b)
        cos_ref[rows, :] = cos.astype(jnp.bfloat16)
        sin_ref[rows, :] = (sin_a * cos_b + cos_a * sin_b).astype(jnp.bfloat16)


def lag_tables(bins, scale, after):
    spec = pl.BlockSpec((BINS_STEP, HALF), lambda i: (i, 0))
    shape = jax.ShapeDtypeStruct((bins, HALF), jnp.bfloat16)
    return pl.pallas_call(
        functools.partial(table_kernel, scale, bins),
        grid=(bins // BINS_STEP,),
        out_shape=(shape, shape, TOKEN),
        in_specs=[pl.BlockSpec(memory_space=pl.ANY)],
        out_specs=(spec, spec, whole(TOKEN.shape)),
        scratch_shapes=[
            pltpu.VMEM((2, bins // TABLE_ROWS, HALF), jnp.float32),
            pltpu.VMEM((2, TABLE_ROWS, HALF), jnp.float32),
        ],
        cost_estimate=light(),
        compiler_params=params(12),
        name="lag_tables",
    )(after)


def source_spots(chan_rows, chan_size, me, turn, ids_row):
    count = ids_row.shape[1]
    shift = chan_rows.bit_length() - 1
    ids_row = jnp.broadcast_to(ids_row, (count, count))
    rows = lax.broadcasted_iota(jnp.int32, (count, count), 0)
    columns = lax.broadcasted_iota(jnp.int32, (count, count), 1)
    ids = jnp.sum(jnp.where(rows == columns, ids_row, 0).astype(jnp.float32), axis=1, keepdims=True)
    owner = jnp.broadcast_to(ids.astype(jnp.int32) >> shift, (count, count))
    earlier = (owner == (ids_row >> shift)) & (columns < rows)
    rank = jnp.sum(jnp.where(earlier, 1.0, 0.0), axis=1, keepdims=True)
    turns = (jnp.max(rank).astype(jnp.int32) + PICK) // PICK
    rank = rank.astype(jnp.int32) - turn * PICK
    owner = owner[:, 0:1]

    hop = ring_hop(me, owner, chan_size)
    return jnp.where((rank >= 0) & (rank < PICK), hop * PICK + rank, -1), turns


def flat(value):
    return jnp.concatenate([value[i : i + 1, :] for i in range(8)], axis=1)


def unlisted(halves, band):
    upper, lower = [half.astype(jnp.int32) for half in halves]
    return upper[0:8] - 1, upper[8:16] * 16 + (lower[0:8] & 15) - band, lower[0:8] >> 4


def ranked(taken):
    marks = jnp.concatenate([jnp.where(mask, 1.0, 0.0) for mask in taken], axis=0)
    rows = marks.shape[0]
    earlier = lax.broadcasted_iota(jnp.int32, (EXTRA, EXTRA), 0) < lax.broadcasted_iota(
        jnp.int32, (EXTRA, EXTRA), 1
    )
    rank = jnp.dot(
        marks.astype(jnp.bfloat16),
        jnp.where(earlier, 1.0, 0.0).astype(jnp.bfloat16),
        preferred_element_type=jnp.float32,
    )
    sums = jnp.broadcast_to(jnp.sum(marks, axis=1, keepdims=True), marks.shape)
    row = lax.broadcasted_iota(jnp.int32, (rows, rows), 0)
    column = lax.broadcasted_iota(jnp.int32, (rows, rows), 1)
    above_it = ((row >> 3) == (column >> 3)) & (column < row)
    rank = rank + jnp.dot(
        jnp.where(above_it, 1.0, 0.0).astype(jnp.bfloat16),
        sums.astype(jnp.bfloat16),
        preferred_element_type=jnp.float32,
    )
    rank = rank.astype(jnp.int32)
    return [rank[8 * i : 8 * i + 8] for i in range(len(taken))]


def jobs_of(spots, source, receiver, position, count):
    source, receiver, position = flat(source), flat(receiver), flat(position)
    slots = source.shape[1]
    names = lax.broadcasted_iota(jnp.int32, (spots.shape[0], slots), 0)
    field_row = lax.broadcasted_iota(jnp.int32, (8, slots), 0)
    spot = jnp.where(names == source, spots + 1, 0).astype(jnp.float32)
    spot = jnp.sum(spot, axis=0, keepdims=True).astype(jnp.int32) - 1
    fields = jnp.where(field_row == 0, spot >> 4, jnp.where(field_row == 1, spot & (PICK - 1), 0))
    fields = jnp.where(field_row == 2, receiver, jnp.where(field_row == 3, 1, fields))
    fields = jnp.where((position >= 0) & (spot >= 0), fields, 0)
    wanted = lax.broadcasted_iota(jnp.int32, (count, slots), 0)
    chosen = jnp.where(wanted == position, 1.0, 0.0).astype(jnp.bfloat16)
    return lax.dot_general(
        chosen,
        fields.astype(jnp.float32).astype(jnp.bfloat16),
        (((1,), (1,)), ((), ())),
        preferred_element_type=jnp.float32,
    )


def write_picks(jobs, start, src_ref, rec_ref):
    count = jobs.shape[0]
    jobs = jobs.astype(jnp.int32)
    busy = jobs[:, 3:4] > 0
    part = pl.ds(start, count)
    column = jnp.where(busy, jobs[:, 0:1] * PICK + jobs[:, 1:2], -1)
    lane = lax.broadcasted_iota(jnp.int32, (count, src_ref.shape[1]), 1)
    src_ref[part, :] = jnp.where(column == lane, 1.0, 0.0).astype(jnp.bfloat16)
    column = jnp.where(busy, jobs[:, 2:3], -1)
    lane = lax.broadcasted_iota(jnp.int32, (count, rec_ref.shape[1]), 1)
    rec_ref[part, :] = jnp.where(column == lane, 1.0, 0.0).astype(jnp.bfloat16)


def early_kernel(chan_rows, chan_size, turns_ref, ids_ref, after_ref, own_ref, src_ref, rec_ref, token_ref):
    token_ref[...] = jnp.zeros_like(token_ref)
    me = lax.axis_index("chan")
    count = src_ref.shape[0]
    lanes = pl.ds(own_ref.shape[2] - EXTRA, EXTRA)
    spots, _ = source_spots(chan_rows, chan_size, me, turns_ref[0], ids_ref[...])
    halves = [own_ref[half, :, lanes].astype(jnp.float32) for half in range(2)]
    source, offset, late = unlisted(halves, chan_rows // 2)
    early = (source >= 0) & (offset >= 0) & (offset < chan_rows) & (late == 0)
    (rank,) = ranked((early,))
    rank = jnp.where(early & (rank < count) & (turns_ref[1] == 0), rank, -1)
    write_picks(jobs_of(spots, source, offset, rank, count), 0, src_ref, rec_ref)


def prepare_early(turns, source_ids, own, chan_rows, chan_size, count, after):
    vmem = pl.BlockSpec(memory_space=pltpu.VMEM)
    return pl.pallas_call(
        functools.partial(early_kernel, chan_rows, chan_size),
        out_shape=(
            jax.ShapeDtypeStruct((count, chan_size * PICK), jnp.bfloat16),
            jax.ShapeDtypeStruct((count, chan_rows), jnp.bfloat16),
            TOKEN,
        ),
        in_specs=[
            pl.BlockSpec(memory_space=pltpu.SMEM), vmem, pl.BlockSpec(memory_space=pl.ANY), vmem,
        ],
        out_specs=(vmem, vmem, vmem),
        cost_estimate=light(),
        compiler_params=params(12),
        name="prepare_early",
    )(turns, source_ids.reshape(1, -1), after, own)


def prepare_kernel(chan_rows, chan_size, window, turns_ref, ids_ref, after_ref, passed_ref, *refs):
    chunk_refs = refs[:chan_size]
    src_ref, rec_ref, place_ref, needed_ref, _, token_ref = refs[chan_size:]
    token_ref[...] = jnp.zeros_like(token_ref)
    me = lax.axis_index("chan")
    turn = turns_ref[1]
    slots = place_ref.shape[1]
    room = 2 * window
    spots, needed = source_spots(chan_rows, chan_size, me, turns_ref[0], ids_ref[...])
    needed_ref[0] = needed

    lanes = pl.ds(chunk_refs[0].shape[2] - EXTRA, EXTRA)
    left_hop = jnp.where(me > 0, ring_hop(me, me - 1, chan_size), -1)
    right_hop = jnp.where(me < chan_size - 1, ring_hop(me, me + 1, chan_size), -1)
    listed = []
    for wanted in (left_hop, right_hop, 0):
        halves = []
        for half in range(2):
            value = jnp.zeros((PICK, EXTRA), jnp.float32)
            for hop, ref in enumerate(chunk_refs):
                value = jnp.where(wanted == hop, ref[half, :, lanes].astype(jnp.float32), value)
            halves.append(value)
        listed.append(unlisted(halves, chan_rows // 2))
    (left_src, left_off, _), (right_src, right_off, _), (own_src, own_off, own_late) = listed
    inside = (own_src >= 0) & (own_off >= 0) & (own_off < chan_rows)
    early = inside & (own_late == 0)
    taken = (
        (left_src >= 0) & (left_off >= chan_rows),
        (right_src >= 0) & (right_off < 0),
        (own_src >= 0) & (own_off < 0),
        (own_src >= 0) & (own_off >= chan_rows),
        inside,
        early,
    )
    ranks = ranked(taken)
    left_total = jnp.sum(jnp.where(taken[0], 1.0, 0.0)).astype(jnp.int32)
    right_total = jnp.sum(jnp.where(taken[1], 1.0, 0.0)).astype(jnp.int32)

    def done_before(amount, index):
        return jnp.minimum(amount, index * window)

    left_before = done_before(left_total, turn)
    right_before = done_before(right_total, turn)
    left_now = done_before(left_total, turn + 1) - left_before
    right_now = done_before(right_total, turn + 1) - right_before

    def in_window(index):
        shifted = ranks[index] - turn * window
        return shifted, taken[index] & (shifted >= 0) & (shifted < window)

    left_rank, left_ok = in_window(0)
    right_rank, right_ok = in_window(1)
    below_rank, below_ok = in_window(2)
    above_rank, above_ok = in_window(3)

    first = early & (ranks[5] < slots - room)
    own_rank = ranks[4] - jnp.minimum(ranks[5], slots - room)
    own_rank = own_rank - (turn * room - left_before - right_before)
    own_ok = inside & ~first & (own_rank >= 0) & (own_rank < room - left_now - right_now)
    own_pos = own_rank + left_now
    own_pos = jnp.where(own_pos < window, own_pos, own_pos + right_now)
    own_pos = jnp.where(own_ok, own_pos, -1)
    place = jnp.where(first & (turn == 0), ranks[5] + room, own_pos)
    place = jnp.where(below_ok, below_rank + slots, place)
    place = jnp.where(above_ok, above_rank + slots + window, place)
    place_ref[...] = jnp.broadcast_to(flat(place), place_ref.shape)

    left_jobs = jobs_of(spots, left_src, left_off - chan_rows, jnp.where(left_ok, left_rank, -1), window)
    right_jobs = jobs_of(
        spots, right_src, right_off + chan_rows, jnp.where(right_ok, right_rank, -1), window
    )
    own_jobs = jobs_of(spots, own_src, own_off, own_pos, room)
    write_picks(left_jobs + own_jobs[0:window], 0, src_ref, rec_ref)
    write_picks(right_jobs + own_jobs[window:room], window, src_ref, rec_ref)


def prepare(turns, source_ids, chunks, slots, chan_rows, window, after, passed):
    chan_size = len(chunks)
    vmem = pl.BlockSpec(memory_space=pltpu.VMEM)
    smem = pl.BlockSpec(memory_space=pltpu.SMEM)
    return pl.pallas_call(
        functools.partial(prepare_kernel, chan_rows, chan_size, window),
        out_shape=(
            jax.ShapeDtypeStruct((2 * window, chan_size * PICK), jnp.bfloat16),
            jax.ShapeDtypeStruct((2 * window, chan_rows), jnp.bfloat16),
            jax.ShapeDtypeStruct((8, slots), jnp.int32),
            jax.ShapeDtypeStruct((1,), jnp.int32),
            jax.ShapeDtypeStruct(passed.shape, passed.dtype),
            TOKEN,
        ),
        in_specs=[smem, vmem] + [pl.BlockSpec(memory_space=pl.ANY)] * 2 + [vmem] * len(chunks),
        out_specs=(vmem, vmem, vmem, smem, pl.BlockSpec(memory_space=pl.ANY), vmem),
        input_output_aliases={3: 4},
        cost_estimate=light(),
        compiler_params=params(16),
        name="prepare",
    )(turns, source_ids.reshape(1, -1), after, passed, *chunks)


def turns_kernel(chan_size, window, source_turns_ref, *refs):
    chunk_refs = refs[:chan_size]
    left_ref, pairs_ref = refs[-2:]
    me = lax.axis_index("chan")
    steps = chan_size // 2
    place = ring_place(me, chan_size)
    block = lax.broadcasted_iota(jnp.int32, (chan_size, EXTRA), 0)
    notes = jnp.zeros((chan_size, EXTRA), jnp.float32)
    for hop, ref in enumerate(chunk_refs):
        spot = place - hop if hop <= steps else place + hop - steps
        spot = jnp.where(spot < 0, spot + chan_size, spot)
        spot = jnp.where(spot >= chan_size, spot - chan_size, spot)
        owner = ring_block(spot, chan_size)
        notes = jnp.where(block == owner, ref[0][8:9, :].astype(jnp.float32), notes)
    lane = lax.broadcasted_iota(jnp.int32, notes.shape, 1)

    def total(index):
        value = jnp.where(lane == 2 * index, 32.0 * notes, 0.0)
        value = value + jnp.where(lane == 2 * index + 1, notes, 0.0)
        return jnp.broadcast_to(jnp.sum(value, axis=1, keepdims=True), notes.shape)

    left = jnp.where(block == 0, 0.0, pltpu.roll(total(0), 1, 0))
    right = jnp.where(block == chan_size - 1, 0.0, pltpu.roll(total(1), chan_size - 1, 0))
    aside = jnp.max(jnp.maximum(left, right)).astype(jnp.int32)
    whole_sum = jnp.max(left + right + total(2)).astype(jnp.int32)
    room = 2 * window
    needed = jnp.maximum((aside + window - 1) // window, (whole_sum + room - 1) // room)
    needed = jnp.maximum(needed, 1)
    pairs_ref[0] = needed
    left_ref[0] = needed * source_turns_ref[0] - 1


def count_turns(source_turns, chunks, window, after):
    _, _, width = chunks[0].shape
    last = width // EXTRA - 1
    specs = [pl.BlockSpec((1, PICK, EXTRA), lambda i: (1, 0, last)) for _ in chunks]
    return pl.pallas_call(
        functools.partial(turns_kernel, len(chunks), window),
        grid=(1,),
        out_shape=[jax.ShapeDtypeStruct((1,), jnp.int32)] * 2,
        in_specs=[pl.BlockSpec(memory_space=pltpu.SMEM), *specs]
        + [pl.BlockSpec(memory_space=pl.ANY)] * len(after),
        out_specs=[pl.BlockSpec(memory_space=pltpu.SMEM)] * 2,
        cost_estimate=light(),
        compiler_params=params(8),
        name="count_turns",
    )(source_turns, *chunks, *after)


def transform_kernel(shards, scale, start, chunks, src_ref, rec_ref, *refs):
    chunk_refs = refs[:chunks]
    cells_ref, cos_ref, sin_ref = refs[chunks : chunks + 3]
    keep_ref, send_ref, token_ref = refs[-3:]
    token_ref[...] = jnp.zeros_like(token_ref)
    rows = keep_ref.shape[1]
    bins = cos_ref.shape[0]
    step = min(BINS_STEP, bins)
    eighth = lax.broadcasted_iota(jnp.int32, (1, 128), 1) & 7
    root = math.sqrt(0.5)
    edge = jnp.where((eighth == 1) | (eighth == 7), root, 0.0)
    edge = jnp.where((eighth == 3) | (eighth == 5), -root, edge)
    edge = jnp.where(eighth == 0, 1.0, jnp.where(eighth == 4, -1.0, edge)) * scale
    edge = edge.astype(jnp.bfloat16).astype(jnp.float32)

    by_src = src_ref[pl.ds(start, rows), :]
    by_rec = rec_ref[pl.ds(start, rows), :]
    even = odd = corner = None
    for first in range(0, bins, step):
        lanes = pl.ds(first, step)
        source_real = jnp.concatenate([ref[0, :, lanes] for ref in chunk_refs], axis=0)
        source_imag = jnp.concatenate([ref[1, :, lanes] for ref in chunk_refs], axis=0)
        sr = jnp.dot(by_src, source_real, preferred_element_type=jnp.float32)
        si = jnp.dot(by_src, source_imag, preferred_element_type=jnp.float32)
        rr = jnp.dot(by_rec, cells_ref[0, :, lanes], preferred_element_type=jnp.float32)
        ri = jnp.dot(by_rec, cells_ref[1, :, lanes], preferred_element_type=jnp.float32)
        real = (sr * rr + si * ri).astype(jnp.bfloat16)
        imag = (si * rr - sr * ri).astype(jnp.bfloat16)
        more_even = jnp.dot(real, cos_ref[lanes, :], preferred_element_type=jnp.float32)
        more_odd = jnp.dot(imag, sin_ref[lanes, :], preferred_element_type=jnp.float32)
        wide = real.astype(jnp.float32)
        sums = wide[:, 0:128]
        for lane in range(128, step, 128):
            sums = sums + wide[:, lane : lane + 128]
        even = more_even if even is None else even + more_even
        odd = more_odd if odd is None else odd + more_odd
        corner = sums if corner is None else corner + sums

    me = lax.axis_index("seg")
    width = LAGS // shards
    corner = jnp.sum(corner * edge, axis=1, keepdims=True)
    first = lax.broadcasted_iota(jnp.int32, even.shape, 1) == 0
    later = even - jnp.where(first, 0.0, odd)
    sooner = jnp.where(first, corner, even) + odd
    sooner = pltpu.roll(sooner, HALF - 1, 1)
    for shard in range(shards):
        half = shards // 2
        if shard < half:
            lane = (half - 1 - shard) * width
            value = sooner[:, lane : lane + width]
        else:
            lane = (shard - half) * width
            value = later[:, lane : lane + width]
        place = me ^ shard

        @pl.when((place & 1) == 0)
        def _():
            keep_ref[place >> 1] = value

        @pl.when((place & 1) == 1)
        def _():
            send_ref[place >> 1] = value.astype(jnp.bfloat16)


def transform(picks, chunks, cells, tables, shards, scale, start, rows, weight, *after):
    width = LAGS // shards
    shape = (shards // 2, rows, width)
    vmem = pl.BlockSpec(memory_space=pltpu.VMEM)
    return pl.pallas_call(
        functools.partial(transform_kernel, shards, scale, start, len(chunks)),
        out_shape=(
            jax.ShapeDtypeStruct(shape, jnp.float32),
            jax.ShapeDtypeStruct(shape, jnp.bfloat16),
            TOKEN,
        ),
        in_specs=[vmem] * (5 + len(chunks))
        + [pl.BlockSpec(memory_space=pl.ANY)] * len(after),
        out_specs=(vmem, vmem, vmem),
        cost_estimate=weight,
        compiler_params=params(16),
        name="transform",
    )(*picks, *chunks, cells, *tables, *after)


def swap(send, bit):
    size = lax.axis_size("seg")
    return lax.ppermute(send, "seg", [(i, i ^ bit) for i in range(size)])


def halve(keep, got):
    total = keep + got.astype(jnp.float32)
    return total[0::2], total[1::2].astype(jnp.bfloat16)


def reduce_further(keep, got, bit):
    while keep.shape[0] > 1:
        keep, send = halve(keep, got)
        bit *= 2
        got = swap(send, bit)
    return (keep[0] + got[0].astype(jnp.float32)).astype(jnp.bfloat16)


def place_kernel(start, further, place_ref, *refs):
    parts, (out_ref, made_ref, sems) = refs[:-3], refs[-3:]
    width, slots = made_ref.shape
    flip = lax.axis_index("seg") < lax.axis_size("seg") // 2
    rows = lax.broadcasted_iota(jnp.int32, (width, width), 0)
    columns = lax.broadcasted_iota(jnp.int32, (width, width), 1)
    wanted = jnp.where(flip, width - 1 - rows, rows)
    turned = jnp.where(wanted == columns, 1.0, 0.0).astype(jnp.bfloat16)
    across = [
        lax.dot_general(
            turned, ref[...], (((1,), (1,)), ((), ())), preferred_element_type=jnp.float32
        ).astype(jnp.bfloat16)
        for ref in parts[further:]
    ]
    step = min(256, slots)
    copies = []
    for index in range(slots // step):
        lanes = pl.ds(index * step, step)
        first = start
        total = parts[0][:, lanes] if further else None
        for part in across:
            count = part.shape[1]
            spot = lax.broadcasted_iota(jnp.int32, (count, step), 0) + first
            chosen = jnp.where(spot == place_ref[0:1, lanes], 1.0, 0.0).astype(jnp.bfloat16)
            more = jnp.dot(part, chosen, preferred_element_type=jnp.float32)
            total = more if total is None else total + more
            first += count
        if further:
            made_ref[:, lanes] = total
            copy = pltpu.make_async_copy(made_ref.at[:, lanes], out_ref.at[:, lanes], sems.at[index])
            copy.start()
            copies.append(copy)
        else:
            out_ref[:, lanes] = total
    for copy in copies:
        copy.wait()


def place_rows(place, parts, start, total=None):
    width = parts[0].shape[1]
    slots = place.shape[1]
    further = total is not None
    given = [total, *parts] if further else list(parts)
    vmem = pl.BlockSpec(memory_space=pltpu.VMEM)
    return pl.pallas_call(
        functools.partial(place_kernel, start, further),
        out_shape=jax.ShapeDtypeStruct((width, slots), jnp.float32),
        in_specs=[vmem] * (1 + len(given)),
        out_specs=pl.BlockSpec(memory_space=pltpu.HBM) if further else vmem,
        scratch_shapes=[
            pltpu.VMEM((width, slots), jnp.float32),
            pltpu.SemaphoreType.DMA((slots // min(256, slots),)),
        ],
        cost_estimate=light(),
        compiler_params=params(16),
        name="place_rows",
    )(place, *given)


def per_device(spectra, source_ids, pair_source, pair_offset, pair_counts):
    chan_rows = spectra.shape[1]
    bins = spectra.shape[3]
    seg_size = lax.axis_size("seg")
    chan_size = lax.axis_size("chan")
    slots = pair_source.shape[0]
    window = 3 * slots // 8
    scale = 1.0 / math.sqrt(bins * seg_size)
    join = lax.optimization_barrier

    ring = list(range(0, chan_size, 2)) + list(range(1, chan_size, 2))[::-1]
    ahead = [(ring[i], ring[(i + 1) % chan_size]) for i in range(chan_size)]
    back = [(b, a) for a, b in ahead]
    leftward = [(i + 1, i) for i in range(chan_size - 1)]
    rightward = [(i, i + 1) for i in range(chan_size - 1)]

    def one_turn(turns):
        first_rows = slots - 2 * window
        own = pick_rows(turns, pair_counts, source_ids, pair_source, pair_offset, spectra, first_rows)
        if turns is None:
            turns = jnp.zeros((2,), jnp.int32)
        forward, backward = [own], [own]
        steps = chan_size // 2

        def step_beside(work=None):
            ahead_of = forward[-1], backward[-1]
            forward.append(lax.ppermute(ahead_of[0], "chan", ahead))
            if len(backward) < chan_size - steps:
                backward.append(lax.ppermute(ahead_of[1], "chan", back))
            if work is not None:
                *results, token = work()
                if len(backward) == len(forward):
                    token, forward[-1], backward[-1] = join((token, forward[-1], backward[-1]))
                else:
                    token, forward[-1] = join((token, forward[-1]))
                return results, token

        tables, token = step_beside(lambda: lag_tables(bins, scale, own))
        cells = jnp.transpose(spectra[0], (1, 0, 2))
        (whitened,), token = step_beside(lambda: whiten_rows(cells, token))
        for _ in range(3, steps - 1):
            step_beside()
        picks, token = step_beside(
            lambda: prepare_early(turns, source_ids, own, chan_rows, chan_size, first_rows, token)
        )

        def piece(picks, chunks, start, rows, *after, weight=light()):
            return transform(
                picks, chunks, whitened, tables, seg_size, scale, start, rows, weight, *after
            )

        chunks = [*forward, own, *backward[1:]]
        full = pl.CostEstimate(
            flops=first_rows * bins * 4096, bytes_accessed=16 * bins * HALF, transcendentals=0
        )
        (keep_own, send), token = step_beside(
            lambda: piece(picks, chunks, 0, first_rows, token, weight=full)
        )
        chunks = forward + backward[1:]
        *picks, place, source_turns, send, token = prepare(
            turns, source_ids, chunks, slots, chan_rows, window, token, send
        )
        got_own = swap(send, 1)
        keep_left, send, token = piece(picks, chunks, 0, window, token)
        token, got_own = join((token, got_own))
        keep_own, send_own = halve(keep_own, got_own)
        got_left = swap(send, 1)
        got_own = swap(send_own, 2)
        keep_right, send, token = piece(picks, chunks, window, window, token, send_own)
        token, got_left, got_own = join((token, got_left, got_own))
        got_right = swap(send, 1)
        left = reduce_further(keep_left, got_left, 1)
        right = reduce_further(keep_right, got_right, 1)
        own = reduce_further(keep_own, got_own, 2)
        from_right = lax.ppermute(left, "chan", leftward)
        from_left = lax.ppermute(right, "chan", rightward)
        total = place_rows(place, (left, right, own), 0)
        result = place_rows(place, (from_left, from_right), slots, total)
        return result, (right, token), chunks, source_turns

    first, after, chunks, source_turns = one_turn(None)
    turns_left, pair_turns = [count[0] for count in count_turns(source_turns, chunks, window, after)]

    def further(state):
        turn, total = state
        turns = jnp.stack([lax.div(turn, pair_turns), lax.rem(turn, pair_turns)])
        return turn - 1, total + one_turn(turns)[0]

    return lax.while_loop(lambda state: state[0] > 0, further, (turns_left, first))[1]


def solution(mesh):
    in_specs = (P("seg", "chan", None, None), P(), P("chan"), P("chan"), P("chan"))
    out_specs = P("seg", "chan")
    return jax.shard_map(
        per_device, mesh=mesh, in_specs=in_specs, out_specs=out_specs, check_vma=False
    )
```

```python
import functools
import math

import jax
import jax.numpy as jnp
from jax import lax
from jax.experimental import pallas as pl
from jax.experimental.pallas import tpu as pltpu
from jax.sharding import PartitionSpec as P

LAGS = 1024
HALF = LAGS // 2
WBLOCK = 64
PICK = 16
BINS_STEP = 512
TABLE_ROWS = 64
EXTRA = 128


def params(mebibytes):
    return pltpu.CompilerParams(vmem_limit_bytes=mebibytes * 1024 * 1024)


def light():
    return pl.CostEstimate(flops=1024, bytes_accessed=1024, transcendentals=0)


TOKEN = jax.ShapeDtypeStruct((8, 128), jnp.float32)


def whole(shape):
    return pl.BlockSpec(shape, lambda *_: (0,) * len(shape))


def ring_place(block, chan_size):
    return jnp.where((block & 1) == 0, block >> 1, chan_size - 1 - (block >> 1))


def ring_block(place, chan_size):
    return jnp.where(place < chan_size // 2, 2 * place, 2 * (chan_size - place) - 1)


def far_block(me, chan_size):
    place = ring_place(me, chan_size) - chan_size // 2
    return ring_block(jnp.where(place < 0, place + chan_size, place), chan_size)


def ring_hop(me, block, chan_size):
    steps = chan_size // 2
    distance = ring_place(me, chan_size) - ring_place(block, chan_size)
    distance = jnp.where(distance < 0, distance + chan_size, distance)
    return jnp.where(distance <= steps, distance, steps + chan_size - distance)


def pick_kernel(chan_rows, band, first_rows, *refs):
    counts_ref, ids_ref, source_ref, offset_ref, cells_ref, out_ref, rows_ref, held_ref, sems = refs[-9:]
    first = lax.axis_index("chan") * chan_rows
    turn = refs[0][0] if len(refs) > 9 else 0
    bins = cells_ref.shape[3]
    for i in range(PICK):
        rows_ref[i] = 0
    rank = jnp.int32(0)
    for i in range(ids_ref.shape[0]):
        row = ids_ref[i] - first
        mine = (row >= 0) & (row < chan_rows)
        spot = rank - turn * PICK
        rows_ref[jnp.where(mine & (spot >= 0) & (spot < PICK), spot, PICK)] = row
        rank = rank + mine.astype(jnp.int32)
    far = far_block(lax.axis_index("chan"), lax.axis_size("chan")) * chan_rows
    late = [jnp.int32(0), jnp.int32(0)]
    for i in range(ids_ref.shape[0]):
        row = ids_ref[i] - far
        late[i // 32] = late[i // 32] | (((row >= 0) & (row < chan_rows)).astype(jnp.int32) << (i % 32))
    copies = [
        pltpu.make_async_copy(cells_ref.at[0, rows_ref[i]], held_ref.at[i], sems.at[i])
        for i in range(PICK)
    ]
    for copy in copies:
        copy.start()

    offset = offset_ref[...]
    slot = lax.broadcasted_iota(jnp.int32, offset.shape, 0) * offset.shape[1]
    slot = slot + lax.broadcasted_iota(jnp.int32, offset.shape, 1)
    live = slot < counts_ref[...]
    source = source_ref[...]
    bits = jnp.where(source < 32, late[0], late[1])
    is_late = lax.shift_right_logical(bits, source & 31) & 1
    inside = live & (offset >= 0) & (offset < chan_rows)
    kinds = (live & (offset >= chan_rows), live & (offset < 0), inside, inside & (is_late == 0))
    lane = lax.broadcasted_iota(jnp.int32, offset.shape, 1)
    notes = jnp.zeros(offset.shape, jnp.int32)
    totals = [jnp.sum(jnp.where(kind, 1.0, 0.0)).astype(jnp.int32) for kind in kinds]
    totals = (totals[0], totals[1], totals[2] - jnp.minimum(totals[3], first_rows))
    for index, total in enumerate(totals):
        notes = jnp.where(lane == 2 * index, total >> 5, notes)
        notes = jnp.where(lane == 2 * index + 1, total & 31, notes)
    shifted = offset + band
    source = jnp.where(live, source + 1, 0)

    def coded(upper, lower):
        both = jnp.concatenate([upper.astype(jnp.float32), lower.astype(jnp.float32)], axis=0)
        return both.astype(jnp.bfloat16)

    out_ref[0, :, pl.ds(bins, EXTRA)] = coded(source, shifted >> 4)
    out_ref[1, :, pl.ds(bins, EXTRA)] = coded((shifted & 15) + 16 * is_late, notes)

    for copy in copies:
        copy.wait()
    real = held_ref[:, 0, :].astype(jnp.float32)
    imag = held_ref[:, 1, :].astype(jnp.float32)
    width = min(256, bins)

    def stacked(values):
        return jnp.concatenate([values[:, i : i + width] for i in range(0, bins, width)], axis=0)

    real, imag = whitened_pair(stacked(real), stacked(imag))
    for index in range(bins // width):
        lanes = pl.ds(index * width, width)
        out_ref[0, :, lanes] = real[index * PICK : (index + 1) * PICK]
        out_ref[1, :, lanes] = imag[index * PICK : (index + 1) * PICK]


def pick_rows(turns, counts, source_ids, pair_source, pair_offset, spectra, first_rows):
    _, chan_rows, parts, bins = spectra.shape
    smem = pl.BlockSpec(memory_space=pltpu.SMEM)
    vmem = pl.BlockSpec(memory_space=pltpu.VMEM)
    given = [] if turns is None else [turns]
    return pl.pallas_call(
        functools.partial(pick_kernel, chan_rows, chan_rows // 2, first_rows),
        out_shape=jax.ShapeDtypeStruct((parts, PICK, bins + EXTRA), spectra.dtype),
        in_specs=[smem] * len(given) + [vmem, smem, vmem, vmem, pl.BlockSpec(memory_space=pl.ANY)],
        out_specs=vmem,
        scratch_shapes=[
            pltpu.SMEM((PICK + 1,), jnp.int32),
            pltpu.VMEM((PICK, parts, bins), spectra.dtype),
            pltpu.SemaphoreType.DMA((PICK,)),
        ],
        cost_estimate=light(),
        compiler_params=params(8),
        name="pick_rows",
    )(
        *given,
        counts.reshape(1, 1),
        source_ids,
        pair_source.reshape(-1, EXTRA),
        pair_offset.reshape(-1, EXTRA),
        spectra,
    )


def block_mean(power):
    width = power.shape[1]
    row_group = lax.broadcasted_iota(jnp.int32, (width, width), 0) // WBLOCK
    col_group = lax.broadcasted_iota(jnp.int32, (width, width), 1) // WBLOCK
    spread = jnp.where(row_group == col_group, 1.0 / WBLOCK, 0.0).astype(jnp.bfloat16)
    high = power.astype(jnp.bfloat16)
    low = (power - high.astype(jnp.float32)).astype(jnp.bfloat16)
    total = jnp.dot(low, spread, preferred_element_type=jnp.float32)
    return total + jnp.dot(high, spread, preferred_element_type=jnp.float32)


def whitened_pair(real, imag):
    inverse = lax.rsqrt(block_mean(real * real + imag * imag) + 1e-06)
    return (real * inverse).astype(jnp.bfloat16), (imag * inverse).astype(jnp.bfloat16)


def whiten_kernel(cells_ref, after_ref, out_ref, token_ref):
    token_ref[...] = jnp.zeros_like(token_ref)
    for start in range(0, cells_ref.shape[2], 256):
        lanes = pl.ds(start, 256)
        real = cells_ref[0, :, lanes].astype(jnp.float32)
        imag = cells_ref[1, :, lanes].astype(jnp.float32)
        out_ref[0, :, lanes], out_ref[1, :, lanes] = whitened_pair(real, imag)


def whiten_rows(cells, after):
    _, rows, bins = cells.shape
    spec = pl.BlockSpec((2, rows, BINS_STEP), lambda i: (0, 0, i))
    return pl.pallas_call(
        whiten_kernel,
        grid=(bins // BINS_STEP,),
        out_shape=(jax.ShapeDtypeStruct(cells.shape, jnp.bfloat16), TOKEN),
        in_specs=[spec, pl.BlockSpec(memory_space=pl.ANY)],
        out_specs=(spec, whole(TOKEN.shape)),
        cost_estimate=light(),
        compiler_params=params(12),
        name="whiten_rows",
    )(cells, after)


def table_kernel(scale, all_bins, after_ref, cos_ref, sin_ref, token_ref, coarse_ref, fine_ref):
    token_ref[...] = jnp.zeros_like(token_ref)
    step = pl.program_id(0)
    groups = cos_ref.shape[0] // TABLE_ROWS

    @pl.when(step == 0)
    def _():
        def circle(ref, stride, factor):
            shape = ref.shape[1:]
            bins = lax.broadcasted_iota(jnp.int32, shape, 0) * stride
            lags = lax.broadcasted_iota(jnp.int32, shape, 1)
            lags = jnp.where(lags == 0, HALF, lags)
            theta = ((bins * lags) & (2 * all_bins - 1)).astype(jnp.float32) * (math.pi / all_bins)
            ref[0] = jnp.cos(theta) * factor
            ref[1] = jnp.sin(theta) * factor

        circle(coarse_ref, TABLE_ROWS, scale)
        circle(fine_ref, 1, 1.0)

    cos_b = fine_ref[0]
    sin_b = fine_ref[1]
    first = lax.broadcasted_iota(jnp.int32, cos_b.shape, 1) == 0
    for group in range(groups):
        cos_a = coarse_ref[0, pl.ds(step * groups + group, 1), :]
        sin_a = coarse_ref[1, pl.ds(step * groups + group, 1), :]
        rows = pl.ds(group * TABLE_ROWS, TABLE_ROWS)
        cos = jnp.where(first, scale, cos_a * cos_b - sin_a * sin_b)
        cos_ref[rows, :] = cos.astype(jnp.bfloat16)
        sin_ref[rows, :] = (sin_a * cos_b + cos_a * sin_b).astype(jnp.bfloat16)


def lag_tables(bins, scale, after):
    spec = pl.BlockSpec((BINS_STEP, HALF), lambda i: (i, 0))
    shape = jax.ShapeDtypeStruct((bins, HALF), jnp.bfloat16)
    return pl.pallas_call(
        functools.partial(table_kernel, scale, bins),
        grid=(bins // BINS_STEP,),
        out_shape=(shape, shape, TOKEN),
        in_specs=[pl.BlockSpec(memory_space=pl.ANY)],
        out_specs=(spec, spec, whole(TOKEN.shape)),
        scratch_shapes=[
            pltpu.VMEM((2, bins // TABLE_ROWS, HALF), jnp.float32),
            pltpu.VMEM((2, TABLE_ROWS, HALF), jnp.float32),
        ],
        cost_estimate=light(),
        compiler_params=params(12),
        name="lag_tables",
    )(after)


def source_spots(chan_rows, chan_size, me, turn, ids_row):
    count = ids_row.shape[1]
    shift = chan_rows.bit_length() - 1
    ids_row = jnp.broadcast_to(ids_row, (count, count))
    rows = lax.broadcasted_iota(jnp.int32, (count, count), 0)
    columns = lax.broadcasted_iota(jnp.int32, (count, count), 1)
    ids = jnp.sum(jnp.where(rows == columns, ids_row, 0).astype(jnp.float32), axis=1, keepdims=True)
    owner = jnp.broadcast_to(ids.astype(jnp.int32) >> shift, (count, count))
    earlier = (owner == (ids_row >> shift)) & (columns < rows)
    rank = jnp.sum(jnp.where(earlier, 1.0, 0.0), axis=1, keepdims=True)
    turns = (jnp.max(rank).astype(jnp.int32) + PICK) // PICK
    rank = rank.astype(jnp.int32) - turn * PICK
    owner = owner[:, 0:1]

    hop = ring_hop(me, owner, chan_size)
    return jnp.where((rank >= 0) & (rank < PICK), hop * PICK + rank, -1), turns


def flat(value):
    return jnp.concatenate([value[i : i + 1, :] for i in range(8)], axis=1)


def unlisted(halves, band):
    upper, lower = [half.astype(jnp.int32) for half in halves]
    return upper[0:8] - 1, upper[8:16] * 16 + (lower[0:8] & 15) - band, lower[0:8] >> 4


def ranked(taken):
    marks = jnp.concatenate([jnp.where(mask, 1.0, 0.0) for mask in taken], axis=0)
    rows = marks.shape[0]
    earlier = lax.broadcasted_iota(jnp.int32, (EXTRA, EXTRA), 0) < lax.broadcasted_iota(
        jnp.int32, (EXTRA, EXTRA), 1
    )
    rank = jnp.dot(
        marks.astype(jnp.bfloat16),
        jnp.where(earlier, 1.0, 0.0).astype(jnp.bfloat16),
        preferred_element_type=jnp.float32,
    )
    sums = jnp.broadcast_to(jnp.sum(marks, axis=1, keepdims=True), marks.shape)
    row = lax.broadcasted_iota(jnp.int32, (rows, rows), 0)
    column = lax.broadcasted_iota(jnp.int32, (rows, rows), 1)
    above_it = ((row >> 3) == (column >> 3)) & (column < row)
    rank = rank + jnp.dot(
        jnp.where(above_it, 1.0, 0.0).astype(jnp.bfloat16),
        sums.astype(jnp.bfloat16),
        preferred_element_type=jnp.float32,
    )
    rank = rank.astype(jnp.int32)
    return [rank[8 * i : 8 * i + 8] for i in range(len(taken))]


def jobs_of(spots, source, receiver, position, count):
    source, receiver, position = flat(source), flat(receiver), flat(position)
    slots = source.shape[1]
    names = lax.broadcasted_iota(jnp.int32, (spots.shape[0], slots), 0)
    field_row = lax.broadcasted_iota(jnp.int32, (8, slots), 0)
    spot = jnp.where(names == source, spots + 1, 0).astype(jnp.float32)
    spot = jnp.sum(spot, axis=0, keepdims=True).astype(jnp.int32) - 1
    fields = jnp.where(field_row == 0, spot >> 4, jnp.where(field_row == 1, spot & (PICK - 1), 0))
    fields = jnp.where(field_row == 2, receiver, jnp.where(field_row == 3, 1, fields))
    fields = jnp.where((position >= 0) & (spot >= 0), fields, 0)
    wanted = lax.broadcasted_iota(jnp.int32, (count, slots), 0)
    chosen = jnp.where(wanted == position, 1.0, 0.0).astype(jnp.bfloat16)
    return lax.dot_general(
        chosen,
        fields.astype(jnp.float32).astype(jnp.bfloat16),
        (((1,), (1,)), ((), ())),
        preferred_element_type=jnp.float32,
    )


def write_picks(jobs, start, src_ref, rec_ref):
    count = jobs.shape[0]
    jobs = jobs.astype(jnp.int32)
    busy = jobs[:, 3:4] > 0
    part = pl.ds(start, count)
    column = jnp.where(busy, jobs[:, 0:1] * PICK + jobs[:, 1:2], -1)
    lane = lax.broadcasted_iota(jnp.int32, (count, src_ref.shape[1]), 1)
    src_ref[part, :] = jnp.where(column == lane, 1.0, 0.0).astype(jnp.bfloat16)
    column = jnp.where(busy, jobs[:, 2:3], -1)
    lane = lax.broadcasted_iota(jnp.int32, (count, rec_ref.shape[1]), 1)
    rec_ref[part, :] = jnp.where(column == lane, 1.0, 0.0).astype(jnp.bfloat16)


def early_kernel(chan_rows, chan_size, turns_ref, ids_ref, after_ref, own_ref, src_ref, rec_ref, token_ref):
    token_ref[...] = jnp.zeros_like(token_ref)
    me = lax.axis_index("chan")
    count = src_ref.shape[0]
    lanes = pl.ds(own_ref.shape[2] - EXTRA, EXTRA)
    spots, _ = source_spots(chan_rows, chan_size, me, turns_ref[0], ids_ref[...])
    halves = [own_ref[half, :, lanes].astype(jnp.float32) for half in range(2)]
    source, offset, late = unlisted(halves, chan_rows // 2)
    early = (source >= 0) & (offset >= 0) & (offset < chan_rows) & (late == 0)
    (rank,) = ranked((early,))
    rank = jnp.where(early & (rank < count) & (turns_ref[1] == 0), rank, -1)
    write_picks(jobs_of(spots, source, offset, rank, count), 0, src_ref, rec_ref)


def prepare_early(turns, source_ids, own, chan_rows, chan_size, count, after):
    vmem = pl.BlockSpec(memory_space=pltpu.VMEM)
    return pl.pallas_call(
        functools.partial(early_kernel, chan_rows, chan_size),
        out_shape=(
            jax.ShapeDtypeStruct((count, chan_size * PICK), jnp.bfloat16),
            jax.ShapeDtypeStruct((count, chan_rows), jnp.bfloat16),
            TOKEN,
        ),
        in_specs=[
            pl.BlockSpec(memory_space=pltpu.SMEM), vmem, pl.BlockSpec(memory_space=pl.ANY), vmem,
        ],
        out_specs=(vmem, vmem, vmem),
        cost_estimate=light(),
        compiler_params=params(12),
        name="prepare_early",
    )(turns, source_ids.reshape(1, -1), after, own)


def prepare_kernel(chan_rows, chan_size, window, turns_ref, ids_ref, after_ref, passed_ref, *refs):
    chunk_refs = refs[:chan_size]
    src_ref, rec_ref, place_ref, needed_ref, _, token_ref = refs[chan_size:]
    token_ref[...] = jnp.zeros_like(token_ref)
    me = lax.axis_index("chan")
    turn = turns_ref[1]
    slots = place_ref.shape[1]
    room = 2 * window
    spots, needed = source_spots(chan_rows, chan_size, me, turns_ref[0], ids_ref[...])
    needed_ref[0] = needed

    lanes = pl.ds(chunk_refs[0].shape[2] - EXTRA, EXTRA)
    left_hop = jnp.where(me > 0, ring_hop(me, me - 1, chan_size), -1)
    right_hop = jnp.where(me < chan_size - 1, ring_hop(me, me + 1, chan_size), -1)
    listed = []
    for wanted in (left_hop, right_hop, 0):
        halves = []
        for half in range(2):
            value = jnp.zeros((PICK, EXTRA), jnp.float32)
            for hop, ref in enumerate(chunk_refs):
                value = jnp.where(wanted == hop, ref[half, :, lanes].astype(jnp.float32), value)
            halves.append(value)
        listed.append(unlisted(halves, chan_rows // 2))
    (left_src, left_off, _), (right_src, right_off, _), (own_src, own_off, own_late) = listed
    inside = (own_src >= 0) & (own_off >= 0) & (own_off < chan_rows)
    early = inside & (own_late == 0)
    taken = (
        (left_src >= 0) & (left_off >= chan_rows),
        (right_src >= 0) & (right_off < 0),
        (own_src >= 0) & (own_off < 0),
        (own_src >= 0) & (own_off >= chan_rows),
        inside,
        early,
    )
    ranks = ranked(taken)
    left_total = jnp.sum(jnp.where(taken[0], 1.0, 0.0)).astype(jnp.int32)
    right_total = jnp.sum(jnp.where(taken[1], 1.0, 0.0)).astype(jnp.int32)

    def done_before(amount, index):
        return jnp.minimum(amount, index * window)

    left_before = done_before(left_total, turn)
    right_before = done_before(right_total, turn)
    left_now = done_before(left_total, turn + 1) - left_before
    right_now = done_before(right_total, turn + 1) - right_before

    def in_window(index):
        shifted = ranks[index] - turn * window
        return shifted, taken[index] & (shifted >= 0) & (shifted < window)

    left_rank, left_ok = in_window(0)
    right_rank, right_ok = in_window(1)
    below_rank, below_ok = in_window(2)
    above_rank, above_ok = in_window(3)

    first = early & (ranks[5] < slots - room)
    own_rank = ranks[4] - jnp.minimum(ranks[5], slots - room)
    own_rank = own_rank - (turn * room - left_before - right_before)
    own_ok = inside & ~first & (own_rank >= 0) & (own_rank < room - left_now - right_now)
    own_pos = own_rank + left_now
    own_pos = jnp.where(own_pos < window, own_pos, own_pos + right_now)
    own_pos = jnp.where(own_ok, own_pos, -1)
    place = jnp.where(first & (turn == 0), ranks[5] + room, own_pos)
    place = jnp.where(below_ok, below_rank + slots, place)
    place = jnp.where(above_ok, above_rank + slots + window, place)
    place_ref[...] = jnp.broadcast_to(flat(place), place_ref.shape)

    left_jobs = jobs_of(spots, left_src, left_off - chan_rows, jnp.where(left_ok, left_rank, -1), window)
    right_jobs = jobs_of(
        spots, right_src, right_off + chan_rows, jnp.where(right_ok, right_rank, -1), window
    )
    own_jobs = jobs_of(spots, own_src, own_off, own_pos, room)
    write_picks(left_jobs + own_jobs[0:window], 0, src_ref, rec_ref)
    write_picks(right_jobs + own_jobs[window:room], window, src_ref, rec_ref)


def prepare(turns, source_ids, chunks, slots, chan_rows, window, after, passed):
    chan_size = len(chunks)
    vmem = pl.BlockSpec(memory_space=pltpu.VMEM)
    smem = pl.BlockSpec(memory_space=pltpu.SMEM)
    return pl.pallas_call(
        functools.partial(prepare_kernel, chan_rows, chan_size, window),
        out_shape=(
            jax.ShapeDtypeStruct((2 * window, chan_size * PICK), jnp.bfloat16),
            jax.ShapeDtypeStruct((2 * window, chan_rows), jnp.bfloat16),
            jax.ShapeDtypeStruct((8, slots), jnp.int32),
            jax.ShapeDtypeStruct((1,), jnp.int32),
            jax.ShapeDtypeStruct(passed.shape, passed.dtype),
            TOKEN,
        ),
        in_specs=[smem, vmem] + [pl.BlockSpec(memory_space=pl.ANY)] * 2 + [vmem] * len(chunks),
        out_specs=(vmem, vmem, vmem, smem, pl.BlockSpec(memory_space=pl.ANY), vmem),
        input_output_aliases={3: 4},
        cost_estimate=light(),
        compiler_params=params(16),
        name="prepare",
    )(turns, source_ids.reshape(1, -1), after, passed, *chunks)


def turns_kernel(chan_size, window, source_turns_ref, *refs):
    chunk_refs = refs[:chan_size]
    left_ref, pairs_ref = refs[-2:]
    me = lax.axis_index("chan")
    steps = chan_size // 2
    place = ring_place(me, chan_size)
    block = lax.broadcasted_iota(jnp.int32, (chan_size, EXTRA), 0)
    notes = jnp.zeros((chan_size, EXTRA), jnp.float32)
    for hop, ref in enumerate(chunk_refs):
        spot = place - hop if hop <= steps else place + hop - steps
        spot = jnp.where(spot < 0, spot + chan_size, spot)
        spot = jnp.where(spot >= chan_size, spot - chan_size, spot)
        owner = ring_block(spot, chan_size)
        notes = jnp.where(block == owner, ref[0][8:9, :].astype(jnp.float32), notes)
    lane = lax.broadcasted_iota(jnp.int32, notes.shape, 1)

    def total(index):
        value = jnp.where(lane == 2 * index, 32.0 * notes, 0.0)
        value = value + jnp.where(lane == 2 * index + 1, notes, 0.0)
        return jnp.broadcast_to(jnp.sum(value, axis=1, keepdims=True), notes.shape)

    left = jnp.where(block == 0, 0.0, pltpu.roll(total(0), 1, 0))
    right = jnp.where(block == chan_size - 1, 0.0, pltpu.roll(total(1), chan_size - 1, 0))
    aside = jnp.max(jnp.maximum(left, right)).astype(jnp.int32)
    whole_sum = jnp.max(left + right + total(2)).astype(jnp.int32)
    room = 2 * window
    needed = jnp.maximum((aside + window - 1) // window, (whole_sum + room - 1) // room)
    needed = jnp.maximum(needed, 1)
    pairs_ref[0] = needed
    left_ref[0] = needed * source_turns_ref[0] - 1


def count_turns(source_turns, chunks, window, after):
    _, _, width = chunks[0].shape
    last = width // EXTRA - 1
    specs = [pl.BlockSpec((1, PICK, EXTRA), lambda i: (1, 0, last)) for _ in chunks]
    return pl.pallas_call(
        functools.partial(turns_kernel, len(chunks), window),
        grid=(1,),
        out_shape=[jax.ShapeDtypeStruct((1,), jnp.int32)] * 2,
        in_specs=[pl.BlockSpec(memory_space=pltpu.SMEM), *specs]
        + [pl.BlockSpec(memory_space=pl.ANY)] * len(after),
        out_specs=[pl.BlockSpec(memory_space=pltpu.SMEM)] * 2,
        cost_estimate=light(),
        compiler_params=params(8),
        name="count_turns",
    )(source_turns, *chunks, *after)


def transform_kernel(shards, scale, start, chunks, src_ref, rec_ref, *refs):
    chunk_refs = refs[:chunks]
    cells_ref, cos_ref, sin_ref = refs[chunks : chunks + 3]
    keep_ref, send_ref, token_ref = refs[-3:]
    token_ref[...] = jnp.zeros_like(token_ref)
    rows = keep_ref.shape[1]
    bins = cos_ref.shape[0]
    step = min(BINS_STEP, bins)
    eighth = lax.broadcasted_iota(jnp.int32, (1, 128), 1) & 7
    root = math.sqrt(0.5)
    edge = jnp.where((eighth == 1) | (eighth == 7), root, 0.0)
    edge = jnp.where((eighth == 3) | (eighth == 5), -root, edge)
    edge = jnp.where(eighth == 0, 1.0, jnp.where(eighth == 4, -1.0, edge)) * scale
    edge = edge.astype(jnp.bfloat16).astype(jnp.float32)

    by_src = src_ref[pl.ds(start, rows), :]
    by_rec = rec_ref[pl.ds(start, rows), :]
    even = odd = corner = None
    for first in range(0, bins, step):
        lanes = pl.ds(first, step)
        source_real = jnp.concatenate([ref[0, :, lanes] for ref in chunk_refs], axis=0)
        source_imag = jnp.concatenate([ref[1, :, lanes] for ref in chunk_refs], axis=0)
        sr = jnp.dot(by_src, source_real, preferred_element_type=jnp.float32)
        si = jnp.dot(by_src, source_imag, preferred_element_type=jnp.float32)
        rr = jnp.dot(by_rec, cells_ref[0, :, lanes], preferred_element_type=jnp.float32)
        ri = jnp.dot(by_rec, cells_ref[1, :, lanes], preferred_element_type=jnp.float32)
        real = (sr * rr + si * ri).astype(jnp.bfloat16)
        imag = (si * rr - sr * ri).astype(jnp.bfloat16)
        more_even = jnp.dot(real, cos_ref[lanes, :], preferred_element_type=jnp.float32)
        more_odd = jnp.dot(imag, sin_ref[lanes, :], preferred_element_type=jnp.float32)
        wide = real.astype(jnp.float32)
        sums = wide[:, 0:128]
        for lane in range(128, step, 128):
            sums = sums + wide[:, lane : lane + 128]
        even = more_even if even is None else even + more_even
        odd = more_odd if odd is None else odd + more_odd
        corner = sums if corner is None else corner + sums

    me = lax.axis_index("seg")
    width = LAGS // shards
    corner = jnp.sum(corner * edge, axis=1, keepdims=True)
    first = lax.broadcasted_iota(jnp.int32, even.shape, 1) == 0
    later = even - jnp.where(first, 0.0, odd)
    sooner = jnp.where(first, corner, even) + odd
    sooner = pltpu.roll(sooner, HALF - 1, 1)
    for shard in range(shards):
        half = shards // 2
        if shard < half:
            lane = (half - 1 - shard) * width
            value = sooner[:, lane : lane + width]
        else:
            lane = (shard - half) * width
            value = later[:, lane : lane + width]
        place = me ^ shard

        @pl.when((place & 1) == 0)
        def _():
            keep_ref[place >> 1] = value

        @pl.when((place & 1) == 1)
        def _():
            send_ref[place >> 1] = value.astype(jnp.bfloat16)


def transform(picks, chunks, cells, tables, shards, scale, start, rows, weight, *after):
    width = LAGS // shards
    shape = (shards // 2, rows, width)
    vmem = pl.BlockSpec(memory_space=pltpu.VMEM)
    return pl.pallas_call(
        functools.partial(transform_kernel, shards, scale, start, len(chunks)),
        out_shape=(
            jax.ShapeDtypeStruct(shape, jnp.float32),
            jax.ShapeDtypeStruct(shape, jnp.bfloat16),
            TOKEN,
        ),
        in_specs=[vmem] * (5 + len(chunks))
        + [pl.BlockSpec(memory_space=pl.ANY)] * len(after),
        out_specs=(vmem, vmem, vmem),
        cost_estimate=weight,
        compiler_params=params(16),
        name="transform",
    )(*picks, *chunks, cells, *tables, *after)


def swap(send, bit):
    size = lax.axis_size("seg")
    return lax.ppermute(send, "seg", [(i, i ^ bit) for i in range(size)])


def halve(keep, got):
    total = keep + got.astype(jnp.float32)
    return total[0::2], total[1::2].astype(jnp.bfloat16)


def reduce_further(keep, got, bit):
    while keep.shape[0] > 1:
        keep, send = halve(keep, got)
        bit *= 2
        got = swap(send, bit)
    return (keep[0] + got[0].astype(jnp.float32)).astype(jnp.bfloat16)


def place_kernel(start, further, place_ref, *refs):
    parts, (out_ref, made_ref, sems) = refs[:-3], refs[-3:]
    width, slots = made_ref.shape
    flip = lax.axis_index("seg") < lax.axis_size("seg") // 2
    rows = lax.broadcasted_iota(jnp.int32, (width, width), 0)
    columns = lax.broadcasted_iota(jnp.int32, (width, width), 1)
    wanted = jnp.where(flip, width - 1 - rows, rows)
    turned = jnp.where(wanted == columns, 1.0, 0.0).astype(jnp.bfloat16)
    across = [
        lax.dot_general(
            turned, ref[...], (((1,), (1,)), ((), ())), preferred_element_type=jnp.float32
        ).astype(jnp.bfloat16)
        for ref in parts[further:]
    ]
    step = min(256, slots)
    copies = []
    for index in range(slots // step):
        lanes = pl.ds(index * step, step)
        first = start
        total = parts[0][:, lanes] if further else None
        for part in across:
            count = part.shape[1]
            spot = lax.broadcasted_iota(jnp.int32, (count, step), 0) + first
            chosen = jnp.where(spot == place_ref[0:1, lanes], 1.0, 0.0).astype(jnp.bfloat16)
            more = jnp.dot(part, chosen, preferred_element_type=jnp.float32)
            total = more if total is None else total + more
            first += count
        if further:
            made_ref[:, lanes] = total
            copy = pltpu.make_async_copy(made_ref.at[:, lanes], out_ref.at[:, lanes], sems.at[index])
            copy.start()
            copies.append(copy)
        else:
            out_ref[:, lanes] = total
    for copy in copies:
        copy.wait()


def place_rows(place, parts, start, total=None):
    width = parts[0].shape[1]
    slots = place.shape[1]
    further = total is not None
    given = [total, *parts] if further else list(parts)
    vmem = pl.BlockSpec(memory_space=pltpu.VMEM)
    return pl.pallas_call(
        functools.partial(place_kernel, start, further),
        out_shape=jax.ShapeDtypeStruct((width, slots), jnp.float32),
        in_specs=[vmem] * (1 + len(given)),
        out_specs=pl.BlockSpec(memory_space=pltpu.HBM) if further else vmem,
        scratch_shapes=[
            pltpu.VMEM((width, slots), jnp.float32),
            pltpu.SemaphoreType.DMA((slots // min(256, slots),)),
        ],
        cost_estimate=light(),
        compiler_params=params(16),
        name="place_rows",
    )(place, *given)


def per_device(spectra, source_ids, pair_source, pair_offset, pair_counts):
    chan_rows = spectra.shape[1]
    bins = spectra.shape[3]
    seg_size = lax.axis_size("seg")
    chan_size = lax.axis_size("chan")
    slots = pair_source.shape[0]
    window = 3 * slots // 8
    scale = 1.0 / math.sqrt(bins * seg_size)
    join = lax.optimization_barrier

    ring = list(range(0, chan_size, 2)) + list(range(1, chan_size, 2))[::-1]
    ahead = [(ring[i], ring[(i + 1) % chan_size]) for i in range(chan_size)]
    back = [(b, a) for a, b in ahead]
    leftward = [(i + 1, i) for i in range(chan_size - 1)]
    rightward = [(i, i + 1) for i in range(chan_size - 1)]

    def one_turn(turns):
        first_rows = slots - 2 * window
        own = pick_rows(turns, pair_counts, source_ids, pair_source, pair_offset, spectra, first_rows)
        if turns is None:
            turns = jnp.zeros((2,), jnp.int32)
        forward, backward = [own], [own]
        steps = chan_size // 2

        def step_beside(work=None):
            ahead_of = forward[-1], backward[-1]
            forward.append(lax.ppermute(ahead_of[0], "chan", ahead))
            if len(backward) < chan_size - steps:
                backward.append(lax.ppermute(ahead_of[1], "chan", back))
            if work is not None:
                *results, token = work()
                if len(backward) == len(forward):
                    token, forward[-1], backward[-1] = join((token, forward[-1], backward[-1]))
                else:
                    token, forward[-1] = join((token, forward[-1]))
                return results, token

        tables, token = step_beside(lambda: lag_tables(bins, scale, own))
        cells = jnp.transpose(spectra[0], (1, 0, 2))
        (whitened,), token = step_beside(lambda: whiten_rows(cells, token))
        for _ in range(3, steps - 1):
            step_beside()
        picks, token = step_beside(
            lambda: prepare_early(turns, source_ids, own, chan_rows, chan_size, first_rows, token)
        )

        def piece(picks, chunks, start, rows, *after, weight=light()):
            return transform(
                picks, chunks, whitened, tables, seg_size, scale, start, rows, weight, *after
            )

        chunks = [*forward, own, *backward[1:]]
        full = pl.CostEstimate(
            flops=first_rows * bins * 4096, bytes_accessed=16 * bins * HALF, transcendentals=0
        )
        (keep_own, send), token = step_beside(
            lambda: piece(picks, chunks, 0, first_rows, token, weight=full)
        )
        chunks = forward + backward[1:]
        *picks, place, source_turns, send, token = prepare(
            turns, source_ids, chunks, slots, chan_rows, window, token, send
        )
        got_own = swap(send, 1)
        keep_left, send, token = piece(picks, chunks, 0, window, token)
        token, got_own = join((token, got_own))
        keep_own, send_own = halve(keep_own, got_own)
        got_left = swap(send, 1)
        got_own = swap(send_own, 2)
        keep_right, send, token = piece(picks, chunks, window, window, token, send_own)
        token, got_left, got_own = join((token, got_left, got_own))
        got_right = swap(send, 1)
        keep_left, send_left = halve(keep_left, got_left)
        got_left = swap(send_left, 2)
        keep_right, send_right = halve(keep_right, got_right)
        got_left, send_right = join((got_left, send_right))
        left = reduce_further(keep_left, got_left, 2)
        right = reduce_further(keep_right, swap(send_right, 2), 2)
        own = reduce_further(keep_own, got_own, 2)
        from_right = lax.ppermute(left, "chan", leftward)
        from_left = lax.ppermute(right, "chan", rightward)
        total = place_rows(place, (left, right, own), 0)
        result = place_rows(place, (from_left, from_right), slots, total)
        return result, (right, token), chunks, source_turns

    first, after, chunks, source_turns = one_turn(None)
    turns_left, pair_turns = [count[0] for count in count_turns(source_turns, chunks, window, after)]

    def further(state):
        turn, total = state
        turns = jnp.stack([lax.div(turn, pair_turns), lax.rem(turn, pair_turns)])
        return turn - 1, total + one_turn(turns)[0]

    return lax.while_loop(lambda state: state[0] > 0, further, (turns_left, first))[1]


def solution(mesh):
    in_specs = (P("seg", "chan", None, None), P(), P("chan"), P("chan"), P("chan"))
    out_specs = P("seg", "chan")
    return jax.shard_map(
        per_device, mesh=mesh, in_specs=in_specs, out_specs=out_specs, check_vma=False
    )
```

```python
import functools
import math

import jax
import jax.numpy as jnp
from jax import lax
from jax.experimental import pallas as pl
from jax.experimental.pallas import tpu as pltpu
from jax.sharding import PartitionSpec as P

LAGS = 1024
HALF = LAGS // 2
WBLOCK = 64
PICK = 16
BINS_STEP = 512
TABLE_ROWS = 64
EXTRA = 128


def params(mebibytes):
    return pltpu.CompilerParams(vmem_limit_bytes=mebibytes * 1024 * 1024)


def light():
    return pl.CostEstimate(flops=1024, bytes_accessed=1024, transcendentals=0)


TOKEN = jax.ShapeDtypeStruct((8, 128), jnp.float32)


def whole(shape):
    return pl.BlockSpec(shape, lambda *_: (0,) * len(shape))


def ring_place(block, chan_size):
    return jnp.where((block & 1) == 0, block >> 1, chan_size - 1 - (block >> 1))


def ring_block(place, chan_size):
    return jnp.where(place < chan_size // 2, 2 * place, 2 * (chan_size - place) - 1)


def far_block(me, chan_size):
    place = ring_place(me, chan_size) - chan_size // 2
    return ring_block(jnp.where(place < 0, place + chan_size, place), chan_size)


def ring_hop(me, block, chan_size):
    steps = chan_size // 2
    distance = ring_place(me, chan_size) - ring_place(block, chan_size)
    distance = jnp.where(distance < 0, distance + chan_size, distance)
    return jnp.where(distance <= steps, distance, steps + chan_size - distance)


def pick_kernel(chan_rows, band, first_rows, *refs):
    counts_ref, ids_ref, source_ref, offset_ref, cells_ref, out_ref, rows_ref, held_ref, sems = refs[-9:]
    first = lax.axis_index("chan") * chan_rows
    turn = refs[0][0] if len(refs) > 9 else 0
    bins = cells_ref.shape[3]
    for i in range(PICK):
        rows_ref[i] = 0
    rank = jnp.int32(0)
    for i in range(ids_ref.shape[0]):
        row = ids_ref[i] - first
        mine = (row >= 0) & (row < chan_rows)
        spot = rank - turn * PICK
        rows_ref[jnp.where(mine & (spot >= 0) & (spot < PICK), spot, PICK)] = row
        rank = rank + mine.astype(jnp.int32)
    far = far_block(lax.axis_index("chan"), lax.axis_size("chan")) * chan_rows
    late = [jnp.int32(0), jnp.int32(0)]
    for i in range(ids_ref.shape[0]):
        row = ids_ref[i] - far
        late[i // 32] = late[i // 32] | (((row >= 0) & (row < chan_rows)).astype(jnp.int32) << (i % 32))
    copies = [
        pltpu.make_async_copy(cells_ref.at[0, rows_ref[i]], held_ref.at[i], sems.at[i])
        for i in range(PICK)
    ]
    for copy in copies:
        copy.start()

    offset = offset_ref[...]
    slot = lax.broadcasted_iota(jnp.int32, offset.shape, 0) * offset.shape[1]
    slot = slot + lax.broadcasted_iota(jnp.int32, offset.shape, 1)
    live = slot < counts_ref[...]
    source = source_ref[...]
    bits = jnp.where(source < 32, late[0], late[1])
    is_late = lax.shift_right_logical(bits, source & 31) & 1
    inside = live & (offset >= 0) & (offset < chan_rows)
    kinds = (live & (offset >= chan_rows), live & (offset < 0), inside, inside & (is_late == 0))
    lane = lax.broadcasted_iota(jnp.int32, offset.shape, 1)
    notes = jnp.zeros(offset.shape, jnp.int32)
    totals = [jnp.sum(jnp.where(kind, 1.0, 0.0)).astype(jnp.int32) for kind in kinds]
    totals = (totals[0], totals[1], totals[2] - jnp.minimum(totals[3], first_rows))
    for index, total in enumerate(totals):
        notes = jnp.where(lane == 2 * index, total >> 5, notes)
        notes = jnp.where(lane == 2 * index + 1, total & 31, notes)
    shifted = offset + band
    source = jnp.where(live, source + 1, 0)

    def coded(upper, lower):
        both = jnp.concatenate([upper.astype(jnp.float32), lower.astype(jnp.float32)], axis=0)
        return both.astype(jnp.bfloat16)

    out_ref[0, :, pl.ds(bins, EXTRA)] = coded(source, shifted >> 4)
    out_ref[1, :, pl.ds(bins, EXTRA)] = coded((shifted & 15) + 16 * is_late, notes)

    for copy in copies:
        copy.wait()
    real = held_ref[:, 0, :].astype(jnp.float32)
    imag = held_ref[:, 1, :].astype(jnp.float32)
    width = min(256, bins)

    def stacked(values):
        return jnp.concatenate([values[:, i : i + width] for i in range(0, bins, width)], axis=0)

    real, imag = whitened_pair(stacked(real), stacked(imag))
    for index in range(bins // width):
        lanes = pl.ds(index * width, width)
        out_ref[0, :, lanes] = real[index * PICK : (index + 1) * PICK]
        out_ref[1, :, lanes] = imag[index * PICK : (index + 1) * PICK]


def pick_rows(turns, counts, source_ids, pair_source, pair_offset, spectra, first_rows):
    _, chan_rows, parts, bins = spectra.shape
    smem = pl.BlockSpec(memory_space=pltpu.SMEM)
    vmem = pl.BlockSpec(memory_space=pltpu.VMEM)
    given = [] if turns is None else [turns]
    return pl.pallas_call(
        functools.partial(pick_kernel, chan_rows, chan_rows // 2, first_rows),
        out_shape=jax.ShapeDtypeStruct((parts, PICK, bins + EXTRA), spectra.dtype),
        in_specs=[smem] * len(given) + [vmem, smem, vmem, vmem, pl.BlockSpec(memory_space=pl.ANY)],
        out_specs=vmem,
        scratch_shapes=[
            pltpu.SMEM((PICK + 1,), jnp.int32),
            pltpu.VMEM((PICK, parts, bins), spectra.dtype),
            pltpu.SemaphoreType.DMA((PICK,)),
        ],
        cost_estimate=light(),
        compiler_params=params(8),
        name="pick_rows",
    )(
        *given,
        counts.reshape(1, 1),
        source_ids,
        pair_source.reshape(-1, EXTRA),
        pair_offset.reshape(-1, EXTRA),
        spectra,
    )


def block_mean(power):
    width = power.shape[1]
    row_group = lax.broadcasted_iota(jnp.int32, (width, width), 0) // WBLOCK
    col_group = lax.broadcasted_iota(jnp.int32, (width, width), 1) // WBLOCK
    spread = jnp.where(row_group == col_group, 1.0 / WBLOCK, 0.0).astype(jnp.bfloat16)
    high = power.astype(jnp.bfloat16)
    low = (power - high.astype(jnp.float32)).astype(jnp.bfloat16)
    total = jnp.dot(low, spread, preferred_element_type=jnp.float32)
    return total + jnp.dot(high, spread, preferred_element_type=jnp.float32)


def whitened_pair(real, imag):
    inverse = lax.rsqrt(block_mean(real * real + imag * imag) + 1e-06)
    return (real * inverse).astype(jnp.bfloat16), (imag * inverse).astype(jnp.bfloat16)


def whiten_kernel(cells_ref, after_ref, out_ref, token_ref):
    token_ref[...] = jnp.zeros_like(token_ref)
    for start in range(0, cells_ref.shape[2], 256):
        lanes = pl.ds(start, 256)
        real = cells_ref[0, :, lanes].astype(jnp.float32)
        imag = cells_ref[1, :, lanes].astype(jnp.float32)
        out_ref[0, :, lanes], out_ref[1, :, lanes] = whitened_pair(real, imag)


def whiten_rows(cells, after):
    _, rows, bins = cells.shape
    spec = pl.BlockSpec((2, rows, BINS_STEP), lambda i: (0, 0, i))
    return pl.pallas_call(
        whiten_kernel,
        grid=(bins // BINS_STEP,),
        out_shape=(jax.ShapeDtypeStruct(cells.shape, jnp.bfloat16), TOKEN),
        in_specs=[spec, pl.BlockSpec(memory_space=pl.ANY)],
        out_specs=(spec, whole(TOKEN.shape)),
        cost_estimate=light(),
        compiler_params=params(12),
        name="whiten_rows",
    )(cells, after)


def table_kernel(scale, all_bins, after_ref, cos_ref, sin_ref, token_ref, coarse_ref, fine_ref):
    token_ref[...] = jnp.zeros_like(token_ref)
    step = pl.program_id(0)
    groups = cos_ref.shape[0] // TABLE_ROWS

    @pl.when(step == 0)
    def _():
        def circle(ref, stride, factor):
            shape = ref.shape[1:]
            bins = lax.broadcasted_iota(jnp.int32, shape, 0) * stride
            lags = lax.broadcasted_iota(jnp.int32, shape, 1)
            lags = jnp.where(lags == 0, HALF, lags)
            theta = ((bins * lags) & (2 * all_bins - 1)).astype(jnp.float32) * (math.pi / all_bins)
            ref[0] = jnp.cos(theta) * factor
            ref[1] = jnp.sin(theta) * factor

        circle(coarse_ref, TABLE_ROWS, scale)
        circle(fine_ref, 1, 1.0)

    cos_b = fine_ref[0]
    sin_b = fine_ref[1]
    first = lax.broadcasted_iota(jnp.int32, cos_b.shape, 1) == 0
    for group in range(groups):
        cos_a = coarse_ref[0, pl.ds(step * groups + group, 1), :]
        sin_a = coarse_ref[1, pl.ds(step * groups + group, 1), :]
        rows = pl.ds(group * TABLE_ROWS, TABLE_ROWS)
        cos = jnp.where(first, scale, cos_a * cos_b - sin_a * sin_b)
        cos_ref[rows, :] = cos.astype(jnp.bfloat16)
        sin_ref[rows, :] = (sin_a * cos_b + cos_a * sin_b).astype(jnp.bfloat16)


def lag_tables(bins, scale, after):
    spec = pl.BlockSpec((BINS_STEP, HALF), lambda i: (i, 0))
    shape = jax.ShapeDtypeStruct((bins, HALF), jnp.bfloat16)
    return pl.pallas_call(
        functools.partial(table_kernel, scale, bins),
        grid=(bins // BINS_STEP,),
        out_shape=(shape, shape, TOKEN),
        in_specs=[pl.BlockSpec(memory_space=pl.ANY)],
        out_specs=(spec, spec, whole(TOKEN.shape)),
        scratch_shapes=[
            pltpu.VMEM((2, bins // TABLE_ROWS, HALF), jnp.float32),
            pltpu.VMEM((2, TABLE_ROWS, HALF), jnp.float32),
        ],
        cost_estimate=light(),
        compiler_params=params(12),
        name="lag_tables",
    )(after)


def source_spots(chan_rows, chan_size, me, turn, ids_row):
    count = ids_row.shape[1]
    shift = chan_rows.bit_length() - 1
    ids_row = jnp.broadcast_to(ids_row, (count, count))
    rows = lax.broadcasted_iota(jnp.int32, (count, count), 0)
    columns = lax.broadcasted_iota(jnp.int32, (count, count), 1)
    ids = jnp.sum(jnp.where(rows == columns, ids_row, 0).astype(jnp.float32), axis=1, keepdims=True)
    owner = jnp.broadcast_to(ids.astype(jnp.int32) >> shift, (count, count))
    earlier = (owner == (ids_row >> shift)) & (columns < rows)
    rank = jnp.sum(jnp.where(earlier, 1.0, 0.0), axis=1, keepdims=True)
    turns = (jnp.max(rank).astype(jnp.int32) + PICK) // PICK
    rank = rank.astype(jnp.int32) - turn * PICK
    owner = owner[:, 0:1]

    hop = ring_hop(me, owner, chan_size)
    return jnp.where((rank >= 0) & (rank < PICK), hop * PICK + rank, -1), turns


def flat(value):
    return jnp.concatenate([value[i : i + 1, :] for i in range(8)], axis=1)


def unlisted(halves, band):
    upper, lower = [half.astype(jnp.int32) for half in halves]
    return upper[0:8] - 1, upper[8:16] * 16 + (lower[0:8] & 15) - band, lower[0:8] >> 4


def ranked(taken):
    marks = jnp.concatenate([jnp.where(mask, 1.0, 0.0) for mask in taken], axis=0)
    rows = marks.shape[0]
    earlier = lax.broadcasted_iota(jnp.int32, (EXTRA, EXTRA), 0) < lax.broadcasted_iota(
        jnp.int32, (EXTRA, EXTRA), 1
    )
    rank = jnp.dot(
        marks.astype(jnp.bfloat16),
        jnp.where(earlier, 1.0, 0.0).astype(jnp.bfloat16),
        preferred_element_type=jnp.float32,
    )
    sums = jnp.broadcast_to(jnp.sum(marks, axis=1, keepdims=True), marks.shape)
    row = lax.broadcasted_iota(jnp.int32, (rows, rows), 0)
    column = lax.broadcasted_iota(jnp.int32, (rows, rows), 1)
    above_it = ((row >> 3) == (column >> 3)) & (column < row)
    rank = rank + jnp.dot(
        jnp.where(above_it, 1.0, 0.0).astype(jnp.bfloat16),
        sums.astype(jnp.bfloat16),
        preferred_element_type=jnp.float32,
    )
    rank = rank.astype(jnp.int32)
    return [rank[8 * i : 8 * i + 8] for i in range(len(taken))]


def jobs_of(spots, source, receiver, position, count):
    source, receiver, position = flat(source), flat(receiver), flat(position)
    slots = source.shape[1]
    names = lax.broadcasted_iota(jnp.int32, (spots.shape[0], slots), 0)
    field_row = lax.broadcasted_iota(jnp.int32, (8, slots), 0)
    spot = jnp.where(names == source, spots + 1, 0).astype(jnp.float32)
    spot = jnp.sum(spot, axis=0, keepdims=True).astype(jnp.int32) - 1
    fields = jnp.where(field_row == 0, spot >> 4, jnp.where(field_row == 1, spot & (PICK - 1), 0))
    fields = jnp.where(field_row == 2, receiver, jnp.where(field_row == 3, 1, fields))
    fields = jnp.where((position >= 0) & (spot >= 0), fields, 0)
    wanted = lax.broadcasted_iota(jnp.int32, (count, slots), 0)
    chosen = jnp.where(wanted == position, 1.0, 0.0).astype(jnp.bfloat16)
    return lax.dot_general(
        chosen,
        fields.astype(jnp.float32).astype(jnp.bfloat16),
        (((1,), (1,)), ((), ())),
        preferred_element_type=jnp.float32,
    )


def write_picks(jobs, start, src_ref, rec_ref):
    count = jobs.shape[0]
    jobs = jobs.astype(jnp.int32)
    busy = jobs[:, 3:4] > 0
    part = pl.ds(start, count)
    column = jnp.where(busy, jobs[:, 0:1] * PICK + jobs[:, 1:2], -1)
    lane = lax.broadcasted_iota(jnp.int32, (count, src_ref.shape[1]), 1)
    src_ref[part, :] = jnp.where(column == lane, 1.0, 0.0).astype(jnp.bfloat16)
    column = jnp.where(busy, jobs[:, 2:3], -1)
    lane = lax.broadcasted_iota(jnp.int32, (count, rec_ref.shape[1]), 1)
    rec_ref[part, :] = jnp.where(column == lane, 1.0, 0.0).astype(jnp.bfloat16)


def early_kernel(chan_rows, chan_size, turns_ref, ids_ref, after_ref, own_ref, src_ref, rec_ref, token_ref):
    token_ref[...] = jnp.zeros_like(token_ref)
    me = lax.axis_index("chan")
    count = src_ref.shape[0]
    lanes = pl.ds(own_ref.shape[2] - EXTRA, EXTRA)
    spots, _ = source_spots(chan_rows, chan_size, me, turns_ref[0], ids_ref[...])
    halves = [own_ref[half, :, lanes].astype(jnp.float32) for half in range(2)]
    source, offset, late = unlisted(halves, chan_rows // 2)
    early = (source >= 0) & (offset >= 0) & (offset < chan_rows) & (late == 0)
    (rank,) = ranked((early,))
    rank = jnp.where(early & (rank < count) & (turns_ref[1] == 0), rank, -1)
    write_picks(jobs_of(spots, source, offset, rank, count), 0, src_ref, rec_ref)


def prepare_early(turns, source_ids, own, chan_rows, chan_size, count, after):
    vmem = pl.BlockSpec(memory_space=pltpu.VMEM)
    return pl.pallas_call(
        functools.partial(early_kernel, chan_rows, chan_size),
        out_shape=(
            jax.ShapeDtypeStruct((count, chan_size * PICK), jnp.bfloat16),
            jax.ShapeDtypeStruct((count, chan_rows), jnp.bfloat16),
            TOKEN,
        ),
        in_specs=[
            pl.BlockSpec(memory_space=pltpu.SMEM), vmem, pl.BlockSpec(memory_space=pl.ANY), vmem,
        ],
        out_specs=(vmem, vmem, vmem),
        cost_estimate=light(),
        compiler_params=params(12),
        name="prepare_early",
    )(turns, source_ids.reshape(1, -1), after, own)


def prepare_kernel(chan_rows, chan_size, window, turns_ref, ids_ref, after_ref, passed_ref, *refs):
    chunk_refs = refs[:chan_size]
    src_ref, rec_ref, place_ref, needed_ref, _, token_ref = refs[chan_size:]
    token_ref[...] = jnp.zeros_like(token_ref)
    me = lax.axis_index("chan")
    turn = turns_ref[1]
    slots = place_ref.shape[1]
    room = 2 * window
    spots, needed = source_spots(chan_rows, chan_size, me, turns_ref[0], ids_ref[...])
    needed_ref[0] = needed

    lanes = pl.ds(chunk_refs[0].shape[2] - EXTRA, EXTRA)
    left_hop = jnp.where(me > 0, ring_hop(me, me - 1, chan_size), -1)
    right_hop = jnp.where(me < chan_size - 1, ring_hop(me, me + 1, chan_size), -1)
    listed = []
    for wanted in (left_hop, right_hop, 0):
        halves = []
        for half in range(2):
            value = jnp.zeros((PICK, EXTRA), jnp.float32)
            for hop, ref in enumerate(chunk_refs):
                value = jnp.where(wanted == hop, ref[half, :, lanes].astype(jnp.float32), value)
            halves.append(value)
        listed.append(unlisted(halves, chan_rows // 2))
    (left_src, left_off, _), (right_src, right_off, _), (own_src, own_off, own_late) = listed
    inside = (own_src >= 0) & (own_off >= 0) & (own_off < chan_rows)
    early = inside & (own_late == 0)
    taken = (
        (left_src >= 0) & (left_off >= chan_rows),
        (right_src >= 0) & (right_off < 0),
        (own_src >= 0) & (own_off < 0),
        (own_src >= 0) & (own_off >= chan_rows),
        inside,
        early,
    )
    ranks = ranked(taken)
    left_total = jnp.sum(jnp.where(taken[0], 1.0, 0.0)).astype(jnp.int32)
    right_total = jnp.sum(jnp.where(taken[1], 1.0, 0.0)).astype(jnp.int32)

    def done_before(amount, index):
        return jnp.minimum(amount, index * window)

    left_before = done_before(left_total, turn)
    right_before = done_before(right_total, turn)
    left_now = done_before(left_total, turn + 1) - left_before
    right_now = done_before(right_total, turn + 1) - right_before

    def in_window(index):
        shifted = ranks[index] - turn * window
        return shifted, taken[index] & (shifted >= 0) & (shifted < window)

    left_rank, left_ok = in_window(0)
    right_rank, right_ok = in_window(1)
    below_rank, below_ok = in_window(2)
    above_rank, above_ok = in_window(3)

    first = early & (ranks[5] < slots - room)
    own_rank = ranks[4] - jnp.minimum(ranks[5], slots - room)
    own_rank = own_rank - (turn * room - left_before - right_before)
    own_ok = inside & ~first & (own_rank >= 0) & (own_rank < room - left_now - right_now)
    own_pos = own_rank + left_now
    own_pos = jnp.where(own_pos < window, own_pos, own_pos + right_now)
    own_pos = jnp.where(own_ok, own_pos, -1)
    place = jnp.where(first & (turn == 0), ranks[5] + room, own_pos)
    place = jnp.where(below_ok, below_rank + slots, place)
    place = jnp.where(above_ok, above_rank + slots + window, place)
    place_ref[...] = jnp.broadcast_to(flat(place), place_ref.shape)

    left_jobs = jobs_of(spots, left_src, left_off - chan_rows, jnp.where(left_ok, left_rank, -1), window)
    right_jobs = jobs_of(
        spots, right_src, right_off + chan_rows, jnp.where(right_ok, right_rank, -1), window
    )
    own_jobs = jobs_of(spots, own_src, own_off, own_pos, room)
    write_picks(left_jobs + own_jobs[0:window], 0, src_ref, rec_ref)
    write_picks(right_jobs + own_jobs[window:room], window, src_ref, rec_ref)


def prepare(turns, source_ids, chunks, slots, chan_rows, window, after, passed):
    chan_size = len(chunks)
    vmem = pl.BlockSpec(memory_space=pltpu.VMEM)
    smem = pl.BlockSpec(memory_space=pltpu.SMEM)
    return pl.pallas_call(
        functools.partial(prepare_kernel, chan_rows, chan_size, window),
        out_shape=(
            jax.ShapeDtypeStruct((2 * window, chan_size * PICK), jnp.bfloat16),
            jax.ShapeDtypeStruct((2 * window, chan_rows), jnp.bfloat16),
            jax.ShapeDtypeStruct((8, slots), jnp.int32),
            jax.ShapeDtypeStruct((1,), jnp.int32),
            jax.ShapeDtypeStruct(passed.shape, passed.dtype),
            TOKEN,
        ),
        in_specs=[smem, vmem] + [pl.BlockSpec(memory_space=pl.ANY)] * 2 + [vmem] * len(chunks),
        out_specs=(vmem, vmem, vmem, smem, pl.BlockSpec(memory_space=pl.ANY), vmem),
        input_output_aliases={3: 4},
        cost_estimate=light(),
        compiler_params=params(16),
        name="prepare",
    )(turns, source_ids.reshape(1, -1), after, passed, *chunks)


def turns_kernel(chan_size, window, source_turns_ref, *refs):
    chunk_refs = refs[:chan_size]
    left_ref, pairs_ref = refs[-2:]
    me = lax.axis_index("chan")
    steps = chan_size // 2
    place = ring_place(me, chan_size)
    block = lax.broadcasted_iota(jnp.int32, (chan_size, EXTRA), 0)
    notes = jnp.zeros((chan_size, EXTRA), jnp.float32)
    for hop, ref in enumerate(chunk_refs):
        spot = place - hop if hop <= steps else place + hop - steps
        spot = jnp.where(spot < 0, spot + chan_size, spot)
        spot = jnp.where(spot >= chan_size, spot - chan_size, spot)
        owner = ring_block(spot, chan_size)
        notes = jnp.where(block == owner, ref[0][8:9, :].astype(jnp.float32), notes)
    lane = lax.broadcasted_iota(jnp.int32, notes.shape, 1)

    def total(index):
        value = jnp.where(lane == 2 * index, 32.0 * notes, 0.0)
        value = value + jnp.where(lane == 2 * index + 1, notes, 0.0)
        return jnp.broadcast_to(jnp.sum(value, axis=1, keepdims=True), notes.shape)

    left = jnp.where(block == 0, 0.0, pltpu.roll(total(0), 1, 0))
    right = jnp.where(block == chan_size - 1, 0.0, pltpu.roll(total(1), chan_size - 1, 0))
    aside = jnp.max(jnp.maximum(left, right)).astype(jnp.int32)
    whole_sum = jnp.max(left + right + total(2)).astype(jnp.int32)
    room = 2 * window
    needed = jnp.maximum((aside + window - 1) // window, (whole_sum + room - 1) // room)
    needed = jnp.maximum(needed, 1)
    pairs_ref[0] = needed
    left_ref[0] = needed * source_turns_ref[0] - 1


def count_turns(source_turns, chunks, window, after):
    _, _, width = chunks[0].shape
    last = width // EXTRA - 1
    specs = [pl.BlockSpec((1, PICK, EXTRA), lambda i: (1, 0, last)) for _ in chunks]
    return pl.pallas_call(
        functools.partial(turns_kernel, len(chunks), window),
        grid=(1,),
        out_shape=[jax.ShapeDtypeStruct((1,), jnp.int32)] * 2,
        in_specs=[pl.BlockSpec(memory_space=pltpu.SMEM), *specs]
        + [pl.BlockSpec(memory_space=pl.ANY)] * len(after),
        out_specs=[pl.BlockSpec(memory_space=pltpu.SMEM)] * 2,
        cost_estimate=light(),
        compiler_params=params(8),
        name="count_turns",
    )(source_turns, *chunks, *after)


def transform_kernel(shards, scale, start, chunks, src_ref, rec_ref, *refs):
    chunk_refs = refs[:chunks]
    cells_ref, cos_ref, sin_ref = refs[chunks : chunks + 3]
    keep_ref, send_ref, token_ref = refs[-3:]
    token_ref[...] = jnp.zeros_like(token_ref)
    rows = keep_ref.shape[1]
    bins = cos_ref.shape[0]
    step = min(BINS_STEP, bins)
    eighth = lax.broadcasted_iota(jnp.int32, (1, 128), 1) & 7
    root = math.sqrt(0.5)
    edge = jnp.where((eighth == 1) | (eighth == 7), root, 0.0)
    edge = jnp.where((eighth == 3) | (eighth == 5), -root, edge)
    edge = jnp.where(eighth == 0, 1.0, jnp.where(eighth == 4, -1.0, edge)) * scale
    edge = edge.astype(jnp.bfloat16).astype(jnp.float32)

    by_src = src_ref[pl.ds(start, rows), :]
    by_rec = rec_ref[pl.ds(start, rows), :]
    even = odd = corner = None
    for first in range(0, bins, step):
        lanes = pl.ds(first, step)
        source_real = jnp.concatenate([ref[0, :, lanes] for ref in chunk_refs], axis=0)
        source_imag = jnp.concatenate([ref[1, :, lanes] for ref in chunk_refs], axis=0)
        sr = jnp.dot(by_src, source_real, preferred_element_type=jnp.float32)
        si = jnp.dot(by_src, source_imag, preferred_element_type=jnp.float32)
        rr = jnp.dot(by_rec, cells_ref[0, :, lanes], preferred_element_type=jnp.float32)
        ri = jnp.dot(by_rec, cells_ref[1, :, lanes], preferred_element_type=jnp.float32)
        real = (sr * rr + si * ri).astype(jnp.bfloat16)
        imag = (si * rr - sr * ri).astype(jnp.bfloat16)
        more_even = jnp.dot(real, cos_ref[lanes, :], preferred_element_type=jnp.float32)
        more_odd = jnp.dot(imag, sin_ref[lanes, :], preferred_element_type=jnp.float32)
        wide = real.astype(jnp.float32)
        sums = wide[:, 0:128]
        for lane in range(128, step, 128):
            sums = sums + wide[:, lane : lane + 128]
        even = more_even if even is None else even + more_even
        odd = more_odd if odd is None else odd + more_odd
        corner = sums if corner is None else corner + sums

    me = lax.axis_index("seg")
    width = LAGS // shards
    corner = jnp.sum(corner * edge, axis=1, keepdims=True)
    first = lax.broadcasted_iota(jnp.int32, even.shape, 1) == 0
    later = even - jnp.where(first, 0.0, odd)
    sooner = jnp.where(first, corner, even) + odd
    sooner = pltpu.roll(sooner, HALF - 1, 1)
    for shard in range(shards):
        half = shards // 2
        if shard < half:
            lane = (half - 1 - shard) * width
            value = sooner[:, lane : lane + width]
        else:
            lane = (shard - half) * width
            value = later[:, lane : lane + width]
        place = me ^ shard

        @pl.when((place & 1) == 0)
        def _():
            keep_ref[place >> 1] = value

        @pl.when((place & 1) == 1)
        def _():
            send_ref[place >> 1] = value.astype(jnp.bfloat16)


def transform(picks, chunks, cells, tables, shards, scale, start, rows, weight, *after):
    width = LAGS // shards
    shape = (shards // 2, rows, width)
    vmem = pl.BlockSpec(memory_space=pltpu.VMEM)
    return pl.pallas_call(
        functools.partial(transform_kernel, shards, scale, start, len(chunks)),
        out_shape=(
            jax.ShapeDtypeStruct(shape, jnp.float32),
            jax.ShapeDtypeStruct(shape, jnp.bfloat16),
            TOKEN,
        ),
        in_specs=[vmem] * (5 + len(chunks))
        + [pl.BlockSpec(memory_space=pl.ANY)] * len(after),
        out_specs=(vmem, vmem, vmem),
        cost_estimate=weight,
        compiler_params=params(16),
        name="transform",
    )(*picks, *chunks, cells, *tables, *after)


def swap(send, bit):
    size = lax.axis_size("seg")
    return lax.ppermute(send, "seg", [(i, i ^ bit) for i in range(size)])


def halve(keep, got):
    total = keep + got.astype(jnp.float32)
    return total[0::2], total[1::2].astype(jnp.bfloat16)


def reduce_further(keep, got, bit):
    while keep.shape[0] > 1:
        keep, send = halve(keep, got)
        bit *= 2
        got = swap(send, bit)
    return (keep[0] + got[0].astype(jnp.float32)).astype(jnp.bfloat16)


def turned_parts(refs):
    width = refs[0].shape[1]
    flip = lax.axis_index("seg") < lax.axis_size("seg") // 2
    rows = lax.broadcasted_iota(jnp.int32, (width, width), 0)
    columns = lax.broadcasted_iota(jnp.int32, (width, width), 1)
    wanted = jnp.where(flip, width - 1 - rows, rows)
    turned = jnp.where(wanted == columns, 1.0, 0.0).astype(jnp.bfloat16)
    return [
        lax.dot_general(
            turned, ref[...], (((1,), (1,)), ((), ())), preferred_element_type=jnp.float32
        ).astype(jnp.bfloat16)
        for ref in refs
    ]


def place_kernel(place_ref, *refs):
    parts, (out_ref, later_ref) = refs[:-2], refs[-2:]
    slots = out_ref.shape[1]

    def chosen(start, count):
        spot = lax.broadcasted_iota(jnp.int32, (count, slots), 0) + start
        return jnp.where(spot == place_ref[0:1, :], 1.0, 0.0).astype(jnp.bfloat16)

    total = None
    start = 0
    for part in turned_parts(parts):
        count = part.shape[1]
        more = jnp.dot(part, chosen(start, count), preferred_element_type=jnp.float32)
        total = more if total is None else total + more
        start += count
    out_ref[...] = total
    later_ref[...] = chosen(start, later_ref.shape[0])


def place_rows(place, parts, later):
    width = parts[0].shape[1]
    slots = place.shape[1]
    vmem = pl.BlockSpec(memory_space=pltpu.VMEM)
    return pl.pallas_call(
        place_kernel,
        out_shape=(
            jax.ShapeDtypeStruct((width, slots), jnp.float32),
            jax.ShapeDtypeStruct((later, slots), jnp.bfloat16),
        ),
        in_specs=[vmem] * (1 + len(parts)),
        out_specs=(vmem, vmem),
        cost_estimate=light(),
        compiler_params=params(16),
        name="place_rows",
    )(place, *parts)


def add_kernel(total_ref, chosen_ref, *refs):
    parts, (out_ref, made_ref, sems) = refs[:-3], refs[-3:]
    slots = made_ref.shape[1]
    step = min(256, slots)
    across = jnp.concatenate(turned_parts(parts), axis=1)
    copies = []
    for index in range(slots // step):
        lanes = pl.ds(index * step, step)
        made_ref[:, lanes] = total_ref[:, lanes] + jnp.dot(
            across, chosen_ref[:, lanes], preferred_element_type=jnp.float32
        )
        copy = pltpu.make_async_copy(made_ref.at[:, lanes], out_ref.at[:, lanes], sems.at[index])
        copy.start()
        copies.append(copy)
    for copy in copies:
        copy.wait()


def add_rows(total, chosen, parts):
    width, slots = total.shape
    vmem = pl.BlockSpec(memory_space=pltpu.VMEM)
    return pl.pallas_call(
        add_kernel,
        out_shape=jax.ShapeDtypeStruct((width, slots), jnp.float32),
        in_specs=[vmem] * (2 + len(parts)),
        out_specs=pl.BlockSpec(memory_space=pltpu.HBM),
        scratch_shapes=[
            pltpu.VMEM((width, slots), jnp.float32),
            pltpu.SemaphoreType.DMA((slots // min(256, slots),)),
        ],
        cost_estimate=light(),
        compiler_params=params(16),
        name="add_rows",
    )(total, chosen, *parts)


def per_device(spectra, source_ids, pair_source, pair_offset, pair_counts):
    chan_rows = spectra.shape[1]
    bins = spectra.shape[3]
    seg_size = lax.axis_size("seg")
    chan_size = lax.axis_size("chan")
    slots = pair_source.shape[0]
    window = 3 * slots // 8
    scale = 1.0 / math.sqrt(bins * seg_size)
    join = lax.optimization_barrier

    ring = list(range(0, chan_size, 2)) + list(range(1, chan_size, 2))[::-1]
    ahead = [(ring[i], ring[(i + 1) % chan_size]) for i in range(chan_size)]
    back = [(b, a) for a, b in ahead]
    leftward = [(i + 1, i) for i in range(chan_size - 1)]
    rightward = [(i, i + 1) for i in range(chan_size - 1)]

    def one_turn(turns):
        first_rows = slots - 2 * window
        own = pick_rows(turns, pair_counts, source_ids, pair_source, pair_offset, spectra, first_rows)
        if turns is None:
            turns = jnp.zeros((2,), jnp.int32)
        forward, backward = [own], [own]
        steps = chan_size // 2

        def step_beside(work=None):
            ahead_of = forward[-1], backward[-1]
            forward.append(lax.ppermute(ahead_of[0], "chan", ahead))
            if len(backward) < chan_size - steps:
                backward.append(lax.ppermute(ahead_of[1], "chan", back))
            if work is not None:
                *results, token = work()
                if len(backward) == len(forward):
                    token, forward[-1], backward[-1] = join((token, forward[-1], backward[-1]))
                else:
                    token, forward[-1] = join((token, forward[-1]))
                return results, token

        tables, token = step_beside(lambda: lag_tables(bins, scale, own))
        cells = jnp.transpose(spectra[0], (1, 0, 2))
        (whitened,), token = step_beside(lambda: whiten_rows(cells, token))
        for _ in range(3, steps - 1):
            step_beside()
        picks, token = step_beside(
            lambda: prepare_early(turns, source_ids, own, chan_rows, chan_size, first_rows, token)
        )

        def piece(picks, chunks, start, rows, *after, weight=light()):
            return transform(
                picks, chunks, whitened, tables, seg_size, scale, start, rows, weight, *after
            )

        chunks = [*forward, own, *backward[1:]]
        full = pl.CostEstimate(
            flops=first_rows * bins * 4096, bytes_accessed=16 * bins * HALF, transcendentals=0
        )
        (keep_own, send), token = step_beside(
            lambda: piece(picks, chunks, 0, first_rows, token, weight=full)
        )
        chunks = forward + backward[1:]
        *picks, place, source_turns, send, token = prepare(
            turns, source_ids, chunks, slots, chan_rows, window, token, send
        )
        got_own = swap(send, 1)
        keep_left, send, token = piece(picks, chunks, 0, window, token)
        token, got_own = join((token, got_own))
        keep_own, send_own = halve(keep_own, got_own)
        got_left = swap(send, 1)
        got_own = swap(send_own, 2)
        keep_right, send, token = piece(picks, chunks, window, window, token, send_own)
        token, got_left, got_own = join((token, got_left, got_own))
        got_right = swap(send, 1)
        left = reduce_further(keep_left, got_left, 1)
        right = reduce_further(keep_right, got_right, 1)
        own = reduce_further(keep_own, got_own, 2)
        from_right = lax.ppermute(left, "chan", leftward)
        from_left = lax.ppermute(right, "chan", rightward)
        total, chosen = place_rows(place, (left, right, own), 2 * window)
        result = add_rows(total, chosen, (from_left, from_right))
        return result, (right, token), chunks, source_turns

    first, after, chunks, source_turns = one_turn(None)
    turns_left, pair_turns = [count[0] for count in count_turns(source_turns, chunks, window, after)]

    def further(state):
        turn, total = state
        turns = jnp.stack([lax.div(turn, pair_turns), lax.rem(turn, pair_turns)])
        return turn - 1, total + one_turn(turns)[0]

    return lax.while_loop(lambda state: state[0] > 0, further, (turns_left, first))[1]


def solution(mesh):
    in_specs = (P("seg", "chan", None, None), P(), P("chan"), P("chan"), P("chan"))
    out_specs = P("seg", "chan")
    return jax.shard_map(
        per_device, mesh=mesh, in_specs=in_specs, out_specs=out_specs, check_vma=False
    )
```

```python
import functools
import math

import jax
import jax.numpy as jnp
from jax import lax
from jax.experimental import pallas as pl
from jax.experimental.pallas import tpu as pltpu
from jax.sharding import PartitionSpec as P

LAGS = 1024
HALF = LAGS // 2
WBLOCK = 64
PICK = 16
BINS_STEP = 512
TRANSFORM_STEP = 1024
TABLE_ROWS = 64
EXTRA = 128


def params(mebibytes):
    return pltpu.CompilerParams(vmem_limit_bytes=mebibytes * 1024 * 1024)


def light():
    return pl.CostEstimate(flops=1024, bytes_accessed=1024, transcendentals=0)


TOKEN = jax.ShapeDtypeStruct((8, 128), jnp.float32)


def whole(shape):
    return pl.BlockSpec(shape, lambda *_: (0,) * len(shape))


def ring_place(block, chan_size):
    return jnp.where((block & 1) == 0, block >> 1, chan_size - 1 - (block >> 1))


def ring_block(place, chan_size):
    return jnp.where(place < chan_size // 2, 2 * place, 2 * (chan_size - place) - 1)


def far_block(me, chan_size):
    place = ring_place(me, chan_size) - chan_size // 2
    return ring_block(jnp.where(place < 0, place + chan_size, place), chan_size)


def ring_hop(me, block, chan_size):
    steps = chan_size // 2
    distance = ring_place(me, chan_size) - ring_place(block, chan_size)
    distance = jnp.where(distance < 0, distance + chan_size, distance)
    return jnp.where(distance <= steps, distance, steps + chan_size - distance)


def pick_kernel(chan_rows, band, first_rows, *refs):
    counts_ref, ids_ref, source_ref, offset_ref, cells_ref, out_ref, rows_ref, held_ref, sems = refs[-9:]
    first = lax.axis_index("chan") * chan_rows
    turn = refs[0][0] if len(refs) > 9 else 0
    bins = cells_ref.shape[3]
    for i in range(PICK):
        rows_ref[i] = 0
    rank = jnp.int32(0)
    for i in range(ids_ref.shape[0]):
        row = ids_ref[i] - first
        mine = (row >= 0) & (row < chan_rows)
        spot = rank - turn * PICK
        rows_ref[jnp.where(mine & (spot >= 0) & (spot < PICK), spot, PICK)] = row
        rank = rank + mine.astype(jnp.int32)
    far = far_block(lax.axis_index("chan"), lax.axis_size("chan")) * chan_rows
    late = [jnp.int32(0), jnp.int32(0)]
    for i in range(ids_ref.shape[0]):
        row = ids_ref[i] - far
        late[i // 32] = late[i // 32] | (((row >= 0) & (row < chan_rows)).astype(jnp.int32) << (i % 32))
    copies = [
        pltpu.make_async_copy(cells_ref.at[0, rows_ref[i]], held_ref.at[i], sems.at[i])
        for i in range(PICK)
    ]
    for copy in copies:
        copy.start()

    offset = offset_ref[...]
    slot = lax.broadcasted_iota(jnp.int32, offset.shape, 0) * offset.shape[1]
    slot = slot + lax.broadcasted_iota(jnp.int32, offset.shape, 1)
    live = slot < counts_ref[...]
    source = source_ref[...]
    bits = jnp.where(source < 32, late[0], late[1])
    is_late = lax.shift_right_logical(bits, source & 31) & 1
    inside = live & (offset >= 0) & (offset < chan_rows)
    kinds = (live & (offset >= chan_rows), live & (offset < 0), inside, inside & (is_late == 0))
    lane = lax.broadcasted_iota(jnp.int32, offset.shape, 1)
    notes = jnp.zeros(offset.shape, jnp.int32)
    totals = [jnp.sum(jnp.where(kind, 1.0, 0.0)).astype(jnp.int32) for kind in kinds]
    totals = (totals[0], totals[1], totals[2] - jnp.minimum(totals[3], first_rows))
    for index, total in enumerate(totals):
        notes = jnp.where(lane == 2 * index, total >> 5, notes)
        notes = jnp.where(lane == 2 * index + 1, total & 31, notes)
    shifted = offset + band
    source = jnp.where(live, source + 1, 0)

    def coded(upper, lower):
        both = jnp.concatenate([upper.astype(jnp.float32), lower.astype(jnp.float32)], axis=0)
        return both.astype(jnp.bfloat16)

    out_ref[0, :, pl.ds(bins, EXTRA)] = coded(source, shifted >> 4)
    out_ref[1, :, pl.ds(bins, EXTRA)] = coded((shifted & 15) + 16 * is_late, notes)

    for copy in copies:
        copy.wait()
    real = held_ref[:, 0, :].astype(jnp.float32)
    imag = held_ref[:, 1, :].astype(jnp.float32)
    width = min(256, bins)

    def stacked(values):
        return jnp.concatenate([values[:, i : i + width] for i in range(0, bins, width)], axis=0)

    real, imag = whitened_pair(stacked(real), stacked(imag))
    for index in range(bins // width):
        lanes = pl.ds(index * width, width)
        out_ref[0, :, lanes] = real[index * PICK : (index + 1) * PICK]
        out_ref[1, :, lanes] = imag[index * PICK : (index + 1) * PICK]


def pick_rows(turns, counts, source_ids, pair_source, pair_offset, spectra, first_rows):
    _, chan_rows, parts, bins = spectra.shape
    smem = pl.BlockSpec(memory_space=pltpu.SMEM)
    vmem = pl.BlockSpec(memory_space=pltpu.VMEM)
    given = [] if turns is None else [turns]
    return pl.pallas_call(
        functools.partial(pick_kernel, chan_rows, chan_rows // 2, first_rows),
        out_shape=jax.ShapeDtypeStruct((parts, PICK, bins + EXTRA), spectra.dtype),
        in_specs=[smem] * len(given) + [vmem, smem, vmem, vmem, pl.BlockSpec(memory_space=pl.ANY)],
        out_specs=vmem,
        scratch_shapes=[
            pltpu.SMEM((PICK + 1,), jnp.int32),
            pltpu.VMEM((PICK, parts, bins), spectra.dtype),
            pltpu.SemaphoreType.DMA((PICK,)),
        ],
        cost_estimate=light(),
        compiler_params=params(8),
        name="pick_rows",
    )(
        *given,
        counts.reshape(1, 1),
        source_ids,
        pair_source.reshape(-1, EXTRA),
        pair_offset.reshape(-1, EXTRA),
        spectra,
    )


def block_mean(power):
    width = power.shape[1]
    row_group = lax.broadcasted_iota(jnp.int32, (width, width), 0) // WBLOCK
    col_group = lax.broadcasted_iota(jnp.int32, (width, width), 1) // WBLOCK
    spread = jnp.where(row_group == col_group, 1.0 / WBLOCK, 0.0).astype(jnp.bfloat16)
    high = power.astype(jnp.bfloat16)
    low = (power - high.astype(jnp.float32)).astype(jnp.bfloat16)
    total = jnp.dot(low, spread, preferred_element_type=jnp.float32)
    return total + jnp.dot(high, spread, preferred_element_type=jnp.float32)


def whitened_pair(real, imag):
    inverse = lax.rsqrt(block_mean(real * real + imag * imag) + 1e-06)
    return (real * inverse).astype(jnp.bfloat16), (imag * inverse).astype(jnp.bfloat16)


def whiten_kernel(cells_ref, after_ref, out_ref, token_ref):
    token_ref[...] = jnp.zeros_like(token_ref)
    for start in range(0, cells_ref.shape[2], 256):
        lanes = pl.ds(start, 256)
        real = cells_ref[0, :, lanes].astype(jnp.float32)
        imag = cells_ref[1, :, lanes].astype(jnp.float32)
        out_ref[0, :, lanes], out_ref[1, :, lanes] = whitened_pair(real, imag)


def whiten_rows(cells, after):
    _, rows, bins = cells.shape
    spec = pl.BlockSpec((2, rows, BINS_STEP), lambda i: (0, 0, i))
    return pl.pallas_call(
        whiten_kernel,
        grid=(bins // BINS_STEP,),
        out_shape=(jax.ShapeDtypeStruct(cells.shape, jnp.bfloat16), TOKEN),
        in_specs=[spec, pl.BlockSpec(memory_space=pl.ANY)],
        out_specs=(spec, whole(TOKEN.shape)),
        cost_estimate=light(),
        compiler_params=params(12),
        name="whiten_rows",
    )(cells, after)


def table_kernel(scale, all_bins, after_ref, cos_ref, sin_ref, token_ref, coarse_ref, fine_ref):
    token_ref[...] = jnp.zeros_like(token_ref)
    step = pl.program_id(0)
    groups = cos_ref.shape[0] // TABLE_ROWS

    @pl.when(step == 0)
    def _():
        def circle(ref, stride, factor):
            shape = ref.shape[1:]
            bins = lax.broadcasted_iota(jnp.int32, shape, 0) * stride
            lags = lax.broadcasted_iota(jnp.int32, shape, 1)
            lags = jnp.where(lags == 0, HALF, lags)
            theta = ((bins * lags) & (2 * all_bins - 1)).astype(jnp.float32) * (math.pi / all_bins)
            ref[0] = jnp.cos(theta) * factor
            ref[1] = jnp.sin(theta) * factor

        circle(coarse_ref, TABLE_ROWS, scale)
        circle(fine_ref, 1, 1.0)

    cos_b = fine_ref[0]
    sin_b = fine_ref[1]
    first = lax.broadcasted_iota(jnp.int32, cos_b.shape, 1) == 0
    for group in range(groups):
        cos_a = coarse_ref[0, pl.ds(step * groups + group, 1), :]
        sin_a = coarse_ref[1, pl.ds(step * groups + group, 1), :]
        rows = pl.ds(group * TABLE_ROWS, TABLE_ROWS)
        cos = jnp.where(first, scale, cos_a * cos_b - sin_a * sin_b)
        cos_ref[rows, :] = cos.astype(jnp.bfloat16)
        sin_ref[rows, :] = (sin_a * cos_b + cos_a * sin_b).astype(jnp.bfloat16)


def lag_tables(bins, scale, after):
    spec = pl.BlockSpec((BINS_STEP, HALF), lambda i: (i, 0))
    shape = jax.ShapeDtypeStruct((bins, HALF), jnp.bfloat16)
    return pl.pallas_call(
        functools.partial(table_kernel, scale, bins),
        grid=(bins // BINS_STEP,),
        out_shape=(shape, shape, TOKEN),
        in_specs=[pl.BlockSpec(memory_space=pl.ANY)],
        out_specs=(spec, spec, whole(TOKEN.shape)),
        scratch_shapes=[
            pltpu.VMEM((2, bins // TABLE_ROWS, HALF), jnp.float32),
            pltpu.VMEM((2, TABLE_ROWS, HALF), jnp.float32),
        ],
        cost_estimate=light(),
        compiler_params=params(12),
        name="lag_tables",
    )(after)


def source_spots(chan_rows, chan_size, me, turn, ids_row):
    count = ids_row.shape[1]
    shift = chan_rows.bit_length() - 1
    ids_row = jnp.broadcast_to(ids_row, (count, count))
    rows = lax.broadcasted_iota(jnp.int32, (count, count), 0)
    columns = lax.broadcasted_iota(jnp.int32, (count, count), 1)
    ids = jnp.sum(jnp.where(rows == columns, ids_row, 0).astype(jnp.float32), axis=1, keepdims=True)
    owner = jnp.broadcast_to(ids.astype(jnp.int32) >> shift, (count, count))
    earlier = (owner == (ids_row >> shift)) & (columns < rows)
    rank = jnp.sum(jnp.where(earlier, 1.0, 0.0), axis=1, keepdims=True)
    turns = (jnp.max(rank).astype(jnp.int32) + PICK) // PICK
    rank = rank.astype(jnp.int32) - turn * PICK
    owner = owner[:, 0:1]

    hop = ring_hop(me, owner, chan_size)
    return jnp.where((rank >= 0) & (rank < PICK), hop * PICK + rank, -1), turns


def flat(value):
    return jnp.concatenate([value[i : i + 1, :] for i in range(8)], axis=1)


def unlisted(halves, band):
    upper, lower = [half.astype(jnp.int32) for half in halves]
    return upper[0:8] - 1, upper[8:16] * 16 + (lower[0:8] & 15) - band, lower[0:8] >> 4


def ranked(taken):
    marks = jnp.concatenate([jnp.where(mask, 1.0, 0.0) for mask in taken], axis=0)
    rows = marks.shape[0]
    earlier = lax.broadcasted_iota(jnp.int32, (EXTRA, EXTRA), 0) < lax.broadcasted_iota(
        jnp.int32, (EXTRA, EXTRA), 1
    )
    rank = jnp.dot(
        marks.astype(jnp.bfloat16),
        jnp.where(earlier, 1.0, 0.0).astype(jnp.bfloat16),
        preferred_element_type=jnp.float32,
    )
    sums = jnp.broadcast_to(jnp.sum(marks, axis=1, keepdims=True), marks.shape)
    row = lax.broadcasted_iota(jnp.int32, (rows, rows), 0)
    column = lax.broadcasted_iota(jnp.int32, (rows, rows), 1)
    above_it = ((row >> 3) == (column >> 3)) & (column < row)
    rank = rank + jnp.dot(
        jnp.where(above_it, 1.0, 0.0).astype(jnp.bfloat16),
        sums.astype(jnp.bfloat16),
        preferred_element_type=jnp.float32,
    )
    rank = rank.astype(jnp.int32)
    return [rank[8 * i : 8 * i + 8] for i in range(len(taken))]


def jobs_of(spots, source, receiver, position, count):
    source, receiver, position = flat(source), flat(receiver), flat(position)
    slots = source.shape[1]
    names = lax.broadcasted_iota(jnp.int32, (spots.shape[0], slots), 0)
    field_row = lax.broadcasted_iota(jnp.int32, (8, slots), 0)
    spot = jnp.where(names == source, spots + 1, 0).astype(jnp.float32)
    spot = jnp.sum(spot, axis=0, keepdims=True).astype(jnp.int32) - 1
    fields = jnp.where(field_row == 0, spot >> 4, jnp.where(field_row == 1, spot & (PICK - 1), 0))
    fields = jnp.where(field_row == 2, receiver, jnp.where(field_row == 3, 1, fields))
    fields = jnp.where((position >= 0) & (spot >= 0), fields, 0)
    wanted = lax.broadcasted_iota(jnp.int32, (count, slots), 0)
    chosen = jnp.where(wanted == position, 1.0, 0.0).astype(jnp.bfloat16)
    return lax.dot_general(
        chosen,
        fields.astype(jnp.float32).astype(jnp.bfloat16),
        (((1,), (1,)), ((), ())),
        preferred_element_type=jnp.float32,
    )


def write_picks(jobs, start, src_ref, rec_ref):
    count = jobs.shape[0]
    jobs = jobs.astype(jnp.int32)
    busy = jobs[:, 3:4] > 0
    part = pl.ds(start, count)
    column = jnp.where(busy, jobs[:, 0:1] * PICK + jobs[:, 1:2], -1)
    lane = lax.broadcasted_iota(jnp.int32, (count, src_ref.shape[1]), 1)
    src_ref[part, :] = jnp.where(column == lane, 1.0, 0.0).astype(jnp.bfloat16)
    column = jnp.where(busy, jobs[:, 2:3], -1)
    lane = lax.broadcasted_iota(jnp.int32, (count, rec_ref.shape[1]), 1)
    rec_ref[part, :] = jnp.where(column == lane, 1.0, 0.0).astype(jnp.bfloat16)


def early_kernel(chan_rows, chan_size, turns_ref, ids_ref, after_ref, own_ref, src_ref, rec_ref, token_ref):
    token_ref[...] = jnp.zeros_like(token_ref)
    me = lax.axis_index("chan")
    count = src_ref.shape[0]
    lanes = pl.ds(own_ref.shape[2] - EXTRA, EXTRA)
    spots, _ = source_spots(chan_rows, chan_size, me, turns_ref[0], ids_ref[...])
    halves = [own_ref[half, :, lanes].astype(jnp.float32) for half in range(2)]
    source, offset, late = unlisted(halves, chan_rows // 2)
    early = (source >= 0) & (offset >= 0) & (offset < chan_rows) & (late == 0)
    (rank,) = ranked((early,))
    rank = jnp.where(early & (rank < count) & (turns_ref[1] == 0), rank, -1)
    write_picks(jobs_of(spots, source, offset, rank, count), 0, src_ref, rec_ref)


def prepare_early(turns, source_ids, own, chan_rows, chan_size, count, after):
    vmem = pl.BlockSpec(memory_space=pltpu.VMEM)
    return pl.pallas_call(
        functools.partial(early_kernel, chan_rows, chan_size),
        out_shape=(
            jax.ShapeDtypeStruct((count, chan_size * PICK), jnp.bfloat16),
            jax.ShapeDtypeStruct((count, chan_rows), jnp.bfloat16),
            TOKEN,
        ),
        in_specs=[
            pl.BlockSpec(memory_space=pltpu.SMEM), vmem, pl.BlockSpec(memory_space=pl.ANY), vmem,
        ],
        out_specs=(vmem, vmem, vmem),
        cost_estimate=light(),
        compiler_params=params(12),
        name="prepare_early",
    )(turns, source_ids.reshape(1, -1), after, own)


def prepare_kernel(chan_rows, chan_size, window, turns_ref, ids_ref, after_ref, passed_ref, *refs):
    chunk_refs = refs[:chan_size]
    src_ref, rec_ref, place_ref, needed_ref, _, token_ref = refs[chan_size:]
    token_ref[...] = jnp.zeros_like(token_ref)
    me = lax.axis_index("chan")
    turn = turns_ref[1]
    slots = place_ref.shape[1]
    room = 2 * window
    spots, needed = source_spots(chan_rows, chan_size, me, turns_ref[0], ids_ref[...])
    needed_ref[0] = needed

    lanes = pl.ds(chunk_refs[0].shape[2] - EXTRA, EXTRA)
    left_hop = jnp.where(me > 0, ring_hop(me, me - 1, chan_size), -1)
    right_hop = jnp.where(me < chan_size - 1, ring_hop(me, me + 1, chan_size), -1)
    listed = []
    for wanted in (left_hop, right_hop, 0):
        halves = []
        for half in range(2):
            value = jnp.zeros((PICK, EXTRA), jnp.float32)
            for hop, ref in enumerate(chunk_refs):
                value = jnp.where(wanted == hop, ref[half, :, lanes].astype(jnp.float32), value)
            halves.append(value)
        listed.append(unlisted(halves, chan_rows // 2))
    (left_src, left_off, _), (right_src, right_off, _), (own_src, own_off, own_late) = listed
    inside = (own_src >= 0) & (own_off >= 0) & (own_off < chan_rows)
    early = inside & (own_late == 0)
    taken = (
        (left_src >= 0) & (left_off >= chan_rows),
        (right_src >= 0) & (right_off < 0),
        (own_src >= 0) & (own_off < 0),
        (own_src >= 0) & (own_off >= chan_rows),
        inside,
        early,
    )
    ranks = ranked(taken)
    left_total = jnp.sum(jnp.where(taken[0], 1.0, 0.0)).astype(jnp.int32)
    right_total = jnp.sum(jnp.where(taken[1], 1.0, 0.0)).astype(jnp.int32)

    def done_before(amount, index):
        return jnp.minimum(amount, index * window)

    left_before = done_before(left_total, turn)
    right_before = done_before(right_total, turn)
    left_now = done_before(left_total, turn + 1) - left_before
    right_now = done_before(right_total, turn + 1) - right_before

    def in_window(index):
        shifted = ranks[index] - turn * window
        return shifted, taken[index] & (shifted >= 0) & (shifted < window)

    left_rank, left_ok = in_window(0)
    right_rank, right_ok = in_window(1)
    below_rank, below_ok = in_window(2)
    above_rank, above_ok = in_window(3)

    first = early & (ranks[5] < slots - room)
    own_rank = ranks[4] - jnp.minimum(ranks[5], slots - room)
    own_rank = own_rank - (turn * room - left_before - right_before)
    own_ok = inside & ~first & (own_rank >= 0) & (own_rank < room - left_now - right_now)
    own_pos = own_rank + left_now
    own_pos = jnp.where(own_pos < window, own_pos, own_pos + right_now)
    own_pos = jnp.where(own_ok, own_pos, -1)
    place = jnp.where(first & (turn == 0), ranks[5] + room, own_pos)
    place = jnp.where(below_ok, below_rank + slots, place)
    place = jnp.where(above_ok, above_rank + slots + window, place)
    place_ref[...] = jnp.broadcast_to(flat(place), place_ref.shape)

    left_jobs = jobs_of(spots, left_src, left_off - chan_rows, jnp.where(left_ok, left_rank, -1), window)
    right_jobs = jobs_of(
        spots, right_src, right_off + chan_rows, jnp.where(right_ok, right_rank, -1), window
    )
    own_jobs = jobs_of(spots, own_src, own_off, own_pos, room)
    write_picks(left_jobs + own_jobs[0:window], 0, src_ref, rec_ref)
    write_picks(right_jobs + own_jobs[window:room], window, src_ref, rec_ref)


def prepare(turns, source_ids, chunks, slots, chan_rows, window, after, passed):
    chan_size = len(chunks)
    vmem = pl.BlockSpec(memory_space=pltpu.VMEM)
    smem = pl.BlockSpec(memory_space=pltpu.SMEM)
    return pl.pallas_call(
        functools.partial(prepare_kernel, chan_rows, chan_size, window),
        out_shape=(
            jax.ShapeDtypeStruct((2 * window, chan_size * PICK), jnp.bfloat16),
            jax.ShapeDtypeStruct((2 * window, chan_rows), jnp.bfloat16),
            jax.ShapeDtypeStruct((8, slots), jnp.int32),
            jax.ShapeDtypeStruct((1,), jnp.int32),
            jax.ShapeDtypeStruct(passed.shape, passed.dtype),
            TOKEN,
        ),
        in_specs=[smem, vmem] + [pl.BlockSpec(memory_space=pl.ANY)] * 2 + [vmem] * len(chunks),
        out_specs=(vmem, vmem, vmem, smem, pl.BlockSpec(memory_space=pl.ANY), vmem),
        input_output_aliases={3: 4},
        cost_estimate=light(),
        compiler_params=params(16),
        name="prepare",
    )(turns, source_ids.reshape(1, -1), after, passed, *chunks)


def turns_kernel(chan_size, window, source_turns_ref, *refs):
    chunk_refs = refs[:chan_size]
    left_ref, pairs_ref = refs[-2:]
    me = lax.axis_index("chan")
    steps = chan_size // 2
    place = ring_place(me, chan_size)
    block = lax.broadcasted_iota(jnp.int32, (chan_size, EXTRA), 0)
    notes = jnp.zeros((chan_size, EXTRA), jnp.float32)
    for hop, ref in enumerate(chunk_refs):
        spot = place - hop if hop <= steps else place + hop - steps
        spot = jnp.where(spot < 0, spot + chan_size, spot)
        spot = jnp.where(spot >= chan_size, spot - chan_size, spot)
        owner = ring_block(spot, chan_size)
        notes = jnp.where(block == owner, ref[0][8:9, :].astype(jnp.float32), notes)
    lane = lax.broadcasted_iota(jnp.int32, notes.shape, 1)

    def total(index):
        value = jnp.where(lane == 2 * index, 32.0 * notes, 0.0)
        value = value + jnp.where(lane == 2 * index + 1, notes, 0.0)
        return jnp.broadcast_to(jnp.sum(value, axis=1, keepdims=True), notes.shape)

    left = jnp.where(block == 0, 0.0, pltpu.roll(total(0), 1, 0))
    right = jnp.where(block == chan_size - 1, 0.0, pltpu.roll(total(1), chan_size - 1, 0))
    aside = jnp.max(jnp.maximum(left, right)).astype(jnp.int32)
    whole_sum = jnp.max(left + right + total(2)).astype(jnp.int32)
    room = 2 * window
    needed = jnp.maximum((aside + window - 1) // window, (whole_sum + room - 1) // room)
    needed = jnp.maximum(needed, 1)
    pairs_ref[0] = needed
    left_ref[0] = needed * source_turns_ref[0] - 1


def count_turns(source_turns, chunks, window, after):
    _, _, width = chunks[0].shape
    last = width // EXTRA - 1
    specs = [pl.BlockSpec((1, PICK, EXTRA), lambda i: (1, 0, last)) for _ in chunks]
    return pl.pallas_call(
        functools.partial(turns_kernel, len(chunks), window),
        grid=(1,),
        out_shape=[jax.ShapeDtypeStruct((1,), jnp.int32)] * 2,
        in_specs=[pl.BlockSpec(memory_space=pltpu.SMEM), *specs]
        + [pl.BlockSpec(memory_space=pl.ANY)] * len(after),
        out_specs=[pl.BlockSpec(memory_space=pltpu.SMEM)] * 2,
        cost_estimate=light(),
        compiler_params=params(8),
        name="count_turns",
    )(source_turns, *chunks, *after)


def transform_kernel(shards, scale, start, chunks, src_ref, rec_ref, *refs):
    chunk_refs = refs[:chunks]
    cells_ref, cos_ref, sin_ref = refs[chunks : chunks + 3]
    keep_ref, send_ref, token_ref = refs[-3:]
    token_ref[...] = jnp.zeros_like(token_ref)
    rows = keep_ref.shape[1]
    bins = cos_ref.shape[0]
    step = min(TRANSFORM_STEP, bins)
    eighth = lax.broadcasted_iota(jnp.int32, (1, 128), 1) & 7
    root = math.sqrt(0.5)
    edge = jnp.where((eighth == 1) | (eighth == 7), root, 0.0)
    edge = jnp.where((eighth == 3) | (eighth == 5), -root, edge)
    edge = jnp.where(eighth == 0, 1.0, jnp.where(eighth == 4, -1.0, edge)) * scale
    edge = edge.astype(jnp.bfloat16).astype(jnp.float32)

    by_src = src_ref[pl.ds(start, rows), :]
    by_rec = rec_ref[pl.ds(start, rows), :]
    even = odd = corner = None
    for first in range(0, bins, step):
        lanes = pl.ds(first, step)
        source_real = jnp.concatenate([ref[0, :, lanes] for ref in chunk_refs], axis=0)
        source_imag = jnp.concatenate([ref[1, :, lanes] for ref in chunk_refs], axis=0)
        sr = jnp.dot(by_src, source_real, preferred_element_type=jnp.float32)
        si = jnp.dot(by_src, source_imag, preferred_element_type=jnp.float32)
        rr = jnp.dot(by_rec, cells_ref[0, :, lanes], preferred_element_type=jnp.float32)
        ri = jnp.dot(by_rec, cells_ref[1, :, lanes], preferred_element_type=jnp.float32)
        real = (sr * rr + si * ri).astype(jnp.bfloat16)
        imag = (si * rr - sr * ri).astype(jnp.bfloat16)
        more_even = jnp.dot(real, cos_ref[lanes, :], preferred_element_type=jnp.float32)
        more_odd = jnp.dot(imag, sin_ref[lanes, :], preferred_element_type=jnp.float32)
        wide = real.astype(jnp.float32)
        sums = wide[:, 0:128]
        for lane in range(128, step, 128):
            sums = sums + wide[:, lane : lane + 128]
        even = more_even if even is None else even + more_even
        odd = more_odd if odd is None else odd + more_odd
        corner = sums if corner is None else corner + sums

    me = lax.axis_index("seg")
    width = LAGS // shards
    corner = jnp.sum(corner * edge, axis=1, keepdims=True)
    first = lax.broadcasted_iota(jnp.int32, even.shape, 1) == 0
    later = even - jnp.where(first, 0.0, odd)
    sooner = jnp.where(first, corner, even) + odd
    sooner = pltpu.roll(sooner, HALF - 1, 1)
    for shard in range(shards):
        half = shards // 2
        if shard < half:
            lane = (half - 1 - shard) * width
            value = sooner[:, lane : lane + width]
        else:
            lane = (shard - half) * width
            value = later[:, lane : lane + width]
        place = me ^ shard

        @pl.when((place & 1) == 0)
        def _():
            keep_ref[place >> 1] = value

        @pl.when((place & 1) == 1)
        def _():
            send_ref[place >> 1] = value.astype(jnp.bfloat16)


def transform(picks, chunks, cells, tables, shards, scale, start, rows, weight, *after):
    width = LAGS // shards
    shape = (shards // 2, rows, width)
    vmem = pl.BlockSpec(memory_space=pltpu.VMEM)
    return pl.pallas_call(
        functools.partial(transform_kernel, shards, scale, start, len(chunks)),
        out_shape=(
            jax.ShapeDtypeStruct(shape, jnp.float32),
            jax.ShapeDtypeStruct(shape, jnp.bfloat16),
            TOKEN,
        ),
        in_specs=[vmem] * (5 + len(chunks))
        + [pl.BlockSpec(memory_space=pl.ANY)] * len(after),
        out_specs=(vmem, vmem, vmem),
        cost_estimate=weight,
        compiler_params=params(16),
        name="transform",
    )(*picks, *chunks, cells, *tables, *after)


def swap(send, bit):
    size = lax.axis_size("seg")
    return lax.ppermute(send, "seg", [(i, i ^ bit) for i in range(size)])


def halve(keep, got):
    total = keep + got.astype(jnp.float32)
    return total[0::2], total[1::2].astype(jnp.bfloat16)


def reduce_further(keep, got, bit):
    while keep.shape[0] > 1:
        keep, send = halve(keep, got)
        bit *= 2
        got = swap(send, bit)
    return (keep[0] + got[0].astype(jnp.float32)).astype(jnp.bfloat16)


def turned_parts(refs):
    width = refs[0].shape[1]
    flip = lax.axis_index("seg") < lax.axis_size("seg") // 2
    rows = lax.broadcasted_iota(jnp.int32, (width, width), 0)
    columns = lax.broadcasted_iota(jnp.int32, (width, width), 1)
    wanted = jnp.where(flip, width - 1 - rows, rows)
    turned = jnp.where(wanted == columns, 1.0, 0.0).astype(jnp.bfloat16)
    return [
        lax.dot_general(
            turned, ref[...], (((1,), (1,)), ((), ())), preferred_element_type=jnp.float32
        ).astype(jnp.bfloat16)
        for ref in refs
    ]


def place_kernel(place_ref, *refs):
    parts, (out_ref, later_ref) = refs[:-2], refs[-2:]
    slots = out_ref.shape[1]

    def chosen(start, count):
        spot = lax.broadcasted_iota(jnp.int32, (count, slots), 0) + start
        return jnp.where(spot == place_ref[0:1, :], 1.0, 0.0).astype(jnp.bfloat16)

    total = None
    start = 0
    for part in turned_parts(parts):
        count = part.shape[1]
        more = jnp.dot(part, chosen(start, count), preferred_element_type=jnp.float32)
        total = more if total is None else total + more
        start += count
    out_ref[...] = total
    later_ref[...] = chosen(start, later_ref.shape[0])


def place_rows(place, parts, later):
    width = parts[0].shape[1]
    slots = place.shape[1]
    vmem = pl.BlockSpec(memory_space=pltpu.VMEM)
    return pl.pallas_call(
        place_kernel,
        out_shape=(
            jax.ShapeDtypeStruct((width, slots), jnp.float32),
            jax.ShapeDtypeStruct((later, slots), jnp.bfloat16),
        ),
        in_specs=[vmem] * (1 + len(parts)),
        out_specs=(vmem, vmem),
        cost_estimate=light(),
        compiler_params=params(16),
        name="place_rows",
    )(place, *parts)


def add_kernel(total_ref, chosen_ref, *refs):
    parts, (out_ref, made_ref, sems) = refs[:-3], refs[-3:]
    slots = made_ref.shape[1]
    step = min(256, slots)
    across = jnp.concatenate(turned_parts(parts), axis=1)
    copies = []
    for index in range(slots // step):
        lanes = pl.ds(index * step, step)
        made_ref[:, lanes] = total_ref[:, lanes] + jnp.dot(
            across, chosen_ref[:, lanes], preferred_element_type=jnp.float32
        )
        copy = pltpu.make_async_copy(made_ref.at[:, lanes], out_ref.at[:, lanes], sems.at[index])
        copy.start()
        copies.append(copy)
    for copy in copies:
        copy.wait()


def add_rows(total, chosen, parts):
    width, slots = total.shape
    vmem = pl.BlockSpec(memory_space=pltpu.VMEM)
    return pl.pallas_call(
        add_kernel,
        out_shape=jax.ShapeDtypeStruct((width, slots), jnp.float32),
        in_specs=[vmem] * (2 + len(parts)),
        out_specs=pl.BlockSpec(memory_space=pltpu.HBM),
        scratch_shapes=[
            pltpu.VMEM((width, slots), jnp.float32),
            pltpu.SemaphoreType.DMA((slots // min(256, slots),)),
        ],
        cost_estimate=light(),
        compiler_params=params(16),
        name="add_rows",
    )(total, chosen, *parts)


def per_device(spectra, source_ids, pair_source, pair_offset, pair_counts):
    chan_rows = spectra.shape[1]
    bins = spectra.shape[3]
    seg_size = lax.axis_size("seg")
    chan_size = lax.axis_size("chan")
    slots = pair_source.shape[0]
    window = 3 * slots // 8
    scale = 1.0 / math.sqrt(bins * seg_size)
    join = lax.optimization_barrier

    ring = list(range(0, chan_size, 2)) + list(range(1, chan_size, 2))[::-1]
    ahead = [(ring[i], ring[(i + 1) % chan_size]) for i in range(chan_size)]
    back = [(b, a) for a, b in ahead]
    leftward = [(i + 1, i) for i in range(chan_size - 1)]
    rightward = [(i, i + 1) for i in range(chan_size - 1)]

    def one_turn(turns):
        first_rows = slots - 2 * window
        own = pick_rows(turns, pair_counts, source_ids, pair_source, pair_offset, spectra, first_rows)
        if turns is None:
            turns = jnp.zeros((2,), jnp.int32)
        forward, backward = [own], [own]
        steps = chan_size // 2

        def step_beside(work=None):
            ahead_of = forward[-1], backward[-1]
            forward.append(lax.ppermute(ahead_of[0], "chan", ahead))
            if len(backward) < chan_size - steps:
                backward.append(lax.ppermute(ahead_of[1], "chan", back))
            if work is not None:
                *results, token = work()
                if len(backward) == len(forward):
                    token, forward[-1], backward[-1] = join((token, forward[-1], backward[-1]))
                else:
                    token, forward[-1] = join((token, forward[-1]))
                return results, token

        tables, token = step_beside(lambda: lag_tables(bins, scale, own))
        cells = jnp.transpose(spectra[0], (1, 0, 2))
        (whitened,), token = step_beside(lambda: whiten_rows(cells, token))
        for _ in range(3, steps - 1):
            step_beside()
        picks, token = step_beside(
            lambda: prepare_early(turns, source_ids, own, chan_rows, chan_size, first_rows, token)
        )

        def piece(picks, chunks, start, rows, *after, weight=light()):
            return transform(
                picks, chunks, whitened, tables, seg_size, scale, start, rows, weight, *after
            )

        chunks = [*forward, own, *backward[1:]]
        full = pl.CostEstimate(
            flops=first_rows * bins * 4096, bytes_accessed=16 * bins * HALF, transcendentals=0
        )
        (keep_own, send), token = step_beside(
            lambda: piece(picks, chunks, 0, first_rows, token, weight=full)
        )
        chunks = forward + backward[1:]
        *picks, place, source_turns, send, token = prepare(
            turns, source_ids, chunks, slots, chan_rows, window, token, send
        )
        got_own = swap(send, 1)
        keep_left, send, token = piece(picks, chunks, 0, window, token)
        token, got_own = join((token, got_own))
        keep_own, send_own = halve(keep_own, got_own)
        got_left = swap(send, 1)
        got_own = swap(send_own, 2)
        keep_right, send, token = piece(picks, chunks, window, window, token, send_own)
        token, got_left, got_own = join((token, got_left, got_own))
        got_right = swap(send, 1)
        left = reduce_further(keep_left, got_left, 1)
        right = reduce_further(keep_right, got_right, 1)
        own = reduce_further(keep_own, got_own, 2)
        from_right = lax.ppermute(left, "chan", leftward)
        from_left = lax.ppermute(right, "chan", rightward)
        total, chosen = place_rows(place, (left, right, own), 2 * window)
        result = add_rows(total, chosen, (from_left, from_right))
        return result, (right, token), chunks, source_turns

    first, after, chunks, source_turns = one_turn(None)
    turns_left, pair_turns = [count[0] for count in count_turns(source_turns, chunks, window, after)]

    def further(state):
        turn, total = state
        turns = jnp.stack([lax.div(turn, pair_turns), lax.rem(turn, pair_turns)])
        return turn - 1, total + one_turn(turns)[0]

    return lax.while_loop(lambda state: state[0] > 0, further, (turns_left, first))[1]


def solution(mesh):
    in_specs = (P("seg", "chan", None, None), P(), P("chan"), P("chan"), P("chan"))
    out_specs = P("seg", "chan")
    return jax.shard_map(
        per_device, mesh=mesh, in_specs=in_specs, out_specs=out_specs, check_vma=False
    )
```

```python
import functools
import math

import jax
import jax.numpy as jnp
from jax import lax
from jax.experimental import pallas as pl
from jax.experimental.pallas import tpu as pltpu
from jax.sharding import PartitionSpec as P

LAGS = 1024
HALF = LAGS // 2
WBLOCK = 64
PICK = 16
BINS_STEP = 512
TRANSFORM_STEP = 256
TABLE_ROWS = 64
EXTRA = 128


def params(mebibytes):
    return pltpu.CompilerParams(vmem_limit_bytes=mebibytes * 1024 * 1024)


def light():
    return pl.CostEstimate(flops=1024, bytes_accessed=1024, transcendentals=0)


TOKEN = jax.ShapeDtypeStruct((8, 128), jnp.float32)


def whole(shape):
    return pl.BlockSpec(shape, lambda *_: (0,) * len(shape))


def ring_place(block, chan_size):
    return jnp.where((block & 1) == 0, block >> 1, chan_size - 1 - (block >> 1))


def ring_block(place, chan_size):
    return jnp.where(place < chan_size // 2, 2 * place, 2 * (chan_size - place) - 1)


def far_block(me, chan_size):
    place = ring_place(me, chan_size) - chan_size // 2
    return ring_block(jnp.where(place < 0, place + chan_size, place), chan_size)


def ring_hop(me, block, chan_size):
    steps = chan_size // 2
    distance = ring_place(me, chan_size) - ring_place(block, chan_size)
    distance = jnp.where(distance < 0, distance + chan_size, distance)
    return jnp.where(distance <= steps, distance, steps + chan_size - distance)


def pick_kernel(chan_rows, band, first_rows, *refs):
    counts_ref, ids_ref, source_ref, offset_ref, cells_ref, out_ref, rows_ref, held_ref, sems = refs[-9:]
    first = lax.axis_index("chan") * chan_rows
    turn = refs[0][0] if len(refs) > 9 else 0
    bins = cells_ref.shape[3]
    for i in range(PICK):
        rows_ref[i] = 0
    rank = jnp.int32(0)
    for i in range(ids_ref.shape[0]):
        row = ids_ref[i] - first
        mine = (row >= 0) & (row < chan_rows)
        spot = rank - turn * PICK
        rows_ref[jnp.where(mine & (spot >= 0) & (spot < PICK), spot, PICK)] = row
        rank = rank + mine.astype(jnp.int32)
    far = far_block(lax.axis_index("chan"), lax.axis_size("chan")) * chan_rows
    late = [jnp.int32(0), jnp.int32(0)]
    for i in range(ids_ref.shape[0]):
        row = ids_ref[i] - far
        late[i // 32] = late[i // 32] | (((row >= 0) & (row < chan_rows)).astype(jnp.int32) << (i % 32))
    copies = [
        pltpu.make_async_copy(cells_ref.at[0, rows_ref[i]], held_ref.at[i], sems.at[i])
        for i in range(PICK)
    ]
    for copy in copies:
        copy.start()

    offset = offset_ref[...]
    slot = lax.broadcasted_iota(jnp.int32, offset.shape, 0) * offset.shape[1]
    slot = slot + lax.broadcasted_iota(jnp.int32, offset.shape, 1)
    live = slot < counts_ref[...]
    source = source_ref[...]
    bits = jnp.where(source < 32, late[0], late[1])
    is_late = lax.shift_right_logical(bits, source & 31) & 1
    inside = live & (offset >= 0) & (offset < chan_rows)
    kinds = (live & (offset >= chan_rows), live & (offset < 0), inside, inside & (is_late == 0))
    lane = lax.broadcasted_iota(jnp.int32, offset.shape, 1)
    notes = jnp.zeros(offset.shape, jnp.int32)
    totals = [jnp.sum(jnp.where(kind, 1.0, 0.0)).astype(jnp.int32) for kind in kinds]
    totals = (totals[0], totals[1], totals[2] - jnp.minimum(totals[3], first_rows))
    for index, total in enumerate(totals):
        notes = jnp.where(lane == 2 * index, total >> 5, notes)
        notes = jnp.where(lane == 2 * index + 1, total & 31, notes)
    shifted = offset + band
    source = jnp.where(live, source + 1, 0)

    def coded(upper, lower):
        both = jnp.concatenate([upper.astype(jnp.float32), lower.astype(jnp.float32)], axis=0)
        return both.astype(jnp.bfloat16)

    out_ref[0, :, pl.ds(bins, EXTRA)] = coded(source, shifted >> 4)
    out_ref[1, :, pl.ds(bins, EXTRA)] = coded((shifted & 15) + 16 * is_late, notes)

    for copy in copies:
        copy.wait()
    real = held_ref[:, 0, :].astype(jnp.float32)
    imag = held_ref[:, 1, :].astype(jnp.float32)
    width = min(256, bins)

    def stacked(values):
        return jnp.concatenate([values[:, i : i + width] for i in range(0, bins, width)], axis=0)

    real, imag = whitened_pair(stacked(real), stacked(imag))
    for index in range(bins // width):
        lanes = pl.ds(index * width, width)
        out_ref[0, :, lanes] = real[index * PICK : (index + 1) * PICK]
        out_ref[1, :, lanes] = imag[index * PICK : (index + 1) * PICK]


def pick_rows(turns, counts, source_ids, pair_source, pair_offset, spectra, first_rows):
    _, chan_rows, parts, bins = spectra.shape
    smem = pl.BlockSpec(memory_space=pltpu.SMEM)
    vmem = pl.BlockSpec(memory_space=pltpu.VMEM)
    given = [] if turns is None else [turns]
    return pl.pallas_call(
        functools.partial(pick_kernel, chan_rows, chan_rows // 2, first_rows),
        out_shape=jax.ShapeDtypeStruct((parts, PICK, bins + EXTRA), spectra.dtype),
        in_specs=[smem] * len(given) + [vmem, smem, vmem, vmem, pl.BlockSpec(memory_space=pl.ANY)],
        out_specs=vmem,
        scratch_shapes=[
            pltpu.SMEM((PICK + 1,), jnp.int32),
            pltpu.VMEM((PICK, parts, bins), spectra.dtype),
            pltpu.SemaphoreType.DMA((PICK,)),
        ],
        cost_estimate=light(),
        compiler_params=params(8),
        name="pick_rows",
    )(
        *given,
        counts.reshape(1, 1),
        source_ids,
        pair_source.reshape(-1, EXTRA),
        pair_offset.reshape(-1, EXTRA),
        spectra,
    )


def block_mean(power):
    width = power.shape[1]
    row_group = lax.broadcasted_iota(jnp.int32, (width, width), 0) // WBLOCK
    col_group = lax.broadcasted_iota(jnp.int32, (width, width), 1) // WBLOCK
    spread = jnp.where(row_group == col_group, 1.0 / WBLOCK, 0.0).astype(jnp.bfloat16)
    high = power.astype(jnp.bfloat16)
    low = (power - high.astype(jnp.float32)).astype(jnp.bfloat16)
    total = jnp.dot(low, spread, preferred_element_type=jnp.float32)
    return total + jnp.dot(high, spread, preferred_element_type=jnp.float32)


def whitened_pair(real, imag):
    inverse = lax.rsqrt(block_mean(real * real + imag * imag) + 1e-06)
    return (real * inverse).astype(jnp.bfloat16), (imag * inverse).astype(jnp.bfloat16)


def whiten_kernel(cells_ref, after_ref, out_ref, token_ref):
    token_ref[...] = jnp.zeros_like(token_ref)
    for start in range(0, cells_ref.shape[2], 256):
        lanes = pl.ds(start, 256)
        real = cells_ref[0, :, lanes].astype(jnp.float32)
        imag = cells_ref[1, :, lanes].astype(jnp.float32)
        out_ref[0, :, lanes], out_ref[1, :, lanes] = whitened_pair(real, imag)


def whiten_rows(cells, after):
    _, rows, bins = cells.shape
    spec = pl.BlockSpec((2, rows, BINS_STEP), lambda i: (0, 0, i))
    return pl.pallas_call(
        whiten_kernel,
        grid=(bins // BINS_STEP,),
        out_shape=(jax.ShapeDtypeStruct(cells.shape, jnp.bfloat16), TOKEN),
        in_specs=[spec, pl.BlockSpec(memory_space=pl.ANY)],
        out_specs=(spec, whole(TOKEN.shape)),
        cost_estimate=light(),
        compiler_params=params(12),
        name="whiten_rows",
    )(cells, after)


def table_kernel(scale, all_bins, after_ref, cos_ref, sin_ref, token_ref, coarse_ref, fine_ref):
    token_ref[...] = jnp.zeros_like(token_ref)
    step = pl.program_id(0)
    groups = cos_ref.shape[0] // TABLE_ROWS

    @pl.when(step == 0)
    def _():
        def circle(ref, stride, factor):
            shape = ref.shape[1:]
            bins = lax.broadcasted_iota(jnp.int32, shape, 0) * stride
            lags = lax.broadcasted_iota(jnp.int32, shape, 1)
            lags = jnp.where(lags == 0, HALF, lags)
            theta = ((bins * lags) & (2 * all_bins - 1)).astype(jnp.float32) * (math.pi / all_bins)
            ref[0] = jnp.cos(theta) * factor
            ref[1] = jnp.sin(theta) * factor

        circle(coarse_ref, TABLE_ROWS, scale)
        circle(fine_ref, 1, 1.0)

    cos_b = fine_ref[0]
    sin_b = fine_ref[1]
    first = lax.broadcasted_iota(jnp.int32, cos_b.shape, 1) == 0
    for group in range(groups):
        cos_a = coarse_ref[0, pl.ds(step * groups + group, 1), :]
        sin_a = coarse_ref[1, pl.ds(step * groups + group, 1), :]
        rows = pl.ds(group * TABLE_ROWS, TABLE_ROWS)
        cos = jnp.where(first, scale, cos_a * cos_b - sin_a * sin_b)
        cos_ref[rows, :] = cos.astype(jnp.bfloat16)
        sin_ref[rows, :] = (sin_a * cos_b + cos_a * sin_b).astype(jnp.bfloat16)


def lag_tables(bins, scale, after):
    spec = pl.BlockSpec((BINS_STEP, HALF), lambda i: (i, 0))
    shape = jax.ShapeDtypeStruct((bins, HALF), jnp.bfloat16)
    return pl.pallas_call(
        functools.partial(table_kernel, scale, bins),
        grid=(bins // BINS_STEP,),
        out_shape=(shape, shape, TOKEN),
        in_specs=[pl.BlockSpec(memory_space=pl.ANY)],
        out_specs=(spec, spec, whole(TOKEN.shape)),
        scratch_shapes=[
            pltpu.VMEM((2, bins // TABLE_ROWS, HALF), jnp.float32),
            pltpu.VMEM((2, TABLE_ROWS, HALF), jnp.float32),
        ],
        cost_estimate=light(),
        compiler_params=params(12),
        name="lag_tables",
    )(after)


def source_spots(chan_rows, chan_size, me, turn, ids_row):
    count = ids_row.shape[1]
    shift = chan_rows.bit_length() - 1
    ids_row = jnp.broadcast_to(ids_row, (count, count))
    rows = lax.broadcasted_iota(jnp.int32, (count, count), 0)
    columns = lax.broadcasted_iota(jnp.int32, (count, count), 1)
    ids = jnp.sum(jnp.where(rows == columns, ids_row, 0).astype(jnp.float32), axis=1, keepdims=True)
    owner = jnp.broadcast_to(ids.astype(jnp.int32) >> shift, (count, count))
    earlier = (owner == (ids_row >> shift)) & (columns < rows)
    rank = jnp.sum(jnp.where(earlier, 1.0, 0.0), axis=1, keepdims=True)
    turns = (jnp.max(rank).astype(jnp.int32) + PICK) // PICK
    rank = rank.astype(jnp.int32) - turn * PICK
    owner = owner[:, 0:1]

    hop = ring_hop(me, owner, chan_size)
    return jnp.where((rank >= 0) & (rank < PICK), hop * PICK + rank, -1), turns


def flat(value):
    return jnp.concatenate([value[i : i + 1, :] for i in range(8)], axis=1)


def unlisted(halves, band):
    upper, lower = [half.astype(jnp.int32) for half in halves]
    return upper[0:8] - 1, upper[8:16] * 16 + (lower[0:8] & 15) - band, lower[0:8] >> 4


def ranked(taken):
    marks = jnp.concatenate([jnp.where(mask, 1.0, 0.0) for mask in taken], axis=0)
    rows = marks.shape[0]
    earlier = lax.broadcasted_iota(jnp.int32, (EXTRA, EXTRA), 0) < lax.broadcasted_iota(
        jnp.int32, (EXTRA, EXTRA), 1
    )
    rank = jnp.dot(
        marks.astype(jnp.bfloat16),
        jnp.where(earlier, 1.0, 0.0).astype(jnp.bfloat16),
        preferred_element_type=jnp.float32,
    )
    sums = jnp.broadcast_to(jnp.sum(marks, axis=1, keepdims=True), marks.shape)
    row = lax.broadcasted_iota(jnp.int32, (rows, rows), 0)
    column = lax.broadcasted_iota(jnp.int32, (rows, rows), 1)
    above_it = ((row >> 3) == (column >> 3)) & (column < row)
    rank = rank + jnp.dot(
        jnp.where(above_it, 1.0, 0.0).astype(jnp.bfloat16),
        sums.astype(jnp.bfloat16),
        preferred_element_type=jnp.float32,
    )
    rank = rank.astype(jnp.int32)
    return [rank[8 * i : 8 * i + 8] for i in range(len(taken))]


def jobs_of(spots, source, receiver, position, count):
    source, receiver, position = flat(source), flat(receiver), flat(position)
    slots = source.shape[1]
    names = lax.broadcasted_iota(jnp.int32, (spots.shape[0], slots), 0)
    field_row = lax.broadcasted_iota(jnp.int32, (8, slots), 0)
    spot = jnp.where(names == source, spots + 1, 0).astype(jnp.float32)
    spot = jnp.sum(spot, axis=0, keepdims=True).astype(jnp.int32) - 1
    fields = jnp.where(field_row == 0, spot >> 4, jnp.where(field_row == 1, spot & (PICK - 1), 0))
    fields = jnp.where(field_row == 2, receiver, jnp.where(field_row == 3, 1, fields))
    fields = jnp.where((position >= 0) & (spot >= 0), fields, 0)
    wanted = lax.broadcasted_iota(jnp.int32, (count, slots), 0)
    chosen = jnp.where(wanted == position, 1.0, 0.0).astype(jnp.bfloat16)
    return lax.dot_general(
        chosen,
        fields.astype(jnp.float32).astype(jnp.bfloat16),
        (((1,), (1,)), ((), ())),
        preferred_element_type=jnp.float32,
    )


def write_picks(jobs, start, src_ref, rec_ref):
    count = jobs.shape[0]
    jobs = jobs.astype(jnp.int32)
    busy = jobs[:, 3:4] > 0
    part = pl.ds(start, count)
    column = jnp.where(busy, jobs[:, 0:1] * PICK + jobs[:, 1:2], -1)
    lane = lax.broadcasted_iota(jnp.int32, (count, src_ref.shape[1]), 1)
    src_ref[part, :] = jnp.where(column == lane, 1.0, 0.0).astype(jnp.bfloat16)
    column = jnp.where(busy, jobs[:, 2:3], -1)
    lane = lax.broadcasted_iota(jnp.int32, (count, rec_ref.shape[1]), 1)
    rec_ref[part, :] = jnp.where(column == lane, 1.0, 0.0).astype(jnp.bfloat16)


def early_kernel(chan_rows, chan_size, turns_ref, ids_ref, after_ref, own_ref, src_ref, rec_ref, token_ref):
    token_ref[...] = jnp.zeros_like(token_ref)
    me = lax.axis_index("chan")
    count = src_ref.shape[0]
    lanes = pl.ds(own_ref.shape[2] - EXTRA, EXTRA)
    spots, _ = source_spots(chan_rows, chan_size, me, turns_ref[0], ids_ref[...])
    halves = [own_ref[half, :, lanes].astype(jnp.float32) for half in range(2)]
    source, offset, late = unlisted(halves, chan_rows // 2)
    early = (source >= 0) & (offset >= 0) & (offset < chan_rows) & (late == 0)
    (rank,) = ranked((early,))
    rank = jnp.where(early & (rank < count) & (turns_ref[1] == 0), rank, -1)
    write_picks(jobs_of(spots, source, offset, rank, count), 0, src_ref, rec_ref)


def prepare_early(turns, source_ids, own, chan_rows, chan_size, count, after):
    vmem = pl.BlockSpec(memory_space=pltpu.VMEM)
    return pl.pallas_call(
        functools.partial(early_kernel, chan_rows, chan_size),
        out_shape=(
            jax.ShapeDtypeStruct((count, chan_size * PICK), jnp.bfloat16),
            jax.ShapeDtypeStruct((count, chan_rows), jnp.bfloat16),
            TOKEN,
        ),
        in_specs=[
            pl.BlockSpec(memory_space=pltpu.SMEM), vmem, pl.BlockSpec(memory_space=pl.ANY), vmem,
        ],
        out_specs=(vmem, vmem, vmem),
        cost_estimate=light(),
        compiler_params=params(12),
        name="prepare_early",
    )(turns, source_ids.reshape(1, -1), after, own)


def prepare_kernel(chan_rows, chan_size, window, turns_ref, ids_ref, after_ref, passed_ref, *refs):
    chunk_refs = refs[:chan_size]
    src_ref, rec_ref, place_ref, needed_ref, _, token_ref = refs[chan_size:]
    token_ref[...] = jnp.zeros_like(token_ref)
    me = lax.axis_index("chan")
    turn = turns_ref[1]
    slots = place_ref.shape[1]
    room = 2 * window
    spots, needed = source_spots(chan_rows, chan_size, me, turns_ref[0], ids_ref[...])
    needed_ref[0] = needed

    lanes = pl.ds(chunk_refs[0].shape[2] - EXTRA, EXTRA)
    left_hop = jnp.where(me > 0, ring_hop(me, me - 1, chan_size), -1)
    right_hop = jnp.where(me < chan_size - 1, ring_hop(me, me + 1, chan_size), -1)
    listed = []
    for wanted in (left_hop, right_hop, 0):
        halves = []
        for half in range(2):
            value = jnp.zeros((PICK, EXTRA), jnp.float32)
            for hop, ref in enumerate(chunk_refs):
                value = jnp.where(wanted == hop, ref[half, :, lanes].astype(jnp.float32), value)
            halves.append(value)
        listed.append(unlisted(halves, chan_rows // 2))
    (left_src, left_off, _), (right_src, right_off, _), (own_src, own_off, own_late) = listed
    inside = (own_src >= 0) & (own_off >= 0) & (own_off < chan_rows)
    early = inside & (own_late == 0)
    taken = (
        (left_src >= 0) & (left_off >= chan_rows),
        (right_src >= 0) & (right_off < 0),
        (own_src >= 0) & (own_off < 0),
        (own_src >= 0) & (own_off >= chan_rows),
        inside,
        early,
    )
    ranks = ranked(taken)
    left_total = jnp.sum(jnp.where(taken[0], 1.0, 0.0)).astype(jnp.int32)
    right_total = jnp.sum(jnp.where(taken[1], 1.0, 0.0)).astype(jnp.int32)

    def done_before(amount, index):
        return jnp.minimum(amount, index * window)

    left_before = done_before(left_total, turn)
    right_before = done_before(right_total, turn)
    left_now = done_before(left_total, turn + 1) - left_before
    right_now = done_before(right_total, turn + 1) - right_before

    def in_window(index):
        shifted = ranks[index] - turn * window
        return shifted, taken[index] & (shifted >= 0) & (shifted < window)

    left_rank, left_ok = in_window(0)
    right_rank, right_ok = in_window(1)
    below_rank, below_ok = in_window(2)
    above_rank, above_ok = in_window(3)

    first = early & (ranks[5] < slots - room)
    own_rank = ranks[4] - jnp.minimum(ranks[5], slots - room)
    own_rank = own_rank - (turn * room - left_before - right_before)
    own_ok = inside & ~first & (own_rank >= 0) & (own_rank < room - left_now - right_now)
    own_pos = own_rank + left_now
    own_pos = jnp.where(own_pos < window, own_pos, own_pos + right_now)
    own_pos = jnp.where(own_ok, own_pos, -1)
    place = jnp.where(first & (turn == 0), ranks[5] + room, own_pos)
    place = jnp.where(below_ok, below_rank + slots, place)
    place = jnp.where(above_ok, above_rank + slots + window, place)
    place_ref[...] = jnp.broadcast_to(flat(place), place_ref.shape)

    left_jobs = jobs_of(spots, left_src, left_off - chan_rows, jnp.where(left_ok, left_rank, -1), window)
    right_jobs = jobs_of(
        spots, right_src, right_off + chan_rows, jnp.where(right_ok, right_rank, -1), window
    )
    own_jobs = jobs_of(spots, own_src, own_off, own_pos, room)
    write_picks(left_jobs + own_jobs[0:window], 0, src_ref, rec_ref)
    write_picks(right_jobs + own_jobs[window:room], window, src_ref, rec_ref)


def prepare(turns, source_ids, chunks, slots, chan_rows, window, after, passed):
    chan_size = len(chunks)
    vmem = pl.BlockSpec(memory_space=pltpu.VMEM)
    smem = pl.BlockSpec(memory_space=pltpu.SMEM)
    return pl.pallas_call(
        functools.partial(prepare_kernel, chan_rows, chan_size, window),
        out_shape=(
            jax.ShapeDtypeStruct((2 * window, chan_size * PICK), jnp.bfloat16),
            jax.ShapeDtypeStruct((2 * window, chan_rows), jnp.bfloat16),
            jax.ShapeDtypeStruct((8, slots), jnp.int32),
            jax.ShapeDtypeStruct((1,), jnp.int32),
            jax.ShapeDtypeStruct(passed.shape, passed.dtype),
            TOKEN,
        ),
        in_specs=[smem, vmem] + [pl.BlockSpec(memory_space=pl.ANY)] * 2 + [vmem] * len(chunks),
        out_specs=(vmem, vmem, vmem, smem, pl.BlockSpec(memory_space=pl.ANY), vmem),
        input_output_aliases={3: 4},
        cost_estimate=light(),
        compiler_params=params(16),
        name="prepare",
    )(turns, source_ids.reshape(1, -1), after, passed, *chunks)


def turns_kernel(chan_size, window, source_turns_ref, *refs):
    chunk_refs = refs[:chan_size]
    left_ref, pairs_ref = refs[-2:]
    me = lax.axis_index("chan")
    steps = chan_size // 2
    place = ring_place(me, chan_size)
    block = lax.broadcasted_iota(jnp.int32, (chan_size, EXTRA), 0)
    notes = jnp.zeros((chan_size, EXTRA), jnp.float32)
    for hop, ref in enumerate(chunk_refs):
        spot = place - hop if hop <= steps else place + hop - steps
        spot = jnp.where(spot < 0, spot + chan_size, spot)
        spot = jnp.where(spot >= chan_size, spot - chan_size, spot)
        owner = ring_block(spot, chan_size)
        notes = jnp.where(block == owner, ref[0][8:9, :].astype(jnp.float32), notes)
    lane = lax.broadcasted_iota(jnp.int32, notes.shape, 1)

    def total(index):
        value = jnp.where(lane == 2 * index, 32.0 * notes, 0.0)
        value = value + jnp.where(lane == 2 * index + 1, notes, 0.0)
        return jnp.broadcast_to(jnp.sum(value, axis=1, keepdims=True), notes.shape)

    left = jnp.where(block == 0, 0.0, pltpu.roll(total(0), 1, 0))
    right = jnp.where(block == chan_size - 1, 0.0, pltpu.roll(total(1), chan_size - 1, 0))
    aside = jnp.max(jnp.maximum(left, right)).astype(jnp.int32)
    whole_sum = jnp.max(left + right + total(2)).astype(jnp.int32)
    room = 2 * window
    needed = jnp.maximum((aside + window - 1) // window, (whole_sum + room - 1) // room)
    needed = jnp.maximum(needed, 1)
    pairs_ref[0] = needed
    left_ref[0] = needed * source_turns_ref[0] - 1


def count_turns(source_turns, chunks, window, after):
    _, _, width = chunks[0].shape
    last = width // EXTRA - 1
    specs = [pl.BlockSpec((1, PICK, EXTRA), lambda i: (1, 0, last)) for _ in chunks]
    return pl.pallas_call(
        functools.partial(turns_kernel, len(chunks), window),
        grid=(1,),
        out_shape=[jax.ShapeDtypeStruct((1,), jnp.int32)] * 2,
        in_specs=[pl.BlockSpec(memory_space=pltpu.SMEM), *specs]
        + [pl.BlockSpec(memory_space=pl.ANY)] * len(after),
        out_specs=[pl.BlockSpec(memory_space=pltpu.SMEM)] * 2,
        cost_estimate=light(),
        compiler_params=params(8),
        name="count_turns",
    )(source_turns, *chunks, *after)


def transform_kernel(shards, scale, start, chunks, src_ref, rec_ref, *refs):
    chunk_refs = refs[:chunks]
    cells_ref, cos_ref, sin_ref = refs[chunks : chunks + 3]
    keep_ref, send_ref, token_ref = refs[-3:]
    token_ref[...] = jnp.zeros_like(token_ref)
    rows = keep_ref.shape[1]
    bins = cos_ref.shape[0]
    step = min(TRANSFORM_STEP, bins)
    eighth = lax.broadcasted_iota(jnp.int32, (1, 128), 1) & 7
    root = math.sqrt(0.5)
    edge = jnp.where((eighth == 1) | (eighth == 7), root, 0.0)
    edge = jnp.where((eighth == 3) | (eighth == 5), -root, edge)
    edge = jnp.where(eighth == 0, 1.0, jnp.where(eighth == 4, -1.0, edge)) * scale
    edge = edge.astype(jnp.bfloat16).astype(jnp.float32)

    by_src = src_ref[pl.ds(start, rows), :]
    by_rec = rec_ref[pl.ds(start, rows), :]
    even = odd = corner = None
    for first in range(0, bins, step):
        lanes = pl.ds(first, step)
        source_real = jnp.concatenate([ref[0, :, lanes] for ref in chunk_refs], axis=0)
        source_imag = jnp.concatenate([ref[1, :, lanes] for ref in chunk_refs], axis=0)
        sr = jnp.dot(by_src, source_real, preferred_element_type=jnp.float32)
        si = jnp.dot(by_src, source_imag, preferred_element_type=jnp.float32)
        rr = jnp.dot(by_rec, cells_ref[0, :, lanes], preferred_element_type=jnp.float32)
        ri = jnp.dot(by_rec, cells_ref[1, :, lanes], preferred_element_type=jnp.float32)
        real = (sr * rr + si * ri).astype(jnp.bfloat16)
        imag = (si * rr - sr * ri).astype(jnp.bfloat16)
        more_even = jnp.dot(real, cos_ref[lanes, :], preferred_element_type=jnp.float32)
        more_odd = jnp.dot(imag, sin_ref[lanes, :], preferred_element_type=jnp.float32)
        wide = real.astype(jnp.float32)
        sums = wide[:, 0:128]
        for lane in range(128, step, 128):
            sums = sums + wide[:, lane : lane + 128]
        even = more_even if even is None else even + more_even
        odd = more_odd if odd is None else odd + more_odd
        corner = sums if corner is None else corner + sums

    me = lax.axis_index("seg")
    width = LAGS // shards
    corner = jnp.sum(corner * edge, axis=1, keepdims=True)
    first = lax.broadcasted_iota(jnp.int32, even.shape, 1) == 0
    later = even - jnp.where(first, 0.0, odd)
    sooner = jnp.where(first, corner, even) + odd
    sooner = pltpu.roll(sooner, HALF - 1, 1)
    for shard in range(shards):
        half = shards // 2
        if shard < half:
            lane = (half - 1 - shard) * width
            value = sooner[:, lane : lane + width]
        else:
            lane = (shard - half) * width
            value = later[:, lane : lane + width]
        place = me ^ shard

        @pl.when((place & 1) == 0)
        def _():
            keep_ref[place >> 1] = value

        @pl.when((place & 1) == 1)
        def _():
            send_ref[place >> 1] = value.astype(jnp.bfloat16)


def transform(picks, chunks, cells, tables, shards, scale, start, rows, weight, *after):
    width = LAGS // shards
    shape = (shards // 2, rows, width)
    vmem = pl.BlockSpec(memory_space=pltpu.VMEM)
    return pl.pallas_call(
        functools.partial(transform_kernel, shards, scale, start, len(chunks)),
        out_shape=(
            jax.ShapeDtypeStruct(shape, jnp.float32),
            jax.ShapeDtypeStruct(shape, jnp.bfloat16),
            TOKEN,
        ),
        in_specs=[vmem] * (5 + len(chunks))
        + [pl.BlockSpec(memory_space=pl.ANY)] * len(after),
        out_specs=(vmem, vmem, vmem),
        cost_estimate=weight,
        compiler_params=params(16),
        name="transform",
    )(*picks, *chunks, cells, *tables, *after)


def swap(send, bit):
    size = lax.axis_size("seg")
    return lax.ppermute(send, "seg", [(i, i ^ bit) for i in range(size)])


def halve(keep, got):
    total = keep + got.astype(jnp.float32)
    return total[0::2], total[1::2].astype(jnp.bfloat16)


def reduce_further(keep, got, bit):
    while keep.shape[0] > 1:
        keep, send = halve(keep, got)
        bit *= 2
        got = swap(send, bit)
    return (keep[0] + got[0].astype(jnp.float32)).astype(jnp.bfloat16)


def turned_parts(refs):
    width = refs[0].shape[1]
    flip = lax.axis_index("seg") < lax.axis_size("seg") // 2
    rows = lax.broadcasted_iota(jnp.int32, (width, width), 0)
    columns = lax.broadcasted_iota(jnp.int32, (width, width), 1)
    wanted = jnp.where(flip, width - 1 - rows, rows)
    turned = jnp.where(wanted == columns, 1.0, 0.0).astype(jnp.bfloat16)
    return [
        lax.dot_general(
            turned, ref[...], (((1,), (1,)), ((), ())), preferred_element_type=jnp.float32
        ).astype(jnp.bfloat16)
        for ref in refs
    ]


def place_kernel(place_ref, *refs):
    parts, (out_ref, later_ref) = refs[:-2], refs[-2:]
    slots = out_ref.shape[1]

    def chosen(start, count):
        spot = lax.broadcasted_iota(jnp.int32, (count, slots), 0) + start
        return jnp.where(spot == place_ref[0:1, :], 1.0, 0.0).astype(jnp.bfloat16)

    total = None
    start = 0
    for part in turned_parts(parts):
        count = part.shape[1]
        more = jnp.dot(part, chosen(start, count), preferred_element_type=jnp.float32)
        total = more if total is None else total + more
        start += count
    out_ref[...] = total
    later_ref[...] = chosen(start, later_ref.shape[0])


def place_rows(place, parts, later):
    width = parts[0].shape[1]
    slots = place.shape[1]
    vmem = pl.BlockSpec(memory_space=pltpu.VMEM)
    return pl.pallas_call(
        place_kernel,
        out_shape=(
            jax.ShapeDtypeStruct((width, slots), jnp.float32),
            jax.ShapeDtypeStruct((later, slots), jnp.bfloat16),
        ),
        in_specs=[vmem] * (1 + len(parts)),
        out_specs=(vmem, vmem),
        cost_estimate=light(),
        compiler_params=params(16),
        name="place_rows",
    )(place, *parts)


def add_kernel(total_ref, chosen_ref, *refs):
    parts, (out_ref, made_ref, sems) = refs[:-3], refs[-3:]
    slots = made_ref.shape[1]
    step = min(256, slots)
    across = jnp.concatenate(turned_parts(parts), axis=1)
    copies = []
    for index in range(slots // step):
        lanes = pl.ds(index * step, step)
        made_ref[:, lanes] = total_ref[:, lanes] + jnp.dot(
            across, chosen_ref[:, lanes], preferred_element_type=jnp.float32
        )
        copy = pltpu.make_async_copy(made_ref.at[:, lanes], out_ref.at[:, lanes], sems.at[index])
        copy.start()
        copies.append(copy)
    for copy in copies:
        copy.wait()


def add_rows(total, chosen, parts):
    width, slots = total.shape
    vmem = pl.BlockSpec(memory_space=pltpu.VMEM)
    return pl.pallas_call(
        add_kernel,
        out_shape=jax.ShapeDtypeStruct((width, slots), jnp.float32),
        in_specs=[vmem] * (2 + len(parts)),
        out_specs=pl.BlockSpec(memory_space=pltpu.HBM),
        scratch_shapes=[
            pltpu.VMEM((width, slots), jnp.float32),
            pltpu.SemaphoreType.DMA((slots // min(256, slots),)),
        ],
        cost_estimate=light(),
        compiler_params=params(16),
        name="add_rows",
    )(total, chosen, *parts)


def per_device(spectra, source_ids, pair_source, pair_offset, pair_counts):
    chan_rows = spectra.shape[1]
    bins = spectra.shape[3]
    seg_size = lax.axis_size("seg")
    chan_size = lax.axis_size("chan")
    slots = pair_source.shape[0]
    window = 3 * slots // 8
    scale = 1.0 / math.sqrt(bins * seg_size)
    join = lax.optimization_barrier

    ring = list(range(0, chan_size, 2)) + list(range(1, chan_size, 2))[::-1]
    ahead = [(ring[i], ring[(i + 1) % chan_size]) for i in range(chan_size)]
    back = [(b, a) for a, b in ahead]
    leftward = [(i + 1, i) for i in range(chan_size - 1)]
    rightward = [(i, i + 1) for i in range(chan_size - 1)]

    def one_turn(turns):
        first_rows = slots - 2 * window
        own = pick_rows(turns, pair_counts, source_ids, pair_source, pair_offset, spectra, first_rows)
        if turns is None:
            turns = jnp.zeros((2,), jnp.int32)
        forward, backward = [own], [own]
        steps = chan_size // 2

        def step_beside(work=None):
            ahead_of = forward[-1], backward[-1]
            forward.append(lax.ppermute(ahead_of[0], "chan", ahead))
            if len(backward) < chan_size - steps:
                backward.append(lax.ppermute(ahead_of[1], "chan", back))
            if work is not None:
                *results, token = work()
                if len(backward) == len(forward):
                    token, forward[-1], backward[-1] = join((token, forward[-1], backward[-1]))
                else:
                    token, forward[-1] = join((token, forward[-1]))
                return results, token

        tables, token = step_beside(lambda: lag_tables(bins, scale, own))
        cells = jnp.transpose(spectra[0], (1, 0, 2))
        (whitened,), token = step_beside(lambda: whiten_rows(cells, token))
        for _ in range(3, steps - 1):
            step_beside()
        picks, token = step_beside(
            lambda: prepare_early(turns, source_ids, own, chan_rows, chan_size, first_rows, token)
        )

        def piece(picks, chunks, start, rows, *after, weight=light()):
            return transform(
                picks, chunks, whitened, tables, seg_size, scale, start, rows, weight, *after
            )

        chunks = [*forward, own, *backward[1:]]
        full = pl.CostEstimate(
            flops=first_rows * bins * 4096, bytes_accessed=16 * bins * HALF, transcendentals=0
        )
        (keep_own, send), token = step_beside(
            lambda: piece(picks, chunks, 0, first_rows, token, weight=full)
        )
        chunks = forward + backward[1:]
        *picks, place, source_turns, send, token = prepare(
            turns, source_ids, chunks, slots, chan_rows, window, token, send
        )
        got_own = swap(send, 1)
        keep_left, send, token = piece(picks, chunks, 0, window, token)
        token, got_own = join((token, got_own))
        keep_own, send_own = halve(keep_own, got_own)
        got_left = swap(send, 1)
        got_own = swap(send_own, 2)
        keep_right, send, token = piece(picks, chunks, window, window, token, send_own)
        token, got_left, got_own = join((token, got_left, got_own))
        got_right = swap(send, 1)
        left = reduce_further(keep_left, got_left, 1)
        right = reduce_further(keep_right, got_right, 1)
        own = reduce_further(keep_own, got_own, 2)
        from_right = lax.ppermute(left, "chan", leftward)
        from_left = lax.ppermute(right, "chan", rightward)
        total, chosen = place_rows(place, (left, right, own), 2 * window)
        result = add_rows(total, chosen, (from_left, from_right))
        return result, (right, token), chunks, source_turns

    first, after, chunks, source_turns = one_turn(None)
    turns_left, pair_turns = [count[0] for count in count_turns(source_turns, chunks, window, after)]

    def further(state):
        turn, total = state
        turns = jnp.stack([lax.div(turn, pair_turns), lax.rem(turn, pair_turns)])
        return turn - 1, total + one_turn(turns)[0]

    return lax.while_loop(lambda state: state[0] > 0, further, (turns_left, first))[1]


def solution(mesh):
    in_specs = (P("seg", "chan", None, None), P(), P("chan"), P("chan"), P("chan"))
    out_specs = P("seg", "chan")
    return jax.shard_map(
        per_device, mesh=mesh, in_specs=in_specs, out_specs=out_specs, check_vma=False
    )
```

```python
import functools
import math

import jax
import jax.numpy as jnp
from jax import lax
from jax.experimental import pallas as pl
from jax.experimental.pallas import tpu as pltpu
from jax.sharding import PartitionSpec as P

LAGS = 1024
HALF = LAGS // 2
WBLOCK = 64
PICK = 16
BINS_STEP = 512
TRANSFORM_STEP = 256
TABLE_ROWS = 64
EXTRA = 128


def params(mebibytes):
    return pltpu.CompilerParams(vmem_limit_bytes=mebibytes * 1024 * 1024)


def light():
    return pl.CostEstimate(flops=1024, bytes_accessed=1024, transcendentals=0)


TOKEN = jax.ShapeDtypeStruct((8, 128), jnp.float32)


def whole(shape):
    return pl.BlockSpec(shape, lambda *_: (0,) * len(shape))


def ring_place(block, chan_size):
    return jnp.where((block & 1) == 0, block >> 1, chan_size - 1 - (block >> 1))


def ring_block(place, chan_size):
    return jnp.where(place < chan_size // 2, 2 * place, 2 * (chan_size - place) - 1)


def far_block(me, chan_size):
    place = ring_place(me, chan_size) - chan_size // 2
    return ring_block(jnp.where(place < 0, place + chan_size, place), chan_size)


def ring_hop(me, block, chan_size):
    steps = chan_size // 2
    distance = ring_place(me, chan_size) - ring_place(block, chan_size)
    distance = jnp.where(distance < 0, distance + chan_size, distance)
    return jnp.where(distance <= steps, distance, steps + chan_size - distance)


def pick_kernel(chan_rows, band, first_rows, *refs):
    counts_ref, ids_ref, source_ref, offset_ref, cells_ref, out_ref, rows_ref, held_ref, sems = refs[-9:]
    first = lax.axis_index("chan") * chan_rows
    turn = refs[0][0] if len(refs) > 9 else 0
    bins = cells_ref.shape[3]
    for i in range(PICK):
        rows_ref[i] = 0
    rank = jnp.int32(0)
    for i in range(ids_ref.shape[0]):
        row = ids_ref[i] - first
        mine = (row >= 0) & (row < chan_rows)
        spot = rank - turn * PICK
        rows_ref[jnp.where(mine & (spot >= 0) & (spot < PICK), spot, PICK)] = row
        rank = rank + mine.astype(jnp.int32)
    far = far_block(lax.axis_index("chan"), lax.axis_size("chan")) * chan_rows
    late = [jnp.int32(0), jnp.int32(0)]
    for i in range(ids_ref.shape[0]):
        row = ids_ref[i] - far
        late[i // 32] = late[i // 32] | (((row >= 0) & (row < chan_rows)).astype(jnp.int32) << (i % 32))
    copies = [
        pltpu.make_async_copy(cells_ref.at[0, rows_ref[i]], held_ref.at[i], sems.at[i])
        for i in range(PICK)
    ]
    for copy in copies:
        copy.start()

    offset = offset_ref[...]
    slot = lax.broadcasted_iota(jnp.int32, offset.shape, 0) * offset.shape[1]
    slot = slot + lax.broadcasted_iota(jnp.int32, offset.shape, 1)
    live = slot < counts_ref[...]
    source = source_ref[...]
    bits = jnp.where(source < 32, late[0], late[1])
    is_late = lax.shift_right_logical(bits, source & 31) & 1
    inside = live & (offset >= 0) & (offset < chan_rows)
    kinds = (live & (offset >= chan_rows), live & (offset < 0), inside, inside & (is_late == 0))
    lane = lax.broadcasted_iota(jnp.int32, offset.shape, 1)
    notes = jnp.zeros(offset.shape, jnp.int32)
    totals = [jnp.sum(jnp.where(kind, 1.0, 0.0)).astype(jnp.int32) for kind in kinds]
    totals = (totals[0], totals[1], totals[2] - jnp.minimum(totals[3], first_rows))
    for index, total in enumerate(totals):
        notes = jnp.where(lane == 2 * index, total >> 5, notes)
        notes = jnp.where(lane == 2 * index + 1, total & 31, notes)
    shifted = offset + band
    source = jnp.where(live, source + 1, 0)

    def coded(upper, lower):
        both = jnp.concatenate([upper.astype(jnp.float32), lower.astype(jnp.float32)], axis=0)
        return both.astype(jnp.bfloat16)

    out_ref[0, :, pl.ds(bins, EXTRA)] = coded(source, shifted >> 4)
    out_ref[1, :, pl.ds(bins, EXTRA)] = coded((shifted & 15) + 16 * is_late, notes)

    for copy in copies:
        copy.wait()
    real = held_ref[:, 0, :].astype(jnp.float32)
    imag = held_ref[:, 1, :].astype(jnp.float32)
    width = min(256, bins)

    def stacked(values):
        return jnp.concatenate([values[:, i : i + width] for i in range(0, bins, width)], axis=0)

    real, imag = whitened_pair(stacked(real), stacked(imag))
    for index in range(bins // width):
        lanes = pl.ds(index * width, width)
        out_ref[0, :, lanes] = real[index * PICK : (index + 1) * PICK]
        out_ref[1, :, lanes] = imag[index * PICK : (index + 1) * PICK]


def pick_rows(turns, counts, source_ids, pair_source, pair_offset, spectra, first_rows):
    _, chan_rows, parts, bins = spectra.shape
    smem = pl.BlockSpec(memory_space=pltpu.SMEM)
    vmem = pl.BlockSpec(memory_space=pltpu.VMEM)
    given = [] if turns is None else [turns]
    return pl.pallas_call(
        functools.partial(pick_kernel, chan_rows, chan_rows // 2, first_rows),
        out_shape=jax.ShapeDtypeStruct((parts, PICK, bins + EXTRA), spectra.dtype),
        in_specs=[smem] * len(given) + [vmem, smem, vmem, vmem, pl.BlockSpec(memory_space=pl.ANY)],
        out_specs=vmem,
        scratch_shapes=[
            pltpu.SMEM((PICK + 1,), jnp.int32),
            pltpu.VMEM((PICK, parts, bins), spectra.dtype),
            pltpu.SemaphoreType.DMA((PICK,)),
        ],
        cost_estimate=light(),
        compiler_params=params(8),
        name="pick_rows",
    )(
        *given,
        counts.reshape(1, 1),
        source_ids,
        pair_source.reshape(-1, EXTRA),
        pair_offset.reshape(-1, EXTRA),
        spectra,
    )


def block_mean(power):
    width = power.shape[1]
    row_group = lax.broadcasted_iota(jnp.int32, (width, width), 0) // WBLOCK
    col_group = lax.broadcasted_iota(jnp.int32, (width, width), 1) // WBLOCK
    spread = jnp.where(row_group == col_group, 1.0 / WBLOCK, 0.0).astype(jnp.bfloat16)
    high = power.astype(jnp.bfloat16)
    low = (power - high.astype(jnp.float32)).astype(jnp.bfloat16)
    total = jnp.dot(low, spread, preferred_element_type=jnp.float32)
    return total + jnp.dot(high, spread, preferred_element_type=jnp.float32)


def whitened_pair(real, imag):
    inverse = lax.rsqrt(block_mean(real * real + imag * imag) + 1e-06)
    return (real * inverse).astype(jnp.bfloat16), (imag * inverse).astype(jnp.bfloat16)


def whiten_kernel(cells_ref, after_ref, out_ref, token_ref):
    token_ref[...] = jnp.zeros_like(token_ref)
    for start in range(0, cells_ref.shape[2], 256):
        lanes = pl.ds(start, 256)
        real = cells_ref[0, :, lanes].astype(jnp.float32)
        imag = cells_ref[1, :, lanes].astype(jnp.float32)
        out_ref[0, :, lanes], out_ref[1, :, lanes] = whitened_pair(real, imag)


def whiten_rows(cells, after):
    _, rows, bins = cells.shape
    spec = pl.BlockSpec((2, rows, BINS_STEP), lambda i: (0, 0, i))
    return pl.pallas_call(
        whiten_kernel,
        grid=(bins // BINS_STEP,),
        out_shape=(jax.ShapeDtypeStruct(cells.shape, jnp.bfloat16), TOKEN),
        in_specs=[spec, pl.BlockSpec(memory_space=pl.ANY)],
        out_specs=(spec, whole(TOKEN.shape)),
        cost_estimate=light(),
        compiler_params=params(12),
        name="whiten_rows",
    )(cells, after)


def table_kernel(scale, all_bins, after_ref, cos_ref, sin_ref, token_ref, coarse_ref, fine_ref):
    token_ref[...] = jnp.zeros_like(token_ref)
    step = pl.program_id(0)
    groups = cos_ref.shape[0] // TABLE_ROWS

    @pl.when(step == 0)
    def _():
        def circle(ref, stride, factor):
            shape = ref.shape[1:]
            bins = lax.broadcasted_iota(jnp.int32, shape, 0) * stride
            lags = lax.broadcasted_iota(jnp.int32, shape, 1)
            lags = jnp.where(lags == 0, HALF, lags)
            theta = ((bins * lags) & (2 * all_bins - 1)).astype(jnp.float32) * (math.pi / all_bins)
            ref[0] = jnp.cos(theta) * factor
            ref[1] = jnp.sin(theta) * factor

        circle(coarse_ref, TABLE_ROWS, scale)
        circle(fine_ref, 1, 1.0)

    cos_b = fine_ref[0]
    sin_b = fine_ref[1]
    first = lax.broadcasted_iota(jnp.int32, cos_b.shape, 1) == 0
    for group in range(groups):
        cos_a = coarse_ref[0, pl.ds(step * groups + group, 1), :]
        sin_a = coarse_ref[1, pl.ds(step * groups + group, 1), :]
        rows = pl.ds(group * TABLE_ROWS, TABLE_ROWS)
        cos = jnp.where(first, scale, cos_a * cos_b - sin_a * sin_b)
        cos_ref[rows, :] = cos.astype(jnp.bfloat16)
        sin_ref[rows, :] = (sin_a * cos_b + cos_a * sin_b).astype(jnp.bfloat16)


def lag_tables(bins, scale, after):
    spec = pl.BlockSpec((BINS_STEP, HALF), lambda i: (i, 0))
    shape = jax.ShapeDtypeStruct((bins, HALF), jnp.bfloat16)
    return pl.pallas_call(
        functools.partial(table_kernel, scale, bins),
        grid=(bins // BINS_STEP,),
        out_shape=(shape, shape, TOKEN),
        in_specs=[pl.BlockSpec(memory_space=pl.ANY)],
        out_specs=(spec, spec, whole(TOKEN.shape)),
        scratch_shapes=[
            pltpu.VMEM((2, bins // TABLE_ROWS, HALF), jnp.float32),
            pltpu.VMEM((2, TABLE_ROWS, HALF), jnp.float32),
        ],
        cost_estimate=light(),
        compiler_params=params(12),
        name="lag_tables",
    )(after)


def source_spots(chan_rows, chan_size, me, turn, ids_row):
    count = ids_row.shape[1]
    shift = chan_rows.bit_length() - 1
    ids_row = jnp.broadcast_to(ids_row, (count, count))
    rows = lax.broadcasted_iota(jnp.int32, (count, count), 0)
    columns = lax.broadcasted_iota(jnp.int32, (count, count), 1)
    ids = jnp.sum(jnp.where(rows == columns, ids_row, 0).astype(jnp.float32), axis=1, keepdims=True)
    owner = jnp.broadcast_to(ids.astype(jnp.int32) >> shift, (count, count))
    earlier = (owner == (ids_row >> shift)) & (columns < rows)
    rank = jnp.sum(jnp.where(earlier, 1.0, 0.0), axis=1, keepdims=True)
    turns = (jnp.max(rank).astype(jnp.int32) + PICK) // PICK
    rank = rank.astype(jnp.int32) - turn * PICK
    owner = owner[:, 0:1]

    hop = ring_hop(me, owner, chan_size)
    return jnp.where((rank >= 0) & (rank < PICK), hop * PICK + rank, -1), turns


def flat(value):
    return jnp.concatenate([value[i : i + 1, :] for i in range(8)], axis=1)


def unlisted(halves, band):
    upper, lower = [half.astype(jnp.int32) for half in halves]
    return upper[0:8] - 1, upper[8:16] * 16 + (lower[0:8] & 15) - band, lower[0:8] >> 4


def ranked(taken):
    marks = jnp.concatenate([jnp.where(mask, 1.0, 0.0) for mask in taken], axis=0)
    rows = marks.shape[0]
    earlier = lax.broadcasted_iota(jnp.int32, (EXTRA, EXTRA), 0) < lax.broadcasted_iota(
        jnp.int32, (EXTRA, EXTRA), 1
    )
    rank = jnp.dot(
        marks.astype(jnp.bfloat16),
        jnp.where(earlier, 1.0, 0.0).astype(jnp.bfloat16),
        preferred_element_type=jnp.float32,
    )
    sums = jnp.broadcast_to(jnp.sum(marks, axis=1, keepdims=True), marks.shape)
    row = lax.broadcasted_iota(jnp.int32, (rows, rows), 0)
    column = lax.broadcasted_iota(jnp.int32, (rows, rows), 1)
    above_it = ((row >> 3) == (column >> 3)) & (column < row)
    rank = rank + jnp.dot(
        jnp.where(above_it, 1.0, 0.0).astype(jnp.bfloat16),
        sums.astype(jnp.bfloat16),
        preferred_element_type=jnp.float32,
    )
    rank = rank.astype(jnp.int32)
    return [rank[8 * i : 8 * i + 8] for i in range(len(taken))]


def jobs_of(spots, source, receiver, position, count):
    source, receiver, position = flat(source), flat(receiver), flat(position)
    slots = source.shape[1]
    names = lax.broadcasted_iota(jnp.int32, (spots.shape[0], slots), 0)
    field_row = lax.broadcasted_iota(jnp.int32, (8, slots), 0)
    spot = jnp.where(names == source, spots + 1, 0).astype(jnp.float32)
    spot = jnp.sum(spot, axis=0, keepdims=True).astype(jnp.int32) - 1
    fields = jnp.where(field_row == 0, spot >> 4, jnp.where(field_row == 1, spot & (PICK - 1), 0))
    fields = jnp.where(field_row == 2, receiver, jnp.where(field_row == 3, 1, fields))
    fields = jnp.where((position >= 0) & (spot >= 0), fields, 0)
    wanted = lax.broadcasted_iota(jnp.int32, (count, slots), 0)
    chosen = jnp.where(wanted == position, 1.0, 0.0).astype(jnp.bfloat16)
    return lax.dot_general(
        chosen,
        fields.astype(jnp.float32).astype(jnp.bfloat16),
        (((1,), (1,)), ((), ())),
        preferred_element_type=jnp.float32,
    )


def write_picks(jobs, start, src_ref, rec_ref):
    count = jobs.shape[0]
    jobs = jobs.astype(jnp.int32)
    busy = jobs[:, 3:4] > 0
    part = pl.ds(start, count)
    column = jnp.where(busy, jobs[:, 0:1] * PICK + jobs[:, 1:2], -1)
    lane = lax.broadcasted_iota(jnp.int32, (count, src_ref.shape[1]), 1)
    src_ref[part, :] = jnp.where(column == lane, 1.0, 0.0).astype(jnp.bfloat16)
    column = jnp.where(busy, jobs[:, 2:3], -1)
    lane = lax.broadcasted_iota(jnp.int32, (count, rec_ref.shape[1]), 1)
    rec_ref[part, :] = jnp.where(column == lane, 1.0, 0.0).astype(jnp.bfloat16)


def early_kernel(chan_rows, chan_size, turns_ref, ids_ref, after_ref, own_ref, src_ref, rec_ref, token_ref):
    token_ref[...] = jnp.zeros_like(token_ref)
    me = lax.axis_index("chan")
    count = src_ref.shape[0]
    lanes = pl.ds(own_ref.shape[2] - EXTRA, EXTRA)
    spots, _ = source_spots(chan_rows, chan_size, me, turns_ref[0], ids_ref[...])
    halves = [own_ref[half, :, lanes].astype(jnp.float32) for half in range(2)]
    source, offset, late = unlisted(halves, chan_rows // 2)
    early = (source >= 0) & (offset >= 0) & (offset < chan_rows) & (late == 0)
    (rank,) = ranked((early,))
    rank = jnp.where(early & (rank < count) & (turns_ref[1] == 0), rank, -1)
    write_picks(jobs_of(spots, source, offset, rank, count), 0, src_ref, rec_ref)


def prepare_early(turns, source_ids, own, chan_rows, chan_size, count, after):
    vmem = pl.BlockSpec(memory_space=pltpu.VMEM)
    return pl.pallas_call(
        functools.partial(early_kernel, chan_rows, chan_size),
        out_shape=(
            jax.ShapeDtypeStruct((count, chan_size * PICK), jnp.bfloat16),
            jax.ShapeDtypeStruct((count, chan_rows), jnp.bfloat16),
            TOKEN,
        ),
        in_specs=[
            pl.BlockSpec(memory_space=pltpu.SMEM), vmem, pl.BlockSpec(memory_space=pl.ANY), vmem,
        ],
        out_specs=(vmem, vmem, vmem),
        cost_estimate=light(),
        compiler_params=params(12),
        name="prepare_early",
    )(turns, source_ids.reshape(1, -1), after, own)


def prepare_kernel(chan_rows, chan_size, window, turns_ref, ids_ref, after_ref, passed_ref, *refs):
    chunk_refs = refs[:chan_size]
    src_ref, rec_ref, place_ref, needed_ref, _, token_ref = refs[chan_size:]
    token_ref[...] = jnp.zeros_like(token_ref)
    me = lax.axis_index("chan")
    turn = turns_ref[1]
    slots = place_ref.shape[1]
    room = 2 * window
    spots, needed = source_spots(chan_rows, chan_size, me, turns_ref[0], ids_ref[...])
    needed_ref[0] = needed

    lanes = pl.ds(chunk_refs[0].shape[2] - EXTRA, EXTRA)
    left_hop = jnp.where(me > 0, ring_hop(me, me - 1, chan_size), -1)
    right_hop = jnp.where(me < chan_size - 1, ring_hop(me, me + 1, chan_size), -1)
    listed = []
    for wanted in (left_hop, right_hop, 0):
        halves = []
        for half in range(2):
            value = jnp.zeros((PICK, EXTRA), jnp.float32)
            for hop, ref in enumerate(chunk_refs):
                value = jnp.where(wanted == hop, ref[half, :, lanes].astype(jnp.float32), value)
            halves.append(value)
        listed.append(unlisted(halves, chan_rows // 2))
    (left_src, left_off, _), (right_src, right_off, _), (own_src, own_off, own_late) = listed
    inside = (own_src >= 0) & (own_off >= 0) & (own_off < chan_rows)
    early = inside & (own_late == 0)
    taken = (
        (left_src >= 0) & (left_off >= chan_rows),
        (right_src >= 0) & (right_off < 0),
        (own_src >= 0) & (own_off < 0),
        (own_src >= 0) & (own_off >= chan_rows),
        inside,
        early,
    )
    ranks = ranked(taken)
    left_total = jnp.sum(jnp.where(taken[0], 1.0, 0.0)).astype(jnp.int32)
    right_total = jnp.sum(jnp.where(taken[1], 1.0, 0.0)).astype(jnp.int32)

    def done_before(amount, index):
        return jnp.minimum(amount, index * window)

    left_before = done_before(left_total, turn)
    right_before = done_before(right_total, turn)
    left_now = done_before(left_total, turn + 1) - left_before
    right_now = done_before(right_total, turn + 1) - right_before

    def in_window(index):
        shifted = ranks[index] - turn * window
        return shifted, taken[index] & (shifted >= 0) & (shifted < window)

    left_rank, left_ok = in_window(0)
    right_rank, right_ok = in_window(1)
    below_rank, below_ok = in_window(2)
    above_rank, above_ok = in_window(3)

    first = early & (ranks[5] < slots - room)
    own_rank = ranks[4] - jnp.minimum(ranks[5], slots - room)
    own_rank = own_rank - (turn * room - left_before - right_before)
    own_ok = inside & ~first & (own_rank >= 0) & (own_rank < room - left_now - right_now)
    own_pos = own_rank + left_now
    own_pos = jnp.where(own_pos < window, own_pos, own_pos + right_now)
    own_pos = jnp.where(own_ok, own_pos, -1)
    place = jnp.where(first & (turn == 0), ranks[5] + room, own_pos)
    place = jnp.where(below_ok, below_rank + slots, place)
    place = jnp.where(above_ok, above_rank + slots + window, place)
    place_ref[...] = jnp.broadcast_to(flat(place), place_ref.shape)

    left_jobs = jobs_of(spots, left_src, left_off - chan_rows, jnp.where(left_ok, left_rank, -1), window)
    right_jobs = jobs_of(
        spots, right_src, right_off + chan_rows, jnp.where(right_ok, right_rank, -1), window
    )
    own_jobs = jobs_of(spots, own_src, own_off, own_pos, room)
    write_picks(left_jobs + own_jobs[0:window], 0, src_ref, rec_ref)
    write_picks(right_jobs + own_jobs[window:room], window, src_ref, rec_ref)


def prepare(turns, source_ids, chunks, slots, chan_rows, window, after, passed):
    chan_size = len(chunks)
    vmem = pl.BlockSpec(memory_space=pltpu.VMEM)
    smem = pl.BlockSpec(memory_space=pltpu.SMEM)
    return pl.pallas_call(
        functools.partial(prepare_kernel, chan_rows, chan_size, window),
        out_shape=(
            jax.ShapeDtypeStruct((2 * window, chan_size * PICK), jnp.bfloat16),
            jax.ShapeDtypeStruct((2 * window, chan_rows), jnp.bfloat16),
            jax.ShapeDtypeStruct((8, slots), jnp.int32),
            jax.ShapeDtypeStruct((1,), jnp.int32),
            jax.ShapeDtypeStruct(passed.shape, passed.dtype),
            TOKEN,
        ),
        in_specs=[smem, vmem] + [pl.BlockSpec(memory_space=pl.ANY)] * 2 + [vmem] * len(chunks),
        out_specs=(vmem, vmem, vmem, smem, pl.BlockSpec(memory_space=pl.ANY), vmem),
        input_output_aliases={3: 4},
        cost_estimate=light(),
        compiler_params=params(16),
        name="prepare",
    )(turns, source_ids.reshape(1, -1), after, passed, *chunks)


def turns_kernel(chan_size, window, source_turns_ref, *refs):
    chunk_refs = refs[:chan_size]
    left_ref, pairs_ref = refs[-2:]
    me = lax.axis_index("chan")
    steps = chan_size // 2
    place = ring_place(me, chan_size)
    block = lax.broadcasted_iota(jnp.int32, (chan_size, EXTRA), 0)
    notes = jnp.zeros((chan_size, EXTRA), jnp.float32)
    for hop, ref in enumerate(chunk_refs):
        spot = place - hop if hop <= steps else place + hop - steps
        spot = jnp.where(spot < 0, spot + chan_size, spot)
        spot = jnp.where(spot >= chan_size, spot - chan_size, spot)
        owner = ring_block(spot, chan_size)
        notes = jnp.where(block == owner, ref[0][8:9, :].astype(jnp.float32), notes)
    lane = lax.broadcasted_iota(jnp.int32, notes.shape, 1)

    def total(index):
        value = jnp.where(lane == 2 * index, 32.0 * notes, 0.0)
        value = value + jnp.where(lane == 2 * index + 1, notes, 0.0)
        return jnp.broadcast_to(jnp.sum(value, axis=1, keepdims=True), notes.shape)

    left = jnp.where(block == 0, 0.0, pltpu.roll(total(0), 1, 0))
    right = jnp.where(block == chan_size - 1, 0.0, pltpu.roll(total(1), chan_size - 1, 0))
    aside = jnp.max(jnp.maximum(left, right)).astype(jnp.int32)
    whole_sum = jnp.max(left + right + total(2)).astype(jnp.int32)
    room = 2 * window
    needed = jnp.maximum((aside + window - 1) // window, (whole_sum + room - 1) // room)
    needed = jnp.maximum(needed, 1)
    pairs_ref[0] = needed
    left_ref[0] = needed * source_turns_ref[0] - 1


def count_turns(source_turns, chunks, window, after):
    _, _, width = chunks[0].shape
    last = width // EXTRA - 1
    specs = [pl.BlockSpec((1, PICK, EXTRA), lambda i: (1, 0, last)) for _ in chunks]
    return pl.pallas_call(
        functools.partial(turns_kernel, len(chunks), window),
        grid=(1,),
        out_shape=[jax.ShapeDtypeStruct((1,), jnp.int32)] * 2,
        in_specs=[pl.BlockSpec(memory_space=pltpu.SMEM), *specs]
        + [pl.BlockSpec(memory_space=pl.ANY)] * len(after),
        out_specs=[pl.BlockSpec(memory_space=pltpu.SMEM)] * 2,
        cost_estimate=light(),
        compiler_params=params(8),
        name="count_turns",
    )(source_turns, *chunks, *after)


def transform_kernel(shards, scale, start, chunks, src_ref, rec_ref, *refs):
    chunk_refs = refs[:chunks]
    cells_ref, cos_ref, sin_ref = refs[chunks : chunks + 3]
    keep_ref, send_ref, token_ref = refs[-3:]
    token_ref[...] = jnp.zeros_like(token_ref)
    rows = keep_ref.shape[1]
    bins = cos_ref.shape[0]
    step = min(TRANSFORM_STEP, bins)
    eighth = lax.broadcasted_iota(jnp.int32, (1, 128), 1) & 7
    root = math.sqrt(0.5)
    edge = jnp.where((eighth == 1) | (eighth == 7), root, 0.0)
    edge = jnp.where((eighth == 3) | (eighth == 5), -root, edge)
    edge = jnp.where(eighth == 0, 1.0, jnp.where(eighth == 4, -1.0, edge)) * scale
    edge = edge.astype(jnp.bfloat16).astype(jnp.float32)

    by_src = src_ref[pl.ds(start, rows), :]
    by_rec = rec_ref[pl.ds(start, rows), :]
    even = odd = corner = None
    for first in range(0, bins, step):
        lanes = pl.ds(first, step)
        source_real = jnp.concatenate([ref[0, :, lanes] for ref in chunk_refs], axis=0)
        source_imag = jnp.concatenate([ref[1, :, lanes] for ref in chunk_refs], axis=0)
        sr = jnp.dot(by_src, source_real, preferred_element_type=jnp.float32)
        si = jnp.dot(by_src, source_imag, preferred_element_type=jnp.float32)
        rr = jnp.dot(by_rec, cells_ref[0, :, lanes], preferred_element_type=jnp.float32)
        ri = jnp.dot(by_rec, cells_ref[1, :, lanes], preferred_element_type=jnp.float32)
        real = (sr * rr + si * ri).astype(jnp.bfloat16)
        imag = (si * rr - sr * ri).astype(jnp.bfloat16)
        more_even = jnp.dot(real, cos_ref[lanes, :], preferred_element_type=jnp.float32)
        more_odd = jnp.dot(imag, sin_ref[lanes, :], preferred_element_type=jnp.float32)
        wide = real.astype(jnp.float32)
        sums = wide[:, 0:128]
        for lane in range(128, step, 128):
            sums = sums + wide[:, lane : lane + 128]
        even = more_even if even is None else even + more_even
        odd = more_odd if odd is None else odd + more_odd
        corner = sums if corner is None else corner + sums

    me = lax.axis_index("seg")
    width = LAGS // shards
    corner = jnp.sum(corner * edge, axis=1, keepdims=True)
    first = lax.broadcasted_iota(jnp.int32, even.shape, 1) == 0
    later = even - jnp.where(first, 0.0, odd)
    sooner = jnp.where(first, corner, even) + odd
    sooner = pltpu.roll(sooner, HALF - 1, 1)
    for shard in range(shards):
        half = shards // 2
        if shard < half:
            lane = (half - 1 - shard) * width
            value = sooner[:, lane : lane + width]
        else:
            lane = (shard - half) * width
            value = later[:, lane : lane + width]
        place = me ^ shard

        @pl.when((place & 1) == 0)
        def _():
            keep_ref[place >> 1] = value

        @pl.when((place & 1) == 1)
        def _():
            send_ref[place >> 1] = value.astype(jnp.bfloat16)


def transform(picks, chunks, cells, tables, shards, scale, start, rows, weight, *after):
    width = LAGS // shards
    shape = (shards // 2, rows, width)
    vmem = pl.BlockSpec(memory_space=pltpu.VMEM)
    return pl.pallas_call(
        functools.partial(transform_kernel, shards, scale, start, len(chunks)),
        out_shape=(
            jax.ShapeDtypeStruct(shape, jnp.float32),
            jax.ShapeDtypeStruct(shape, jnp.bfloat16),
            TOKEN,
        ),
        in_specs=[vmem] * (5 + len(chunks))
        + [pl.BlockSpec(memory_space=pl.ANY)] * len(after),
        out_specs=(vmem, vmem, vmem),
        cost_estimate=weight,
        compiler_params=params(16),
        name="transform",
    )(*picks, *chunks, cells, *tables, *after)


def swap(send, bit):
    size = lax.axis_size("seg")
    return lax.ppermute(send, "seg", [(i, i ^ bit) for i in range(size)])


def halve(keep, got):
    total = keep + got.astype(jnp.float32)
    return total[0::2], total[1::2].astype(jnp.bfloat16)


def reduce_further(keep, got, bit):
    while keep.shape[0] > 1:
        keep, send = halve(keep, got)
        bit *= 2
        got = swap(send, bit)
    return (keep[0] + got[0].astype(jnp.float32)).astype(jnp.bfloat16)


def turned_parts(refs):
    width = refs[0].shape[1]
    flip = lax.axis_index("seg") < lax.axis_size("seg") // 2
    rows = lax.broadcasted_iota(jnp.int32, (width, width), 0)
    columns = lax.broadcasted_iota(jnp.int32, (width, width), 1)
    wanted = jnp.where(flip, width - 1 - rows, rows)
    turned = jnp.where(wanted == columns, 1.0, 0.0).astype(jnp.bfloat16)
    return [
        lax.dot_general(
            turned, ref[...], (((1,), (1,)), ((), ())), preferred_element_type=jnp.float32
        ).astype(jnp.bfloat16)
        for ref in refs
    ]


def place_kernel(place_ref, *refs):
    parts, (out_ref, later_ref) = refs[:-2], refs[-2:]
    slots = out_ref.shape[1]

    def chosen(start, count):
        spot = lax.broadcasted_iota(jnp.int32, (count, slots), 0) + start
        return jnp.where(spot == place_ref[0:1, :], 1.0, 0.0).astype(jnp.bfloat16)

    total = None
    start = 0
    for part in turned_parts(parts):
        count = part.shape[1]
        more = jnp.dot(part, chosen(start, count), preferred_element_type=jnp.float32)
        total = more if total is None else total + more
        start += count
    out_ref[...] = total
    later_ref[...] = chosen(start, later_ref.shape[0])


def place_rows(place, parts, later):
    width = parts[0].shape[1]
    slots = place.shape[1]
    vmem = pl.BlockSpec(memory_space=pltpu.VMEM)
    return pl.pallas_call(
        place_kernel,
        out_shape=(
            jax.ShapeDtypeStruct((width, slots), jnp.float32),
            jax.ShapeDtypeStruct((later, slots), jnp.bfloat16),
        ),
        in_specs=[vmem] * (1 + len(parts)),
        out_specs=(vmem, vmem),
        cost_estimate=light(),
        compiler_params=params(16),
        name="place_rows",
    )(place, *parts)


def add_kernel(total_ref, chosen_ref, *refs):
    parts, (out_ref, made_ref, sems) = refs[:-3], refs[-3:]
    slots = made_ref.shape[1]
    step = min(512, slots)
    across = jnp.concatenate(turned_parts(parts), axis=1)
    copies = []
    for index in range(slots // step):
        lanes = pl.ds(index * step, step)
        made_ref[:, lanes] = total_ref[:, lanes] + jnp.dot(
            across, chosen_ref[:, lanes], preferred_element_type=jnp.float32
        )
        copy = pltpu.make_async_copy(made_ref.at[:, lanes], out_ref.at[:, lanes], sems.at[index])
        copy.start()
        copies.append(copy)
    for copy in copies:
        copy.wait()


def add_rows(total, chosen, parts):
    width, slots = total.shape
    vmem = pl.BlockSpec(memory_space=pltpu.VMEM)
    return pl.pallas_call(
        add_kernel,
        out_shape=jax.ShapeDtypeStruct((width, slots), jnp.float32),
        in_specs=[vmem] * (2 + len(parts)),
        out_specs=pl.BlockSpec(memory_space=pltpu.HBM),
        scratch_shapes=[
            pltpu.VMEM((width, slots), jnp.float32),
            pltpu.SemaphoreType.DMA((slots // min(512, slots),)),
        ],
        cost_estimate=light(),
        compiler_params=params(16),
        name="add_rows",
    )(total, chosen, *parts)


def per_device(spectra, source_ids, pair_source, pair_offset, pair_counts):
    chan_rows = spectra.shape[1]
    bins = spectra.shape[3]
    seg_size = lax.axis_size("seg")
    chan_size = lax.axis_size("chan")
    slots = pair_source.shape[0]
    window = 3 * slots // 8
    scale = 1.0 / math.sqrt(bins * seg_size)
    join = lax.optimization_barrier

    ring = list(range(0, chan_size, 2)) + list(range(1, chan_size, 2))[::-1]
    ahead = [(ring[i], ring[(i + 1) % chan_size]) for i in range(chan_size)]
    back = [(b, a) for a, b in ahead]
    leftward = [(i + 1, i) for i in range(chan_size - 1)]
    rightward = [(i, i + 1) for i in range(chan_size - 1)]

    def one_turn(turns):
        first_rows = slots - 2 * window
        own = pick_rows(turns, pair_counts, source_ids, pair_source, pair_offset, spectra, first_rows)
        if turns is None:
            turns = jnp.zeros((2,), jnp.int32)
        forward, backward = [own], [own]
        steps = chan_size // 2

        def step_beside(work=None):
            ahead_of = forward[-1], backward[-1]
            forward.append(lax.ppermute(ahead_of[0], "chan", ahead))
            if len(backward) < chan_size - steps:
                backward.append(lax.ppermute(ahead_of[1], "chan", back))
            if work is not None:
                *results, token = work()
                if len(backward) == len(forward):
                    token, forward[-1], backward[-1] = join((token, forward[-1], backward[-1]))
                else:
                    token, forward[-1] = join((token, forward[-1]))
                return results, token

        tables, token = step_beside(lambda: lag_tables(bins, scale, own))
        cells = jnp.transpose(spectra[0], (1, 0, 2))
        (whitened,), token = step_beside(lambda: whiten_rows(cells, token))
        for _ in range(3, steps - 1):
            step_beside()
        picks, token = step_beside(
            lambda: prepare_early(turns, source_ids, own, chan_rows, chan_size, first_rows, token)
        )

        def piece(picks, chunks, start, rows, *after, weight=light()):
            return transform(
                picks, chunks, whitened, tables, seg_size, scale, start, rows, weight, *after
            )

        chunks = [*forward, own, *backward[1:]]
        full = pl.CostEstimate(
            flops=first_rows * bins * 4096, bytes_accessed=16 * bins * HALF, transcendentals=0
        )
        (keep_own, send), token = step_beside(
            lambda: piece(picks, chunks, 0, first_rows, token, weight=full)
        )
        chunks = forward + backward[1:]
        *picks, place, source_turns, send, token = prepare(
            turns, source_ids, chunks, slots, chan_rows, window, token, send
        )
        got_own = swap(send, 1)
        keep_left, send, token = piece(picks, chunks, 0, window, token)
        token, got_own = join((token, got_own))
        keep_own, send_own = halve(keep_own, got_own)
        got_left = swap(send, 1)
        got_own = swap(send_own, 2)
        keep_right, send, token = piece(picks, chunks, window, window, token, send_own)
        token, got_left, got_own = join((token, got_left, got_own))
        got_right = swap(send, 1)
        left = reduce_further(keep_left, got_left, 1)
        right = reduce_further(keep_right, got_right, 1)
        own = reduce_further(keep_own, got_own, 2)
        from_right = lax.ppermute(left, "chan", leftward)
        from_left = lax.ppermute(right, "chan", rightward)
        total, chosen = place_rows(place, (left, right, own), 2 * window)
        result = add_rows(total, chosen, (from_left, from_right))
        return result, (right, token), chunks, source_turns

    first, after, chunks, source_turns = one_turn(None)
    turns_left, pair_turns = [count[0] for count in count_turns(source_turns, chunks, window, after)]

    def further(state):
        turn, total = state
        turns = jnp.stack([lax.div(turn, pair_turns), lax.rem(turn, pair_turns)])
        return turn - 1, total + one_turn(turns)[0]

    return lax.while_loop(lambda state: state[0] > 0, further, (turns_left, first))[1]


def solution(mesh):
    in_specs = (P("seg", "chan", None, None), P(), P("chan"), P("chan"), P("chan"))
    out_specs = P("seg", "chan")
    return jax.shard_map(
        per_device, mesh=mesh, in_specs=in_specs, out_specs=out_specs, check_vma=False
    )
```
